32 devices in a mesh: dp: 16 (over z, y, x), tensor: 2 (over core).
Axes of the slice: x: 2, y: 2, z: 4, core: 2. Of those that a mesh axis runs over, the one named last changes fastest.
Arguments:
- tokens: bfloat16 [16384, 1024], P(('dp', 'tensor')), may hold values from -6 to 6
- cont_prompt: int32 [16], replicated, may hold values from 0 to 1
- routes: int32 [16384, 1], P(('dp', 'tensor')), may hold values from 0 to 15, as said below
- norm1_gain: bfloat16 [1024], P('dp'), may hold values from 0.5 to 1.5
- w_query: bfloat16 [1024, 1024], P('dp', 'tensor'), may hold values from -0.1875 to 0.1875
- w_key: bfloat16 [1024, 1024], P('dp', 'tensor'), may hold values from -0.1875 to 0.1875
- w_value: bfloat16 [1024, 1024], P('dp', 'tensor'), may hold values from -0.1875 to 0.1875
- w_attn_out: bfloat16 [1024, 1024], P('tensor', 'dp'), may hold values from -3 to 3
- norm2_gain: bfloat16 [1024], P('dp'), may hold values from 0.5 to 1.5
- w_ffn_in: bfloat16 [1024, 4096], P('dp', 'tensor'), may hold values from -0.1875 to 0.1875
- w_ffn_out: bfloat16 [4096, 1024], P('tensor', 'dp'), may hold values from -0.09375 to 0.09375
- centroids: bfloat16 [16, 1024], P('dp'), may hold values from -0.09375 to 0.09375
- expert_in_a: bfloat16 [16, 1024, 4096], P('dp', None, 'tensor'), may hold values from -0.1875 to 0.1875
- expert_out_a: bfloat16 [16, 4096, 1024], P('dp', 'tensor'), may hold values from -0.09375 to 0.09375
- expert_in_b: bfloat16 [16, 1024, 4096], P('dp', None, 'tensor'), may hold values from -0.1875 to 0.1875
- expert_out_b: bfloat16 [16, 4096, 1024], P('dp', 'tensor'), may hold values from -0.09375 to 0.09375
- grad_out: bfloat16 [16384, 1024], P(('dp', 'tensor')), may hold values from -6 to 6
Outputs:
- out: bfloat16 [16384, 1024], P(('dp', 'tensor'))
- grad_tokens: bfloat16 [16384, 1024], P(('dp', 'tensor'))
- grad_norm1_gain: float32 [1024], P('dp')
- grad_w_query: float32 [1024, 1024], P('dp', 'tensor')
- grad_w_key: float32 [1024, 1024], P('dp', 'tensor')
- grad_w_value: float32 [1024, 1024], P('dp', 'tensor')
- grad_w_attn_out: float32 [1024, 1024], P('tensor', 'dp')
- grad_norm2_gain: float32 [1024], P('dp')
- grad_w_ffn_in: float32 [1024, 4096], P('dp', 'tensor')
- grad_w_ffn_out: float32 [4096, 1024], P('tensor', 'dp')
- grad_centroids: float32 [16, 1024], P('dp')
- grad_expert_in_a: float32 [16, 1024, 4096], P('dp', None, 'tensor')
- grad_expert_out_a: float32 [16, 4096, 1024], P('dp', 'tensor')
- grad_expert_in_b: float32 [16, 1024, 4096], P('dp', None, 'tensor')
- grad_expert_out_b: float32 [16, 4096, 1024], P('dp', 'tensor')
The draws below stay inside these ranges and needn't reach their ends.
Inputs may be any that keep to these rules, and one draw needn't show every extreme that they name: Continuation j follows prompt cont_prompt[j]. `routes`: each row names one expert; among the 512 rows of one device at most 48 name the same expert, and in every draw some device has exactly 48 rows naming one expert.
All inputs are finite; a program needn't handle non-finite values.
Results may differ from the reference program's by a relative error of at most 0.03.
Values may be sent and summed in bfloat16 or wider, within the bound.
No kernel may reach another device: no remote copies, remote signals or barrier semaphores. Data moves between devices by JAX's collectives and lax.ppermute only.
A program may use at most 384 MiB of HBM per device.

```python
import jax
import jax.numpy as jnp
from jax import lax

D = 1024
HEADS = 16
HEAD = 64
FF = 4096
EFF = 4096
PLEN = 4096
CONT = 512
NPROMPT = 2
EXPERTS = 16
PRM_DEV = 512
ROWS_DP = 1024
ROWS_DEV = 512
TOKENS = 16384
CAP = 1280
SEND = 48
N_DP = 16


def draw_routes(key, part):
    key = jax.random.fold_in(key, 7)
    groups = (ROWS_DEV + SEND - 1) // SEND
    hot_count = max(groups - 1, EXPERTS // 2)
    order = jax.random.permutation(jax.random.fold_in(key, 1), EXPERTS).astype(jnp.int32)
    offset = jax.random.randint(jax.random.fold_in(key, 2), (), 0, EXPERTS, dtype=jnp.int32)
    row_ids = jnp.arange(TOKENS, dtype=jnp.int32)
    device = row_ids // ROWS_DEV
    group = row_ids % ROWS_DEV // SEND
    hot_pick = order[(device + offset + group - 1) % hot_count]
    cold_pick = order[hot_count + (device + offset) % (EXPERTS - hot_count)]
    route = jnp.where(group == 0, cold_pick, hot_pick)
    return route[:, None].astype(jnp.int32)


def touch_ends(drawn, rng, smallest, largest):
    spot = [jax.random.randint(jax.random.fold_in(rng, axis), (), 0, length) for axis, length in enumerate(drawn.shape)]
    main_axis = drawn.shape.index(max(drawn.shape))
    beside = spot[:main_axis] + [(spot[main_axis] + 1) % drawn.shape[main_axis]] + spot[main_axis + 1:]
    return drawn.at[tuple(spot)].set(smallest).at[tuple(beside)].set(largest)


def steps_of(rng, dims, split, low, top_value):
    loudness = 1.0
    for dim, blocks in split:
        heights = jax.random.uniform(jax.random.fold_in(jax.random.fold_in(rng, 6), dim), (blocks,), jnp.float32, low / len(split), top_value / len(split))
        loudness = loudness * jnp.repeat(jnp.exp(heights), dims[dim] // blocks).reshape((-1,) + (1,) * (len(dims) - 1 - dim))
    return loudness


def noise(stream_key, shape, width, reach, split=(), held_as=jnp.bfloat16):
    values = jax.random.normal(stream_key, shape, jnp.float32) * width
    if len(split) > 0:
        values = steps_of(stream_key, shape, split, -0.22, 0.18) * values
    return jnp.clip(values, min=-reach, max=reach).astype(held_as)


def setup_inputs(seed: int = 0) -> dict:
    splits = jax.random.split(jax.random.key(seed), 18)
    tokens = noise(splits[0], (TOKENS, D), 1.0, 6.0, ((0, 32),))
    cont_prompt = touch_ends(jax.random.randint(splits[1], (N_DP,), 0, NPROMPT), jax.random.fold_in(splits[1], 1), 0, NPROMPT - 1).astype(jnp.int32)
    routes = draw_routes(jax.random.fold_in(splits[17], 71), 0)
    norm1_gain = jnp.clip(1.0 + 0.1 * jax.random.normal(splits[3], (D,), jnp.float32), 0.5, 1.5).astype(jnp.bfloat16)
    w_query = noise(splits[4], (D, D), D ** -0.5, 0.1875, ((0, 16), (1, 2)))
    w_key = noise(splits[5], (D, D), D ** -0.5, 0.1875, ((0, 16), (1, 2)))
    w_value = noise(splits[6], (D, D), D ** -0.5, 0.1875, ((0, 16), (1, 2)))
    w_attn_out = noise(splits[7], (D, D), 4 ** -0.5, 3.0, ((0, 2), (1, 16)))
    norm2_gain = jnp.clip(1.0 + 0.1 * jax.random.normal(splits[8], (D,), jnp.float32), 0.5, 1.5).astype(jnp.bfloat16)
    w_ffn_in = noise(splits[9], (D, FF), D ** -0.5, 0.1875, ((0, 16), (1, 2)))
    w_ffn_out = noise(splits[10], (FF, D), FF ** -0.5, 0.09375, ((0, 2), (1, 16)))
    centroids = noise(splits[11], (EXPERTS, D), (4 * D) ** -0.5, 0.09375, ((0, 16),))
    expert_in_a = noise(splits[12], (EXPERTS, D, EFF), D ** -0.5, 0.1875, ((0, 16), (2, 2)))
    expert_out_a = noise(splits[13], (EXPERTS, EFF, D), EFF ** -0.5, 0.09375, ((0, 16), (1, 2)))
    expert_in_b = noise(splits[14], (EXPERTS, D, EFF), D ** -0.5, 0.1875, ((0, 16), (2, 2)))
    expert_out_b = noise(splits[15], (EXPERTS, EFF, D), EFF ** -0.5, 0.09375, ((0, 16), (1, 2)))
    grad_out = noise(splits[16], (TOKENS, D), 1.0, 6.0, ((0, 32),))
    return {"tokens": tokens, "cont_prompt": cont_prompt, "routes": routes, "norm1_gain": norm1_gain, "w_query": w_query, "w_key": w_key, "w_value": w_value, "w_attn_out": w_attn_out, "norm2_gain": norm2_gain, "w_ffn_in": w_ffn_in, "w_ffn_out": w_ffn_out, "centroids": centroids, "expert_in_a": expert_in_a, "expert_out_a": expert_out_a, "expert_in_b": expert_in_b, "expert_out_b": expert_out_b, "grad_out": grad_out}


@jax.custom_vjp
def low(v):
    return lax.optimization_barrier(v.astype(jnp.bfloat16)).astype(jnp.float32)

@jax.custom_vjp
def low_back(v):
    return v

def low_keep(v):
    return (low(v), None)

def low_pass(kept, grad):
    return (grad,)

def back_keep(v):
    return (v, None)

def back_low(kept, grad):
    return (low(grad),)
low.defvjp(low_keep, low_pass)
low_back.defvjp(back_keep, back_low)

def matmul(left, right):
    return jnp.dot(left, right, precision=lax.Precision.HIGHEST, preferred_element_type=jnp.float32)

def layer_norm(hidden, gain):
    mean_row = lax.optimization_barrier(jnp.mean(hidden, -1, keepdims=True))
    centred = hidden - mean_row
    return centred * lax.rsqrt(lax.optimization_barrier(jnp.mean(centred * centred, -1, keepdims=True)) + 1e-05) * gain

def attend(queries, keys, values, allowed):
    scores = low_back(jnp.einsum('qhd,khd->hqk', queries, keys, precision=lax.Precision.HIGHEST) * HEAD ** (-0.5))
    scores = jnp.where(allowed[None], scores, -1e+30)
    expo = jnp.exp(scores - lax.optimization_barrier(jnp.max(scores, -1, keepdims=True)))
    probs = expo / lax.optimization_barrier(jnp.sum(expo, -1, keepdims=True))
    return jnp.einsum('hqk,khd->qhd', low(probs), values, precision=lax.Precision.HIGHEST)

def prompt_block(pieces):
    queries, keys, values = pieces
    places = jnp.arange(PLEN)
    return attend(queries, keys, values, places[None, :] <= places[:, None])

def expert_block(pieces):
    rows, centre, in_a, out_a, in_b, out_b = pieces
    gate_value = jax.nn.sigmoid(matmul(rows, centre))
    branch_a = low_back(matmul(low(jax.nn.gelu(low_back(matmul(rows, in_a)))), out_a))
    middle = low(rows + branch_a)
    branch_b = low_back(matmul(low(jax.nn.gelu(low_back(matmul(middle, in_b)))), out_b))
    return low_back(low(gate_value[:, None] * (branch_a + branch_b)))

def reference(tokens, cont_prompt, routes, norm1_gain, w_query, w_key, w_value, w_attn_out, norm2_gain, w_ffn_in, w_ffn_out, centroids, expert_in_a, expert_out_a, expert_in_b, expert_out_b, grad_out):
    route = routes[:, 0].astype(jnp.int32)
    onehot = (route[:, None] == jnp.arange(EXPERTS, dtype=jnp.int32)[None, :]).astype(jnp.int32)
    ranks = lax.optimization_barrier(jnp.sum((jnp.cumsum(onehot, 0) - 1) * onehot, 1)).astype(jnp.int32)
    place = jnp.where(ranks < CAP, route * CAP + ranks, EXPERTS * CAP).astype(jnp.int32)
    weights = tuple((item.astype(jnp.float32) for item in (norm1_gain, w_query, w_key, w_value, w_attn_out, norm2_gain, w_ffn_in, w_ffn_out, centroids, expert_in_a, expert_out_a, expert_in_b, expert_out_b)))

    def forward(inputs, params):
        gain_one, query_w, key_w, value_w, attn_w, gain_two, ffn_in, ffn_out, centres, in_a, out_a, in_b, out_b = params
        normed = low(layer_norm(inputs, gain_one))
        head_shape = (N_DP, ROWS_DP, HEADS, HEAD)
        queries = low_back(low(matmul(normed, query_w))).reshape(head_shape)
        keys = low_back(low(matmul(normed, key_w))).reshape(head_shape)
        values = low_back(low(matmul(normed, value_w))).reshape(head_shape)
        prompt_shape = (NPROMPT, PLEN, HEADS, HEAD)
        keys_prompt = keys[:, :PRM_DEV].reshape(prompt_shape)
        values_prompt = values[:, :PRM_DEV].reshape(prompt_shape)
        prompt_out = lax.map(jax.checkpoint(prompt_block), (queries[:, :PRM_DEV].reshape(prompt_shape), keys_prompt, values_prompt))

        def cont_block(pieces):
            cont_q, cont_k, cont_v, which = pieces
            prompt_k = lax.dynamic_index_in_dim(keys_prompt, which, 0, keepdims=False)
            prompt_v = lax.dynamic_index_in_dim(values_prompt, which, 0, keepdims=False)
            places = jnp.arange(CONT)
            allowed = jnp.concatenate([jnp.ones((CONT, PLEN), jnp.bool_), places[None, :] <= places[:, None]], 1)
            return attend(cont_q, jnp.concatenate([prompt_k, cont_k], 0), jnp.concatenate([prompt_v, cont_v], 0), allowed)
        cont_out = lax.map(jax.checkpoint(cont_block), (queries[:, PRM_DEV:], keys[:, PRM_DEV:], values[:, PRM_DEV:], cont_prompt))
        attended = jnp.concatenate([prompt_out.reshape(N_DP, PRM_DEV, D), cont_out.reshape(N_DP, CONT, D)], 1).reshape(TOKENS, D)
        attended = low_back(low(attended))
        hidden_one = inputs + low_back(matmul(attended, attn_w))
        normed_two = low(layer_norm(hidden_one, gain_two))
        ffn_act = low(jax.nn.gelu(low_back(matmul(normed_two, ffn_in))))
        hidden_two = hidden_one + low_back(matmul(ffn_act, ffn_out))
        expert_in = low_back(low(hidden_two))
        buffer = jnp.zeros((EXPERTS * CAP + 1, D), jnp.float32).at[place].add(expert_in)
        results = lax.map(jax.checkpoint(expert_block), (buffer[:-1].reshape(EXPERTS, CAP, D), centres, in_a, out_a, in_b, out_b))
        padded = jnp.concatenate([results.reshape(EXPERTS * CAP, D), jnp.zeros((1, D), jnp.float32)], 0)
        return hidden_two + padded[place]
    result, pull = jax.vjp(forward, tokens.astype(jnp.float32), weights)
    grad_inputs, grads = pull(grad_out.astype(jnp.float32))
    return (result.astype(jnp.bfloat16), grad_inputs.astype(jnp.bfloat16), grads[0], grads[1], grads[2], grads[3], grads[4], grads[5], grads[6], grads[7], grads[8], grads[9], grads[10], grads[11], grads[12])
```

```python
import functools

import jax
import jax.numpy as jnp
from jax import lax
from jax.experimental import pallas as pl
from jax.experimental.pallas import tpu as pltpu
from jax.sharding import PartitionSpec as P

HEAD = 64
PLEN = 4096
CONT = 512


def shortened(value):

    def short(part):
        return part.astype(jnp.bfloat16) if part.dtype == jnp.float32 else part

    return jax.tree.map(short, value)


def carried_in(value, axis, combine, identity):
    peers, place = (lax.axis_size(axis), lax.axis_index(axis))
    everything = lax.all_gather(value, axis)
    start = jnp.broadcast_to(jnp.asarray(identity, value.dtype), value.shape)

    def turn(k, before):
        reached = k < place
        new = combine(before, everything[k])
        return jnp.where(reached, new, before)

    return lax.fori_loop(0, peers, turn, start)


def rows_gather(value):
    return lax.all_gather(value, "tensor", axis=0, tiled=True)


def rows_scatter(value):
    return lax.psum_scatter(
        value.astype(jnp.bfloat16), "tensor", scatter_dimension=0, tiled=True
    ).astype(jnp.float32)


def pair_total(value):
    return jax.tree.map(lambda part: part.astype(jnp.float32), lax.psum(shortened(value), "tensor"))


def to_experts(value):
    return lax.all_to_all(value, "dp", split_axis=0, concat_axis=0, tiled=True)


def matmul(left, right):
    return jnp.dot(left, right, preferred_element_type=jnp.float32)


def matmul_tn(left, right):
    return lax.dot_general(
        left, right, (((0,), (0,)), ((), ())), preferred_element_type=jnp.float32
    )


def matmul_nt(left, right):
    return lax.dot_general(
        left, right, (((1,), (1,)), ((), ())), preferred_element_type=jnp.float32
    )


def norm_forward(hidden, gain):
    mean_row = jnp.mean(hidden, -1, keepdims=True)
    centred = hidden - mean_row
    scale_inv = lax.rsqrt(jnp.mean(centred * centred, -1, keepdims=True) + 1e-05)
    normed = centred * scale_inv
    return (normed * gain, normed, scale_inv)


def norm_backward(grad_m, normed, scale_inv, gain):
    grad_hat = grad_m * gain
    inner = (
        grad_hat
        - jnp.mean(grad_hat, -1, keepdims=True)
        - normed * jnp.mean(grad_hat * normed, -1, keepdims=True)
    )
    return (inner * scale_inv, jnp.sum(grad_m * normed, 0))


def gelu_grad(preact, grad):
    unused, pull = jax.vjp(jax.nn.gelu, preact)
    return pull(grad)[0]


def add_counts(first, second):
    return first + second


def attend(queries, keys, values, allowed, heads):
    scale = HEAD ** (-0.5)

    def head_step(head, carry):
        outputs, log_sums = carry
        query_h = lax.dynamic_slice_in_dim(queries, head * HEAD, HEAD, 1)
        key_h = lax.dynamic_slice_in_dim(keys, head * HEAD, HEAD, 1)
        value_h = lax.dynamic_slice_in_dim(values, head * HEAD, HEAD, 1)
        scores = jnp.where(allowed, matmul_nt(query_h, key_h) * scale, -1e30)
        top_score = jnp.max(scores, 1, keepdims=True)
        expo = jnp.exp(scores - top_score)
        total = jnp.sum(expo, 1, keepdims=True)
        probs = (expo / total).astype(jnp.bfloat16)
        outputs = lax.dynamic_update_slice_in_dim(outputs, matmul(probs, value_h), head * HEAD, 1)
        log_sums = lax.dynamic_update_index_in_dim(
            log_sums, top_score[:, 0] + jnp.log(total[:, 0]), head, 0
        )
        return (outputs, log_sums)

    start_state = (
        jnp.zeros((queries.shape[0], heads * HEAD), jnp.float32),
        jnp.zeros((heads, queries.shape[0]), jnp.float32),
    )
    return lax.fori_loop(0, heads, head_step, start_state)


def attend_back(queries, keys, values, allowed, log_sums, grad_attended, heads):
    scale = HEAD ** (-0.5)

    def head_step(head, carry):
        grad_q, grad_k, grad_v = carry
        query_h = lax.dynamic_slice_in_dim(queries, head * HEAD, HEAD, 1)
        key_h = lax.dynamic_slice_in_dim(keys, head * HEAD, HEAD, 1)
        value_h = lax.dynamic_slice_in_dim(values, head * HEAD, HEAD, 1)
        grad_o = lax.dynamic_slice_in_dim(grad_attended, head * HEAD, HEAD, 1)
        scores = jnp.where(allowed, matmul_nt(query_h, key_h) * scale, -1e30)
        probs = jnp.exp(
            scores - lax.dynamic_index_in_dim(log_sums, head, 0, keepdims=False)[:, None]
        )
        grad_p = matmul_nt(grad_o, value_h)
        grad_s = (probs * (grad_p - jnp.sum(probs * grad_p, 1, keepdims=True))).astype(jnp.bfloat16)
        grad_q = lax.dynamic_update_slice_in_dim(
            grad_q, matmul(grad_s, key_h) * scale, head * HEAD, 1
        )
        grad_k = lax.dynamic_update_slice_in_dim(
            grad_k, matmul_tn(grad_s, query_h) * scale, head * HEAD, 1
        )
        grad_v = lax.dynamic_update_slice_in_dim(
            grad_v, matmul_tn(probs.astype(jnp.bfloat16), grad_o), head * HEAD, 1
        )
        return (grad_q, grad_k, grad_v)

    start_state = (
        jnp.zeros(queries.shape, jnp.float32),
        jnp.zeros(keys.shape, jnp.float32),
        jnp.zeros(values.shape, jnp.float32),
    )
    return lax.fori_loop(0, heads, head_step, start_state)


def add_block(buffer, block, start):
    length = block.shape[0]
    current = lax.dynamic_slice_in_dim(buffer, start, length, 0)
    return lax.dynamic_update_slice_in_dim(buffer, current + block, start, 0)


def body_general(
    tokens,
    cont_prompt,
    routes,
    norm1_gain,
    w_query,
    w_key,
    w_value,
    w_attn_out,
    norm2_gain,
    w_ffn_in,
    w_ffn_out,
    centroids,
    expert_in_a,
    expert_out_a,
    expert_in_b,
    expert_out_b,
    grad_out,
):
    experts = lax.axis_size("dp")
    pair_size = lax.axis_size("tensor")
    dp_index = lax.axis_index("dp")
    tensor_index = lax.axis_index("tensor")
    rows_dev = tokens.shape[0]
    rows_dp = rows_dev * pair_size
    prm_dev = rows_dp - CONT
    pkeys = experts * prm_dev
    heads = w_query.shape[1] // HEAD
    width = tokens.shape[1]
    span = PLEN // prm_dev
    owner_start = dp_index // span * PLEN
    mapped_start = cont_prompt[dp_index] * PLEN
    gain_one, query_full, key_full, value_full, attn_full, gain_two, ffn_in_full, ffn_out_full = (
        lax.all_gather(norm1_gain, "dp", axis=0, tiled=True),
        lax.all_gather(w_query, "dp", axis=0, tiled=True),
        lax.all_gather(w_key, "dp", axis=0, tiled=True),
        lax.all_gather(w_value, "dp", axis=0, tiled=True),
        lax.all_gather(w_attn_out, "dp", axis=1, tiled=True),
        lax.all_gather(norm2_gain, "dp", axis=0, tiled=True),
        lax.all_gather(w_ffn_in, "dp", axis=0, tiled=True),
        lax.all_gather(w_ffn_out, "dp", axis=1, tiled=True),
    )
    inputs = tokens.astype(jnp.float32)
    normed_one, hat_one, inv_one = norm_forward(inputs, gain_one.astype(jnp.float32))
    rows_one = rows_gather(normed_one.astype(jnp.bfloat16))
    queries = matmul(rows_one, query_full).astype(jnp.bfloat16)
    keys_own = matmul(rows_one, key_full).astype(jnp.bfloat16)
    values_own = matmul(rows_one, value_full).astype(jnp.bfloat16)
    prompt_keys, prompt_values = (
        lax.all_gather(keys_own[:prm_dev], "dp", axis=0, tiled=True),
        lax.all_gather(values_own[:prm_dev], "dp", axis=0, tiled=True),
    )
    keys_first = lax.dynamic_slice_in_dim(prompt_keys, owner_start, PLEN, 0)
    values_first = lax.dynamic_slice_in_dim(prompt_values, owner_start, PLEN, 0)
    first_row = lax.broadcasted_iota(jnp.int32, (prm_dev, 1), 0)
    first_column = lax.broadcasted_iota(jnp.int32, (1, PLEN), 1)
    allowed_first = first_column <= dp_index % span * prm_dev + first_row
    keys_second = jnp.concatenate(
        [lax.dynamic_slice_in_dim(prompt_keys, mapped_start, PLEN, 0), keys_own[prm_dev:]], 0
    )
    values_second = jnp.concatenate(
        [lax.dynamic_slice_in_dim(prompt_values, mapped_start, PLEN, 0), values_own[prm_dev:]], 0
    )
    second_row = lax.broadcasted_iota(jnp.int32, (CONT, 1), 0)
    second_column = lax.broadcasted_iota(jnp.int32, (1, PLEN + CONT), 1)
    allowed_second = (second_column < PLEN) | (second_column - PLEN <= second_row)
    attn_first, sums_first = attend(
        queries[:prm_dev], keys_first, values_first, allowed_first, heads
    )
    attn_second, sums_second = attend(
        queries[prm_dev:], keys_second, values_second, allowed_second, heads
    )
    attn_low = jnp.concatenate([attn_first, attn_second], 0).astype(jnp.bfloat16)
    hidden_one = inputs + rows_scatter(matmul(attn_low, attn_full))
    normed_two, hat_two, inv_two = norm_forward(hidden_one, gain_two.astype(jnp.float32))
    rows_two = rows_gather(normed_two.astype(jnp.bfloat16))
    ffn_pre = matmul(rows_two, ffn_in_full)
    ffn_act = jax.nn.gelu(ffn_pre).astype(jnp.bfloat16)
    hidden_two = hidden_one + rows_scatter(matmul(ffn_act, ffn_out_full))
    route = routes[:, 0]
    slots_per = max(2, (3 * rows_dev + 2 * experts - 1) // (2 * experts))
    capacity = 5 * rows_dp // 4
    expert_ids = lax.broadcasted_iota(jnp.int32, (1, experts), 1)
    onehot = (route[:, None] == expert_ids).astype(jnp.int32)
    offsets = carried_in(
        jnp.sum(onehot, 0), ("dp", "tensor"), add_counts, jnp.zeros((experts,), jnp.int32)
    )
    local_rank = jnp.sum((jnp.cumsum(onehot, 0) - 1) * onehot, 1)
    global_slot = local_rank + jnp.sum(onehot * offsets[None, :], 1)
    kept = global_slot < capacity
    target = route * slots_per + local_rank
    columns = lax.broadcasted_iota(jnp.int32, (1, experts * slots_per), 1)
    placer = ((columns == target[:, None]) & kept[:, None]).astype(jnp.bfloat16)
    sent_rows = (
        matmul_tn(placer, hidden_two.astype(jnp.bfloat16))
        .astype(jnp.bfloat16)
        .reshape(experts, slots_per, width)
    )
    expert_rows = rows_gather(to_experts(sent_rows)).reshape(-1, width)
    centre = centroids[0]
    gate_value = jax.nn.sigmoid(matmul(expert_rows, centre))
    pre_a = matmul(expert_rows, expert_in_a[0])
    act_a = jax.nn.gelu(pre_a).astype(jnp.bfloat16)
    branch_a = pair_total(matmul(act_a, expert_out_a[0]))
    middle = (expert_rows.astype(jnp.float32) + branch_a).astype(jnp.bfloat16)
    pre_b = matmul(middle, expert_in_b[0])
    act_b = jax.nn.gelu(pre_b).astype(jnp.bfloat16)
    branch_b = rows_scatter(matmul(act_b, expert_out_b[0]))
    half_rows = expert_rows.shape[0] // pair_size
    start_row = tensor_index * half_rows
    branch_half = lax.dynamic_slice_in_dim(branch_a, start_row, half_rows, 0) + branch_b
    gate_half = lax.dynamic_slice_in_dim(gate_value, start_row, half_rows, 0)
    returned = (
        (gate_half[:, None] * branch_half).astype(jnp.bfloat16).reshape(experts, slots_per, width)
    )
    came_back = to_experts(returned).reshape(experts * slots_per, width)
    output = hidden_two + matmul(placer, came_back)
    cotangent = grad_out.astype(jnp.float32)
    sent_grad = matmul_tn(placer, grad_out).astype(jnp.bfloat16).reshape(experts, slots_per, width)
    grad_half = to_experts(sent_grad).reshape(half_rows, width)
    grad_returned = rows_gather(grad_half).astype(jnp.float32)
    grad_gate_half = jnp.sum(grad_half.astype(jnp.float32) * branch_half, 1)
    grad_logit_half = grad_gate_half * gate_half * (1.0 - gate_half)
    rows_half = lax.dynamic_slice_in_dim(expert_rows, start_row, half_rows, 0)
    centre_part = matmul(grad_logit_half, rows_half.astype(jnp.float32))
    grad_branch = gate_value[:, None] * grad_returned
    grad_b = grad_branch.astype(jnp.bfloat16)
    grad_pre_b = gelu_grad(pre_b, matmul_nt(grad_b, expert_out_b[0])).astype(jnp.bfloat16)
    grad_out_b = matmul_tn(act_b, grad_b)
    grad_in_b = matmul_tn(middle, grad_pre_b)
    grad_middle = pair_total(matmul_nt(grad_pre_b, expert_in_b[0]))
    grad_a = (grad_branch + grad_middle).astype(jnp.bfloat16)
    grad_pre_a = gelu_grad(pre_a, matmul_nt(grad_a, expert_out_a[0])).astype(jnp.bfloat16)
    grad_out_a = matmul_tn(act_a, grad_a)
    grad_in_a = matmul_tn(expert_rows, grad_pre_a)
    grad_rows = (
        rows_scatter(matmul_nt(grad_pre_a, expert_in_a[0]))
        + lax.dynamic_slice_in_dim(grad_middle, start_row, half_rows, 0)
        + grad_logit_half[:, None] * centre.astype(jnp.float32)[None, :]
    )
    grad_back = to_experts(
        grad_rows.astype(jnp.bfloat16).reshape(experts, slots_per, width)
    ).reshape(experts * slots_per, width)
    grad_two = cotangent + matmul(placer, grad_back)
    gain_one, query_full, key_full, value_full, attn_full, gain_two, ffn_in_full, ffn_out_full = (
        lax.all_gather(norm1_gain, "dp", axis=0, tiled=True),
        lax.all_gather(w_query, "dp", axis=0, tiled=True),
        lax.all_gather(w_key, "dp", axis=0, tiled=True),
        lax.all_gather(w_value, "dp", axis=0, tiled=True),
        lax.all_gather(w_attn_out, "dp", axis=1, tiled=True),
        lax.all_gather(norm2_gain, "dp", axis=0, tiled=True),
        lax.all_gather(w_ffn_in, "dp", axis=0, tiled=True),
        lax.all_gather(w_ffn_out, "dp", axis=1, tiled=True),
    )
    rows_down = rows_gather(grad_two.astype(jnp.bfloat16))
    grad_ffn_pre = gelu_grad(ffn_pre, matmul_nt(rows_down, ffn_out_full)).astype(jnp.bfloat16)
    grad_ffn_out = matmul_tn(ffn_act, rows_down)
    grad_ffn_in = matmul_tn(rows_two, grad_ffn_pre)
    grad_norm_two = rows_scatter(matmul_nt(grad_ffn_pre, ffn_in_full))
    back_two, grad_gain_two = norm_backward(
        grad_norm_two, hat_two, inv_two, gain_two.astype(jnp.float32)
    )
    grad_one = grad_two + back_two
    rows_attn = rows_gather(grad_one.astype(jnp.bfloat16))
    grad_attn_out = matmul_tn(attn_low, rows_attn)
    grad_attended = matmul_nt(rows_attn, attn_full).astype(jnp.bfloat16)
    grad_q_first, grad_k_first, grad_v_first = attend_back(
        queries[:prm_dev],
        keys_first,
        values_first,
        allowed_first,
        sums_first,
        grad_attended[:prm_dev],
        heads,
    )
    grad_q_second, grad_k_second, grad_v_second = attend_back(
        queries[prm_dev:],
        keys_second,
        values_second,
        allowed_second,
        sums_second,
        grad_attended[prm_dev:],
        heads,
    )
    local_width = keys_own.shape[1]
    buffer_k = jnp.zeros((pkeys, local_width), jnp.float32)
    buffer_v = jnp.zeros((pkeys, local_width), jnp.float32)
    buffer_k = add_block(
        add_block(buffer_k, grad_k_first, owner_start), grad_k_second[:PLEN], mapped_start
    )
    buffer_v = add_block(
        add_block(buffer_v, grad_v_first, owner_start), grad_v_second[:PLEN], mapped_start
    )
    prompt_grad_k, prompt_grad_v = (
        lax.psum_scatter(buffer_k, "dp", scatter_dimension=0, tiled=True),
        lax.psum_scatter(buffer_v, "dp", scatter_dimension=0, tiled=True),
    )
    grad_keys = jnp.concatenate([prompt_grad_k, grad_k_second[PLEN:]], 0).astype(jnp.bfloat16)
    grad_values = jnp.concatenate([prompt_grad_v, grad_v_second[PLEN:]], 0).astype(jnp.bfloat16)
    grad_queries = jnp.concatenate([grad_q_first, grad_q_second], 0).astype(jnp.bfloat16)
    grad_query = matmul_tn(rows_one, grad_queries)
    grad_key = matmul_tn(rows_one, grad_keys)
    grad_value = matmul_tn(rows_one, grad_values)
    grad_norm_one = rows_scatter(
        matmul_nt(grad_queries, query_full)
        + matmul_nt(grad_keys, key_full)
        + matmul_nt(grad_values, value_full)
    )
    back_one, grad_gain_one = norm_backward(
        grad_norm_one, hat_one, inv_one, gain_one.astype(jnp.float32)
    )
    grad_input = grad_one + back_one
    (
        gain_one_part,
        query_shard,
        key_shard,
        value_shard,
        attn_shard,
        gain_two_part,
        ffn_in_shard,
        ffn_out_shard,
    ) = (
        lax.psum_scatter(grad_gain_one, "dp", scatter_dimension=0, tiled=True),
        lax.psum_scatter(grad_query, "dp", scatter_dimension=0, tiled=True),
        lax.psum_scatter(grad_key, "dp", scatter_dimension=0, tiled=True),
        lax.psum_scatter(grad_value, "dp", scatter_dimension=0, tiled=True),
        lax.psum_scatter(grad_attn_out, "dp", scatter_dimension=1, tiled=True),
        lax.psum_scatter(grad_gain_two, "dp", scatter_dimension=0, tiled=True),
        lax.psum_scatter(grad_ffn_in, "dp", scatter_dimension=0, tiled=True),
        lax.psum_scatter(grad_ffn_out, "dp", scatter_dimension=1, tiled=True),
    )
    gain_one_shard, gain_two_shard, centre_grad = pair_total(
        (gain_one_part, gain_two_part, centre_part)
    )
    return (
        output.astype(jnp.bfloat16),
        grad_input.astype(jnp.bfloat16),
        gain_one_shard,
        query_shard,
        key_shard,
        value_shard,
        attn_shard,
        gain_two_shard,
        ffn_in_shard,
        ffn_out_shard,
        centre_grad[None, :],
        grad_in_a[None],
        grad_out_a[None],
        grad_in_b[None],
        grad_out_b[None],
    )


LOG2E = 1.4426950408889634
BF16 = jnp.bfloat16
F32 = jnp.float32


def dot_tt(left, right):
    return lax.dot_general(left, right, (((0,), (0,)), ((), ())), preferred_element_type=F32)


def attn_fwd_kernel(plan, own, prompts, out, log_sums, *, head, factor):
    step_id = pl.program_id(0)
    block, full, first = plan[0, step_id], plan[1, step_id], plan[2, step_id]

    @pl.when(plan[3, step_id] > 0)
    def _():
        query = own[block, 0:head, :]

        def tile(key, value, carry, diagonal):
            scores = dot_tt(key, query) * factor
            if diagonal:
                key_at = lax.broadcasted_iota(jnp.int32, scores.shape, 0)
                query_at = lax.broadcasted_iota(jnp.int32, scores.shape, 1)
                scores = jnp.where(key_at <= query_at, scores, -1e30)
            top = jnp.max(scores, 0, keepdims=True)
            if carry is None:
                expo = jnp.exp2(scores - top)
                return top, jnp.sum(expo, 0, keepdims=True), matmul(value, expo.astype(BF16))
            before, total, result = carry
            top = jnp.maximum(before, top)
            expo = jnp.exp2(scores - top)
            shrink = jnp.exp2(before - top)
            return (
                top,
                total * shrink + jnp.sum(expo, 0, keepdims=True),
                result * shrink + matmul(value, expo.astype(BF16)),
            )

        carry = tile(own[block, head : 2 * head, :], own[block, 2 * head : 3 * head, :], None, True)

        def step(k, carry):
            at = first + k
            return tile(prompts[at, 0:head, :], prompts[at, head : 2 * head, :], carry, False)

        top, total, result = lax.fori_loop(0, full, step, carry)
        out[block] = (result / total).astype(BF16)
        log_sums[block] = top + jnp.log2(total)


def attn_bwd_kernel(
    plan, own, prompts, grad, out, log_sums, grad_own, grad_prompts, sum_k, sum_v, *, head, factor, scale
):
    step_id = pl.program_id(0)
    block, full, first = plan[0, step_id], plan[1, step_id], plan[2, step_id]

    @pl.when(step_id == 0)
    def _():
        sum_k[...] = jnp.zeros_like(sum_k)
        sum_v[...] = jnp.zeros_like(sum_v)

    @pl.when(plan[3, step_id] > 0)
    def _():
        query_t, grad_t, log_sum = own[block, 0:head, :], grad[block], log_sums[block]
        inner = jnp.sum(grad_t.astype(F32) * out[block].astype(F32), 0, keepdims=True)
        query, grad_o = query_t.T, grad_t.T

        def tile(key, value, diagonal):
            probs = jnp.exp2(dot_tt(key, query_t) * factor - log_sum)
            if diagonal:
                key_at = lax.broadcasted_iota(jnp.int32, probs.shape, 0)
                query_at = lax.broadcasted_iota(jnp.int32, probs.shape, 1)
                probs = jnp.where(key_at <= query_at, probs, 0.0)
            grad_s = (probs * (dot_tt(value, grad_t) - inner)).astype(BF16)
            return matmul(grad_s, query), matmul(probs.astype(BF16), grad_o), matmul(key, grad_s)

        grad_k, grad_v, grad_q = tile(
            own[block, head : 2 * head, :], own[block, 2 * head : 3 * head, :], True
        )
        grad_own[block, head : 2 * head, :] = (grad_k * scale).T.astype(BF16)
        grad_own[block, 2 * head : 3 * head, :] = grad_v.T.astype(BF16)

        def step(k, grad_q):
            at = first + k
            more_k, more_v, more_q = tile(
                prompts[at, 0:head, :], prompts[at, head : 2 * head, :], False
            )
            sum_k[at] += more_k
            sum_v[at] += more_v
            return grad_q + more_q

        grad_q = lax.fori_loop(0, full, step, grad_q)
        grad_own[block, 0:head, :] = (grad_q * scale).astype(BF16)

    @pl.when(step_id == pl.num_programs(0) - 1)
    def _():
        def finish(k, carry):
            grad_prompts[k, 0:head, :] = (sum_k[k] * scale).T.astype(BF16)
            grad_prompts[k, head : 2 * head, :] = sum_v[k].T.astype(BF16)
            return carry

        lax.fori_loop(0, sum_k.shape[0], finish, 0)


def attn_forward(plan, own, prompts):
    blocks, triple, length = own.shape
    head = triple // 3
    whole = pl.BlockSpec(memory_space=pltpu.VMEM)
    return pl.pallas_call(
        functools.partial(attn_fwd_kernel, head=head, factor=head**-0.5 * LOG2E),
        grid_spec=pltpu.PrefetchScalarGridSpec(
            num_scalar_prefetch=1,
            grid=(plan.shape[1],),
            in_specs=[whole, whole],
            out_specs=[whole, whole],
        ),
        out_shape=[
            jax.ShapeDtypeStruct((blocks, head, length), BF16),
            jax.ShapeDtypeStruct((blocks, 1, length), F32),
        ],
        compiler_params=pltpu.CompilerParams(vmem_limit_bytes=40 * 2**20),
        cost_estimate=pl.CostEstimate(
            flops=100 * length * length * 256 * 4,
            bytes_accessed=8 * 2**20,
            transcendentals=100 * length * length,
        ),
        name="attn_fwd",
    )(plan, own, prompts)


def attn_backward(plan, own, prompts, grad, out, log_sums):
    blocks, triple, length = own.shape
    head = triple // 3
    whole = pl.BlockSpec(memory_space=pltpu.VMEM)
    return pl.pallas_call(
        functools.partial(
            attn_bwd_kernel, head=head, factor=head**-0.5 * LOG2E, scale=head**-0.5
        ),
        grid_spec=pltpu.PrefetchScalarGridSpec(
            num_scalar_prefetch=1,
            grid=(plan.shape[1],),
            in_specs=[whole] * 5,
            out_specs=[whole, whole],
            scratch_shapes=[pltpu.VMEM((prompts.shape[0], length, head), F32)] * 2,
        ),
        out_shape=[
            jax.ShapeDtypeStruct(own.shape, BF16),
            jax.ShapeDtypeStruct(prompts.shape, BF16),
        ],
        compiler_params=pltpu.CompilerParams(vmem_limit_bytes=48 * 2**20),
        cost_estimate=pl.CostEstimate(
            flops=100 * length * length * 256 * 10,
            bytes_accessed=16 * 2**20,
            transcendentals=100 * length * length,
        ),
        name="attn_bwd",
    )(plan, own, prompts, grad, out, log_sums)


def swap(value):
    return lax.ppermute(value, "tensor", [(0, 1), (1, 0)])


def to_core_one(value):
    return lax.ppermute(value, "tensor", [(0, 1)])


def to_core_zero(value):
    return lax.ppermute(value, "tensor", [(1, 0)])


def with_other(value):
    return jnp.concatenate([value, swap(value)], 0)


def keep_rows(value):
    half = value.shape[0] // 2
    return value[:half] + swap(value[half:].astype(BF16)).astype(F32)


def pair_sum(value):
    half = value.shape[0] // 2
    other = swap(value.astype(BF16)).astype(F32)
    return value + jnp.concatenate([other[half:], other[:half]], 0)


def fits_paired(mesh):
    return mesh.shape["tensor"] == 2 and mesh.shape["dp"] == 16


def body_paired(
    tokens,
    cont_prompt,
    routes,
    norm1_gain,
    w_query,
    w_key,
    w_value,
    w_attn_out,
    norm2_gain,
    w_ffn_in,
    w_ffn_out,
    centroids,
    expert_in_a,
    expert_out_a,
    expert_in_b,
    expert_out_b,
    grad_out,
):
    experts = lax.axis_size("dp")
    dp_index = lax.axis_index("dp")
    core_zero = lax.axis_index("tensor") == 0
    rows, width = tokens.shape
    rows_dp = 2 * rows
    shard = w_query.shape[0]
    half_heads = w_query.shape[1] // HEAD
    hidden = w_ffn_in.shape[1]
    triple = 3 * HEAD
    heads = 2 * half_heads
    both = lambda lower, upper: (jnp.where(core_zero, lower, upper), jnp.where(core_zero, upper, lower))

    route = routes[:, 0]
    slots_per = max(2, (3 * rows + 2 * experts - 1) // (2 * experts))
    capacity = 5 * rows_dp // 4
    onehot = route[:, None] == lax.broadcasted_iota(jnp.int32, (1, experts), 1)
    onehot_low = onehot.astype(BF16)
    below = lax.broadcasted_iota(jnp.int32, (rows, rows), 0) > lax.broadcasted_iota(
        jnp.int32, (rows, rows), 1
    )
    earlier = matmul(below.astype(BF16), onehot_low)
    local_rank = jnp.sum(jnp.where(onehot, earlier, 0.0), 1).astype(jnp.int32)
    target = route * slots_per + local_rank
    columns = lax.broadcasted_iota(jnp.int32, (1, experts * slots_per), 1)
    placer = (columns == target[:, None]).astype(BF16)
    counts = jnp.sum(onehot_low.astype(F32), 0).astype(BF16)
    counts_pair = jnp.concatenate(both(counts, swap(counts)), 0)

    qkv_shard = jnp.stack(
        [part.reshape(shard, half_heads, HEAD) for part in (w_query, w_key, w_value)], 2
    ).reshape(shard, half_heads * triple)
    extra = jnp.concatenate([norm1_gain, norm2_gain, counts_pair], 0)
    extra = jnp.pad(extra[None, :], ((0, 7), (0, half_heads * triple - extra.shape[0])))
    first_all = lax.all_gather(jnp.concatenate([qkv_shard, extra], 0), "dp")
    qkv_full = first_all[:, :shard].reshape(width, half_heads * triple)
    gain_one = first_all[:, shard, :shard].reshape(width).astype(F32)
    gain_two = first_all[:, shard, shard : 2 * shard].reshape(width).astype(F32)
    counts_all = first_all[:, shard, 2 * shard : 2 * shard + 2 * experts].reshape(experts, 2, experts)
    second_all = lax.all_gather(
        jnp.concatenate([w_ffn_in, w_ffn_out.T, w_attn_out.T], 1), "dp", axis=0, tiled=True
    )
    ffn_in = second_all[:, :hidden]
    ffn_out_t = second_all[:, hidden : 2 * hidden]
    attn_half = second_all[:, 2 * hidden :]

    sent_grad = matmul_tn(placer, grad_out).astype(BF16).reshape(experts, slots_per, width)
    grad_own = to_experts(sent_grad).reshape(-1, width)

    mine = jnp.sum(
        jnp.where(lax.broadcasted_iota(jnp.int32, (1, 1, experts), 2) == dp_index, counts_all.astype(F32), 0.0),
        2,
    )
    per_chip = jnp.sum(mine, 1)
    chip_before = jnp.sum(
        jnp.where(
            lax.broadcasted_iota(jnp.int32, (experts, experts), 1)
            < lax.broadcasted_iota(jnp.int32, (experts, experts), 0),
            per_chip[None, :],
            0.0,
        ),
        1,
    )
    starts = both(chip_before, chip_before + mine[:, 0])
    slot_at = lax.broadcasted_iota(jnp.int32, (1, slots_per), 1).astype(F32)
    kept = jnp.concatenate(
        [(start[:, None] + slot_at < capacity).reshape(-1, 1) for start in starts], 0
    )
    half_rows = experts * slots_per
    grad_returned = jnp.where(kept, with_other(grad_own).astype(F32), 0.0)

    pair_tokens = with_other(tokens).astype(F32)
    normed_one, hat_pair, inv_pair = norm_forward(pair_tokens, gain_one)
    inputs, hat_one, inv_one = pair_tokens[:rows], hat_pair[:rows], inv_pair[:rows]
    rows_one = normed_one.astype(BF16)
    other_t = lax.dot_general(
        qkv_full, rows_one[rows:], (((0,), (1,)), ((), ())), preferred_element_type=F32
    ).astype(BF16)
    own_t = lax.dot_general(
        qkv_full, rows_one[:rows], (((0,), (1,)), ((), ())), preferred_element_type=F32
    ).astype(BF16)
    qkv_t = jnp.concatenate(both(own_t, swap(other_t)), 0).reshape(heads, triple, rows)
    by_head = lax.all_to_all(qkv_t, "dp", split_axis=0, concat_axis=0, tiled=True)

    lent = experts // 4
    span = PLEN // rows
    own_blocks = jnp.concatenate([by_head, to_core_zero(by_head[:lent])], 0)
    prompt_kv = jnp.where(core_zero, by_head[:, HEAD:], to_core_one(by_head[:, HEAD:]))
    places = jnp.arange(experts + lent, dtype=jnp.int32)
    follows = cont_prompt * span
    plan_zero = jnp.stack(
        [
            places,
            jnp.where(places < experts, places % span, span),
            jnp.concatenate([places[:experts] // span * span, follows[:lent]], 0),
            jnp.ones_like(places),
        ]
    )
    plan_one = jnp.stack(
        [
            jnp.minimum(places + lent, experts - 1),
            jnp.full_like(places, span),
            jnp.concatenate([follows[lent:], jnp.zeros((2 * lent,), jnp.int32)], 0),
            (places < experts - lent).astype(jnp.int32),
        ]
    )
    plan = jnp.where(core_zero, plan_zero, plan_one)
    attn_blocks, log_sums = attn_forward(plan, own_blocks, prompt_kv)
    lent_back = to_core_one(attn_blocks[experts:])
    attn_own = jnp.concatenate(
        [jnp.where(core_zero, attn_blocks[:lent], lent_back), attn_blocks[lent:experts]], 0
    )
    attn_t = lax.all_to_all(attn_own, "dp", split_axis=0, concat_axis=0, tiled=True).reshape(
        width, rows
    )

    attn_out_t = jnp.concatenate(both(attn_half, swap(attn_half)), 1)
    hidden_one = inputs + lax.dot_general(
        attn_t, attn_out_t, (((0,), (1,)), ((), ())), preferred_element_type=F32
    )
    normed_two, hat_two, inv_two = norm_forward(hidden_one, gain_two)
    rows_two = with_other(normed_two.astype(BF16))
    ffn_pre = matmul(rows_two, ffn_in).astype(BF16)
    ffn_act = jax.nn.gelu(ffn_pre.astype(F32)).astype(BF16)
    hidden_two = hidden_one + keep_rows(matmul_nt(ffn_act, ffn_out_t))

    sent_rows = (
        matmul_tn(placer, hidden_two.astype(BF16)).astype(BF16).reshape(experts, slots_per, width)
    )
    expert_rows = with_other(to_experts(sent_rows).reshape(-1, width))
    centre = centroids[0]
    gate_value = jax.nn.sigmoid(matmul(expert_rows, centre))
    pre_a = matmul(expert_rows, expert_in_a[0]).astype(BF16)
    act_a = jax.nn.gelu(pre_a.astype(F32)).astype(BF16)
    branch_a = pair_sum(matmul(act_a, expert_out_a[0]))
    middle = (expert_rows.astype(F32) + branch_a).astype(BF16)
    pre_b = matmul(middle, expert_in_b[0]).astype(BF16)
    act_b = jax.nn.gelu(pre_b.astype(F32)).astype(BF16)
    branch_half = branch_a[:half_rows] + keep_rows(matmul(act_b, expert_out_b[0]))
    gate_half = gate_value[:half_rows]
    returned = (
        jnp.where(kept[:half_rows], gate_half[:, None] * branch_half, 0.0)
        .astype(BF16)
        .reshape(experts, slots_per, width)
    )
    came_back = to_experts(returned).reshape(half_rows, width)
    output = hidden_two + matmul(placer, came_back)

    grad_half = grad_returned[:half_rows]
    grad_logit_half = jnp.sum(grad_half * branch_half, 1) * gate_half * (1.0 - gate_half)
    centre_part = matmul(grad_logit_half, expert_rows[:half_rows].astype(F32))
    grad_branch = gate_value[:, None] * grad_returned
    grad_b = grad_branch.astype(BF16)
    grad_pre_b = gelu_grad(pre_b.astype(F32), matmul_nt(grad_b, expert_out_b[0])).astype(BF16)
    grad_middle = pair_sum(matmul_nt(grad_pre_b, expert_in_b[0]))
    grad_a = (grad_branch + grad_middle).astype(BF16)
    grad_pre_a = gelu_grad(pre_a.astype(F32), matmul_nt(grad_a, expert_out_a[0])).astype(BF16)
    grad_rows = (
        keep_rows(matmul_nt(grad_pre_a, expert_in_a[0]))
        + grad_middle[:half_rows]
        + grad_logit_half[:, None] * centre.astype(F32)[None, :]
    )
    grad_back = to_experts(grad_rows.astype(BF16).reshape(experts, slots_per, width)).reshape(
        half_rows, width
    )
    grad_out_b = matmul_tn(act_b, grad_b)
    grad_in_b = matmul_tn(middle, grad_pre_b)
    grad_out_a = matmul_tn(act_a, grad_a)
    grad_in_a = matmul_tn(expert_rows, grad_pre_a)
    grad_two = grad_out.astype(F32) + matmul(placer, grad_back)

    rows_down = with_other(grad_two.astype(BF16))
    grad_ffn_pre = gelu_grad(ffn_pre.astype(F32), matmul(rows_down, ffn_out_t)).astype(BF16)
    grad_ffn_out_t = matmul_tn(rows_down, ffn_act)
    grad_ffn_in = matmul_tn(rows_two, grad_ffn_pre)
    grad_norm_two = keep_rows(matmul_nt(grad_ffn_pre, ffn_in))
    back_two, grad_gain_two = norm_backward(grad_norm_two, hat_two, inv_two, gain_two)
    grad_one = grad_two + back_two

    grad_branch_one = grad_one.astype(BF16)
    grad_attn_t = lax.dot_general(
        attn_out_t, grad_branch_one, (((0,), (1,)), ((), ())), preferred_element_type=F32
    ).astype(BF16)
    grad_by_head = lax.all_to_all(
        grad_attn_t.reshape(heads, HEAD, rows), "dp", split_axis=0, concat_axis=0, tiled=True
    )
    grad_attn_out = lax.dot_general(
        grad_branch_one, attn_t, (((0,), (1,)), ((), ())), preferred_element_type=F32
    )
    half_width = width // 2
    part_own, part_other = both(grad_attn_out[:, :half_width], grad_attn_out[:, half_width:])
    grad_attn_half = part_own + swap(part_other.astype(BF16)).astype(F32)
    second_sum = lax.psum_scatter(
        jnp.concatenate(
            [grad_ffn_in.astype(BF16), grad_ffn_out_t.astype(BF16), grad_attn_half.astype(BF16)], 1
        ),
        "dp",
        scatter_dimension=0,
        tiled=True,
    ).astype(F32)
    grad_blocks = jnp.concatenate([grad_by_head, to_core_zero(grad_by_head[:lent])], 0)
    grad_own_blocks, grad_prompts = attn_backward(
        plan, own_blocks, prompt_kv, grad_blocks, attn_blocks, log_sums
    )
    lent_grad = to_core_one(grad_own_blocks[experts:])
    prompt_sum = grad_prompts.astype(F32) + to_core_zero(grad_prompts).astype(F32)
    prompt_part = jnp.concatenate(
        [
            grad_own_blocks[:experts, :HEAD],
            (grad_own_blocks[:experts, HEAD:].astype(F32) + prompt_sum).astype(BF16),
        ],
        1,
    )
    cont_part = jnp.concatenate([lent_grad, grad_own_blocks[lent:experts]], 0)
    grad_qkv = lax.all_to_all(
        jnp.where(core_zero, prompt_part, cont_part), "dp", split_axis=0, concat_axis=0, tiled=True
    ).reshape(2, half_heads * triple, rows)
    keep_half, send_half = both(grad_qkv[0], grad_qkv[1])
    grad_qkv_t = jnp.concatenate([keep_half, swap(send_half)], 1)
    grad_qkv_w = lax.dot_general(
        rows_one, grad_qkv_t, (((0,), (1,)), ((), ())), preferred_element_type=F32
    )
    grad_norm_one = keep_rows(
        lax.dot_general(
            grad_qkv_t, qkv_full, (((0,), (1,)), ((), ())), preferred_element_type=F32
        )
    )
    back_one, grad_gain_one = norm_backward(grad_norm_one, hat_one, inv_one, gain_one)
    grad_input = grad_one + back_one

    gains = jnp.stack([grad_gain_one, grad_gain_two], 0)
    gains = (gains + swap(gains)).reshape(2, experts, shard).transpose(1, 0, 2).reshape(experts, 1, 2 * shard)
    gains = jnp.pad(gains.astype(BF16), ((0, 0), (0, 7), (0, half_heads * triple - 2 * shard)))
    first_sum = lax.psum_scatter(
        jnp.concatenate([grad_qkv_w.astype(BF16).reshape(experts, shard, -1), gains], 1),
        "dp",
        scatter_dimension=0,
        tiled=False,
    ).astype(F32)
    qkv_sum = first_sum[:shard].reshape(shard, half_heads, 3, HEAD)
    query_shard, key_shard, value_shard = (
        qkv_sum[:, :, part].reshape(shard, half_heads * HEAD) for part in range(3)
    )
    centre_grad = centre_part + swap(centre_part)
    return (
        output.astype(BF16),
        grad_input.astype(BF16),
        first_sum[shard, :shard],
        query_shard,
        key_shard,
        value_shard,
        second_sum[:, 2 * hidden :].T,
        first_sum[shard, shard : 2 * shard],
        second_sum[:, :hidden],
        second_sum[:, hidden : 2 * hidden].T,
        centre_grad[None, :],
        grad_in_a[None],
        grad_out_a[None],
        grad_in_b[None],
        grad_out_b[None],
    )


def solution(mesh):
    body = body_paired if fits_paired(mesh) else body_general
    return jax.shard_map(
        body,
        mesh=mesh,
        in_specs=(
            P(("dp", "tensor"), None),
            P(),
            P(("dp", "tensor"), None),
            P("dp"),
            P("dp", "tensor"),
            P("dp", "tensor"),
            P("dp", "tensor"),
            P("tensor", "dp"),
            P("dp"),
            P("dp", "tensor"),
            P("tensor", "dp"),
            P("dp", None),
            P("dp", None, "tensor"),
            P("dp", "tensor", None),
            P("dp", None, "tensor"),
            P("dp", "tensor", None),
            P(("dp", "tensor"), None),
        ),
        out_specs=(
            P(("dp", "tensor"), None),
            P(("dp", "tensor"), None),
            P("dp"),
            P("dp", "tensor"),
            P("dp", "tensor"),
            P("dp", "tensor"),
            P("tensor", "dp"),
            P("dp"),
            P("dp", "tensor"),
            P("tensor", "dp"),
            P("dp", None),
            P("dp", None, "tensor"),
            P("dp", "tensor", None),
            P("dp", None, "tensor"),
            P("dp", "tensor", None),
        ),
        check_vma=False,
    )
```

```python
import functools

import jax
import jax.numpy as jnp
from jax import lax
from jax.experimental import pallas as pl
from jax.experimental.pallas import tpu as pltpu
from jax.sharding import PartitionSpec as P

HEAD = 64
PLEN = 4096
CONT = 512


def shortened(value):

    def short(part):
        return part.astype(jnp.bfloat16) if part.dtype == jnp.float32 else part

    return jax.tree.map(short, value)


def carried_in(value, axis, combine, identity):
    peers, place = (lax.axis_size(axis), lax.axis_index(axis))
    everything = lax.all_gather(value, axis)
    start = jnp.broadcast_to(jnp.asarray(identity, value.dtype), value.shape)

    def turn(k, before):
        reached = k < place
        new = combine(before, everything[k])
        return jnp.where(reached, new, before)

    return lax.fori_loop(0, peers, turn, start)


def rows_gather(value):
    return lax.all_gather(value, "tensor", axis=0, tiled=True)


def rows_scatter(value):
    return lax.psum_scatter(
        value.astype(jnp.bfloat16), "tensor", scatter_dimension=0, tiled=True
    ).astype(jnp.float32)


def pair_total(value):
    return jax.tree.map(lambda part: part.astype(jnp.float32), lax.psum(shortened(value), "tensor"))


def to_experts(value):
    return lax.all_to_all(value, "dp", split_axis=0, concat_axis=0, tiled=True)


def matmul(left, right):
    return jnp.dot(left, right, preferred_element_type=jnp.float32)


def matmul_tn(left, right):
    return lax.dot_general(
        left, right, (((0,), (0,)), ((), ())), preferred_element_type=jnp.float32
    )


def matmul_nt(left, right):
    return lax.dot_general(
        left, right, (((1,), (1,)), ((), ())), preferred_element_type=jnp.float32
    )


def norm_forward(hidden, gain):
    mean_row = jnp.mean(hidden, -1, keepdims=True)
    centred = hidden - mean_row
    scale_inv = lax.rsqrt(jnp.mean(centred * centred, -1, keepdims=True) + 1e-05)
    normed = centred * scale_inv
    return (normed * gain, normed, scale_inv)


def norm_backward(grad_m, normed, scale_inv, gain):
    grad_hat = grad_m * gain
    inner = (
        grad_hat
        - jnp.mean(grad_hat, -1, keepdims=True)
        - normed * jnp.mean(grad_hat * normed, -1, keepdims=True)
    )
    return (inner * scale_inv, jnp.sum(grad_m * normed, 0))


def gelu_grad(preact, grad):
    unused, pull = jax.vjp(jax.nn.gelu, preact)
    return pull(grad)[0]


def add_counts(first, second):
    return first + second


def attend(queries, keys, values, allowed, heads):
    scale = HEAD ** (-0.5)

    def head_step(head, carry):
        outputs, log_sums = carry
        query_h = lax.dynamic_slice_in_dim(queries, head * HEAD, HEAD, 1)
        key_h = lax.dynamic_slice_in_dim(keys, head * HEAD, HEAD, 1)
        value_h = lax.dynamic_slice_in_dim(values, head * HEAD, HEAD, 1)
        scores = jnp.where(allowed, matmul_nt(query_h, key_h) * scale, -1e30)
        top_score = jnp.max(scores, 1, keepdims=True)
        expo = jnp.exp(scores - top_score)
        total = jnp.sum(expo, 1, keepdims=True)
        probs = (expo / total).astype(jnp.bfloat16)
        outputs = lax.dynamic_update_slice_in_dim(outputs, matmul(probs, value_h), head * HEAD, 1)
        log_sums = lax.dynamic_update_index_in_dim(
            log_sums, top_score[:, 0] + jnp.log(total[:, 0]), head, 0
        )
        return (outputs, log_sums)

    start_state = (
        jnp.zeros((queries.shape[0], heads * HEAD), jnp.float32),
        jnp.zeros((heads, queries.shape[0]), jnp.float32),
    )
    return lax.fori_loop(0, heads, head_step, start_state)


def attend_back(queries, keys, values, allowed, log_sums, grad_attended, heads):
    scale = HEAD ** (-0.5)

    def head_step(head, carry):
        grad_q, grad_k, grad_v = carry
        query_h = lax.dynamic_slice_in_dim(queries, head * HEAD, HEAD, 1)
        key_h = lax.dynamic_slice_in_dim(keys, head * HEAD, HEAD, 1)
        value_h = lax.dynamic_slice_in_dim(values, head * HEAD, HEAD, 1)
        grad_o = lax.dynamic_slice_in_dim(grad_attended, head * HEAD, HEAD, 1)
        scores = jnp.where(allowed, matmul_nt(query_h, key_h) * scale, -1e30)
        probs = jnp.exp(
            scores - lax.dynamic_index_in_dim(log_sums, head, 0, keepdims=False)[:, None]
        )
        grad_p = matmul_nt(grad_o, value_h)
        grad_s = (probs * (grad_p - jnp.sum(probs * grad_p, 1, keepdims=True))).astype(jnp.bfloat16)
        grad_q = lax.dynamic_update_slice_in_dim(
            grad_q, matmul(grad_s, key_h) * scale, head * HEAD, 1
        )
        grad_k = lax.dynamic_update_slice_in_dim(
            grad_k, matmul_tn(grad_s, query_h) * scale, head * HEAD, 1
        )
        grad_v = lax.dynamic_update_slice_in_dim(
            grad_v, matmul_tn(probs.astype(jnp.bfloat16), grad_o), head * HEAD, 1
        )
        return (grad_q, grad_k, grad_v)

    start_state = (
        jnp.zeros(queries.shape, jnp.float32),
        jnp.zeros(keys.shape, jnp.float32),
        jnp.zeros(values.shape, jnp.float32),
    )
    return lax.fori_loop(0, heads, head_step, start_state)


def add_block(buffer, block, start):
    length = block.shape[0]
    current = lax.dynamic_slice_in_dim(buffer, start, length, 0)
    return lax.dynamic_update_slice_in_dim(buffer, current + block, start, 0)


def body_general(
    tokens,
    cont_prompt,
    routes,
    norm1_gain,
    w_query,
    w_key,
    w_value,
    w_attn_out,
    norm2_gain,
    w_ffn_in,
    w_ffn_out,
    centroids,
    expert_in_a,
    expert_out_a,
    expert_in_b,
    expert_out_b,
    grad_out,
):
    experts = lax.axis_size("dp")
    pair_size = lax.axis_size("tensor")
    dp_index = lax.axis_index("dp")
    tensor_index = lax.axis_index("tensor")
    rows_dev = tokens.shape[0]
    rows_dp = rows_dev * pair_size
    prm_dev = rows_dp - CONT
    pkeys = experts * prm_dev
    heads = w_query.shape[1] // HEAD
    width = tokens.shape[1]
    span = PLEN // prm_dev
    owner_start = dp_index // span * PLEN
    mapped_start = cont_prompt[dp_index] * PLEN
    gain_one, query_full, key_full, value_full, attn_full, gain_two, ffn_in_full, ffn_out_full = (
        lax.all_gather(norm1_gain, "dp", axis=0, tiled=True),
        lax.all_gather(w_query, "dp", axis=0, tiled=True),
        lax.all_gather(w_key, "dp", axis=0, tiled=True),
        lax.all_gather(w_value, "dp", axis=0, tiled=True),
        lax.all_gather(w_attn_out, "dp", axis=1, tiled=True),
        lax.all_gather(norm2_gain, "dp", axis=0, tiled=True),
        lax.all_gather(w_ffn_in, "dp", axis=0, tiled=True),
        lax.all_gather(w_ffn_out, "dp", axis=1, tiled=True),
    )
    inputs = tokens.astype(jnp.float32)
    normed_one, hat_one, inv_one = norm_forward(inputs, gain_one.astype(jnp.float32))
    rows_one = rows_gather(normed_one.astype(jnp.bfloat16))
    queries = matmul(rows_one, query_full).astype(jnp.bfloat16)
    keys_own = matmul(rows_one, key_full).astype(jnp.bfloat16)
    values_own = matmul(rows_one, value_full).astype(jnp.bfloat16)
    prompt_keys, prompt_values = (
        lax.all_gather(keys_own[:prm_dev], "dp", axis=0, tiled=True),
        lax.all_gather(values_own[:prm_dev], "dp", axis=0, tiled=True),
    )
    keys_first = lax.dynamic_slice_in_dim(prompt_keys, owner_start, PLEN, 0)
    values_first = lax.dynamic_slice_in_dim(prompt_values, owner_start, PLEN, 0)
    first_row = lax.broadcasted_iota(jnp.int32, (prm_dev, 1), 0)
    first_column = lax.broadcasted_iota(jnp.int32, (1, PLEN), 1)
    allowed_first = first_column <= dp_index % span * prm_dev + first_row
    keys_second = jnp.concatenate(
        [lax.dynamic_slice_in_dim(prompt_keys, mapped_start, PLEN, 0), keys_own[prm_dev:]], 0
    )
    values_second = jnp.concatenate(
        [lax.dynamic_slice_in_dim(prompt_values, mapped_start, PLEN, 0), values_own[prm_dev:]], 0
    )
    second_row = lax.broadcasted_iota(jnp.int32, (CONT, 1), 0)
    second_column = lax.broadcasted_iota(jnp.int32, (1, PLEN + CONT), 1)
    allowed_second = (second_column < PLEN) | (second_column - PLEN <= second_row)
    attn_first, sums_first = attend(
        queries[:prm_dev], keys_first, values_first, allowed_first, heads
    )
    attn_second, sums_second = attend(
        queries[prm_dev:], keys_second, values_second, allowed_second, heads
    )
    attn_low = jnp.concatenate([attn_first, attn_second], 0).astype(jnp.bfloat16)
    hidden_one = inputs + rows_scatter(matmul(attn_low, attn_full))
    normed_two, hat_two, inv_two = norm_forward(hidden_one, gain_two.astype(jnp.float32))
    rows_two = rows_gather(normed_two.astype(jnp.bfloat16))
    ffn_pre = matmul(rows_two, ffn_in_full)
    ffn_act = jax.nn.gelu(ffn_pre).astype(jnp.bfloat16)
    hidden_two = hidden_one + rows_scatter(matmul(ffn_act, ffn_out_full))
    route = routes[:, 0]
    slots_per = max(2, (3 * rows_dev + 2 * experts - 1) // (2 * experts))
    capacity = 5 * rows_dp // 4
    expert_ids = lax.broadcasted_iota(jnp.int32, (1, experts), 1)
    onehot = (route[:, None] == expert_ids).astype(jnp.int32)
    offsets = carried_in(
        jnp.sum(onehot, 0), ("dp", "tensor"), add_counts, jnp.zeros((experts,), jnp.int32)
    )
    local_rank = jnp.sum((jnp.cumsum(onehot, 0) - 1) * onehot, 1)
    global_slot = local_rank + jnp.sum(onehot * offsets[None, :], 1)
    kept = global_slot < capacity
    target = route * slots_per + local_rank
    columns = lax.broadcasted_iota(jnp.int32, (1, experts * slots_per), 1)
    placer = ((columns == target[:, None]) & kept[:, None]).astype(jnp.bfloat16)
    sent_rows = (
        matmul_tn(placer, hidden_two.astype(jnp.bfloat16))
        .astype(jnp.bfloat16)
        .reshape(experts, slots_per, width)
    )
    expert_rows = rows_gather(to_experts(sent_rows)).reshape(-1, width)
    centre = centroids[0]
    gate_value = jax.nn.sigmoid(matmul(expert_rows, centre))
    pre_a = matmul(expert_rows, expert_in_a[0])
    act_a = jax.nn.gelu(pre_a).astype(jnp.bfloat16)
    branch_a = pair_total(matmul(act_a, expert_out_a[0]))
    middle = (expert_rows.astype(jnp.float32) + branch_a).astype(jnp.bfloat16)
    pre_b = matmul(middle, expert_in_b[0])
    act_b = jax.nn.gelu(pre_b).astype(jnp.bfloat16)
    branch_b = rows_scatter(matmul(act_b, expert_out_b[0]))
    half_rows = expert_rows.shape[0] // pair_size
    start_row = tensor_index * half_rows
    branch_half = lax.dynamic_slice_in_dim(branch_a, start_row, half_rows, 0) + branch_b
    gate_half = lax.dynamic_slice_in_dim(gate_value, start_row, half_rows, 0)
    returned = (
        (gate_half[:, None] * branch_half).astype(jnp.bfloat16).reshape(experts, slots_per, width)
    )
    came_back = to_experts(returned).reshape(experts * slots_per, width)
    output = hidden_two + matmul(placer, came_back)
    cotangent = grad_out.astype(jnp.float32)
    sent_grad = matmul_tn(placer, grad_out).astype(jnp.bfloat16).reshape(experts, slots_per, width)
    grad_half = to_experts(sent_grad).reshape(half_rows, width)
    grad_returned = rows_gather(grad_half).astype(jnp.float32)
    grad_gate_half = jnp.sum(grad_half.astype(jnp.float32) * branch_half, 1)
    grad_logit_half = grad_gate_half * gate_half * (1.0 - gate_half)
    rows_half = lax.dynamic_slice_in_dim(expert_rows, start_row, half_rows, 0)
    centre_part = matmul(grad_logit_half, rows_half.astype(jnp.float32))
    grad_branch = gate_value[:, None] * grad_returned
    grad_b = grad_branch.astype(jnp.bfloat16)
    grad_pre_b = gelu_grad(pre_b, matmul_nt(grad_b, expert_out_b[0])).astype(jnp.bfloat16)
    grad_out_b = matmul_tn(act_b, grad_b)
    grad_in_b = matmul_tn(middle, grad_pre_b)
    grad_middle = pair_total(matmul_nt(grad_pre_b, expert_in_b[0]))
    grad_a = (grad_branch + grad_middle).astype(jnp.bfloat16)
    grad_pre_a = gelu_grad(pre_a, matmul_nt(grad_a, expert_out_a[0])).astype(jnp.bfloat16)
    grad_out_a = matmul_tn(act_a, grad_a)
    grad_in_a = matmul_tn(expert_rows, grad_pre_a)
    grad_rows = (
        rows_scatter(matmul_nt(grad_pre_a, expert_in_a[0]))
        + lax.dynamic_slice_in_dim(grad_middle, start_row, half_rows, 0)
        + grad_logit_half[:, None] * centre.astype(jnp.float32)[None, :]
    )
    grad_back = to_experts(
        grad_rows.astype(jnp.bfloat16).reshape(experts, slots_per, width)
    ).reshape(experts * slots_per, width)
    grad_two = cotangent + matmul(placer, grad_back)
    gain_one, query_full, key_full, value_full, attn_full, gain_two, ffn_in_full, ffn_out_full = (
        lax.all_gather(norm1_gain, "dp", axis=0, tiled=True),
        lax.all_gather(w_query, "dp", axis=0, tiled=True),
        lax.all_gather(w_key, "dp", axis=0, tiled=True),
        lax.all_gather(w_value, "dp", axis=0, tiled=True),
        lax.all_gather(w_attn_out, "dp", axis=1, tiled=True),
        lax.all_gather(norm2_gain, "dp", axis=0, tiled=True),
        lax.all_gather(w_ffn_in, "dp", axis=0, tiled=True),
        lax.all_gather(w_ffn_out, "dp", axis=1, tiled=True),
    )
    rows_down = rows_gather(grad_two.astype(jnp.bfloat16))
    grad_ffn_pre = gelu_grad(ffn_pre, matmul_nt(rows_down, ffn_out_full)).astype(jnp.bfloat16)
    grad_ffn_out = matmul_tn(ffn_act, rows_down)
    grad_ffn_in = matmul_tn(rows_two, grad_ffn_pre)
    grad_norm_two = rows_scatter(matmul_nt(grad_ffn_pre, ffn_in_full))
    back_two, grad_gain_two = norm_backward(
        grad_norm_two, hat_two, inv_two, gain_two.astype(jnp.float32)
    )
    grad_one = grad_two + back_two
    rows_attn = rows_gather(grad_one.astype(jnp.bfloat16))
    grad_attn_out = matmul_tn(attn_low, rows_attn)
    grad_attended = matmul_nt(rows_attn, attn_full).astype(jnp.bfloat16)
    grad_q_first, grad_k_first, grad_v_first = attend_back(
        queries[:prm_dev],
        keys_first,
        values_first,
        allowed_first,
        sums_first,
        grad_attended[:prm_dev],
        heads,
    )
    grad_q_second, grad_k_second, grad_v_second = attend_back(
        queries[prm_dev:],
        keys_second,
        values_second,
        allowed_second,
        sums_second,
        grad_attended[prm_dev:],
        heads,
    )
    local_width = keys_own.shape[1]
    buffer_k = jnp.zeros((pkeys, local_width), jnp.float32)
    buffer_v = jnp.zeros((pkeys, local_width), jnp.float32)
    buffer_k = add_block(
        add_block(buffer_k, grad_k_first, owner_start), grad_k_second[:PLEN], mapped_start
    )
    buffer_v = add_block(
        add_block(buffer_v, grad_v_first, owner_start), grad_v_second[:PLEN], mapped_start
    )
    prompt_grad_k, prompt_grad_v = (
        lax.psum_scatter(buffer_k, "dp", scatter_dimension=0, tiled=True),
        lax.psum_scatter(buffer_v, "dp", scatter_dimension=0, tiled=True),
    )
    grad_keys = jnp.concatenate([prompt_grad_k, grad_k_second[PLEN:]], 0).astype(jnp.bfloat16)
    grad_values = jnp.concatenate([prompt_grad_v, grad_v_second[PLEN:]], 0).astype(jnp.bfloat16)
    grad_queries = jnp.concatenate([grad_q_first, grad_q_second], 0).astype(jnp.bfloat16)
    grad_query = matmul_tn(rows_one, grad_queries)
    grad_key = matmul_tn(rows_one, grad_keys)
    grad_value = matmul_tn(rows_one, grad_values)
    grad_norm_one = rows_scatter(
        matmul_nt(grad_queries, query_full)
        + matmul_nt(grad_keys, key_full)
        + matmul_nt(grad_values, value_full)
    )
    back_one, grad_gain_one = norm_backward(
        grad_norm_one, hat_one, inv_one, gain_one.astype(jnp.float32)
    )
    grad_input = grad_one + back_one
    (
        gain_one_part,
        query_shard,
        key_shard,
        value_shard,
        attn_shard,
        gain_two_part,
        ffn_in_shard,
        ffn_out_shard,
    ) = (
        lax.psum_scatter(grad_gain_one, "dp", scatter_dimension=0, tiled=True),
        lax.psum_scatter(grad_query, "dp", scatter_dimension=0, tiled=True),
        lax.psum_scatter(grad_key, "dp", scatter_dimension=0, tiled=True),
        lax.psum_scatter(grad_value, "dp", scatter_dimension=0, tiled=True),
        lax.psum_scatter(grad_attn_out, "dp", scatter_dimension=1, tiled=True),
        lax.psum_scatter(grad_gain_two, "dp", scatter_dimension=0, tiled=True),
        lax.psum_scatter(grad_ffn_in, "dp", scatter_dimension=0, tiled=True),
        lax.psum_scatter(grad_ffn_out, "dp", scatter_dimension=1, tiled=True),
    )
    gain_one_shard, gain_two_shard, centre_grad = pair_total(
        (gain_one_part, gain_two_part, centre_part)
    )
    return (
        output.astype(jnp.bfloat16),
        grad_input.astype(jnp.bfloat16),
        gain_one_shard,
        query_shard,
        key_shard,
        value_shard,
        attn_shard,
        gain_two_shard,
        ffn_in_shard,
        ffn_out_shard,
        centre_grad[None, :],
        grad_in_a[None],
        grad_out_a[None],
        grad_in_b[None],
        grad_out_b[None],
    )


LOG2E = 1.4426950408889634
BF16 = jnp.bfloat16
F32 = jnp.float32


def dot_tt(left, right):
    return lax.dot_general(left, right, (((0,), (0,)), ((), ())), preferred_element_type=F32)


def attn_fwd_kernel(plan, own, prompts, out, log_sums, *, head, factor):
    step_id = pl.program_id(0)
    block, full, first = plan[0, step_id], plan[1, step_id], plan[2, step_id]

    @pl.when(plan[3, step_id] > 0)
    def _():
        query = own[block, 0:head, :]

        def tile(key, value, carry, diagonal):
            scores = dot_tt(key, query) * factor
            if diagonal:
                key_at = lax.broadcasted_iota(jnp.int32, scores.shape, 0)
                query_at = lax.broadcasted_iota(jnp.int32, scores.shape, 1)
                scores = jnp.where(key_at <= query_at, scores, -1e30)
            top = jnp.max(scores, 0, keepdims=True)
            if carry is None:
                expo = jnp.exp2(scores - top)
                return top, jnp.sum(expo, 0, keepdims=True), matmul(value, expo.astype(BF16))
            before, total, result = carry
            top = jnp.maximum(before, top)
            expo = jnp.exp2(scores - top)
            shrink = jnp.exp2(before - top)
            return (
                top,
                total * shrink + jnp.sum(expo, 0, keepdims=True),
                result * shrink + matmul(value, expo.astype(BF16)),
            )

        carry = tile(own[block, head : 2 * head, :], own[block, 2 * head : 3 * head, :], None, True)

        def step(k, carry):
            at = first + k
            return tile(prompts[at, 0:head, :], prompts[at, head : 2 * head, :], carry, False)

        top, total, result = lax.fori_loop(0, full, step, carry)
        out[block] = (result / total).astype(BF16)
        log_sums[block] = top + jnp.log2(total)


def attn_bwd_kernel(
    plan, own, prompts, grad, out, log_sums, grad_own, grad_prompts, sum_k, sum_v, *, head, factor, scale
):
    step_id = pl.program_id(0)
    block, full, first = plan[0, step_id], plan[1, step_id], plan[2, step_id]

    @pl.when(step_id == 0)
    def _():
        sum_k[...] = jnp.zeros_like(sum_k)
        sum_v[...] = jnp.zeros_like(sum_v)

    @pl.when(plan[3, step_id] > 0)
    def _():
        query_t, grad_t, log_sum = own[block, 0:head, :], grad[block], log_sums[block]
        inner = jnp.sum(grad_t.astype(F32) * out[block].astype(F32), 0, keepdims=True)
        query, grad_o = query_t.T, grad_t.T

        def tile(key, value, diagonal):
            probs = jnp.exp2(dot_tt(key, query_t) * factor - log_sum)
            if diagonal:
                key_at = lax.broadcasted_iota(jnp.int32, probs.shape, 0)
                query_at = lax.broadcasted_iota(jnp.int32, probs.shape, 1)
                probs = jnp.where(key_at <= query_at, probs, 0.0)
            grad_s = (probs * (dot_tt(value, grad_t) - inner)).astype(BF16)
            return matmul(grad_s, query), matmul(probs.astype(BF16), grad_o), matmul(key, grad_s)

        grad_k, grad_v, grad_q = tile(
            own[block, head : 2 * head, :], own[block, 2 * head : 3 * head, :], True
        )
        grad_own[block, head : 2 * head, :] = (grad_k * scale).T.astype(BF16)
        grad_own[block, 2 * head : 3 * head, :] = grad_v.T.astype(BF16)

        def step(k, grad_q):
            at = first + k
            more_k, more_v, more_q = tile(
                prompts[at, 0:head, :], prompts[at, head : 2 * head, :], False
            )
            sum_k[at] += more_k
            sum_v[at] += more_v
            return grad_q + more_q

        grad_q = lax.fori_loop(0, full, step, grad_q)
        grad_own[block, 0:head, :] = (grad_q * scale).astype(BF16)

    @pl.when(step_id == pl.num_programs(0) - 1)
    def _():
        def finish(k, carry):
            grad_prompts[k, 0:head, :] = (sum_k[k] * scale).T.astype(BF16)
            grad_prompts[k, head : 2 * head, :] = sum_v[k].T.astype(BF16)
            return carry

        lax.fori_loop(0, sum_k.shape[0], finish, 0)


def attn_forward(plan, own, prompts):
    blocks, triple, length = own.shape
    head = triple // 3
    whole = pl.BlockSpec(memory_space=pltpu.VMEM)
    return pl.pallas_call(
        functools.partial(attn_fwd_kernel, head=head, factor=head**-0.5 * LOG2E),
        grid_spec=pltpu.PrefetchScalarGridSpec(
            num_scalar_prefetch=1,
            grid=(plan.shape[1],),
            in_specs=[whole, whole],
            out_specs=[whole, whole],
        ),
        out_shape=[
            jax.ShapeDtypeStruct((blocks, head, length), BF16),
            jax.ShapeDtypeStruct((blocks, 1, length), F32),
        ],
        compiler_params=pltpu.CompilerParams(vmem_limit_bytes=40 * 2**20),
        cost_estimate=pl.CostEstimate(
            flops=100 * length * length * 256 * 4,
            bytes_accessed=8 * 2**20,
            transcendentals=100 * length * length,
        ),
        name="attn_fwd",
    )(plan, own, prompts)


def attn_backward(plan, own, prompts, grad, out, log_sums):
    blocks, triple, length = own.shape
    head = triple // 3
    whole = pl.BlockSpec(memory_space=pltpu.VMEM)
    return pl.pallas_call(
        functools.partial(
            attn_bwd_kernel, head=head, factor=head**-0.5 * LOG2E, scale=head**-0.5
        ),
        grid_spec=pltpu.PrefetchScalarGridSpec(
            num_scalar_prefetch=1,
            grid=(plan.shape[1],),
            in_specs=[whole] * 5,
            out_specs=[whole, whole],
            scratch_shapes=[pltpu.VMEM((prompts.shape[0], length, head), F32)] * 2,
        ),
        out_shape=[
            jax.ShapeDtypeStruct(own.shape, BF16),
            jax.ShapeDtypeStruct(prompts.shape, BF16),
        ],
        compiler_params=pltpu.CompilerParams(vmem_limit_bytes=48 * 2**20),
        cost_estimate=pl.CostEstimate(
            flops=100 * length * length * 256 * 10,
            bytes_accessed=16 * 2**20,
            transcendentals=100 * length * length,
        ),
        name="attn_bwd",
    )(plan, own, prompts, grad, out, log_sums)


def swap(value):
    return lax.ppermute(value, "tensor", [(0, 1), (1, 0)])


def to_core_one(value):
    return lax.ppermute(value, "tensor", [(0, 1)])


def to_core_zero(value):
    return lax.ppermute(value, "tensor", [(1, 0)])


def with_other(value):
    return jnp.concatenate([value, swap(value)], 0)


def keep_rows(value):
    half = value.shape[0] // 2
    return value[:half] + swap(value[half:].astype(BF16)).astype(F32)


def pair_sum(value):
    half = value.shape[0] // 2
    other = swap(value.astype(BF16)).astype(F32)
    return value + jnp.concatenate([other[half:], other[:half]], 0)


def fits_paired(mesh):
    return mesh.shape["tensor"] == 2 and mesh.shape["dp"] == 16


def body_paired(
    tokens,
    cont_prompt,
    routes,
    norm1_gain,
    w_query,
    w_key,
    w_value,
    w_attn_out,
    norm2_gain,
    w_ffn_in,
    w_ffn_out,
    centroids,
    expert_in_a,
    expert_out_a,
    expert_in_b,
    expert_out_b,
    grad_out,
):
    experts = lax.axis_size("dp")
    dp_index = lax.axis_index("dp")
    core_zero = lax.axis_index("tensor") == 0
    rows, width = tokens.shape
    rows_dp = 2 * rows
    shard = w_query.shape[0]
    half_heads = w_query.shape[1] // HEAD
    hidden = w_ffn_in.shape[1]
    triple = 3 * HEAD
    heads = 2 * half_heads
    both = lambda lower, upper: (jnp.where(core_zero, lower, upper), jnp.where(core_zero, upper, lower))

    route = routes[:, 0]
    slots_per = max(2, (3 * rows + 2 * experts - 1) // (2 * experts))
    capacity = 5 * rows_dp // 4
    onehot = route[:, None] == lax.broadcasted_iota(jnp.int32, (1, experts), 1)
    onehot_low = onehot.astype(BF16)
    below = lax.broadcasted_iota(jnp.int32, (rows, rows), 0) > lax.broadcasted_iota(
        jnp.int32, (rows, rows), 1
    )
    earlier = matmul(below.astype(BF16), onehot_low)
    local_rank = jnp.sum(jnp.where(onehot, earlier, 0.0), 1).astype(jnp.int32)
    target = route * slots_per + local_rank
    columns = lax.broadcasted_iota(jnp.int32, (1, experts * slots_per), 1)
    placer = (columns == target[:, None]).astype(BF16)
    counts = jnp.sum(onehot_low.astype(F32), 0).astype(BF16)
    counts_pair = jnp.concatenate(both(counts, swap(counts)), 0)

    qkv_shard = jnp.stack(
        [part.reshape(shard, half_heads, HEAD) for part in (w_query, w_key, w_value)], 2
    ).reshape(shard, half_heads * triple)
    extra = jnp.concatenate([norm1_gain, norm2_gain, counts_pair], 0)
    extra = jnp.pad(extra[None, :], ((0, 7), (0, half_heads * triple - extra.shape[0])))
    first_all = lax.all_gather(jnp.concatenate([qkv_shard, extra], 0), "dp")
    sent_grad = matmul_tn(placer, grad_out).astype(BF16).reshape(experts, slots_per, width)
    grad_own, first_all = lax.optimization_barrier((to_experts(sent_grad), first_all))
    grad_own = grad_own.reshape(-1, width)

    qkv_full = first_all[:, :shard].reshape(width, half_heads * triple)
    gain_one = first_all[:, shard, :shard].reshape(width).astype(F32)
    gain_two = first_all[:, shard, shard : 2 * shard].reshape(width).astype(F32)
    counts_all = first_all[:, shard, 2 * shard : 2 * shard + 2 * experts].reshape(experts, 2, experts)

    mine = jnp.sum(
        jnp.where(lax.broadcasted_iota(jnp.int32, (1, 1, experts), 2) == dp_index, counts_all.astype(F32), 0.0),
        2,
    )
    per_chip = jnp.sum(mine, 1)
    chip_before = jnp.sum(
        jnp.where(
            lax.broadcasted_iota(jnp.int32, (experts, experts), 1)
            < lax.broadcasted_iota(jnp.int32, (experts, experts), 0),
            per_chip[None, :],
            0.0,
        ),
        1,
    )
    starts = both(chip_before, chip_before + mine[:, 0])
    slot_at = lax.broadcasted_iota(jnp.int32, (1, slots_per), 1).astype(F32)
    kept = jnp.concatenate(
        [(start[:, None] + slot_at < capacity).reshape(-1, 1) for start in starts], 0
    )
    half_rows = experts * slots_per
    grad_returned = jnp.where(kept, with_other(grad_own).astype(F32), 0.0)

    pair_tokens = with_other(tokens).astype(F32)
    normed_one, hat_pair, inv_pair = norm_forward(pair_tokens, gain_one)
    inputs, hat_one, inv_one = pair_tokens[:rows], hat_pair[:rows], inv_pair[:rows]
    rows_one = normed_one.astype(BF16)
    other_t = lax.dot_general(
        qkv_full, rows_one[rows:], (((0,), (1,)), ((), ())), preferred_element_type=F32
    ).astype(BF16)
    own_t = lax.dot_general(
        qkv_full, rows_one[:rows], (((0,), (1,)), ((), ())), preferred_element_type=F32
    ).astype(BF16)
    qkv_t = jnp.concatenate(both(own_t, swap(other_t)), 0).reshape(heads, triple, rows)
    by_head = lax.all_to_all(qkv_t, "dp", split_axis=0, concat_axis=0, tiled=True)

    second_shard = jnp.concatenate([w_ffn_in, w_ffn_out.T, w_attn_out.T], 1)
    by_head, second_shard = lax.optimization_barrier((by_head, second_shard))
    second_all = lax.all_gather(
        second_shard, "dp", axis=0, tiled=True
    )
    ffn_in = second_all[:, :hidden]
    ffn_out_t = second_all[:, hidden : 2 * hidden]
    attn_half = second_all[:, 2 * hidden :]


    lent = experts // 4
    span = PLEN // rows
    own_blocks = jnp.concatenate([by_head, to_core_zero(by_head[:lent])], 0)
    prompt_kv = jnp.where(core_zero, by_head[:, HEAD:], to_core_one(by_head[:, HEAD:]))
    places = jnp.arange(experts + lent, dtype=jnp.int32)
    follows = cont_prompt * span
    plan_zero = jnp.stack(
        [
            places,
            jnp.where(places < experts, places % span, span),
            jnp.concatenate([places[:experts] // span * span, follows[:lent]], 0),
            jnp.ones_like(places),
        ]
    )
    plan_one = jnp.stack(
        [
            jnp.minimum(places + lent, experts - 1),
            jnp.full_like(places, span),
            jnp.concatenate([follows[lent:], jnp.zeros((2 * lent,), jnp.int32)], 0),
            (places < experts - lent).astype(jnp.int32),
        ]
    )
    plan = jnp.where(core_zero, plan_zero, plan_one)
    attn_blocks, log_sums = attn_forward(plan, own_blocks, prompt_kv)
    lent_back = to_core_one(attn_blocks[experts:])
    attn_own = jnp.concatenate(
        [jnp.where(core_zero, attn_blocks[:lent], lent_back), attn_blocks[lent:experts]], 0
    )
    attn_t = lax.all_to_all(attn_own, "dp", split_axis=0, concat_axis=0, tiled=True).reshape(
        width, rows
    )

    attn_out_t = jnp.concatenate(both(attn_half, swap(attn_half)), 1)
    hidden_one = inputs + lax.dot_general(
        attn_t, attn_out_t, (((0,), (1,)), ((), ())), preferred_element_type=F32
    )
    normed_two, hat_two, inv_two = norm_forward(hidden_one, gain_two)
    rows_two = with_other(normed_two.astype(BF16))
    ffn_pre = matmul(rows_two, ffn_in).astype(BF16)
    ffn_act = jax.nn.gelu(ffn_pre.astype(F32)).astype(BF16)
    hidden_two = hidden_one + keep_rows(matmul_nt(ffn_act, ffn_out_t))

    sent_rows = (
        matmul_tn(placer, hidden_two.astype(BF16)).astype(BF16).reshape(experts, slots_per, width)
    )
    own_rows, normed_own = lax.optimization_barrier((to_experts(sent_rows), rows_one[:rows]))
    normed_all = lax.all_gather(normed_own, "dp")
    expert_rows = with_other(own_rows.reshape(-1, width))
    centre = centroids[0]
    gate_value = jax.nn.sigmoid(matmul(expert_rows, centre))
    pre_a = matmul(expert_rows, expert_in_a[0]).astype(BF16)
    act_a = jax.nn.gelu(pre_a.astype(F32)).astype(BF16)
    branch_a = pair_sum(matmul(act_a, expert_out_a[0]))
    middle = (expert_rows.astype(F32) + branch_a).astype(BF16)
    pre_b = matmul(middle, expert_in_b[0]).astype(BF16)
    act_b = jax.nn.gelu(pre_b.astype(F32)).astype(BF16)
    branch_half = branch_a[:half_rows] + keep_rows(matmul(act_b, expert_out_b[0]))
    gate_half = gate_value[:half_rows]
    returned = (
        jnp.where(kept[:half_rows], gate_half[:, None] * branch_half, 0.0)
        .astype(BF16)
        .reshape(experts, slots_per, width)
    )
    came_back = to_experts(returned).reshape(half_rows, width)

    grad_half = grad_returned[:half_rows]
    grad_logit_half = jnp.sum(grad_half * branch_half, 1) * gate_half * (1.0 - gate_half)
    centre_part = matmul(grad_logit_half, expert_rows[:half_rows].astype(F32))
    grad_branch = gate_value[:, None] * grad_returned
    grad_b = grad_branch.astype(BF16)
    grad_pre_b = gelu_grad(pre_b.astype(F32), matmul_nt(grad_b, expert_out_b[0])).astype(BF16)
    grad_middle = pair_sum(matmul_nt(grad_pre_b, expert_in_b[0]))
    grad_a = (grad_branch + grad_middle).astype(BF16)
    grad_pre_a = gelu_grad(pre_a.astype(F32), matmul_nt(grad_a, expert_out_a[0])).astype(BF16)
    grad_rows = (
        keep_rows(matmul_nt(grad_pre_a, expert_in_a[0]))
        + grad_middle[:half_rows]
        + grad_logit_half[:, None] * centre.astype(F32)[None, :]
    )
    grad_out_b = matmul_tn(act_b, grad_b)
    grad_in_b = matmul_tn(middle, grad_pre_b)
    grad_out_a = matmul_tn(act_a, grad_a)
    grad_in_a = matmul_tn(expert_rows, grad_pre_a)
    grad_rows, came_back = lax.optimization_barrier((grad_rows.astype(BF16), came_back))
    output = hidden_two + matmul(placer, came_back)
    grad_back = to_experts(grad_rows.reshape(experts, slots_per, width))
    grad_back, grad_out_b, grad_in_b, grad_out_a, grad_in_a = lax.optimization_barrier(
        (grad_back, grad_out_b, grad_in_b, grad_out_a, grad_in_a)
    )
    grad_back = grad_back.reshape(half_rows, width)
    grad_two = grad_out.astype(F32) + matmul(placer, grad_back)

    rows_down = with_other(grad_two.astype(BF16))
    grad_ffn_pre = gelu_grad(ffn_pre.astype(F32), matmul(rows_down, ffn_out_t)).astype(BF16)
    grad_ffn_out_t = matmul_tn(rows_down, ffn_act)
    grad_ffn_in = matmul_tn(rows_two, grad_ffn_pre)
    grad_norm_two = keep_rows(matmul_nt(grad_ffn_pre, ffn_in))
    back_two = norm_backward(grad_norm_two, hat_two, inv_two, gain_two)[0]
    grad_one = grad_two + back_two

    grad_branch_one = grad_one.astype(BF16)
    grad_attn_t = lax.dot_general(
        attn_out_t, grad_branch_one, (((0,), (1,)), ((), ())), preferred_element_type=F32
    ).astype(BF16)
    grad_by_head = lax.all_to_all(
        grad_attn_t.reshape(heads, HEAD, rows), "dp", split_axis=0, concat_axis=0, tiled=True
    )
    grad_attn_out = lax.dot_general(
        grad_branch_one, attn_t, (((0,), (1,)), ((), ())), preferred_element_type=F32
    )
    half_width = width // 2
    part_own, part_other = both(grad_attn_out[:, :half_width], grad_attn_out[:, half_width:])
    grad_attn_half = part_own + swap(part_other.astype(BF16)).astype(F32)
    second_sum = lax.psum_scatter(
        jnp.concatenate(
            [grad_ffn_in.astype(BF16), grad_ffn_out_t.astype(BF16), grad_attn_half.astype(BF16)], 1
        ),
        "dp",
        scatter_dimension=0,
        tiled=True,
    ).astype(F32)
    grad_blocks = jnp.concatenate([grad_by_head, to_core_zero(grad_by_head[:lent])], 0)
    grad_own_blocks, grad_prompts = attn_backward(
        plan, own_blocks, prompt_kv, grad_blocks, attn_blocks, log_sums
    )
    lent_grad = to_core_one(grad_own_blocks[experts:])
    prompt_sum = grad_prompts.astype(F32) + to_core_zero(grad_prompts).astype(F32)
    prompt_part = jnp.concatenate(
        [
            grad_own_blocks[:experts, :HEAD],
            (grad_own_blocks[:experts, HEAD:].astype(F32) + prompt_sum).astype(BF16),
        ],
        1,
    )
    cont_part = jnp.concatenate([lent_grad, grad_own_blocks[lent:experts]], 0)
    grad_head = jnp.where(core_zero, prompt_part, cont_part)
    grad_qkv = lax.all_to_all(grad_head, "dp", split_axis=0, concat_axis=0, tiled=True)
    grad_head_w = lax.dot_general(
        normed_all, grad_head, (((0, 1), (0, 2)), ((), ())), preferred_element_type=F32
    ).astype(BF16)
    grad_head_w = (grad_head_w.astype(F32) + swap(grad_head_w).astype(F32)).astype(BF16)
    grad_qkv, grad_head_w = lax.optimization_barrier((grad_qkv, grad_head_w))
    by_row = lax.all_to_all(
        grad_head_w.reshape(experts, shard, triple), "dp", split_axis=0, concat_axis=0, tiled=True
    )
    qkv_sum = jnp.where(core_zero, by_row[:half_heads], by_row[half_heads:]).astype(F32)
    query_shard, key_shard, value_shard = (
        qkv_sum[:, :, part * HEAD : (part + 1) * HEAD].transpose(1, 0, 2).reshape(shard, half_heads * HEAD)
        for part in range(3)
    )
    grad_qkv = grad_qkv.reshape(2, half_heads * triple, rows)
    keep_half, send_half = both(grad_qkv[0], grad_qkv[1])
    grad_qkv_t = jnp.concatenate([keep_half, swap(send_half)], 1)
    grad_norm_one = keep_rows(
        lax.dot_general(
            grad_qkv_t, qkv_full, (((0,), (1,)), ((), ())), preferred_element_type=F32
        )
    )
    back_one = norm_backward(grad_norm_one, hat_one, inv_one, gain_one)[0]
    grad_input = grad_one + back_one

    ffn_in_sum = second_sum[:, :hidden]
    gains = jnp.stack(
        [
            jnp.sum(query_shard * w_query + key_shard * w_key + value_shard * w_value, 1)
            / norm1_gain.astype(F32),
            jnp.sum(ffn_in_sum * w_ffn_in, 1) / norm2_gain.astype(F32),
        ]
    )
    gains = gains + swap(gains)
    centre_grad = centre_part + swap(centre_part)
    return (
        output.astype(BF16),
        grad_input.astype(BF16),
        gains[0],
        query_shard,
        key_shard,
        value_shard,
        second_sum[:, 2 * hidden :].T,
        gains[1],
        ffn_in_sum,
        second_sum[:, hidden : 2 * hidden].T,
        centre_grad[None, :],
        grad_in_a[None],
        grad_out_a[None],
        grad_in_b[None],
        grad_out_b[None],
    )


def solution(mesh):
    body = body_paired if fits_paired(mesh) else body_general
    return jax.shard_map(
        body,
        mesh=mesh,
        in_specs=(
            P(("dp", "tensor"), None),
            P(),
            P(("dp", "tensor"), None),
            P("dp"),
            P("dp", "tensor"),
            P("dp", "tensor"),
            P("dp", "tensor"),
            P("tensor", "dp"),
            P("dp"),
            P("dp", "tensor"),
            P("tensor", "dp"),
            P("dp", None),
            P("dp", None, "tensor"),
            P("dp", "tensor", None),
            P("dp", None, "tensor"),
            P("dp", "tensor", None),
            P(("dp", "tensor"), None),
        ),
        out_specs=(
            P(("dp", "tensor"), None),
            P(("dp", "tensor"), None),
            P("dp"),
            P("dp", "tensor"),
            P("dp", "tensor"),
            P("dp", "tensor"),
            P("tensor", "dp"),
            P("dp"),
            P("dp", "tensor"),
            P("tensor", "dp"),
            P("dp", None),
            P("dp", None, "tensor"),
            P("dp", "tensor", None),
            P("dp", None, "tensor"),
            P("dp", "tensor", None),
        ),
        check_vma=False,
    )
```

```python
import functools

import jax
import jax.numpy as jnp
from jax import lax
from jax.experimental import pallas as pl
from jax.experimental.pallas import tpu as pltpu
from jax.sharding import PartitionSpec as P

HEAD = 64
PLEN = 4096
CONT = 512


def shortened(value):

    def short(part):
        return part.astype(jnp.bfloat16) if part.dtype == jnp.float32 else part

    return jax.tree.map(short, value)


def carried_in(value, axis, combine, identity):
    peers, place = (lax.axis_size(axis), lax.axis_index(axis))
    everything = lax.all_gather(value, axis)
    start = jnp.broadcast_to(jnp.asarray(identity, value.dtype), value.shape)

    def turn(k, before):
        reached = k < place
        new = combine(before, everything[k])
        return jnp.where(reached, new, before)

    return lax.fori_loop(0, peers, turn, start)


def rows_gather(value):
    return lax.all_gather(value, "tensor", axis=0, tiled=True)


def rows_scatter(value):
    return lax.psum_scatter(
        value.astype(jnp.bfloat16), "tensor", scatter_dimension=0, tiled=True
    ).astype(jnp.float32)


def pair_total(value):
    return jax.tree.map(lambda part: part.astype(jnp.float32), lax.psum(shortened(value), "tensor"))


def to_experts(value):
    return lax.all_to_all(value, "dp", split_axis=0, concat_axis=0, tiled=True)


def matmul(left, right):
    return jnp.dot(left, right, preferred_element_type=jnp.float32)


def matmul_tn(left, right):
    return lax.dot_general(
        left, right, (((0,), (0,)), ((), ())), preferred_element_type=jnp.float32
    )


def matmul_nt(left, right):
    return lax.dot_general(
        left, right, (((1,), (1,)), ((), ())), preferred_element_type=jnp.float32
    )


def norm_forward(hidden, gain):
    mean_row = jnp.mean(hidden, -1, keepdims=True)
    centred = hidden - mean_row
    scale_inv = lax.rsqrt(jnp.mean(centred * centred, -1, keepdims=True) + 1e-05)
    normed = centred * scale_inv
    return (normed * gain, normed, scale_inv)


def norm_backward(grad_m, normed, scale_inv, gain):
    grad_hat = grad_m * gain
    inner = (
        grad_hat
        - jnp.mean(grad_hat, -1, keepdims=True)
        - normed * jnp.mean(grad_hat * normed, -1, keepdims=True)
    )
    return (inner * scale_inv, jnp.sum(grad_m * normed, 0))


def gelu_grad(preact, grad):
    unused, pull = jax.vjp(jax.nn.gelu, preact)
    return pull(grad)[0]


def add_counts(first, second):
    return first + second


def attend(queries, keys, values, allowed, heads):
    scale = HEAD ** (-0.5)

    def head_step(head, carry):
        outputs, log_sums = carry
        query_h = lax.dynamic_slice_in_dim(queries, head * HEAD, HEAD, 1)
        key_h = lax.dynamic_slice_in_dim(keys, head * HEAD, HEAD, 1)
        value_h = lax.dynamic_slice_in_dim(values, head * HEAD, HEAD, 1)
        scores = jnp.where(allowed, matmul_nt(query_h, key_h) * scale, -1e30)
        top_score = jnp.max(scores, 1, keepdims=True)
        expo = jnp.exp(scores - top_score)
        total = jnp.sum(expo, 1, keepdims=True)
        probs = (expo / total).astype(jnp.bfloat16)
        outputs = lax.dynamic_update_slice_in_dim(outputs, matmul(probs, value_h), head * HEAD, 1)
        log_sums = lax.dynamic_update_index_in_dim(
            log_sums, top_score[:, 0] + jnp.log(total[:, 0]), head, 0
        )
        return (outputs, log_sums)

    start_state = (
        jnp.zeros((queries.shape[0], heads * HEAD), jnp.float32),
        jnp.zeros((heads, queries.shape[0]), jnp.float32),
    )
    return lax.fori_loop(0, heads, head_step, start_state)


def attend_back(queries, keys, values, allowed, log_sums, grad_attended, heads):
    scale = HEAD ** (-0.5)

    def head_step(head, carry):
        grad_q, grad_k, grad_v = carry
        query_h = lax.dynamic_slice_in_dim(queries, head * HEAD, HEAD, 1)
        key_h = lax.dynamic_slice_in_dim(keys, head * HEAD, HEAD, 1)
        value_h = lax.dynamic_slice_in_dim(values, head * HEAD, HEAD, 1)
        grad_o = lax.dynamic_slice_in_dim(grad_attended, head * HEAD, HEAD, 1)
        scores = jnp.where(allowed, matmul_nt(query_h, key_h) * scale, -1e30)
        probs = jnp.exp(
            scores - lax.dynamic_index_in_dim(log_sums, head, 0, keepdims=False)[:, None]
        )
        grad_p = matmul_nt(grad_o, value_h)
        grad_s = (probs * (grad_p - jnp.sum(probs * grad_p, 1, keepdims=True))).astype(jnp.bfloat16)
        grad_q = lax.dynamic_update_slice_in_dim(
            grad_q, matmul(grad_s, key_h) * scale, head * HEAD, 1
        )
        grad_k = lax.dynamic_update_slice_in_dim(
            grad_k, matmul_tn(grad_s, query_h) * scale, head * HEAD, 1
        )
        grad_v = lax.dynamic_update_slice_in_dim(
            grad_v, matmul_tn(probs.astype(jnp.bfloat16), grad_o), head * HEAD, 1
        )
        return (grad_q, grad_k, grad_v)

    start_state = (
        jnp.zeros(queries.shape, jnp.float32),
        jnp.zeros(keys.shape, jnp.float32),
        jnp.zeros(values.shape, jnp.float32),
    )
    return lax.fori_loop(0, heads, head_step, start_state)


def add_block(buffer, block, start):
    length = block.shape[0]
    current = lax.dynamic_slice_in_dim(buffer, start, length, 0)
    return lax.dynamic_update_slice_in_dim(buffer, current + block, start, 0)


def body_general(
    tokens,
    cont_prompt,
    routes,
    norm1_gain,
    w_query,
    w_key,
    w_value,
    w_attn_out,
    norm2_gain,
    w_ffn_in,
    w_ffn_out,
    centroids,
    expert_in_a,
    expert_out_a,
    expert_in_b,
    expert_out_b,
    grad_out,
):
    experts = lax.axis_size("dp")
    pair_size = lax.axis_size("tensor")
    dp_index = lax.axis_index("dp")
    tensor_index = lax.axis_index("tensor")
    rows_dev = tokens.shape[0]
    rows_dp = rows_dev * pair_size
    prm_dev = rows_dp - CONT
    pkeys = experts * prm_dev
    heads = w_query.shape[1] // HEAD
    width = tokens.shape[1]
    span = PLEN // prm_dev
    owner_start = dp_index // span * PLEN
    mapped_start = cont_prompt[dp_index] * PLEN
    gain_one, query_full, key_full, value_full, attn_full, gain_two, ffn_in_full, ffn_out_full = (
        lax.all_gather(norm1_gain, "dp", axis=0, tiled=True),
        lax.all_gather(w_query, "dp", axis=0, tiled=True),
        lax.all_gather(w_key, "dp", axis=0, tiled=True),
        lax.all_gather(w_value, "dp", axis=0, tiled=True),
        lax.all_gather(w_attn_out, "dp", axis=1, tiled=True),
        lax.all_gather(norm2_gain, "dp", axis=0, tiled=True),
        lax.all_gather(w_ffn_in, "dp", axis=0, tiled=True),
        lax.all_gather(w_ffn_out, "dp", axis=1, tiled=True),
    )
    inputs = tokens.astype(jnp.float32)
    normed_one, hat_one, inv_one = norm_forward(inputs, gain_one.astype(jnp.float32))
    rows_one = rows_gather(normed_one.astype(jnp.bfloat16))
    queries = matmul(rows_one, query_full).astype(jnp.bfloat16)
    keys_own = matmul(rows_one, key_full).astype(jnp.bfloat16)
    values_own = matmul(rows_one, value_full).astype(jnp.bfloat16)
    prompt_keys, prompt_values = (
        lax.all_gather(keys_own[:prm_dev], "dp", axis=0, tiled=True),
        lax.all_gather(values_own[:prm_dev], "dp", axis=0, tiled=True),
    )
    keys_first = lax.dynamic_slice_in_dim(prompt_keys, owner_start, PLEN, 0)
    values_first = lax.dynamic_slice_in_dim(prompt_values, owner_start, PLEN, 0)
    first_row = lax.broadcasted_iota(jnp.int32, (prm_dev, 1), 0)
    first_column = lax.broadcasted_iota(jnp.int32, (1, PLEN), 1)
    allowed_first = first_column <= dp_index % span * prm_dev + first_row
    keys_second = jnp.concatenate(
        [lax.dynamic_slice_in_dim(prompt_keys, mapped_start, PLEN, 0), keys_own[prm_dev:]], 0
    )
    values_second = jnp.concatenate(
        [lax.dynamic_slice_in_dim(prompt_values, mapped_start, PLEN, 0), values_own[prm_dev:]], 0
    )
    second_row = lax.broadcasted_iota(jnp.int32, (CONT, 1), 0)
    second_column = lax.broadcasted_iota(jnp.int32, (1, PLEN + CONT), 1)
    allowed_second = (second_column < PLEN) | (second_column - PLEN <= second_row)
    attn_first, sums_first = attend(
        queries[:prm_dev], keys_first, values_first, allowed_first, heads
    )
    attn_second, sums_second = attend(
        queries[prm_dev:], keys_second, values_second, allowed_second, heads
    )
    attn_low = jnp.concatenate([attn_first, attn_second], 0).astype(jnp.bfloat16)
    hidden_one = inputs + rows_scatter(matmul(attn_low, attn_full))
    normed_two, hat_two, inv_two = norm_forward(hidden_one, gain_two.astype(jnp.float32))
    rows_two = rows_gather(normed_two.astype(jnp.bfloat16))
    ffn_pre = matmul(rows_two, ffn_in_full)
    ffn_act = jax.nn.gelu(ffn_pre).astype(jnp.bfloat16)
    hidden_two = hidden_one + rows_scatter(matmul(ffn_act, ffn_out_full))
    route = routes[:, 0]
    slots_per = max(2, (3 * rows_dev + 2 * experts - 1) // (2 * experts))
    capacity = 5 * rows_dp // 4
    expert_ids = lax.broadcasted_iota(jnp.int32, (1, experts), 1)
    onehot = (route[:, None] == expert_ids).astype(jnp.int32)
    offsets = carried_in(
        jnp.sum(onehot, 0), ("dp", "tensor"), add_counts, jnp.zeros((experts,), jnp.int32)
    )
    local_rank = jnp.sum((jnp.cumsum(onehot, 0) - 1) * onehot, 1)
    global_slot = local_rank + jnp.sum(onehot * offsets[None, :], 1)
    kept = global_slot < capacity
    target = route * slots_per + local_rank
    columns = lax.broadcasted_iota(jnp.int32, (1, experts * slots_per), 1)
    placer = ((columns == target[:, None]) & kept[:, None]).astype(jnp.bfloat16)
    sent_rows = (
        matmul_tn(placer, hidden_two.astype(jnp.bfloat16))
        .astype(jnp.bfloat16)
        .reshape(experts, slots_per, width)
    )
    expert_rows = rows_gather(to_experts(sent_rows)).reshape(-1, width)
    centre = centroids[0]
    gate_value = jax.nn.sigmoid(matmul(expert_rows, centre))
    pre_a = matmul(expert_rows, expert_in_a[0])
    act_a = jax.nn.gelu(pre_a).astype(jnp.bfloat16)
    branch_a = pair_total(matmul(act_a, expert_out_a[0]))
    middle = (expert_rows.astype(jnp.float32) + branch_a).astype(jnp.bfloat16)
    pre_b = matmul(middle, expert_in_b[0])
    act_b = jax.nn.gelu(pre_b).astype(jnp.bfloat16)
    branch_b = rows_scatter(matmul(act_b, expert_out_b[0]))
    half_rows = expert_rows.shape[0] // pair_size
    start_row = tensor_index * half_rows
    branch_half = lax.dynamic_slice_in_dim(branch_a, start_row, half_rows, 0) + branch_b
    gate_half = lax.dynamic_slice_in_dim(gate_value, start_row, half_rows, 0)
    returned = (
        (gate_half[:, None] * branch_half).astype(jnp.bfloat16).reshape(experts, slots_per, width)
    )
    came_back = to_experts(returned).reshape(experts * slots_per, width)
    output = hidden_two + matmul(placer, came_back)
    cotangent = grad_out.astype(jnp.float32)
    sent_grad = matmul_tn(placer, grad_out).astype(jnp.bfloat16).reshape(experts, slots_per, width)
    grad_half = to_experts(sent_grad).reshape(half_rows, width)
    grad_returned = rows_gather(grad_half).astype(jnp.float32)
    grad_gate_half = jnp.sum(grad_half.astype(jnp.float32) * branch_half, 1)
    grad_logit_half = grad_gate_half * gate_half * (1.0 - gate_half)
    rows_half = lax.dynamic_slice_in_dim(expert_rows, start_row, half_rows, 0)
    centre_part = matmul(grad_logit_half, rows_half.astype(jnp.float32))
    grad_branch = gate_value[:, None] * grad_returned
    grad_b = grad_branch.astype(jnp.bfloat16)
    grad_pre_b = gelu_grad(pre_b, matmul_nt(grad_b, expert_out_b[0])).astype(jnp.bfloat16)
    grad_out_b = matmul_tn(act_b, grad_b)
    grad_in_b = matmul_tn(middle, grad_pre_b)
    grad_middle = pair_total(matmul_nt(grad_pre_b, expert_in_b[0]))
    grad_a = (grad_branch + grad_middle).astype(jnp.bfloat16)
    grad_pre_a = gelu_grad(pre_a, matmul_nt(grad_a, expert_out_a[0])).astype(jnp.bfloat16)
    grad_out_a = matmul_tn(act_a, grad_a)
    grad_in_a = matmul_tn(expert_rows, grad_pre_a)
    grad_rows = (
        rows_scatter(matmul_nt(grad_pre_a, expert_in_a[0]))
        + lax.dynamic_slice_in_dim(grad_middle, start_row, half_rows, 0)
        + grad_logit_half[:, None] * centre.astype(jnp.float32)[None, :]
    )
    grad_back = to_experts(
        grad_rows.astype(jnp.bfloat16).reshape(experts, slots_per, width)
    ).reshape(experts * slots_per, width)
    grad_two = cotangent + matmul(placer, grad_back)
    gain_one, query_full, key_full, value_full, attn_full, gain_two, ffn_in_full, ffn_out_full = (
        lax.all_gather(norm1_gain, "dp", axis=0, tiled=True),
        lax.all_gather(w_query, "dp", axis=0, tiled=True),
        lax.all_gather(w_key, "dp", axis=0, tiled=True),
        lax.all_gather(w_value, "dp", axis=0, tiled=True),
        lax.all_gather(w_attn_out, "dp", axis=1, tiled=True),
        lax.all_gather(norm2_gain, "dp", axis=0, tiled=True),
        lax.all_gather(w_ffn_in, "dp", axis=0, tiled=True),
        lax.all_gather(w_ffn_out, "dp", axis=1, tiled=True),
    )
    rows_down = rows_gather(grad_two.astype(jnp.bfloat16))
    grad_ffn_pre = gelu_grad(ffn_pre, matmul_nt(rows_down, ffn_out_full)).astype(jnp.bfloat16)
    grad_ffn_out = matmul_tn(ffn_act, rows_down)
    grad_ffn_in = matmul_tn(rows_two, grad_ffn_pre)
    grad_norm_two = rows_scatter(matmul_nt(grad_ffn_pre, ffn_in_full))
    back_two, grad_gain_two = norm_backward(
        grad_norm_two, hat_two, inv_two, gain_two.astype(jnp.float32)
    )
    grad_one = grad_two + back_two
    rows_attn = rows_gather(grad_one.astype(jnp.bfloat16))
    grad_attn_out = matmul_tn(attn_low, rows_attn)
    grad_attended = matmul_nt(rows_attn, attn_full).astype(jnp.bfloat16)
    grad_q_first, grad_k_first, grad_v_first = attend_back(
        queries[:prm_dev],
        keys_first,
        values_first,
        allowed_first,
        sums_first,
        grad_attended[:prm_dev],
        heads,
    )
    grad_q_second, grad_k_second, grad_v_second = attend_back(
        queries[prm_dev:],
        keys_second,
        values_second,
        allowed_second,
        sums_second,
        grad_attended[prm_dev:],
        heads,
    )
    local_width = keys_own.shape[1]
    buffer_k = jnp.zeros((pkeys, local_width), jnp.float32)
    buffer_v = jnp.zeros((pkeys, local_width), jnp.float32)
    buffer_k = add_block(
        add_block(buffer_k, grad_k_first, owner_start), grad_k_second[:PLEN], mapped_start
    )
    buffer_v = add_block(
        add_block(buffer_v, grad_v_first, owner_start), grad_v_second[:PLEN], mapped_start
    )
    prompt_grad_k, prompt_grad_v = (
        lax.psum_scatter(buffer_k, "dp", scatter_dimension=0, tiled=True),
        lax.psum_scatter(buffer_v, "dp", scatter_dimension=0, tiled=True),
    )
    grad_keys = jnp.concatenate([prompt_grad_k, grad_k_second[PLEN:]], 0).astype(jnp.bfloat16)
    grad_values = jnp.concatenate([prompt_grad_v, grad_v_second[PLEN:]], 0).astype(jnp.bfloat16)
    grad_queries = jnp.concatenate([grad_q_first, grad_q_second], 0).astype(jnp.bfloat16)
    grad_query = matmul_tn(rows_one, grad_queries)
    grad_key = matmul_tn(rows_one, grad_keys)
    grad_value = matmul_tn(rows_one, grad_values)
    grad_norm_one = rows_scatter(
        matmul_nt(grad_queries, query_full)
        + matmul_nt(grad_keys, key_full)
        + matmul_nt(grad_values, value_full)
    )
    back_one, grad_gain_one = norm_backward(
        grad_norm_one, hat_one, inv_one, gain_one.astype(jnp.float32)
    )
    grad_input = grad_one + back_one
    (
        gain_one_part,
        query_shard,
        key_shard,
        value_shard,
        attn_shard,
        gain_two_part,
        ffn_in_shard,
        ffn_out_shard,
    ) = (
        lax.psum_scatter(grad_gain_one, "dp", scatter_dimension=0, tiled=True),
        lax.psum_scatter(grad_query, "dp", scatter_dimension=0, tiled=True),
        lax.psum_scatter(grad_key, "dp", scatter_dimension=0, tiled=True),
        lax.psum_scatter(grad_value, "dp", scatter_dimension=0, tiled=True),
        lax.psum_scatter(grad_attn_out, "dp", scatter_dimension=1, tiled=True),
        lax.psum_scatter(grad_gain_two, "dp", scatter_dimension=0, tiled=True),
        lax.psum_scatter(grad_ffn_in, "dp", scatter_dimension=0, tiled=True),
        lax.psum_scatter(grad_ffn_out, "dp", scatter_dimension=1, tiled=True),
    )
    gain_one_shard, gain_two_shard, centre_grad = pair_total(
        (gain_one_part, gain_two_part, centre_part)
    )
    return (
        output.astype(jnp.bfloat16),
        grad_input.astype(jnp.bfloat16),
        gain_one_shard,
        query_shard,
        key_shard,
        value_shard,
        attn_shard,
        gain_two_shard,
        ffn_in_shard,
        ffn_out_shard,
        centre_grad[None, :],
        grad_in_a[None],
        grad_out_a[None],
        grad_in_b[None],
        grad_out_b[None],
    )


LOG2E = 1.4426950408889634
GELU_A = 0.7978845608028654
GELU_B = 0.044715
BF16 = jnp.bfloat16
F32 = jnp.float32


def dot_tt(left, right):
    return lax.dot_general(left, right, (((0,), (0,)), ((), ())), preferred_element_type=F32)


def attn_fwd_kernel(plan, own, prompts, out, log_sums, *, head, factor):
    step_id = pl.program_id(0)
    block, full, first = plan[0, step_id], plan[1, step_id], plan[2, step_id]

    @pl.when(plan[3, step_id] > 0)
    def _():
        query = own[block, 0:head, :]

        def tile(key, value, carry, diagonal):
            scores = dot_tt(key, query) * factor
            if diagonal:
                key_at = lax.broadcasted_iota(jnp.int32, scores.shape, 0)
                query_at = lax.broadcasted_iota(jnp.int32, scores.shape, 1)
                scores = jnp.where(key_at <= query_at, scores, -1e30)
            top = jnp.max(scores, 0, keepdims=True)
            if carry is None:
                expo = jnp.exp2(scores - top)
                return top, jnp.sum(expo, 0, keepdims=True), matmul(value, expo.astype(BF16))
            before, total, result = carry
            top = jnp.maximum(before, top)
            expo = jnp.exp2(scores - top)
            shrink = jnp.exp2(before - top)
            return (
                top,
                total * shrink + jnp.sum(expo, 0, keepdims=True),
                result * shrink + matmul(value, expo.astype(BF16)),
            )

        carry = tile(own[block, head : 2 * head, :], own[block, 2 * head : 3 * head, :], None, True)

        def step(k, carry):
            at = first + k
            return tile(prompts[at, 0:head, :], prompts[at, head : 2 * head, :], carry, False)

        top, total, result = lax.fori_loop(0, full, step, carry)
        out[block] = (result / total).astype(BF16)
        log_sums[block] = top + jnp.log2(total)


def attn_bwd_kernel(
    plan, own, prompts, grad, out, log_sums, grad_own, grad_prompts, sum_k, sum_v, *, head, factor, scale
):
    step_id = pl.program_id(0)
    block, full, first = plan[0, step_id], plan[1, step_id], plan[2, step_id]

    @pl.when(step_id == 0)
    def _():
        sum_k[...] = jnp.zeros_like(sum_k)
        sum_v[...] = jnp.zeros_like(sum_v)

    @pl.when(plan[3, step_id] > 0)
    def _():
        query_t, grad_t, log_sum = own[block, 0:head, :], grad[block], log_sums[block]
        inner = jnp.sum(grad_t.astype(F32) * out[block].astype(F32), 0, keepdims=True)
        query, grad_o = query_t.T, grad_t.T

        def tile(key, value, diagonal):
            probs = jnp.exp2(dot_tt(key, query_t) * factor - log_sum)
            if diagonal:
                key_at = lax.broadcasted_iota(jnp.int32, probs.shape, 0)
                query_at = lax.broadcasted_iota(jnp.int32, probs.shape, 1)
                probs = jnp.where(key_at <= query_at, probs, 0.0)
            grad_s = (probs * (dot_tt(value, grad_t) - inner)).astype(BF16)
            return matmul(grad_s, query), matmul(probs.astype(BF16), grad_o), matmul(key, grad_s)

        grad_k, grad_v, grad_q = tile(
            own[block, head : 2 * head, :], own[block, 2 * head : 3 * head, :], True
        )
        grad_own[block, head : 2 * head, :] = (grad_k * scale).T.astype(BF16)
        grad_own[block, 2 * head : 3 * head, :] = grad_v.T.astype(BF16)

        def step(k, grad_q):
            at = first + k
            more_k, more_v, more_q = tile(
                prompts[at, 0:head, :], prompts[at, head : 2 * head, :], False
            )
            sum_k[at] += more_k
            sum_v[at] += more_v
            return grad_q + more_q

        grad_q = lax.fori_loop(0, full, step, grad_q)
        grad_own[block, 0:head, :] = (grad_q * scale).astype(BF16)

    @pl.when(step_id == pl.num_programs(0) - 1)
    def _():
        def finish(k, carry):
            grad_prompts[k, 0:head, :] = (sum_k[k] * scale).T.astype(BF16)
            grad_prompts[k, head : 2 * head, :] = sum_v[k].T.astype(BF16)
            return carry

        lax.fori_loop(0, sum_k.shape[0], finish, 0)


def attn_forward(plan, own, prompts):
    blocks, triple, length = own.shape
    head = triple // 3
    whole = pl.BlockSpec(memory_space=pltpu.VMEM)
    return pl.pallas_call(
        functools.partial(attn_fwd_kernel, head=head, factor=head**-0.5 * LOG2E),
        grid_spec=pltpu.PrefetchScalarGridSpec(
            num_scalar_prefetch=1,
            grid=(plan.shape[1],),
            in_specs=[whole, whole],
            out_specs=[whole, whole],
        ),
        out_shape=[
            jax.ShapeDtypeStruct((blocks, head, length), BF16),
            jax.ShapeDtypeStruct((blocks, 1, length), F32),
        ],
        compiler_params=pltpu.CompilerParams(vmem_limit_bytes=40 * 2**20),
        cost_estimate=pl.CostEstimate(
            flops=100 * length * length * 256 * 4,
            bytes_accessed=8 * 2**20,
            transcendentals=100 * length * length,
        ),
        name="attn_fwd",
    )(plan, own, prompts)


def attn_backward(plan, own, prompts, grad, out, log_sums):
    blocks, triple, length = own.shape
    head = triple // 3
    whole = pl.BlockSpec(memory_space=pltpu.VMEM)
    return pl.pallas_call(
        functools.partial(
            attn_bwd_kernel, head=head, factor=head**-0.5 * LOG2E, scale=head**-0.5
        ),
        grid_spec=pltpu.PrefetchScalarGridSpec(
            num_scalar_prefetch=1,
            grid=(plan.shape[1],),
            in_specs=[whole] * 5,
            out_specs=[whole, whole],
            scratch_shapes=[pltpu.VMEM((prompts.shape[0], length, head), F32)] * 2,
        ),
        out_shape=[
            jax.ShapeDtypeStruct(own.shape, BF16),
            jax.ShapeDtypeStruct(prompts.shape, BF16),
        ],
        compiler_params=pltpu.CompilerParams(vmem_limit_bytes=48 * 2**20),
        cost_estimate=pl.CostEstimate(
            flops=100 * length * length * 256 * 10,
            bytes_accessed=16 * 2**20,
            transcendentals=100 * length * length,
        ),
        name="attn_bwd",
    )(plan, own, prompts, grad, out, log_sums)


def swap(value):
    return lax.ppermute(value, "tensor", [(0, 1), (1, 0)])


def to_core_one(value):
    return lax.ppermute(value, "tensor", [(0, 1)])


def to_core_zero(value):
    return lax.ppermute(value, "tensor", [(1, 0)])


def with_other(value):
    return jnp.concatenate([value, swap(value)], 0)


def keep_rows(value):
    half = value.shape[0] // 2
    return value[:half] + swap(value[half:].astype(BF16)).astype(F32)


def pair_parts(value):
    half = value.shape[0] // 2
    low = value.astype(BF16)
    other = swap(low)
    return low, jnp.concatenate([other[half:], other[:half]], 0)


def gelu_pair(preact):
    square = preact * preact
    tanh = jnp.tanh(preact * (GELU_A + GELU_A * GELU_B * square))
    half = 0.5 * preact
    act = half + half * tanh
    slope = 0.5 + 0.5 * tanh + half * (1.0 - tanh * tanh) * (GELU_A + 3.0 * GELU_A * GELU_B * square)
    return lax.optimization_barrier((act.astype(BF16), slope.astype(BF16)))


def from_bit(value, bit):
    return lax.ppermute(value, "dp", [(i, i ^ bit) for i in range(lax.axis_size("dp"))])


def chip_place():
    place = lax.axis_index("dp")
    return place // 4, place // 2 % 2, place % 2


def ordered(bit, own, other, axis):
    return jnp.where(
        bit == 0, jnp.stack([own, other], axis), jnp.stack([other, own], axis)
    )


def gather_chips(value):
    planes = lax.axis_size("dp") // 4
    half = value.shape[1] // 2
    z, y, x = chip_place()
    blocks = jnp.stack([value] + [from_bit(value, 4 * k) for k in range(1, planes)])
    line = jnp.stack(
        [lax.dynamic_index_in_dim(blocks, z ^ k, 0, keepdims=False) for k in range(planes)]
    )
    first, second = line[:, :, :half], line[:, :, half:]
    first = ordered(y, first, from_bit(first, 2), 1)
    second = ordered(x, second, from_bit(second, 1), 1)
    return ordered(x, first, from_bit(first, 1), 2), ordered(y, second, from_bit(second, 2), 1)


def halve(value, bit, axis, partner):
    lower = lax.index_in_dim(value, 0, axis, keepdims=False)
    upper = lax.index_in_dim(value, 1, axis, keepdims=False)
    keep, send = jnp.where(bit == 0, lower, upper), jnp.where(bit == 0, upper, lower)
    return keep.astype(F32) + from_bit(send, partner).astype(F32)


def scatter_chips(first, second):
    planes = first.shape[0]
    z, y, x = chip_place()
    first = halve(first, x, 2, 1).astype(BF16)
    second = halve(second, y, 1, 2).astype(BF16)
    line = jnp.concatenate([halve(first, y, 1, 2), halve(second, x, 1, 1)], -1).astype(BF16)
    total = lax.dynamic_index_in_dim(line, z, 0, keepdims=False).astype(F32)
    for k in range(1, planes):
        part = lax.dynamic_index_in_dim(line, z ^ k, 0, keepdims=False)
        total = total + from_bit(part, 4 * k).astype(F32)
    return total


def fits_paired(mesh):
    return mesh.shape["tensor"] == 2 and mesh.shape["dp"] == 16


def body_paired(
    tokens,
    cont_prompt,
    routes,
    norm1_gain,
    w_query,
    w_key,
    w_value,
    w_attn_out,
    norm2_gain,
    w_ffn_in,
    w_ffn_out,
    centroids,
    expert_in_a,
    expert_out_a,
    expert_in_b,
    expert_out_b,
    grad_out,
):
    experts = lax.axis_size("dp")
    dp_index = lax.axis_index("dp")
    core_zero = lax.axis_index("tensor") == 0
    rows, width = tokens.shape
    rows_dp = 2 * rows
    shard = w_query.shape[0]
    half_heads = w_query.shape[1] // HEAD
    hidden = w_ffn_in.shape[1]
    triple = 3 * HEAD
    heads = 2 * half_heads
    both = lambda lower, upper: (jnp.where(core_zero, lower, upper), jnp.where(core_zero, upper, lower))

    route = routes[:, 0]
    slots_per = max(2, (3 * rows + 2 * experts - 1) // (2 * experts))
    capacity = 5 * rows_dp // 4
    onehot = route[:, None] == lax.broadcasted_iota(jnp.int32, (1, experts), 1)
    onehot_low = onehot.astype(BF16)
    below = lax.broadcasted_iota(jnp.int32, (rows, rows), 0) > lax.broadcasted_iota(
        jnp.int32, (rows, rows), 1
    )
    earlier = matmul(below.astype(BF16), onehot_low)
    local_rank = jnp.sum(jnp.where(onehot, earlier, 0.0), 1).astype(jnp.int32)
    target = route * slots_per + local_rank
    columns = lax.broadcasted_iota(jnp.int32, (1, experts * slots_per), 1)
    placer = (columns == target[:, None]).astype(BF16)
    counts = jnp.sum(onehot_low.astype(F32), 0).astype(BF16)
    counts_pair = jnp.concatenate(both(counts, swap(counts)), 0)

    qkv_shard = jnp.stack(
        [part.reshape(shard, half_heads, HEAD) for part in (w_query, w_key, w_value)], 2
    ).reshape(shard, half_heads * triple)
    extra = jnp.concatenate([norm1_gain, norm2_gain, counts_pair], 0)
    extra = jnp.pad(extra[None, :], ((0, 7), (0, half_heads * triple - extra.shape[0])))
    first_all, last_all = gather_chips(jnp.concatenate([qkv_shard, extra], 0))
    qkv_full = jnp.concatenate([first_all[..., :shard, :], last_all[..., :shard, :]], -1).reshape(
        width, half_heads * triple
    )
    extra_all = first_all[..., shard, :].reshape(experts, -1)
    gain_one = extra_all[:, :shard].reshape(width).astype(F32)
    gain_two = extra_all[:, shard : 2 * shard].reshape(width).astype(F32)
    counts_all = extra_all[:, 2 * shard : 2 * shard + 2 * experts].reshape(experts, 2, experts)

    mine = jnp.sum(
        jnp.where(lax.broadcasted_iota(jnp.int32, (1, 1, experts), 2) == dp_index, counts_all.astype(F32), 0.0),
        2,
    )
    per_chip = jnp.sum(mine, 1)
    chip_before = jnp.sum(
        jnp.where(
            lax.broadcasted_iota(jnp.int32, (experts, experts), 1)
            < lax.broadcasted_iota(jnp.int32, (experts, experts), 0),
            per_chip[None, :],
            0.0,
        ),
        1,
    )
    starts = both(chip_before, chip_before + mine[:, 0])
    slot_at = lax.broadcasted_iota(jnp.int32, (1, slots_per), 1).astype(F32)
    kept = jnp.concatenate(
        [(start[:, None] + slot_at < capacity).reshape(-1, 1) for start in starts], 0
    )
    half_rows = experts * slots_per

    pair_tokens = with_other(tokens).astype(F32)
    normed_one, hat_pair, inv_pair = norm_forward(pair_tokens, gain_one)
    inputs, hat_one, inv_one = pair_tokens[:rows], hat_pair[:rows], inv_pair[:rows]
    rows_one = normed_one.astype(BF16)
    other_t = lax.dot_general(
        qkv_full, rows_one[rows:], (((0,), (1,)), ((), ())), preferred_element_type=F32
    ).astype(BF16)
    own_t = lax.dot_general(
        qkv_full, rows_one[:rows], (((0,), (1,)), ((), ())), preferred_element_type=F32
    ).astype(BF16)
    qkv_t = jnp.concatenate(both(own_t, swap(other_t)), 0).reshape(heads, triple, rows)
    by_head = lax.all_to_all(qkv_t, "dp", split_axis=0, concat_axis=0, tiled=True)

    second_shard = jnp.concatenate([w_ffn_in, w_ffn_out.T, w_attn_out.T], 1)
    by_head, second_shard = lax.optimization_barrier((by_head, second_shard))
    second_all = lax.all_gather(
        second_shard, "dp", axis=0, tiled=True
    )
    ffn_in = second_all[:, :hidden]
    ffn_out_t = second_all[:, hidden : 2 * hidden]
    attn_half = second_all[:, 2 * hidden :]


    lent = experts // 4
    span = PLEN // rows
    own_blocks = jnp.concatenate([by_head, to_core_zero(by_head[:lent])], 0)
    prompt_kv = jnp.where(core_zero, by_head[:, HEAD:], to_core_one(by_head[:, HEAD:]))
    places = jnp.arange(experts + lent, dtype=jnp.int32)
    follows = cont_prompt * span
    plan_zero = jnp.stack(
        [
            places,
            jnp.where(places < experts, places % span, span),
            jnp.concatenate([places[:experts] // span * span, follows[:lent]], 0),
            jnp.ones_like(places),
        ]
    )
    plan_one = jnp.stack(
        [
            jnp.minimum(places + lent, experts - 1),
            jnp.full_like(places, span),
            jnp.concatenate([follows[lent:], jnp.zeros((2 * lent,), jnp.int32)], 0),
            (places < experts - lent).astype(jnp.int32),
        ]
    )
    plan = jnp.where(core_zero, plan_zero, plan_one)
    attn_blocks, log_sums = attn_forward(plan, own_blocks, prompt_kv)
    lent_back = to_core_one(attn_blocks[experts:])
    attn_own = jnp.concatenate(
        [jnp.where(core_zero, attn_blocks[:lent], lent_back), attn_blocks[lent:experts]], 0
    )
    attn_t = lax.all_to_all(attn_own, "dp", split_axis=0, concat_axis=0, tiled=True).reshape(
        width, rows
    )

    attn_out_t = jnp.concatenate(both(attn_half, swap(attn_half)), 1)
    hidden_one = inputs + lax.dot_general(
        attn_t, attn_out_t, (((0,), (1,)), ((), ())), preferred_element_type=F32
    )
    normed_two, hat_two, inv_two = norm_forward(hidden_one, gain_two)
    rows_two = with_other(normed_two.astype(BF16))
    ffn_act, ffn_slope = gelu_pair(matmul(rows_two, ffn_in))
    hidden_two = hidden_one + keep_rows(matmul_nt(ffn_act, ffn_out_t))

    sent_rows = (
        matmul_tn(placer, hidden_two.astype(BF16)).astype(BF16).reshape(experts, slots_per, width)
    )
    sent_grad = matmul_tn(placer, grad_out).astype(BF16).reshape(experts, slots_per, width)
    own_rows, sent_grad = lax.optimization_barrier((to_experts(sent_rows), sent_grad))
    grad_own = to_experts(sent_grad)
    expert_rows = with_other(own_rows.reshape(-1, width))
    centre = centroids[0]
    gate_value = jax.nn.sigmoid(matmul(expert_rows, centre))
    act_a, slope_a = gelu_pair(matmul(expert_rows, expert_in_a[0]))
    part_a, other_a = pair_parts(matmul(act_a, expert_out_a[0]))
    middle = (expert_rows.astype(F32) + part_a.astype(F32) + other_a.astype(F32)).astype(BF16)
    act_b, slope_b = gelu_pair(matmul(middle, expert_in_b[0]))
    act_b, grad_own = lax.optimization_barrier((act_b, grad_own))
    branch_half = (
        part_a[:half_rows].astype(F32)
        + other_a[:half_rows].astype(F32)
        + keep_rows(matmul(act_b, expert_out_b[0]))
    )
    gate_half = gate_value[:half_rows]
    returned = (
        jnp.where(kept[:half_rows], gate_half[:, None] * branch_half, 0.0)
        .astype(BF16)
        .reshape(experts, slots_per, width)
    )
    came_back = to_experts(returned).reshape(half_rows, width)

    grad_returned = jnp.where(kept, with_other(grad_own.reshape(-1, width)), 0.0).astype(BF16)
    grad_half = grad_returned[:half_rows].astype(F32)
    grad_logit_half = jnp.sum(grad_half * branch_half, 1) * gate_half * (1.0 - gate_half)
    centre_part = matmul(grad_logit_half, expert_rows[:half_rows].astype(F32))
    grad_branch = gate_value[:, None] * grad_returned.astype(F32)
    grad_b = grad_branch.astype(BF16)
    grad_pre_b = (matmul_nt(grad_b, expert_out_b[0]) * slope_b.astype(F32)).astype(BF16)
    part_m, other_m = pair_parts(matmul_nt(grad_pre_b, expert_in_b[0]))
    grad_a = (grad_branch + part_m.astype(F32) + other_m.astype(F32)).astype(BF16)
    grad_pre_a = (matmul_nt(grad_a, expert_out_a[0]) * slope_a.astype(F32)).astype(BF16)
    grad_rows = (
        keep_rows(matmul_nt(grad_pre_a, expert_in_a[0]))
        + part_m[:half_rows].astype(F32)
        + other_m[:half_rows].astype(F32)
        + grad_logit_half[:, None] * centre.astype(F32)[None, :]
    )
    grad_out_b = matmul_tn(act_b, grad_b)
    grad_in_b = matmul_tn(middle, grad_pre_b)
    grad_out_a = matmul_tn(act_a, grad_a)
    grad_in_a = matmul_tn(expert_rows, grad_pre_a)
    grad_rows, came_back = lax.optimization_barrier((grad_rows.astype(BF16), came_back))
    output = hidden_two + matmul(placer, came_back)
    grad_back = to_experts(grad_rows.reshape(experts, slots_per, width))
    grad_back, grad_out_b, grad_in_b, grad_out_a, grad_in_a = lax.optimization_barrier(
        (grad_back, grad_out_b, grad_in_b, grad_out_a, grad_in_a)
    )
    grad_back = grad_back.reshape(half_rows, width)
    grad_two = grad_out.astype(F32) + matmul(placer, grad_back)

    rows_down = with_other(grad_two.astype(BF16))
    grad_ffn_pre = (matmul(rows_down, ffn_out_t) * ffn_slope.astype(F32)).astype(BF16)
    grad_ffn_out_t = matmul_tn(rows_down, ffn_act)
    grad_ffn_in = matmul_tn(rows_two, grad_ffn_pre)
    grad_norm_two = keep_rows(matmul_nt(grad_ffn_pre, ffn_in))
    back_two = norm_backward(grad_norm_two, hat_two, inv_two, gain_two)[0]
    grad_one = grad_two + back_two

    grad_branch_one = grad_one.astype(BF16)
    grad_attn_t = lax.dot_general(
        attn_out_t, grad_branch_one, (((0,), (1,)), ((), ())), preferred_element_type=F32
    ).astype(BF16)
    grad_by_head = lax.all_to_all(
        grad_attn_t.reshape(heads, HEAD, rows), "dp", split_axis=0, concat_axis=0, tiled=True
    )
    grad_attn_out = lax.dot_general(
        grad_branch_one, attn_t, (((0,), (1,)), ((), ())), preferred_element_type=F32
    )
    half_width = width // 2
    part_own, part_other = both(grad_attn_out[:, :half_width], grad_attn_out[:, half_width:])
    grad_attn_half = part_own + swap(part_other.astype(BF16)).astype(F32)
    second_sum = lax.psum_scatter(
        jnp.concatenate(
            [grad_ffn_in.astype(BF16), grad_ffn_out_t.astype(BF16), grad_attn_half.astype(BF16)], 1
        ),
        "dp",
        scatter_dimension=0,
        tiled=True,
    ).astype(F32)
    grad_blocks = jnp.concatenate([grad_by_head, to_core_zero(grad_by_head[:lent])], 0)
    grad_own_blocks, grad_prompts = attn_backward(
        plan, own_blocks, prompt_kv, grad_blocks, attn_blocks, log_sums
    )
    lent_grad = to_core_one(grad_own_blocks[experts:])
    prompt_sum = grad_prompts.astype(F32) + to_core_zero(grad_prompts).astype(F32)
    prompt_part = jnp.concatenate(
        [
            grad_own_blocks[:experts, :HEAD],
            (grad_own_blocks[:experts, HEAD:].astype(F32) + prompt_sum).astype(BF16),
        ],
        1,
    )
    cont_part = jnp.concatenate([lent_grad, grad_own_blocks[lent:experts]], 0)
    grad_qkv = lax.all_to_all(
        jnp.where(core_zero, prompt_part, cont_part), "dp", split_axis=0, concat_axis=0, tiled=True
    ).reshape(2, half_heads * triple, rows)
    keep_half, send_half = both(grad_qkv[0], grad_qkv[1])
    grad_qkv_t = jnp.concatenate([keep_half, swap(send_half)], 1)
    grad_qkv_w = lax.dot_general(
        rows_one, grad_qkv_t, (((0,), (1,)), ((), ())), preferred_element_type=F32
    ).astype(BF16)
    by_chip = grad_qkv_w.reshape(experts // 4, 2, 2, shard, half_heads * triple)
    half_columns = half_heads * triple // 2
    qkv_sum = scatter_chips(by_chip[..., :half_columns], by_chip[..., half_columns:])
    grad_norm_one = keep_rows(
        lax.dot_general(
            grad_qkv_t, qkv_full, (((0,), (1,)), ((), ())), preferred_element_type=F32
        )
    )
    back_one = norm_backward(grad_norm_one, hat_one, inv_one, gain_one)[0]
    grad_input = grad_one + back_one
    qkv_sum = qkv_sum.reshape(shard, half_heads, 3, HEAD)
    query_shard, key_shard, value_shard = (
        qkv_sum[:, :, part].reshape(shard, half_heads * HEAD) for part in range(3)
    )

    ffn_in_sum = second_sum[:, :hidden]
    gains = jnp.stack(
        [
            jnp.sum(query_shard * w_query + key_shard * w_key + value_shard * w_value, 1)
            / norm1_gain.astype(F32),
            jnp.sum(ffn_in_sum * w_ffn_in, 1) / norm2_gain.astype(F32),
        ]
    )
    gains = gains + swap(gains)
    centre_grad = centre_part + swap(centre_part)
    return (
        output.astype(BF16),
        grad_input.astype(BF16),
        gains[0],
        query_shard,
        key_shard,
        value_shard,
        second_sum[:, 2 * hidden :].T,
        gains[1],
        ffn_in_sum,
        second_sum[:, hidden : 2 * hidden].T,
        centre_grad[None, :],
        grad_in_a[None],
        grad_out_a[None],
        grad_in_b[None],
        grad_out_b[None],
    )


def solution(mesh):
    body = body_paired if fits_paired(mesh) else body_general
    return jax.shard_map(
        body,
        mesh=mesh,
        in_specs=(
            P(("dp", "tensor"), None),
            P(),
            P(("dp", "tensor"), None),
            P("dp"),
            P("dp", "tensor"),
            P("dp", "tensor"),
            P("dp", "tensor"),
            P("tensor", "dp"),
            P("dp"),
            P("dp", "tensor"),
            P("tensor", "dp"),
            P("dp", None),
            P("dp", None, "tensor"),
            P("dp", "tensor", None),
            P("dp", None, "tensor"),
            P("dp", "tensor", None),
            P(("dp", "tensor"), None),
        ),
        out_specs=(
            P(("dp", "tensor"), None),
            P(("dp", "tensor"), None),
            P("dp"),
            P("dp", "tensor"),
            P("dp", "tensor"),
            P("dp", "tensor"),
            P("tensor", "dp"),
            P("dp"),
            P("dp", "tensor"),
            P("tensor", "dp"),
            P("dp", None),
            P("dp", None, "tensor"),
            P("dp", "tensor", None),
            P("dp", None, "tensor"),
            P("dp", "tensor", None),
        ),
        check_vma=False,
    )
```

```python
import functools

import jax
import jax.numpy as jnp
import numpy as np
from jax import lax
from jax.experimental import pallas as pl
from jax.experimental.pallas import tpu as pltpu
from jax.sharding import PartitionSpec as P

HEAD = 64
PLEN = 4096
CONT = 512


def shortened(value):

    def short(part):
        return part.astype(jnp.bfloat16) if part.dtype == jnp.float32 else part

    return jax.tree.map(short, value)


def carried_in(value, axis, combine, identity):
    peers, place = (lax.axis_size(axis), lax.axis_index(axis))
    everything = lax.all_gather(value, axis)
    start = jnp.broadcast_to(jnp.asarray(identity, value.dtype), value.shape)

    def turn(k, before):
        reached = k < place
        new = combine(before, everything[k])
        return jnp.where(reached, new, before)

    return lax.fori_loop(0, peers, turn, start)


def rows_gather(value):
    return lax.all_gather(value, "tensor", axis=0, tiled=True)


def rows_scatter(value):
    return lax.psum_scatter(
        value.astype(jnp.bfloat16), "tensor", scatter_dimension=0, tiled=True
    ).astype(jnp.float32)


def pair_total(value):
    return jax.tree.map(lambda part: part.astype(jnp.float32), lax.psum(shortened(value), "tensor"))


def to_experts(value):
    return lax.all_to_all(value, "dp", split_axis=0, concat_axis=0, tiled=True)


def matmul(left, right):
    return jnp.dot(left, right, preferred_element_type=jnp.float32)


def matmul_tn(left, right):
    return lax.dot_general(
        left, right, (((0,), (0,)), ((), ())), preferred_element_type=jnp.float32
    )


def matmul_nt(left, right):
    return lax.dot_general(
        left, right, (((1,), (1,)), ((), ())), preferred_element_type=jnp.float32
    )


def norm_forward(hidden, gain):
    mean_row = jnp.mean(hidden, -1, keepdims=True)
    centred = hidden - mean_row
    scale_inv = lax.rsqrt(jnp.mean(centred * centred, -1, keepdims=True) + 1e-05)
    normed = centred * scale_inv
    return (normed * gain, normed, scale_inv)


def norm_backward(grad_m, normed, scale_inv, gain):
    grad_hat = grad_m * gain
    inner = (
        grad_hat
        - jnp.mean(grad_hat, -1, keepdims=True)
        - normed * jnp.mean(grad_hat * normed, -1, keepdims=True)
    )
    return (inner * scale_inv, jnp.sum(grad_m * normed, 0))


def gelu_grad(preact, grad):
    unused, pull = jax.vjp(jax.nn.gelu, preact)
    return pull(grad)[0]


def add_counts(first, second):
    return first + second


def attend(queries, keys, values, allowed, heads):
    scale = HEAD ** (-0.5)

    def head_step(head, carry):
        outputs, log_sums = carry
        query_h = lax.dynamic_slice_in_dim(queries, head * HEAD, HEAD, 1)
        key_h = lax.dynamic_slice_in_dim(keys, head * HEAD, HEAD, 1)
        value_h = lax.dynamic_slice_in_dim(values, head * HEAD, HEAD, 1)
        scores = jnp.where(allowed, matmul_nt(query_h, key_h) * scale, -1e30)
        top_score = jnp.max(scores, 1, keepdims=True)
        expo = jnp.exp(scores - top_score)
        total = jnp.sum(expo, 1, keepdims=True)
        probs = (expo / total).astype(jnp.bfloat16)
        outputs = lax.dynamic_update_slice_in_dim(outputs, matmul(probs, value_h), head * HEAD, 1)
        log_sums = lax.dynamic_update_index_in_dim(
            log_sums, top_score[:, 0] + jnp.log(total[:, 0]), head, 0
        )
        return (outputs, log_sums)

    start_state = (
        jnp.zeros((queries.shape[0], heads * HEAD), jnp.float32),
        jnp.zeros((heads, queries.shape[0]), jnp.float32),
    )
    return lax.fori_loop(0, heads, head_step, start_state)


def attend_back(queries, keys, values, allowed, log_sums, grad_attended, heads):
    scale = HEAD ** (-0.5)

    def head_step(head, carry):
        grad_q, grad_k, grad_v = carry
        query_h = lax.dynamic_slice_in_dim(queries, head * HEAD, HEAD, 1)
        key_h = lax.dynamic_slice_in_dim(keys, head * HEAD, HEAD, 1)
        value_h = lax.dynamic_slice_in_dim(values, head * HEAD, HEAD, 1)
        grad_o = lax.dynamic_slice_in_dim(grad_attended, head * HEAD, HEAD, 1)
        scores = jnp.where(allowed, matmul_nt(query_h, key_h) * scale, -1e30)
        probs = jnp.exp(
            scores - lax.dynamic_index_in_dim(log_sums, head, 0, keepdims=False)[:, None]
        )
        grad_p = matmul_nt(grad_o, value_h)
        grad_s = (probs * (grad_p - jnp.sum(probs * grad_p, 1, keepdims=True))).astype(jnp.bfloat16)
        grad_q = lax.dynamic_update_slice_in_dim(
            grad_q, matmul(grad_s, key_h) * scale, head * HEAD, 1
        )
        grad_k = lax.dynamic_update_slice_in_dim(
            grad_k, matmul_tn(grad_s, query_h) * scale, head * HEAD, 1
        )
        grad_v = lax.dynamic_update_slice_in_dim(
            grad_v, matmul_tn(probs.astype(jnp.bfloat16), grad_o), head * HEAD, 1
        )
        return (grad_q, grad_k, grad_v)

    start_state = (
        jnp.zeros(queries.shape, jnp.float32),
        jnp.zeros(keys.shape, jnp.float32),
        jnp.zeros(values.shape, jnp.float32),
    )
    return lax.fori_loop(0, heads, head_step, start_state)


def add_block(buffer, block, start):
    length = block.shape[0]
    current = lax.dynamic_slice_in_dim(buffer, start, length, 0)
    return lax.dynamic_update_slice_in_dim(buffer, current + block, start, 0)


def body_general(
    tokens,
    cont_prompt,
    routes,
    norm1_gain,
    w_query,
    w_key,
    w_value,
    w_attn_out,
    norm2_gain,
    w_ffn_in,
    w_ffn_out,
    centroids,
    expert_in_a,
    expert_out_a,
    expert_in_b,
    expert_out_b,
    grad_out,
):
    experts = lax.axis_size("dp")
    pair_size = lax.axis_size("tensor")
    dp_index = lax.axis_index("dp")
    tensor_index = lax.axis_index("tensor")
    rows_dev = tokens.shape[0]
    rows_dp = rows_dev * pair_size
    prm_dev = rows_dp - CONT
    pkeys = experts * prm_dev
    heads = w_query.shape[1] // HEAD
    width = tokens.shape[1]
    span = PLEN // prm_dev
    owner_start = dp_index // span * PLEN
    mapped_start = cont_prompt[dp_index] * PLEN
    gain_one, query_full, key_full, value_full, attn_full, gain_two, ffn_in_full, ffn_out_full = (
        lax.all_gather(norm1_gain, "dp", axis=0, tiled=True),
        lax.all_gather(w_query, "dp", axis=0, tiled=True),
        lax.all_gather(w_key, "dp", axis=0, tiled=True),
        lax.all_gather(w_value, "dp", axis=0, tiled=True),
        lax.all_gather(w_attn_out, "dp", axis=1, tiled=True),
        lax.all_gather(norm2_gain, "dp", axis=0, tiled=True),
        lax.all_gather(w_ffn_in, "dp", axis=0, tiled=True),
        lax.all_gather(w_ffn_out, "dp", axis=1, tiled=True),
    )
    inputs = tokens.astype(jnp.float32)
    normed_one, hat_one, inv_one = norm_forward(inputs, gain_one.astype(jnp.float32))
    rows_one = rows_gather(normed_one.astype(jnp.bfloat16))
    queries = matmul(rows_one, query_full).astype(jnp.bfloat16)
    keys_own = matmul(rows_one, key_full).astype(jnp.bfloat16)
    values_own = matmul(rows_one, value_full).astype(jnp.bfloat16)
    prompt_keys, prompt_values = (
        lax.all_gather(keys_own[:prm_dev], "dp", axis=0, tiled=True),
        lax.all_gather(values_own[:prm_dev], "dp", axis=0, tiled=True),
    )
    keys_first = lax.dynamic_slice_in_dim(prompt_keys, owner_start, PLEN, 0)
    values_first = lax.dynamic_slice_in_dim(prompt_values, owner_start, PLEN, 0)
    first_row = lax.broadcasted_iota(jnp.int32, (prm_dev, 1), 0)
    first_column = lax.broadcasted_iota(jnp.int32, (1, PLEN), 1)
    allowed_first = first_column <= dp_index % span * prm_dev + first_row
    keys_second = jnp.concatenate(
        [lax.dynamic_slice_in_dim(prompt_keys, mapped_start, PLEN, 0), keys_own[prm_dev:]], 0
    )
    values_second = jnp.concatenate(
        [lax.dynamic_slice_in_dim(prompt_values, mapped_start, PLEN, 0), values_own[prm_dev:]], 0
    )
    second_row = lax.broadcasted_iota(jnp.int32, (CONT, 1), 0)
    second_column = lax.broadcasted_iota(jnp.int32, (1, PLEN + CONT), 1)
    allowed_second = (second_column < PLEN) | (second_column - PLEN <= second_row)
    attn_first, sums_first = attend(
        queries[:prm_dev], keys_first, values_first, allowed_first, heads
    )
    attn_second, sums_second = attend(
        queries[prm_dev:], keys_second, values_second, allowed_second, heads
    )
    attn_low = jnp.concatenate([attn_first, attn_second], 0).astype(jnp.bfloat16)
    hidden_one = inputs + rows_scatter(matmul(attn_low, attn_full))
    normed_two, hat_two, inv_two = norm_forward(hidden_one, gain_two.astype(jnp.float32))
    rows_two = rows_gather(normed_two.astype(jnp.bfloat16))
    ffn_pre = matmul(rows_two, ffn_in_full)
    ffn_act = jax.nn.gelu(ffn_pre).astype(jnp.bfloat16)
    hidden_two = hidden_one + rows_scatter(matmul(ffn_act, ffn_out_full))
    route = routes[:, 0]
    slots_per = max(2, (3 * rows_dev + 2 * experts - 1) // (2 * experts))
    capacity = 5 * rows_dp // 4
    expert_ids = lax.broadcasted_iota(jnp.int32, (1, experts), 1)
    onehot = (route[:, None] == expert_ids).astype(jnp.int32)
    offsets = carried_in(
        jnp.sum(onehot, 0), ("dp", "tensor"), add_counts, jnp.zeros((experts,), jnp.int32)
    )
    local_rank = jnp.sum((jnp.cumsum(onehot, 0) - 1) * onehot, 1)
    global_slot = local_rank + jnp.sum(onehot * offsets[None, :], 1)
    kept = global_slot < capacity
    target = route * slots_per + local_rank
    columns = lax.broadcasted_iota(jnp.int32, (1, experts * slots_per), 1)
    placer = ((columns == target[:, None]) & kept[:, None]).astype(jnp.bfloat16)
    sent_rows = (
        matmul_tn(placer, hidden_two.astype(jnp.bfloat16))
        .astype(jnp.bfloat16)
        .reshape(experts, slots_per, width)
    )
    expert_rows = rows_gather(to_experts(sent_rows)).reshape(-1, width)
    centre = centroids[0]
    gate_value = jax.nn.sigmoid(matmul(expert_rows, centre))
    pre_a = matmul(expert_rows, expert_in_a[0])
    act_a = jax.nn.gelu(pre_a).astype(jnp.bfloat16)
    branch_a = pair_total(matmul(act_a, expert_out_a[0]))
    middle = (expert_rows.astype(jnp.float32) + branch_a).astype(jnp.bfloat16)
    pre_b = matmul(middle, expert_in_b[0])
    act_b = jax.nn.gelu(pre_b).astype(jnp.bfloat16)
    branch_b = rows_scatter(matmul(act_b, expert_out_b[0]))
    half_rows = expert_rows.shape[0] // pair_size
    start_row = tensor_index * half_rows
    branch_half = lax.dynamic_slice_in_dim(branch_a, start_row, half_rows, 0) + branch_b
    gate_half = lax.dynamic_slice_in_dim(gate_value, start_row, half_rows, 0)
    returned = (
        (gate_half[:, None] * branch_half).astype(jnp.bfloat16).reshape(experts, slots_per, width)
    )
    came_back = to_experts(returned).reshape(experts * slots_per, width)
    output = hidden_two + matmul(placer, came_back)
    cotangent = grad_out.astype(jnp.float32)
    sent_grad = matmul_tn(placer, grad_out).astype(jnp.bfloat16).reshape(experts, slots_per, width)
    grad_half = to_experts(sent_grad).reshape(half_rows, width)
    grad_returned = rows_gather(grad_half).astype(jnp.float32)
    grad_gate_half = jnp.sum(grad_half.astype(jnp.float32) * branch_half, 1)
    grad_logit_half = grad_gate_half * gate_half * (1.0 - gate_half)
    rows_half = lax.dynamic_slice_in_dim(expert_rows, start_row, half_rows, 0)
    centre_part = matmul(grad_logit_half, rows_half.astype(jnp.float32))
    grad_branch = gate_value[:, None] * grad_returned
    grad_b = grad_branch.astype(jnp.bfloat16)
    grad_pre_b = gelu_grad(pre_b, matmul_nt(grad_b, expert_out_b[0])).astype(jnp.bfloat16)
    grad_out_b = matmul_tn(act_b, grad_b)
    grad_in_b = matmul_tn(middle, grad_pre_b)
    grad_middle = pair_total(matmul_nt(grad_pre_b, expert_in_b[0]))
    grad_a = (grad_branch + grad_middle).astype(jnp.bfloat16)
    grad_pre_a = gelu_grad(pre_a, matmul_nt(grad_a, expert_out_a[0])).astype(jnp.bfloat16)
    grad_out_a = matmul_tn(act_a, grad_a)
    grad_in_a = matmul_tn(expert_rows, grad_pre_a)
    grad_rows = (
        rows_scatter(matmul_nt(grad_pre_a, expert_in_a[0]))
        + lax.dynamic_slice_in_dim(grad_middle, start_row, half_rows, 0)
        + grad_logit_half[:, None] * centre.astype(jnp.float32)[None, :]
    )
    grad_back = to_experts(
        grad_rows.astype(jnp.bfloat16).reshape(experts, slots_per, width)
    ).reshape(experts * slots_per, width)
    grad_two = cotangent + matmul(placer, grad_back)
    gain_one, query_full, key_full, value_full, attn_full, gain_two, ffn_in_full, ffn_out_full = (
        lax.all_gather(norm1_gain, "dp", axis=0, tiled=True),
        lax.all_gather(w_query, "dp", axis=0, tiled=True),
        lax.all_gather(w_key, "dp", axis=0, tiled=True),
        lax.all_gather(w_value, "dp", axis=0, tiled=True),
        lax.all_gather(w_attn_out, "dp", axis=1, tiled=True),
        lax.all_gather(norm2_gain, "dp", axis=0, tiled=True),
        lax.all_gather(w_ffn_in, "dp", axis=0, tiled=True),
        lax.all_gather(w_ffn_out, "dp", axis=1, tiled=True),
    )
    rows_down = rows_gather(grad_two.astype(jnp.bfloat16))
    grad_ffn_pre = gelu_grad(ffn_pre, matmul_nt(rows_down, ffn_out_full)).astype(jnp.bfloat16)
    grad_ffn_out = matmul_tn(ffn_act, rows_down)
    grad_ffn_in = matmul_tn(rows_two, grad_ffn_pre)
    grad_norm_two = rows_scatter(matmul_nt(grad_ffn_pre, ffn_in_full))
    back_two, grad_gain_two = norm_backward(
        grad_norm_two, hat_two, inv_two, gain_two.astype(jnp.float32)
    )
    grad_one = grad_two + back_two
    rows_attn = rows_gather(grad_one.astype(jnp.bfloat16))
    grad_attn_out = matmul_tn(attn_low, rows_attn)
    grad_attended = matmul_nt(rows_attn, attn_full).astype(jnp.bfloat16)
    grad_q_first, grad_k_first, grad_v_first = attend_back(
        queries[:prm_dev],
        keys_first,
        values_first,
        allowed_first,
        sums_first,
        grad_attended[:prm_dev],
        heads,
    )
    grad_q_second, grad_k_second, grad_v_second = attend_back(
        queries[prm_dev:],
        keys_second,
        values_second,
        allowed_second,
        sums_second,
        grad_attended[prm_dev:],
        heads,
    )
    local_width = keys_own.shape[1]
    buffer_k = jnp.zeros((pkeys, local_width), jnp.float32)
    buffer_v = jnp.zeros((pkeys, local_width), jnp.float32)
    buffer_k = add_block(
        add_block(buffer_k, grad_k_first, owner_start), grad_k_second[:PLEN], mapped_start
    )
    buffer_v = add_block(
        add_block(buffer_v, grad_v_first, owner_start), grad_v_second[:PLEN], mapped_start
    )
    prompt_grad_k, prompt_grad_v = (
        lax.psum_scatter(buffer_k, "dp", scatter_dimension=0, tiled=True),
        lax.psum_scatter(buffer_v, "dp", scatter_dimension=0, tiled=True),
    )
    grad_keys = jnp.concatenate([prompt_grad_k, grad_k_second[PLEN:]], 0).astype(jnp.bfloat16)
    grad_values = jnp.concatenate([prompt_grad_v, grad_v_second[PLEN:]], 0).astype(jnp.bfloat16)
    grad_queries = jnp.concatenate([grad_q_first, grad_q_second], 0).astype(jnp.bfloat16)
    grad_query = matmul_tn(rows_one, grad_queries)
    grad_key = matmul_tn(rows_one, grad_keys)
    grad_value = matmul_tn(rows_one, grad_values)
    grad_norm_one = rows_scatter(
        matmul_nt(grad_queries, query_full)
        + matmul_nt(grad_keys, key_full)
        + matmul_nt(grad_values, value_full)
    )
    back_one, grad_gain_one = norm_backward(
        grad_norm_one, hat_one, inv_one, gain_one.astype(jnp.float32)
    )
    grad_input = grad_one + back_one
    (
        gain_one_part,
        query_shard,
        key_shard,
        value_shard,
        attn_shard,
        gain_two_part,
        ffn_in_shard,
        ffn_out_shard,
    ) = (
        lax.psum_scatter(grad_gain_one, "dp", scatter_dimension=0, tiled=True),
        lax.psum_scatter(grad_query, "dp", scatter_dimension=0, tiled=True),
        lax.psum_scatter(grad_key, "dp", scatter_dimension=0, tiled=True),
        lax.psum_scatter(grad_value, "dp", scatter_dimension=0, tiled=True),
        lax.psum_scatter(grad_attn_out, "dp", scatter_dimension=1, tiled=True),
        lax.psum_scatter(grad_gain_two, "dp", scatter_dimension=0, tiled=True),
        lax.psum_scatter(grad_ffn_in, "dp", scatter_dimension=0, tiled=True),
        lax.psum_scatter(grad_ffn_out, "dp", scatter_dimension=1, tiled=True),
    )
    gain_one_shard, gain_two_shard, centre_grad = pair_total(
        (gain_one_part, gain_two_part, centre_part)
    )
    return (
        output.astype(jnp.bfloat16),
        grad_input.astype(jnp.bfloat16),
        gain_one_shard,
        query_shard,
        key_shard,
        value_shard,
        attn_shard,
        gain_two_shard,
        ffn_in_shard,
        ffn_out_shard,
        centre_grad[None, :],
        grad_in_a[None],
        grad_out_a[None],
        grad_in_b[None],
        grad_out_b[None],
    )


LOG2E = 1.4426950408889634
GELU_A = 0.7978845608028654
GELU_B = 0.044715
BF16 = jnp.bfloat16
F32 = jnp.float32


def dot_tt(left, right):
    return lax.dot_general(left, right, (((0,), (0,)), ((), ())), preferred_element_type=F32)


def attn_fwd_kernel(plan, own, prompts, out, log_sums, values, *, head, factor):
    step_id = pl.program_id(0)
    block, full, first = plan[0, step_id], plan[1, step_id], plan[2, step_id]

    def with_ones(value):
        return jnp.concatenate([value.T, jnp.ones((value.shape[1], head), BF16)], 1)

    @pl.when(step_id == 0)
    def _():
        def turn(k, carry):
            values[k] = with_ones(prompts[k, head : 2 * head, :])
            return carry

        lax.fori_loop(0, prompts.shape[0], turn, 0)

    @pl.when(plan[3, step_id] > 0)
    def _():
        query = own[block, 0:head, :].T
        scores = matmul(query, own[block, head : 2 * head, :])
        query_at = lax.broadcasted_iota(jnp.int32, scores.shape, 0)
        key_at = lax.broadcasted_iota(jnp.int32, scores.shape, 1)
        scores = jnp.where(key_at <= query_at, scores, -1e30)
        top = jnp.max(scores, 1, keepdims=True) * factor
        expo = jnp.exp2(scores * factor - top)
        result = matmul(expo.astype(BF16), with_ones(own[block, 2 * head : 3 * head, :]))

        def step(k, carry):
            before, result = carry
            scores = matmul(query, prompts[first + k, 0:head, :])
            top = jnp.maximum(before, jnp.max(scores, 1, keepdims=True) * factor)
            expo = jnp.exp2(scores * factor - top)
            result = result * jnp.exp2(before - top) + matmul(expo.astype(BF16), values[first + k])
            return top, result

        top, result = lax.fori_loop(0, full, step, (top, result))
        result = result.T
        total = result[head : head + 1]
        out[block] = (result[:head] / total).astype(BF16)
        top = jnp.broadcast_to(top, (top.shape[0], 128)).T[0:1]
        log_sums[block] = top + jnp.log2(total)


def attn_bwd_kernel(
    plan, own, prompts, grad, out, log_sums, grad_own, grad_prompts, sum_k, sum_v, *, head, factor, scale
):
    step_id = pl.program_id(0)
    block, full, first = plan[0, step_id], plan[1, step_id], plan[2, step_id]

    @pl.when(step_id == 0)
    def _():
        sum_k[...] = jnp.zeros_like(sum_k)
        sum_v[...] = jnp.zeros_like(sum_v)

    @pl.when(plan[3, step_id] > 0)
    def _():
        query_t, grad_t, log_sum = own[block, 0:head, :], grad[block], log_sums[block]
        inner = jnp.sum(grad_t.astype(F32) * out[block].astype(F32), 0, keepdims=True)
        query, grad_o = query_t.T, grad_t.T

        def tile(key, value, diagonal):
            probs = jnp.exp2(dot_tt(key, query_t) * factor - log_sum)
            if diagonal:
                key_at = lax.broadcasted_iota(jnp.int32, probs.shape, 0)
                query_at = lax.broadcasted_iota(jnp.int32, probs.shape, 1)
                probs = jnp.where(key_at <= query_at, probs, 0.0)
            grad_s = (probs * (dot_tt(value, grad_t) - inner)).astype(BF16)
            return matmul(grad_s, query), matmul(probs.astype(BF16), grad_o), matmul(key, grad_s)

        grad_k, grad_v, grad_q = tile(
            own[block, head : 2 * head, :], own[block, 2 * head : 3 * head, :], True
        )
        grad_own[block, head : 2 * head, :] = (grad_k * scale).T.astype(BF16)
        grad_own[block, 2 * head : 3 * head, :] = grad_v.T.astype(BF16)

        def step(k, grad_q):
            at = first + k
            more_k, more_v, more_q = tile(
                prompts[at, 0:head, :], prompts[at, head : 2 * head, :], False
            )
            sum_k[at] += more_k
            sum_v[at] += more_v
            return grad_q + more_q

        grad_q = lax.fori_loop(0, full, step, grad_q)
        grad_own[block, 0:head, :] = (grad_q * scale).astype(BF16)

    @pl.when(step_id == pl.num_programs(0) - 1)
    def _():
        def finish(k, carry):
            grad_prompts[k, 0:head, :] = (sum_k[k] * scale).T.astype(BF16)
            grad_prompts[k, head : 2 * head, :] = sum_v[k].T.astype(BF16)
            return carry

        lax.fori_loop(0, sum_k.shape[0], finish, 0)


def attn_forward(plan, own, prompts):
    blocks, triple, length = own.shape
    head = triple // 3
    whole = pl.BlockSpec(memory_space=pltpu.VMEM)
    return pl.pallas_call(
        functools.partial(attn_fwd_kernel, head=head, factor=head**-0.5 * LOG2E),
        grid_spec=pltpu.PrefetchScalarGridSpec(
            num_scalar_prefetch=1,
            grid=(plan.shape[1],),
            in_specs=[whole, whole],
            out_specs=[whole, whole],
            scratch_shapes=[pltpu.VMEM((prompts.shape[0], length, 2 * head), BF16)],
        ),
        out_shape=[
            jax.ShapeDtypeStruct((blocks, head, length), BF16),
            jax.ShapeDtypeStruct((blocks, 1, length), F32),
        ],
        compiler_params=pltpu.CompilerParams(vmem_limit_bytes=40 * 2**20),
        cost_estimate=pl.CostEstimate(
            flops=100 * length * length * 256 * 4,
            bytes_accessed=8 * 2**20,
            transcendentals=100 * length * length,
        ),
        name="attn_fwd",
    )(plan, own, prompts)


def attn_backward(plan, own, prompts, grad, out, log_sums):
    blocks, triple, length = own.shape
    head = triple // 3
    whole = pl.BlockSpec(memory_space=pltpu.VMEM)
    return pl.pallas_call(
        functools.partial(
            attn_bwd_kernel, head=head, factor=head**-0.5 * LOG2E, scale=head**-0.5
        ),
        grid_spec=pltpu.PrefetchScalarGridSpec(
            num_scalar_prefetch=1,
            grid=(plan.shape[1],),
            in_specs=[whole] * 5,
            out_specs=[whole, whole],
            scratch_shapes=[pltpu.VMEM((prompts.shape[0], length, head), F32)] * 2,
        ),
        out_shape=[
            jax.ShapeDtypeStruct(own.shape, BF16),
            jax.ShapeDtypeStruct(prompts.shape, BF16),
        ],
        compiler_params=pltpu.CompilerParams(vmem_limit_bytes=48 * 2**20),
        cost_estimate=pl.CostEstimate(
            flops=100 * length * length * 256 * 10,
            bytes_accessed=16 * 2**20,
            transcendentals=100 * length * length,
        ),
        name="attn_bwd",
    )(plan, own, prompts, grad, out, log_sums)


def swap(value):
    return lax.ppermute(value, "tensor", [(0, 1), (1, 0)])


def to_core_one(value):
    return lax.ppermute(value, "tensor", [(0, 1)])


def to_core_zero(value):
    return lax.ppermute(value, "tensor", [(1, 0)])


def with_other(value):
    return jnp.concatenate([value, swap(value)], 0)


def keep_rows(value):
    half = value.shape[0] // 2
    return value[:half].astype(F32) + swap(value[half:].astype(BF16)).astype(F32)


def pair_parts(value):
    half = value.shape[0] // 2
    low = value.astype(BF16)
    other = swap(low)
    return low, jnp.concatenate([other[half:], other[:half]], 0)


def gelu_pair(preact):
    square = preact * preact
    gate = 0.5 + 0.5 * jnp.tanh(preact * (GELU_A + GELU_A * GELU_B * square))
    act = preact * gate
    slope = gate + act * (1.0 - gate) * (2.0 * GELU_A + 6.0 * GELU_A * GELU_B * square)
    return act.astype(BF16), slope.astype(BF16)


def mlp_kernel(*refs, terms, transposed):
    ins, (w_in, w_out), outs = refs[:terms], refs[terms : terms + 2], refs[terms + 2 :]
    rows = ins[0][...]
    if terms > 1:
        total = rows.astype(F32)
        for term in ins[1:]:
            total = total + term[...].astype(F32)
        rows = total.astype(BF16)
        outs[0][...] = rows
    act, slope = gelu_pair(matmul(rows, w_in[...]))
    outs[-3][...] = act
    outs[-2][...] = slope
    outs[-1][...] = (matmul_nt if transposed else matmul)(act, w_out[...]).astype(BF16)


def mlp_forward(terms, w_in, w_out, hidden, length, transposed=False, columns=(0, 0)):
    rows, width = terms[0].shape
    steps = rows // length
    row_block = pl.BlockSpec((length, width), lambda m: (m, 0))
    turned = pl.BlockSpec((length, width), lambda m: ((m + steps // 2) % steps, 0))
    hidden_block = pl.BlockSpec((length, hidden), lambda m: (m, 0))
    once = dict(pipeline_mode=pl.Buffered(1))
    in_block = pl.BlockSpec((width, hidden), lambda m: (0, columns[0]), **once)
    out_block = (
        pl.BlockSpec((width, hidden), lambda m: (0, columns[1]), **once)
        if transposed
        else pl.BlockSpec((hidden, width), lambda m: (0, 0), **once)
    )
    several = len(terms) > 1
    return pl.pallas_call(
        functools.partial(mlp_kernel, terms=len(terms), transposed=transposed),
        grid=(steps,),
        in_specs=([row_block, row_block, turned] if several else [row_block]) + [in_block, out_block],
        out_specs=[row_block] * several + [hidden_block, hidden_block, row_block],
        out_shape=[jax.ShapeDtypeStruct((rows, width), BF16)] * several
        + [jax.ShapeDtypeStruct((rows, hidden), BF16)] * 2
        + [jax.ShapeDtypeStruct((rows, width), BF16)],
        compiler_params=pltpu.CompilerParams(vmem_limit_bytes=52 * 2**20),
        cost_estimate=pl.CostEstimate(
            flops=4 * rows * width * hidden,
            bytes_accessed=4 * width * hidden + 4 * rows * hidden + 4 * rows * width,
            transcendentals=rows * hidden,
        ),
        name="mlp_fwd",
    )(*terms, w_in, w_out)


def from_bit(value, bit):
    return lax.ppermute(value, "dp", [(i, i ^ bit) for i in range(lax.axis_size("dp"))])


def chip_place():
    place = lax.axis_index("dp")
    return place // 4, place // 2 % 2, place % 2


def ordered(bit, own, other, axis):
    return jnp.where(
        bit == 0, jnp.stack([own, other], axis), jnp.stack([other, own], axis)
    )


def gather_line(value):
    planes = lax.axis_size("dp") // 4
    z = chip_place()[0]
    blocks = jnp.stack([value] + [from_bit(value, 4 * k) for k in range(1, planes)])
    return jnp.stack(
        [lax.dynamic_index_in_dim(blocks, z ^ k, 0, keepdims=False) for k in range(planes)]
    )


def gather_second(line):
    half = line.shape[-1] // 2
    y, x = chip_place()[1:]
    first, second = line[..., :half], line[..., half:]
    first = ordered(y, first, from_bit(first, 2), 1)
    second = ordered(x, second, from_bit(second, 1), 1)
    return first, second


def gather_third(first, second, cuts):
    y, x = chip_place()[1:]
    first_other, second_other = from_bit(first, 1), from_bit(second, 2)
    return (
        [ordered(x, first[at], first_other[at], 2) for at in cuts],
        [ordered(y, second[at], second_other[at], 1) for at in cuts],
    )


def halve(value, bit, axis, partner):
    lower = lax.index_in_dim(value, 0, axis, keepdims=False)
    upper = lax.index_in_dim(value, 1, axis, keepdims=False)
    keep, send = jnp.where(bit == 0, lower, upper), jnp.where(bit == 0, upper, lower)
    return keep.astype(F32) + from_bit(send, partner).astype(F32)


def scatter_chips(first, second):
    planes = first.shape[0]
    z, y, x = chip_place()
    first = halve(first, x, 2, 1).astype(BF16)
    second = halve(second, y, 1, 2).astype(BF16)
    line = jnp.concatenate([halve(first, y, 1, 2), halve(second, x, 1, 1)], -1).astype(BF16)
    total = lax.dynamic_index_in_dim(line, z, 0, keepdims=False).astype(F32)
    for k in range(1, planes):
        part = lax.dynamic_index_in_dim(line, z ^ k, 0, keepdims=False)
        total = total + from_bit(part, 4 * k).astype(F32)
    return total


def fits_paired(mesh):
    return mesh.shape["tensor"] == 2 and mesh.shape["dp"] == 16


def body_paired(
    tokens,
    cont_prompt,
    routes,
    norm1_gain,
    w_query,
    w_key,
    w_value,
    w_attn_out,
    norm2_gain,
    w_ffn_in,
    w_ffn_out,
    centroids,
    expert_in_a,
    expert_out_a,
    expert_in_b,
    expert_out_b,
    grad_out,
):
    experts = lax.axis_size("dp")
    dp_index = lax.axis_index("dp")
    core_zero = lax.axis_index("tensor") == 0
    rows, width = tokens.shape
    rows_dp = 2 * rows
    shard = w_query.shape[0]
    half_heads = w_query.shape[1] // HEAD
    hidden = w_ffn_in.shape[1]
    assert expert_in_a.shape[2] == hidden
    triple = 3 * HEAD
    heads = 2 * half_heads
    both = lambda lower, upper: (jnp.where(core_zero, lower, upper), jnp.where(core_zero, upper, lower))

    route = routes[:, 0]
    slots_per = max(2, (3 * rows + 2 * experts - 1) // (2 * experts))
    capacity = 5 * rows_dp // 4
    onehot = route[:, None] == lax.broadcasted_iota(jnp.int32, (1, experts), 1)
    onehot_low = onehot.astype(BF16)
    below = lax.broadcasted_iota(jnp.int32, (rows, rows), 0) > lax.broadcasted_iota(
        jnp.int32, (rows, rows), 1
    )
    earlier = matmul(below.astype(BF16), onehot_low)
    local_rank = jnp.sum(jnp.where(onehot, earlier, 0.0), 1).astype(jnp.int32)
    target = route * slots_per + local_rank
    columns = lax.broadcasted_iota(jnp.int32, (1, experts * slots_per), 1)
    placer = (columns == target[:, None]).astype(BF16)
    counts = jnp.sum(onehot_low.astype(F32), 0).astype(BF16)
    counts_pair = jnp.concatenate(both(counts, swap(counts)), 0)

    qkv_shard = jnp.stack(
        [part.reshape(shard, half_heads, HEAD) for part in (w_query, w_key, w_value)], 2
    ).reshape(shard, half_heads * triple)
    extra = jnp.concatenate([norm1_gain, norm2_gain, counts_pair], 0)
    extra = jnp.pad(extra[None, :], ((0, 7), (0, half_heads * triple - extra.shape[0])))
    line_one = gather_line(jnp.concatenate([qkv_shard, extra], 0))
    second_all = lax.all_gather(
        jnp.concatenate([w_ffn_in, w_ffn_out.T, w_attn_out.T], 1), "dp", axis=0, tiled=True
    )
    ffn_in = second_all[:, :hidden]
    ffn_out_t = second_all[:, hidden : 2 * hidden]
    attn_half = second_all[:, 2 * hidden :]
    weight_rows, extra_row = np.s_[..., :shard, :], np.s_[..., shard, :]
    (first_all, extra_all), (last_all, unused) = gather_third(
        *gather_second(line_one), (weight_rows, extra_row)
    )
    qkv_full = jnp.concatenate([first_all, last_all], -1).reshape(width, half_heads * triple)
    extra_all = extra_all.reshape(experts, -1)
    gain_one = extra_all[:, :shard].reshape(width).astype(F32)
    gain_two = extra_all[:, shard : 2 * shard].reshape(width).astype(F32)
    counts_all = extra_all[:, 2 * shard : 2 * shard + 2 * experts].reshape(experts, 2, experts)

    mine = jnp.sum(
        jnp.where(lax.broadcasted_iota(jnp.int32, (1, 1, experts), 2) == dp_index, counts_all.astype(F32), 0.0),
        2,
    )
    per_chip = jnp.sum(mine, 1)
    chip_before = jnp.sum(
        jnp.where(
            lax.broadcasted_iota(jnp.int32, (experts, experts), 1)
            < lax.broadcasted_iota(jnp.int32, (experts, experts), 0),
            per_chip[None, :],
            0.0,
        ),
        1,
    )
    starts = both(chip_before, chip_before + mine[:, 0])
    slot_at = lax.broadcasted_iota(jnp.int32, (1, slots_per), 1).astype(F32)
    kept = jnp.concatenate(
        [(start[:, None] + slot_at < capacity).reshape(-1, 1) for start in starts], 0
    )
    half_rows = experts * slots_per

    pair_tokens = with_other(tokens).astype(F32)
    normed_one, hat_pair, inv_pair = norm_forward(pair_tokens, gain_one)
    inputs, hat_one, inv_one = pair_tokens[:rows], hat_pair[:rows], inv_pair[:rows]
    rows_one = normed_one.astype(BF16)
    other_t = lax.dot_general(
        qkv_full, rows_one[rows:], (((0,), (1,)), ((), ())), preferred_element_type=F32
    ).astype(BF16)
    own_t = lax.dot_general(
        qkv_full, rows_one[:rows], (((0,), (1,)), ((), ())), preferred_element_type=F32
    ).astype(BF16)
    qkv_t = jnp.concatenate(both(own_t, swap(other_t)), 0).reshape(heads, triple, rows)
    by_head = lax.all_to_all(qkv_t, "dp", split_axis=0, concat_axis=0, tiled=True)

    lent = experts // 4
    span = PLEN // rows
    own_blocks = jnp.concatenate([by_head, to_core_zero(by_head[:lent])], 0)
    prompt_kv = jnp.where(core_zero, by_head[:, HEAD:], to_core_one(by_head[:, HEAD:]))
    places = jnp.arange(experts + lent, dtype=jnp.int32)
    follows = cont_prompt * span
    plan_zero = jnp.stack(
        [
            places,
            jnp.where(places < experts, places % span, span),
            jnp.concatenate([places[:experts] // span * span, follows[:lent]], 0),
            jnp.ones_like(places),
        ]
    )
    plan_one = jnp.stack(
        [
            jnp.minimum(places + lent, experts - 1),
            jnp.full_like(places, span),
            jnp.concatenate([follows[lent:], jnp.zeros((2 * lent,), jnp.int32)], 0),
            (places < experts - lent).astype(jnp.int32),
        ]
    )
    plan = jnp.where(core_zero, plan_zero, plan_one)
    attn_blocks, log_sums = attn_forward(plan, own_blocks, prompt_kv)
    lent_back = to_core_one(attn_blocks[experts:])
    attn_own = jnp.concatenate(
        [jnp.where(core_zero, attn_blocks[:lent], lent_back), attn_blocks[lent:experts]], 0
    )
    attn_t = lax.all_to_all(attn_own, "dp", split_axis=0, concat_axis=0, tiled=True).reshape(
        width, rows
    )

    attn_out_t = jnp.concatenate(both(attn_half, swap(attn_half)), 1)
    hidden_one = inputs + lax.dot_general(
        attn_t, attn_out_t, (((0,), (1,)), ((), ())), preferred_element_type=F32
    )
    normed_two, hat_two, inv_two = norm_forward(hidden_one, gain_two)
    rows_two = with_other(normed_two.astype(BF16))
    ffn_act, ffn_slope, ffn_sum = mlp_forward(
        [rows_two], second_all, second_all, hidden, rows, transposed=True, columns=(0, 1)
    )
    hidden_two = hidden_one + keep_rows(ffn_sum)

    sent_rows = (
        matmul_tn(placer, hidden_two.astype(BF16)).astype(BF16).reshape(experts, slots_per, width)
    )
    sent_grad = matmul_tn(placer, grad_out).astype(BF16).reshape(experts, slots_per, width)
    own_rows, sent_grad = lax.optimization_barrier((to_experts(sent_rows), sent_grad))
    grad_own = to_experts(sent_grad)
    expert_rows = with_other(own_rows.reshape(-1, width))
    centre = centroids[0]
    gate_value = jax.nn.sigmoid(matmul(expert_rows, centre))
    act_a, slope_a, part_a = mlp_forward(
        [expert_rows], expert_in_a[0], expert_out_a[0], hidden, half_rows // 2
    )
    from_a = swap(part_a)
    middle, act_b, slope_b, part_b = mlp_forward(
        [expert_rows, part_a, from_a], expert_in_b[0], expert_out_b[0], hidden, half_rows // 2
    )
    part_b, grad_own = lax.optimization_barrier((part_b, grad_own))
    branch_half = (
        part_a[:half_rows].astype(F32) + from_a[half_rows:].astype(F32) + keep_rows(part_b)
    )
    gate_half = gate_value[:half_rows]
    returned = (
        jnp.where(kept[:half_rows], gate_half[:, None] * branch_half, 0.0)
        .astype(BF16)
        .reshape(experts, slots_per, width)
    )
    came_back = to_experts(returned).reshape(half_rows, width)

    grad_returned = jnp.where(kept, with_other(grad_own.reshape(-1, width)), 0.0).astype(BF16)
    grad_half = grad_returned[:half_rows].astype(F32)
    grad_logit_half = jnp.sum(grad_half * branch_half, 1) * gate_half * (1.0 - gate_half)
    centre_part = matmul(grad_logit_half, expert_rows[:half_rows].astype(F32))
    grad_branch = gate_value[:, None] * grad_returned.astype(F32)
    grad_b = grad_branch.astype(BF16)
    grad_pre_b = (matmul_nt(grad_b, expert_out_b[0]) * slope_b.astype(F32)).astype(BF16)
    part_m, other_m = pair_parts(matmul_nt(grad_pre_b, expert_in_b[0]))
    grad_a = (grad_branch + part_m.astype(F32) + other_m.astype(F32)).astype(BF16)
    grad_pre_a = (matmul_nt(grad_a, expert_out_a[0]) * slope_a.astype(F32)).astype(BF16)
    grad_rows = (
        keep_rows(matmul_nt(grad_pre_a, expert_in_a[0]))
        + part_m[:half_rows].astype(F32)
        + other_m[:half_rows].astype(F32)
        + grad_logit_half[:, None] * centre.astype(F32)[None, :]
    )
    grad_rows, came_back, act_a, grad_a, expert_rows, grad_pre_a = lax.optimization_barrier(
        (grad_rows.astype(BF16), came_back, act_a, grad_a, expert_rows, grad_pre_a)
    )
    grad_out_a = matmul_tn(act_a, grad_a)
    grad_in_a = matmul_tn(expert_rows, grad_pre_a)
    output = hidden_two + matmul(placer, came_back)
    grad_back = to_experts(grad_rows.reshape(experts, slots_per, width))
    grad_back, grad_out_a, grad_in_a = lax.optimization_barrier((grad_back, grad_out_a, grad_in_a))
    grad_back = grad_back.reshape(half_rows, width)
    grad_two = grad_out.astype(F32) + matmul(placer, grad_back)

    rows_down = with_other(grad_two.astype(BF16))
    grad_ffn_pre = (matmul(rows_down, ffn_out_t) * ffn_slope.astype(F32)).astype(BF16)
    grad_ffn_out_t = matmul_tn(rows_down, ffn_act)
    grad_ffn_in = matmul_tn(rows_two, grad_ffn_pre)
    grad_norm_two = keep_rows(matmul_nt(grad_ffn_pre, ffn_in))
    back_two = norm_backward(grad_norm_two, hat_two, inv_two, gain_two)[0]
    grad_one = grad_two + back_two

    grad_branch_one = grad_one.astype(BF16)
    grad_attn_t = lax.dot_general(
        attn_out_t, grad_branch_one, (((0,), (1,)), ((), ())), preferred_element_type=F32
    ).astype(BF16)
    grad_by_head = lax.all_to_all(
        grad_attn_t.reshape(heads, HEAD, rows), "dp", split_axis=0, concat_axis=0, tiled=True
    )
    grad_attn_out = lax.dot_general(
        grad_branch_one, attn_t, (((0,), (1,)), ((), ())), preferred_element_type=F32
    )
    half_width = width // 2
    part_own, part_other = both(grad_attn_out[:, :half_width], grad_attn_out[:, half_width:])
    grad_attn_half = part_own + swap(part_other.astype(BF16)).astype(F32)
    second_part = jnp.concatenate(
        [grad_ffn_in.astype(BF16), grad_ffn_out_t.astype(BF16), grad_attn_half.astype(BF16)], 1
    )
    grad_by_head, second_part = lax.optimization_barrier((grad_by_head, second_part))
    second_sum = lax.psum_scatter(second_part, "dp", scatter_dimension=0, tiled=True).astype(F32)
    grad_blocks = jnp.concatenate([grad_by_head, to_core_zero(grad_by_head[:lent])], 0)
    grad_own_blocks, grad_prompts = attn_backward(
        plan, own_blocks, prompt_kv, grad_blocks, attn_blocks, log_sums
    )
    lent_grad = to_core_one(grad_own_blocks[experts:])
    prompt_sum = grad_prompts.astype(F32) + to_core_zero(grad_prompts).astype(F32)
    prompt_part = jnp.concatenate(
        [
            grad_own_blocks[:experts, :HEAD],
            (grad_own_blocks[:experts, HEAD:].astype(F32) + prompt_sum).astype(BF16),
        ],
        1,
    )
    cont_part = jnp.concatenate([lent_grad, grad_own_blocks[lent:experts]], 0)
    grad_head, act_b, grad_b, middle, grad_pre_b = lax.optimization_barrier(
        (jnp.where(core_zero, prompt_part, cont_part), act_b, grad_b, middle, grad_pre_b)
    )
    grad_qkv = lax.all_to_all(grad_head, "dp", split_axis=0, concat_axis=0, tiled=True)
    grad_out_b = matmul_tn(act_b, grad_b)
    grad_in_b = matmul_tn(middle, grad_pre_b)
    grad_qkv, grad_out_b, grad_in_b = lax.optimization_barrier((grad_qkv, grad_out_b, grad_in_b))
    grad_qkv = grad_qkv.reshape(2, half_heads * triple, rows)
    keep_half, send_half = both(grad_qkv[0], grad_qkv[1])
    grad_qkv_t = jnp.concatenate([keep_half, swap(send_half)], 1)
    grad_qkv_w = lax.dot_general(
        rows_one, grad_qkv_t, (((0,), (1,)), ((), ())), preferred_element_type=F32
    ).astype(BF16)
    by_chip = grad_qkv_w.reshape(experts // 4, 2, 2, shard, half_heads * triple)
    half_columns = half_heads * triple // 2
    qkv_sum = scatter_chips(by_chip[..., :half_columns], by_chip[..., half_columns:])
    grad_norm_one = keep_rows(
        lax.dot_general(
            grad_qkv_t, qkv_full, (((0,), (1,)), ((), ())), preferred_element_type=F32
        )
    )
    back_one = norm_backward(grad_norm_one, hat_one, inv_one, gain_one)[0]
    grad_input = grad_one + back_one
    qkv_sum = qkv_sum.reshape(shard, half_heads, 3, HEAD)
    query_shard, key_shard, value_shard = (
        qkv_sum[:, :, part].reshape(shard, half_heads * HEAD) for part in range(3)
    )

    ffn_in_sum = second_sum[:, :hidden]
    gains = jnp.stack(
        [
            jnp.sum(query_shard * w_query + key_shard * w_key + value_shard * w_value, 1)
            / norm1_gain.astype(F32),
            jnp.sum(ffn_in_sum * w_ffn_in, 1) / norm2_gain.astype(F32),
        ]
    )
    gains = gains + swap(gains)
    centre_grad = centre_part + swap(centre_part)
    return (
        output.astype(BF16),
        grad_input.astype(BF16),
        gains[0],
        query_shard,
        key_shard,
        value_shard,
        second_sum[:, 2 * hidden :].T,
        gains[1],
        ffn_in_sum,
        second_sum[:, hidden : 2 * hidden].T,
        centre_grad[None, :],
        grad_in_a[None],
        grad_out_a[None],
        grad_in_b[None],
        grad_out_b[None],
    )


def solution(mesh):
    body = body_paired if fits_paired(mesh) else body_general
    return jax.shard_map(
        body,
        mesh=mesh,
        in_specs=(
            P(("dp", "tensor"), None),
            P(),
            P(("dp", "tensor"), None),
            P("dp"),
            P("dp", "tensor"),
            P("dp", "tensor"),
            P("dp", "tensor"),
            P("tensor", "dp"),
            P("dp"),
            P("dp", "tensor"),
            P("tensor", "dp"),
            P("dp", None),
            P("dp", None, "tensor"),
            P("dp", "tensor", None),
            P("dp", None, "tensor"),
            P("dp", "tensor", None),
            P(("dp", "tensor"), None),
        ),
        out_specs=(
            P(("dp", "tensor"), None),
            P(("dp", "tensor"), None),
            P("dp"),
            P("dp", "tensor"),
            P("dp", "tensor"),
            P("dp", "tensor"),
            P("tensor", "dp"),
            P("dp"),
            P("dp", "tensor"),
            P("tensor", "dp"),
            P("dp", None),
            P("dp", None, "tensor"),
            P("dp", "tensor", None),
            P("dp", None, "tensor"),
            P("dp", "tensor", None),
        ),
        check_vma=False,
    )
```

```python
import functools

import jax
import jax.numpy as jnp
import numpy as np
from jax import lax
from jax.experimental import pallas as pl
from jax.experimental.pallas import tpu as pltpu
from jax.sharding import PartitionSpec as P

HEAD = 64
PLEN = 4096
CONT = 512


def shortened(value):

    def short(part):
        return part.astype(jnp.bfloat16) if part.dtype == jnp.float32 else part

    return jax.tree.map(short, value)


def carried_in(value, axis, combine, identity):
    peers, place = (lax.axis_size(axis), lax.axis_index(axis))
    everything = lax.all_gather(value, axis)
    start = jnp.broadcast_to(jnp.asarray(identity, value.dtype), value.shape)

    def turn(k, before):
        reached = k < place
        new = combine(before, everything[k])
        return jnp.where(reached, new, before)

    return lax.fori_loop(0, peers, turn, start)


def rows_gather(value):
    return lax.all_gather(value, "tensor", axis=0, tiled=True)


def rows_scatter(value):
    return lax.psum_scatter(
        value.astype(jnp.bfloat16), "tensor", scatter_dimension=0, tiled=True
    ).astype(jnp.float32)


def pair_total(value):
    return jax.tree.map(lambda part: part.astype(jnp.float32), lax.psum(shortened(value), "tensor"))


def to_experts(value):
    return lax.all_to_all(value, "dp", split_axis=0, concat_axis=0, tiled=True)


def matmul(left, right):
    return jnp.dot(left, right, preferred_element_type=jnp.float32)


def matmul_tn(left, right):
    return lax.dot_general(
        left, right, (((0,), (0,)), ((), ())), preferred_element_type=jnp.float32
    )


def matmul_nt(left, right):
    return lax.dot_general(
        left, right, (((1,), (1,)), ((), ())), preferred_element_type=jnp.float32
    )


def norm_forward(hidden, gain):
    mean_row = jnp.mean(hidden, -1, keepdims=True)
    centred = hidden - mean_row
    scale_inv = lax.rsqrt(jnp.mean(centred * centred, -1, keepdims=True) + 1e-05)
    normed = centred * scale_inv
    return (normed * gain, normed, scale_inv)


def norm_backward(grad_m, normed, scale_inv, gain):
    grad_hat = grad_m * gain
    inner = (
        grad_hat
        - jnp.mean(grad_hat, -1, keepdims=True)
        - normed * jnp.mean(grad_hat * normed, -1, keepdims=True)
    )
    return (inner * scale_inv, jnp.sum(grad_m * normed, 0))


def gelu_grad(preact, grad):
    unused, pull = jax.vjp(jax.nn.gelu, preact)
    return pull(grad)[0]


def add_counts(first, second):
    return first + second


def attend(queries, keys, values, allowed, heads):
    scale = HEAD ** (-0.5)

    def head_step(head, carry):
        outputs, log_sums = carry
        query_h = lax.dynamic_slice_in_dim(queries, head * HEAD, HEAD, 1)
        key_h = lax.dynamic_slice_in_dim(keys, head * HEAD, HEAD, 1)
        value_h = lax.dynamic_slice_in_dim(values, head * HEAD, HEAD, 1)
        scores = jnp.where(allowed, matmul_nt(query_h, key_h) * scale, -1e30)
        top_score = jnp.max(scores, 1, keepdims=True)
        expo = jnp.exp(scores - top_score)
        total = jnp.sum(expo, 1, keepdims=True)
        probs = (expo / total).astype(jnp.bfloat16)
        outputs = lax.dynamic_update_slice_in_dim(outputs, matmul(probs, value_h), head * HEAD, 1)
        log_sums = lax.dynamic_update_index_in_dim(
            log_sums, top_score[:, 0] + jnp.log(total[:, 0]), head, 0
        )
        return (outputs, log_sums)

    start_state = (
        jnp.zeros((queries.shape[0], heads * HEAD), jnp.float32),
        jnp.zeros((heads, queries.shape[0]), jnp.float32),
    )
    return lax.fori_loop(0, heads, head_step, start_state)


def attend_back(queries, keys, values, allowed, log_sums, grad_attended, heads):
    scale = HEAD ** (-0.5)

    def head_step(head, carry):
        grad_q, grad_k, grad_v = carry
        query_h = lax.dynamic_slice_in_dim(queries, head * HEAD, HEAD, 1)
        key_h = lax.dynamic_slice_in_dim(keys, head * HEAD, HEAD, 1)
        value_h = lax.dynamic_slice_in_dim(values, head * HEAD, HEAD, 1)
        grad_o = lax.dynamic_slice_in_dim(grad_attended, head * HEAD, HEAD, 1)
        scores = jnp.where(allowed, matmul_nt(query_h, key_h) * scale, -1e30)
        probs = jnp.exp(
            scores - lax.dynamic_index_in_dim(log_sums, head, 0, keepdims=False)[:, None]
        )
        grad_p = matmul_nt(grad_o, value_h)
        grad_s = (probs * (grad_p - jnp.sum(probs * grad_p, 1, keepdims=True))).astype(jnp.bfloat16)
        grad_q = lax.dynamic_update_slice_in_dim(
            grad_q, matmul(grad_s, key_h) * scale, head * HEAD, 1
        )
        grad_k = lax.dynamic_update_slice_in_dim(
            grad_k, matmul_tn(grad_s, query_h) * scale, head * HEAD, 1
        )
        grad_v = lax.dynamic_update_slice_in_dim(
            grad_v, matmul_tn(probs.astype(jnp.bfloat16), grad_o), head * HEAD, 1
        )
        return (grad_q, grad_k, grad_v)

    start_state = (
        jnp.zeros(queries.shape, jnp.float32),
        jnp.zeros(keys.shape, jnp.float32),
        jnp.zeros(values.shape, jnp.float32),
    )
    return lax.fori_loop(0, heads, head_step, start_state)


def add_block(buffer, block, start):
    length = block.shape[0]
    current = lax.dynamic_slice_in_dim(buffer, start, length, 0)
    return lax.dynamic_update_slice_in_dim(buffer, current + block, start, 0)


def body_general(
    tokens,
    cont_prompt,
    routes,
    norm1_gain,
    w_query,
    w_key,
    w_value,
    w_attn_out,
    norm2_gain,
    w_ffn_in,
    w_ffn_out,
    centroids,
    expert_in_a,
    expert_out_a,
    expert_in_b,
    expert_out_b,
    grad_out,
):
    experts = lax.axis_size("dp")
    pair_size = lax.axis_size("tensor")
    dp_index = lax.axis_index("dp")
    tensor_index = lax.axis_index("tensor")
    rows_dev = tokens.shape[0]
    rows_dp = rows_dev * pair_size
    prm_dev = rows_dp - CONT
    pkeys = experts * prm_dev
    heads = w_query.shape[1] // HEAD
    width = tokens.shape[1]
    span = PLEN // prm_dev
    owner_start = dp_index // span * PLEN
    mapped_start = cont_prompt[dp_index] * PLEN
    gain_one, query_full, key_full, value_full, attn_full, gain_two, ffn_in_full, ffn_out_full = (
        lax.all_gather(norm1_gain, "dp", axis=0, tiled=True),
        lax.all_gather(w_query, "dp", axis=0, tiled=True),
        lax.all_gather(w_key, "dp", axis=0, tiled=True),
        lax.all_gather(w_value, "dp", axis=0, tiled=True),
        lax.all_gather(w_attn_out, "dp", axis=1, tiled=True),
        lax.all_gather(norm2_gain, "dp", axis=0, tiled=True),
        lax.all_gather(w_ffn_in, "dp", axis=0, tiled=True),
        lax.all_gather(w_ffn_out, "dp", axis=1, tiled=True),
    )
    inputs = tokens.astype(jnp.float32)
    normed_one, hat_one, inv_one = norm_forward(inputs, gain_one.astype(jnp.float32))
    rows_one = rows_gather(normed_one.astype(jnp.bfloat16))
    queries = matmul(rows_one, query_full).astype(jnp.bfloat16)
    keys_own = matmul(rows_one, key_full).astype(jnp.bfloat16)
    values_own = matmul(rows_one, value_full).astype(jnp.bfloat16)
    prompt_keys, prompt_values = (
        lax.all_gather(keys_own[:prm_dev], "dp", axis=0, tiled=True),
        lax.all_gather(values_own[:prm_dev], "dp", axis=0, tiled=True),
    )
    keys_first = lax.dynamic_slice_in_dim(prompt_keys, owner_start, PLEN, 0)
    values_first = lax.dynamic_slice_in_dim(prompt_values, owner_start, PLEN, 0)
    first_row = lax.broadcasted_iota(jnp.int32, (prm_dev, 1), 0)
    first_column = lax.broadcasted_iota(jnp.int32, (1, PLEN), 1)
    allowed_first = first_column <= dp_index % span * prm_dev + first_row
    keys_second = jnp.concatenate(
        [lax.dynamic_slice_in_dim(prompt_keys, mapped_start, PLEN, 0), keys_own[prm_dev:]], 0
    )
    values_second = jnp.concatenate(
        [lax.dynamic_slice_in_dim(prompt_values, mapped_start, PLEN, 0), values_own[prm_dev:]], 0
    )
    second_row = lax.broadcasted_iota(jnp.int32, (CONT, 1), 0)
    second_column = lax.broadcasted_iota(jnp.int32, (1, PLEN + CONT), 1)
    allowed_second = (second_column < PLEN) | (second_column - PLEN <= second_row)
    attn_first, sums_first = attend(
        queries[:prm_dev], keys_first, values_first, allowed_first, heads
    )
    attn_second, sums_second = attend(
        queries[prm_dev:], keys_second, values_second, allowed_second, heads
    )
    attn_low = jnp.concatenate([attn_first, attn_second], 0).astype(jnp.bfloat16)
    hidden_one = inputs + rows_scatter(matmul(attn_low, attn_full))
    normed_two, hat_two, inv_two = norm_forward(hidden_one, gain_two.astype(jnp.float32))
    rows_two = rows_gather(normed_two.astype(jnp.bfloat16))
    ffn_pre = matmul(rows_two, ffn_in_full)
    ffn_act = jax.nn.gelu(ffn_pre).astype(jnp.bfloat16)
    hidden_two = hidden_one + rows_scatter(matmul(ffn_act, ffn_out_full))
    route = routes[:, 0]
    slots_per = max(2, (3 * rows_dev + 2 * experts - 1) // (2 * experts))
    capacity = 5 * rows_dp // 4
    expert_ids = lax.broadcasted_iota(jnp.int32, (1, experts), 1)
    onehot = (route[:, None] == expert_ids).astype(jnp.int32)
    offsets = carried_in(
        jnp.sum(onehot, 0), ("dp", "tensor"), add_counts, jnp.zeros((experts,), jnp.int32)
    )
    local_rank = jnp.sum((jnp.cumsum(onehot, 0) - 1) * onehot, 1)
    global_slot = local_rank + jnp.sum(onehot * offsets[None, :], 1)
    kept = global_slot < capacity
    target = route * slots_per + local_rank
    columns = lax.broadcasted_iota(jnp.int32, (1, experts * slots_per), 1)
    placer = ((columns == target[:, None]) & kept[:, None]).astype(jnp.bfloat16)
    sent_rows = (
        matmul_tn(placer, hidden_two.astype(jnp.bfloat16))
        .astype(jnp.bfloat16)
        .reshape(experts, slots_per, width)
    )
    expert_rows = rows_gather(to_experts(sent_rows)).reshape(-1, width)
    centre = centroids[0]
    gate_value = jax.nn.sigmoid(matmul(expert_rows, centre))
    pre_a = matmul(expert_rows, expert_in_a[0])
    act_a = jax.nn.gelu(pre_a).astype(jnp.bfloat16)
    branch_a = pair_total(matmul(act_a, expert_out_a[0]))
    middle = (expert_rows.astype(jnp.float32) + branch_a).astype(jnp.bfloat16)
    pre_b = matmul(middle, expert_in_b[0])
    act_b = jax.nn.gelu(pre_b).astype(jnp.bfloat16)
    branch_b = rows_scatter(matmul(act_b, expert_out_b[0]))
    half_rows = expert_rows.shape[0] // pair_size
    start_row = tensor_index * half_rows
    branch_half = lax.dynamic_slice_in_dim(branch_a, start_row, half_rows, 0) + branch_b
    gate_half = lax.dynamic_slice_in_dim(gate_value, start_row, half_rows, 0)
    returned = (
        (gate_half[:, None] * branch_half).astype(jnp.bfloat16).reshape(experts, slots_per, width)
    )
    came_back = to_experts(returned).reshape(experts * slots_per, width)
    output = hidden_two + matmul(placer, came_back)
    cotangent = grad_out.astype(jnp.float32)
    sent_grad = matmul_tn(placer, grad_out).astype(jnp.bfloat16).reshape(experts, slots_per, width)
    grad_half = to_experts(sent_grad).reshape(half_rows, width)
    grad_returned = rows_gather(grad_half).astype(jnp.float32)
    grad_gate_half = jnp.sum(grad_half.astype(jnp.float32) * branch_half, 1)
    grad_logit_half = grad_gate_half * gate_half * (1.0 - gate_half)
    rows_half = lax.dynamic_slice_in_dim(expert_rows, start_row, half_rows, 0)
    centre_part = matmul(grad_logit_half, rows_half.astype(jnp.float32))
    grad_branch = gate_value[:, None] * grad_returned
    grad_b = grad_branch.astype(jnp.bfloat16)
    grad_pre_b = gelu_grad(pre_b, matmul_nt(grad_b, expert_out_b[0])).astype(jnp.bfloat16)
    grad_out_b = matmul_tn(act_b, grad_b)
    grad_in_b = matmul_tn(middle, grad_pre_b)
    grad_middle = pair_total(matmul_nt(grad_pre_b, expert_in_b[0]))
    grad_a = (grad_branch + grad_middle).astype(jnp.bfloat16)
    grad_pre_a = gelu_grad(pre_a, matmul_nt(grad_a, expert_out_a[0])).astype(jnp.bfloat16)
    grad_out_a = matmul_tn(act_a, grad_a)
    grad_in_a = matmul_tn(expert_rows, grad_pre_a)
    grad_rows = (
        rows_scatter(matmul_nt(grad_pre_a, expert_in_a[0]))
        + lax.dynamic_slice_in_dim(grad_middle, start_row, half_rows, 0)
        + grad_logit_half[:, None] * centre.astype(jnp.float32)[None, :]
    )
    grad_back = to_experts(
        grad_rows.astype(jnp.bfloat16).reshape(experts, slots_per, width)
    ).reshape(experts * slots_per, width)
    grad_two = cotangent + matmul(placer, grad_back)
    gain_one, query_full, key_full, value_full, attn_full, gain_two, ffn_in_full, ffn_out_full = (
        lax.all_gather(norm1_gain, "dp", axis=0, tiled=True),
        lax.all_gather(w_query, "dp", axis=0, tiled=True),
        lax.all_gather(w_key, "dp", axis=0, tiled=True),
        lax.all_gather(w_value, "dp", axis=0, tiled=True),
        lax.all_gather(w_attn_out, "dp", axis=1, tiled=True),
        lax.all_gather(norm2_gain, "dp", axis=0, tiled=True),
        lax.all_gather(w_ffn_in, "dp", axis=0, tiled=True),
        lax.all_gather(w_ffn_out, "dp", axis=1, tiled=True),
    )
    rows_down = rows_gather(grad_two.astype(jnp.bfloat16))
    grad_ffn_pre = gelu_grad(ffn_pre, matmul_nt(rows_down, ffn_out_full)).astype(jnp.bfloat16)
    grad_ffn_out = matmul_tn(ffn_act, rows_down)
    grad_ffn_in = matmul_tn(rows_two, grad_ffn_pre)
    grad_norm_two = rows_scatter(matmul_nt(grad_ffn_pre, ffn_in_full))
    back_two, grad_gain_two = norm_backward(
        grad_norm_two, hat_two, inv_two, gain_two.astype(jnp.float32)
    )
    grad_one = grad_two + back_two
    rows_attn = rows_gather(grad_one.astype(jnp.bfloat16))
    grad_attn_out = matmul_tn(attn_low, rows_attn)
    grad_attended = matmul_nt(rows_attn, attn_full).astype(jnp.bfloat16)
    grad_q_first, grad_k_first, grad_v_first = attend_back(
        queries[:prm_dev],
        keys_first,
        values_first,
        allowed_first,
        sums_first,
        grad_attended[:prm_dev],
        heads,
    )
    grad_q_second, grad_k_second, grad_v_second = attend_back(
        queries[prm_dev:],
        keys_second,
        values_second,
        allowed_second,
        sums_second,
        grad_attended[prm_dev:],
        heads,
    )
    local_width = keys_own.shape[1]
    buffer_k = jnp.zeros((pkeys, local_width), jnp.float32)
    buffer_v = jnp.zeros((pkeys, local_width), jnp.float32)
    buffer_k = add_block(
        add_block(buffer_k, grad_k_first, owner_start), grad_k_second[:PLEN], mapped_start
    )
    buffer_v = add_block(
        add_block(buffer_v, grad_v_first, owner_start), grad_v_second[:PLEN], mapped_start
    )
    prompt_grad_k, prompt_grad_v = (
        lax.psum_scatter(buffer_k, "dp", scatter_dimension=0, tiled=True),
        lax.psum_scatter(buffer_v, "dp", scatter_dimension=0, tiled=True),
    )
    grad_keys = jnp.concatenate([prompt_grad_k, grad_k_second[PLEN:]], 0).astype(jnp.bfloat16)
    grad_values = jnp.concatenate([prompt_grad_v, grad_v_second[PLEN:]], 0).astype(jnp.bfloat16)
    grad_queries = jnp.concatenate([grad_q_first, grad_q_second], 0).astype(jnp.bfloat16)
    grad_query = matmul_tn(rows_one, grad_queries)
    grad_key = matmul_tn(rows_one, grad_keys)
    grad_value = matmul_tn(rows_one, grad_values)
    grad_norm_one = rows_scatter(
        matmul_nt(grad_queries, query_full)
        + matmul_nt(grad_keys, key_full)
        + matmul_nt(grad_values, value_full)
    )
    back_one, grad_gain_one = norm_backward(
        grad_norm_one, hat_one, inv_one, gain_one.astype(jnp.float32)
    )
    grad_input = grad_one + back_one
    (
        gain_one_part,
        query_shard,
        key_shard,
        value_shard,
        attn_shard,
        gain_two_part,
        ffn_in_shard,
        ffn_out_shard,
    ) = (
        lax.psum_scatter(grad_gain_one, "dp", scatter_dimension=0, tiled=True),
        lax.psum_scatter(grad_query, "dp", scatter_dimension=0, tiled=True),
        lax.psum_scatter(grad_key, "dp", scatter_dimension=0, tiled=True),
        lax.psum_scatter(grad_value, "dp", scatter_dimension=0, tiled=True),
        lax.psum_scatter(grad_attn_out, "dp", scatter_dimension=1, tiled=True),
        lax.psum_scatter(grad_gain_two, "dp", scatter_dimension=0, tiled=True),
        lax.psum_scatter(grad_ffn_in, "dp", scatter_dimension=0, tiled=True),
        lax.psum_scatter(grad_ffn_out, "dp", scatter_dimension=1, tiled=True),
    )
    gain_one_shard, gain_two_shard, centre_grad = pair_total(
        (gain_one_part, gain_two_part, centre_part)
    )
    return (
        output.astype(jnp.bfloat16),
        grad_input.astype(jnp.bfloat16),
        gain_one_shard,
        query_shard,
        key_shard,
        value_shard,
        attn_shard,
        gain_two_shard,
        ffn_in_shard,
        ffn_out_shard,
        centre_grad[None, :],
        grad_in_a[None],
        grad_out_a[None],
        grad_in_b[None],
        grad_out_b[None],
    )


LOG2E = 1.4426950408889634
GELU_A = 0.7978845608028654
GELU_B = 0.044715
BF16 = jnp.bfloat16
F32 = jnp.float32


def dot_tt(left, right):
    return lax.dot_general(left, right, (((0,), (0,)), ((), ())), preferred_element_type=F32)


def beside(blocks, at, count, start, stop):
    return jnp.concatenate([blocks[at + j, start:stop, :] for j in range(count)], 1)


def in_groups(sizes, first, count, take, carry):
    for size in sizes:
        groups = count // size
        step = take(size)
        carry = lax.fori_loop(
            0, groups, lambda k, value, at=first, n=size, f=step: f(at + k * n, value), carry
        )
        first, count = first + groups * size, count - groups * size
    return carry


def attn_fwd_kernel(plan, own, prompts, out, log_sums, values, *, head, factor):
    step_id = pl.program_id(0)
    block, full, first = plan[0, step_id], plan[1, step_id], plan[2, step_id]

    def with_ones(value):
        return jnp.concatenate([value.T, jnp.ones((value.shape[1], head), BF16)], 1)

    @pl.when(step_id == 0)
    def _():
        def turn(k, carry):
            values[k] = with_ones(prompts[k, head : 2 * head, :])
            return carry

        lax.fori_loop(0, prompts.shape[0], turn, 0)

    @pl.when(plan[3, step_id] > 0)
    def _():
        query = own[block, 0:head, :].T
        scores = matmul(query, own[block, head : 2 * head, :])
        query_at = lax.broadcasted_iota(jnp.int32, scores.shape, 0)
        key_at = lax.broadcasted_iota(jnp.int32, scores.shape, 1)
        scores = jnp.where(key_at <= query_at, scores, -1e30)
        top = jnp.max(scores, 1, keepdims=True) * factor
        expo = jnp.exp2(scores * factor - top)
        result = matmul(expo.astype(BF16), with_ones(own[block, 2 * head : 3 * head, :]))

        def take(count):
            def step(at, carry):
                before, result = carry
                scores = matmul(query, beside(prompts, at, count, 0, head))
                top = jnp.maximum(before, jnp.max(scores, 1, keepdims=True) * factor)
                expo = jnp.exp2(scores * factor - top).astype(BF16)
                rows = jnp.concatenate([values[at + j] for j in range(count)], 0)
                return top, result * jnp.exp2(before - top) + matmul(expo, rows)

            return step

        top, result = in_groups((4, 2, 1), first, full, take, (top, result))
        result = result.T
        total = result[head : head + 1]
        out[block] = (result[:head] / total).astype(BF16)
        top = jnp.broadcast_to(top, (top.shape[0], 128)).T[0:1]
        log_sums[block] = top + jnp.log2(total)


def attn_bwd_kernel(
    plan, own, prompts, grad, out, log_sums, grad_own, grad_prompts, sum_k, sum_v, *, head, factor, scale
):
    step_id = pl.program_id(0)
    block, full, first = plan[0, step_id], plan[1, step_id], plan[2, step_id]

    @pl.when(step_id == 0)
    def _():
        sum_k[...] = jnp.zeros_like(sum_k)
        sum_v[...] = jnp.zeros_like(sum_v)

    @pl.when(plan[3, step_id] > 0)
    def _():
        query_t, grad_t, log_sum = own[block, 0:head, :], grad[block], log_sums[block]
        inner = jnp.sum(grad_t.astype(F32) * out[block].astype(F32), 0, keepdims=True)
        query, grad_o = query_t.T, grad_t.T

        def tile(key, value, diagonal):
            probs = jnp.exp2(dot_tt(key, query_t) * factor - log_sum)
            if diagonal:
                key_at = lax.broadcasted_iota(jnp.int32, probs.shape, 0)
                query_at = lax.broadcasted_iota(jnp.int32, probs.shape, 1)
                probs = jnp.where(key_at <= query_at, probs, 0.0)
            grad_s = (probs * (dot_tt(value, grad_t) - inner)).astype(BF16)
            return matmul(grad_s, query), matmul(probs.astype(BF16), grad_o), matmul(key, grad_s)

        grad_k, grad_v, grad_q = tile(
            own[block, head : 2 * head, :], own[block, 2 * head : 3 * head, :], True
        )
        grad_own[block, head : 2 * head, :] = (grad_k * scale).T.astype(BF16)
        grad_own[block, 2 * head : 3 * head, :] = grad_v.T.astype(BF16)

        def take(count):
            def step(at, grad_q):
                more_k, more_v, more_q = tile(
                    beside(prompts, at, count, 0, head),
                    beside(prompts, at, count, head, 2 * head),
                    False,
                )
                length = more_k.shape[0] // count
                for j in range(count):
                    sum_k[at + j] += more_k[j * length : (j + 1) * length]
                    sum_v[at + j] += more_v[j * length : (j + 1) * length]
                return grad_q + more_q

            return step

        grad_q = in_groups((4, 2, 1), first, full, take, grad_q)
        grad_own[block, 0:head, :] = (grad_q * scale).astype(BF16)

    @pl.when(step_id == pl.num_programs(0) - 1)
    def _():
        def finish(k, carry):
            grad_prompts[k, 0:head, :] = (sum_k[k] * scale).T.astype(BF16)
            grad_prompts[k, head : 2 * head, :] = sum_v[k].T.astype(BF16)
            return carry

        lax.fori_loop(0, sum_k.shape[0], finish, 0)


def attn_forward(plan, own, prompts):
    blocks, triple, length = own.shape
    head = triple // 3
    whole = pl.BlockSpec(memory_space=pltpu.VMEM)
    return pl.pallas_call(
        functools.partial(attn_fwd_kernel, head=head, factor=head**-0.5 * LOG2E),
        grid_spec=pltpu.PrefetchScalarGridSpec(
            num_scalar_prefetch=1,
            grid=(plan.shape[1],),
            in_specs=[whole, whole],
            out_specs=[whole, whole],
            scratch_shapes=[pltpu.VMEM((prompts.shape[0], length, 2 * head), BF16)],
        ),
        out_shape=[
            jax.ShapeDtypeStruct((blocks, head, length), BF16),
            jax.ShapeDtypeStruct((blocks, 1, length), F32),
        ],
        compiler_params=pltpu.CompilerParams(vmem_limit_bytes=40 * 2**20),
        cost_estimate=pl.CostEstimate(
            flops=100 * length * length * 256 * 4,
            bytes_accessed=8 * 2**20,
            transcendentals=100 * length * length,
        ),
        name="attn_fwd",
    )(plan, own, prompts)


def attn_backward(plan, own, prompts, grad, out, log_sums):
    blocks, triple, length = own.shape
    head = triple // 3
    whole = pl.BlockSpec(memory_space=pltpu.VMEM)
    return pl.pallas_call(
        functools.partial(
            attn_bwd_kernel, head=head, factor=head**-0.5 * LOG2E, scale=head**-0.5
        ),
        grid_spec=pltpu.PrefetchScalarGridSpec(
            num_scalar_prefetch=1,
            grid=(plan.shape[1],),
            in_specs=[whole] * 5,
            out_specs=[whole, whole],
            scratch_shapes=[pltpu.VMEM((prompts.shape[0], length, head), F32)] * 2,
        ),
        out_shape=[
            jax.ShapeDtypeStruct(own.shape, BF16),
            jax.ShapeDtypeStruct(prompts.shape, BF16),
        ],
        compiler_params=pltpu.CompilerParams(vmem_limit_bytes=48 * 2**20),
        cost_estimate=pl.CostEstimate(
            flops=100 * length * length * 256 * 10,
            bytes_accessed=16 * 2**20,
            transcendentals=100 * length * length,
        ),
        name="attn_bwd",
    )(plan, own, prompts, grad, out, log_sums)


def swap(value):
    return lax.ppermute(value, "tensor", [(0, 1), (1, 0)])


def to_core_one(value):
    return lax.ppermute(value, "tensor", [(0, 1)])


def to_core_zero(value):
    return lax.ppermute(value, "tensor", [(1, 0)])


def with_other(value):
    return jnp.concatenate([value, swap(value)], 0)


def keep_rows(value):
    half = value.shape[0] // 2
    return value[:half].astype(F32) + swap(value[half:].astype(BF16)).astype(F32)


def gelu_pair(preact):
    square = preact * preact
    gate = 0.5 + 0.5 * jnp.tanh(preact * (GELU_A + GELU_A * GELU_B * square))
    act = preact * gate
    slope = gate + act * (1.0 - gate) * (2.0 * GELU_A + 6.0 * GELU_A * GELU_B * square)
    return act.astype(BF16), slope.astype(BF16)


def mlp_kernel(*refs, terms, transposed):
    ins, (w_in, w_out), outs = refs[:terms], refs[terms : terms + 2], refs[terms + 2 :]
    rows = ins[0][...]
    if terms > 1:
        total = rows.astype(F32)
        for term in ins[1:]:
            total = total + term[...].astype(F32)
        rows = total.astype(BF16)
        outs[0][...] = rows
    act, slope = gelu_pair(matmul(rows, w_in[...]))
    outs[-3][...] = act
    outs[-2][...] = slope
    outs[-1][...] = (matmul_nt if transposed else matmul)(act, w_out[...]).astype(BF16)


def mlp_forward(terms, w_in, w_out, hidden, length, transposed=False, columns=(0, 0)):
    rows, width = terms[0].shape
    steps = rows // length
    row_block = pl.BlockSpec((length, width), lambda m: (m, 0))
    turned = pl.BlockSpec((length, width), lambda m: ((m + steps // 2) % steps, 0))
    hidden_block = pl.BlockSpec((length, hidden), lambda m: (m, 0))
    once = dict(pipeline_mode=pl.Buffered(1))
    in_block = pl.BlockSpec((width, hidden), lambda m: (0, columns[0]), **once)
    out_block = (
        pl.BlockSpec((width, hidden), lambda m: (0, columns[1]), **once)
        if transposed
        else pl.BlockSpec((hidden, width), lambda m: (0, 0), **once)
    )
    several = len(terms) > 1
    return pl.pallas_call(
        functools.partial(mlp_kernel, terms=len(terms), transposed=transposed),
        grid=(steps,),
        in_specs=([row_block, row_block, turned] if several else [row_block]) + [in_block, out_block],
        out_specs=[row_block] * several + [hidden_block, hidden_block, row_block],
        out_shape=[jax.ShapeDtypeStruct((rows, width), BF16)] * several
        + [jax.ShapeDtypeStruct((rows, hidden), BF16)] * 2
        + [jax.ShapeDtypeStruct((rows, width), BF16)],
        compiler_params=pltpu.CompilerParams(vmem_limit_bytes=52 * 2**20),
        cost_estimate=pl.CostEstimate(
            flops=4 * rows * width * hidden,
            bytes_accessed=4 * width * hidden + 4 * rows * hidden + 4 * rows * width,
            transcendentals=rows * hidden,
        ),
        name="mlp_fwd",
    )(*terms, w_in, w_out)


def mlp_back_kernel(*refs, terms, transposed):
    ins, (w_out, w_in, slope), outs = refs[:terms], refs[terms : terms + 3], refs[terms + 3 :]
    if terms > 1:
        total = ins[0][...] * ins[1][...].astype(F32)
        for term in ins[2:]:
            total = total + term[...].astype(F32)
        grad = total.astype(BF16)
        outs[0][...] = grad
    else:
        grad = ins[0][...]
    grad = (matmul_nt if transposed else matmul)(grad, w_out[...])
    grad_pre = (grad * slope[...].astype(F32)).astype(BF16)
    outs[-2][...] = grad_pre
    outs[-1][...] = matmul_nt(grad_pre, w_in[...]).astype(BF16)


def mlp_backward(terms, w_out, w_in, slope, length, transposed=True, columns=(0, 0)):
    rows, width = terms[-1].shape
    hidden = slope.shape[1]
    steps = rows // length
    row_block = pl.BlockSpec((length, width), lambda m: (m, 0))
    turned = pl.BlockSpec((length, width), lambda m: ((m + steps // 2) % steps, 0))
    hidden_block = pl.BlockSpec((length, hidden), lambda m: (m, 0))
    factor_block = pl.BlockSpec((length, 1), lambda m: (m, 0))
    once = dict(pipeline_mode=pl.Buffered(1))
    out_block = (
        pl.BlockSpec((hidden, width), lambda m: (0, 0), **once)
        if transposed
        else pl.BlockSpec((width, hidden), lambda m: (0, columns[1]), **once)
    )
    in_block = pl.BlockSpec((width, hidden), lambda m: (0, columns[0]), **once)
    term_blocks = [row_block] if len(terms) == 1 else [factor_block, row_block, row_block, turned][: len(terms)]
    several = len(terms) > 1
    return pl.pallas_call(
        functools.partial(mlp_back_kernel, terms=len(terms), transposed=transposed),
        grid=(steps,),
        in_specs=term_blocks + [out_block, in_block, hidden_block],
        out_specs=[row_block] * several + [hidden_block, row_block],
        out_shape=[jax.ShapeDtypeStruct((rows, width), BF16)] * several
        + [jax.ShapeDtypeStruct((rows, hidden), BF16), jax.ShapeDtypeStruct((rows, width), BF16)],
        compiler_params=pltpu.CompilerParams(vmem_limit_bytes=52 * 2**20),
        cost_estimate=pl.CostEstimate(
            flops=4 * rows * width * hidden,
            bytes_accessed=4 * width * hidden + 4 * rows * hidden + 4 * rows * width,
            transcendentals=0,
        ),
        name="mlp_bwd",
    )(*terms, w_out, w_in, slope)


def from_bit(value, bit):
    return lax.ppermute(value, "dp", [(i, i ^ bit) for i in range(lax.axis_size("dp"))])


def chip_place():
    place = lax.axis_index("dp")
    return place // 4, place // 2 % 2, place % 2


def ordered(bit, own, other, axis):
    return jnp.where(
        bit == 0, jnp.stack([own, other], axis), jnp.stack([other, own], axis)
    )


def gather_line(value):
    planes = lax.axis_size("dp") // 4
    z = chip_place()[0]
    blocks = jnp.stack([value] + [from_bit(value, 4 * k) for k in range(1, planes)])
    return jnp.stack(
        [lax.dynamic_index_in_dim(blocks, z ^ k, 0, keepdims=False) for k in range(planes)]
    )


def gather_second(line):
    half = line.shape[-1] // 2
    y, x = chip_place()[1:]
    first, second = line[..., :half], line[..., half:]
    first = ordered(y, first, from_bit(first, 2), 1)
    second = ordered(x, second, from_bit(second, 1), 1)
    return first, second


def gather_third(first, second, cuts):
    y, x = chip_place()[1:]
    first_other, second_other = from_bit(first, 1), from_bit(second, 2)
    return (
        [ordered(x, first[at], first_other[at], 2) for at in cuts],
        [ordered(y, second[at], second_other[at], 1) for at in cuts],
    )


def halve(value, bit, axis, partner):
    lower = lax.index_in_dim(value, 0, axis, keepdims=False)
    upper = lax.index_in_dim(value, 1, axis, keepdims=False)
    keep, send = jnp.where(bit == 0, lower, upper), jnp.where(bit == 0, upper, lower)
    return keep.astype(F32) + from_bit(send, partner).astype(F32)


def scatter_chips(first, second):
    planes = first.shape[0]
    z, y, x = chip_place()
    first = halve(first, x, 2, 1).astype(BF16)
    second = halve(second, y, 1, 2).astype(BF16)
    line = jnp.concatenate([halve(first, y, 1, 2), halve(second, x, 1, 1)], -1).astype(BF16)
    total = lax.dynamic_index_in_dim(line, z, 0, keepdims=False).astype(F32)
    for k in range(1, planes):
        part = lax.dynamic_index_in_dim(line, z ^ k, 0, keepdims=False)
        total = total + from_bit(part, 4 * k).astype(F32)
    return total


def fits_paired(mesh):
    return mesh.shape["tensor"] == 2 and mesh.shape["dp"] == 16


def body_paired(
    tokens,
    cont_prompt,
    routes,
    norm1_gain,
    w_query,
    w_key,
    w_value,
    w_attn_out,
    norm2_gain,
    w_ffn_in,
    w_ffn_out,
    centroids,
    expert_in_a,
    expert_out_a,
    expert_in_b,
    expert_out_b,
    grad_out,
):
    experts = lax.axis_size("dp")
    dp_index = lax.axis_index("dp")
    core_zero = lax.axis_index("tensor") == 0
    rows, width = tokens.shape
    rows_dp = 2 * rows
    shard = w_query.shape[0]
    half_heads = w_query.shape[1] // HEAD
    hidden = w_ffn_in.shape[1]
    assert expert_in_a.shape[2] == hidden
    triple = 3 * HEAD
    heads = 2 * half_heads
    both = lambda lower, upper: (jnp.where(core_zero, lower, upper), jnp.where(core_zero, upper, lower))

    route = routes[:, 0]
    slots_per = max(2, (3 * rows + 2 * experts - 1) // (2 * experts))
    capacity = 5 * rows_dp // 4
    onehot = route[:, None] == lax.broadcasted_iota(jnp.int32, (1, experts), 1)
    onehot_low = onehot.astype(BF16)
    below = lax.broadcasted_iota(jnp.int32, (rows, rows), 0) > lax.broadcasted_iota(
        jnp.int32, (rows, rows), 1
    )
    earlier = matmul(below.astype(BF16), onehot_low)
    local_rank = jnp.sum(jnp.where(onehot, earlier, 0.0), 1).astype(jnp.int32)
    target = route * slots_per + local_rank
    columns = lax.broadcasted_iota(jnp.int32, (1, experts * slots_per), 1)
    placer = (columns == target[:, None]).astype(BF16)
    counts = jnp.sum(onehot_low.astype(F32), 0).astype(BF16)
    counts_pair = jnp.concatenate(both(counts, swap(counts)), 0)

    qkv_shard = jnp.stack(
        [part.reshape(shard, half_heads, HEAD) for part in (w_query, w_key, w_value)], 2
    ).reshape(shard, half_heads * triple)
    extra = jnp.concatenate([norm1_gain, norm2_gain, counts_pair], 0)
    extra = jnp.pad(extra[None, :], ((0, 7), (0, half_heads * triple - extra.shape[0])))
    line_one = gather_line(jnp.concatenate([qkv_shard, extra], 0))
    planes = experts // 4
    second_line = lax.all_gather(
        jnp.concatenate([w_ffn_in, w_ffn_out.T, w_attn_out.T], 1),
        "dp",
        axis_index_groups=[[4 * z + k for z in range(planes)] for k in range(4)],
    )
    weight_rows, extra_row = np.s_[..., :shard, :], np.s_[..., shard, :]
    (first_all, extra_all), (last_all, unused) = gather_third(
        *gather_second(line_one), (weight_rows, extra_row)
    )
    qkv_full = jnp.concatenate([first_all, last_all], -1).reshape(width, half_heads * triple)
    extra_all = extra_all.reshape(experts, -1)
    gain_one = extra_all[:, :shard].reshape(width).astype(F32)
    gain_two = extra_all[:, shard : 2 * shard].reshape(width).astype(F32)
    counts_all = extra_all[:, 2 * shard : 2 * shard + 2 * experts].reshape(experts, 2, experts)

    mine = jnp.sum(
        jnp.where(lax.broadcasted_iota(jnp.int32, (1, 1, experts), 2) == dp_index, counts_all.astype(F32), 0.0),
        2,
    )
    per_chip = jnp.sum(mine, 1)
    chip_before = jnp.sum(
        jnp.where(
            lax.broadcasted_iota(jnp.int32, (experts, experts), 1)
            < lax.broadcasted_iota(jnp.int32, (experts, experts), 0),
            per_chip[None, :],
            0.0,
        ),
        1,
    )
    starts = both(chip_before, chip_before + mine[:, 0])
    slot_at = lax.broadcasted_iota(jnp.int32, (1, slots_per), 1).astype(F32)
    kept = jnp.concatenate(
        [(start[:, None] + slot_at < capacity).reshape(-1, 1) for start in starts], 0
    )
    half_rows = experts * slots_per

    pair_tokens = with_other(tokens).astype(F32)
    normed_one, hat_pair, inv_pair = norm_forward(pair_tokens, gain_one)
    inputs, hat_one, inv_one = pair_tokens[:rows], hat_pair[:rows], inv_pair[:rows]
    rows_one = normed_one.astype(BF16)
    other_t = lax.dot_general(
        qkv_full, rows_one[rows:], (((0,), (1,)), ((), ())), preferred_element_type=F32
    ).astype(BF16)
    own_t = lax.dot_general(
        qkv_full, rows_one[:rows], (((0,), (1,)), ((), ())), preferred_element_type=F32
    ).astype(BF16)
    qkv_t = jnp.concatenate(both(own_t, swap(other_t)), 0).reshape(heads, triple, rows)
    qkv_t, second_line = lax.optimization_barrier((qkv_t, second_line))
    by_head = lax.all_to_all(qkv_t, "dp", split_axis=0, concat_axis=0, tiled=True)

    by_head, second_line = lax.optimization_barrier((by_head, second_line))
    second_all = lax.all_gather(
        second_line, "dp", axis_index_groups=[[4 * z + k for k in range(4)] for z in range(planes)]
    )
    second_all = second_all.transpose(1, 0, 2, 3).reshape(width, -1)
    attn_half = second_all[:, 2 * hidden :]

    lent = 3 * experts // 16
    span = PLEN // rows
    own_blocks = jnp.concatenate([by_head, to_core_zero(by_head[:lent])], 0)
    prompt_kv = jnp.where(core_zero, by_head[:, HEAD:], to_core_one(by_head[:, HEAD:]))
    places = jnp.arange(experts + lent, dtype=jnp.int32)
    follows = cont_prompt * span
    plan_zero = jnp.stack(
        [
            places,
            jnp.where(places < experts, places % span, span),
            jnp.concatenate([places[:experts] // span * span, follows[:lent]], 0),
            jnp.ones_like(places),
        ]
    )
    plan_one = jnp.stack(
        [
            jnp.minimum(places + lent, experts - 1),
            jnp.full_like(places, span),
            jnp.concatenate([follows[lent:], jnp.zeros((2 * lent,), jnp.int32)], 0),
            (places < experts - lent).astype(jnp.int32),
        ]
    )
    plan = jnp.where(core_zero, plan_zero, plan_one)
    attn_blocks, log_sums = attn_forward(plan, own_blocks, prompt_kv)
    lent_back = to_core_one(attn_blocks[experts:])
    attn_own = jnp.concatenate(
        [jnp.where(core_zero, attn_blocks[:lent], lent_back), attn_blocks[lent:experts]], 0
    )
    attn_t = lax.all_to_all(attn_own, "dp", split_axis=0, concat_axis=0, tiled=True).reshape(
        width, rows
    )

    attn_out_t = jnp.concatenate(both(attn_half, swap(attn_half)), 1)
    hidden_one = inputs + lax.dot_general(
        attn_t, attn_out_t, (((0,), (1,)), ((), ())), preferred_element_type=F32
    )
    normed_two, hat_two, inv_two = norm_forward(hidden_one, gain_two)
    rows_two = with_other(normed_two.astype(BF16))
    ffn_act, ffn_slope, ffn_sum = mlp_forward(
        [rows_two], second_all, second_all, hidden, rows, transposed=True, columns=(0, 1)
    )
    hidden_two = hidden_one + keep_rows(ffn_sum)

    sent_rows = (
        matmul_tn(placer, hidden_two.astype(BF16)).astype(BF16).reshape(experts, slots_per, width)
    )
    sent_grad = matmul_tn(placer, grad_out).astype(BF16).reshape(experts, slots_per, width)
    own_rows, sent_grad = lax.optimization_barrier((to_experts(sent_rows), sent_grad))
    grad_own = to_experts(sent_grad)
    expert_rows = with_other(own_rows.reshape(-1, width))
    centre = centroids[0]
    gate_value = jax.nn.sigmoid(matmul(expert_rows, centre))
    act_a, slope_a, part_a = mlp_forward(
        [expert_rows], expert_in_a[0], expert_out_a[0], hidden, half_rows // 2
    )
    from_a = swap(part_a)
    middle, act_b, slope_b, part_b = mlp_forward(
        [expert_rows, part_a, from_a], expert_in_b[0], expert_out_b[0], hidden, half_rows // 2
    )
    part_b, grad_own = lax.optimization_barrier((part_b, grad_own))
    branch_half = (
        part_a[:half_rows].astype(F32) + from_a[half_rows:].astype(F32) + keep_rows(part_b)
    )
    gate_half = gate_value[:half_rows]
    returned = (
        jnp.where(kept[:half_rows], gate_half[:, None] * branch_half, 0.0)
        .astype(BF16)
        .reshape(experts, slots_per, width)
    )
    came_back = to_experts(returned).reshape(half_rows, width)

    grad_returned = jnp.where(kept, with_other(grad_own.reshape(-1, width)), 0.0).astype(BF16)
    grad_half = grad_returned[:half_rows].astype(F32)
    grad_logit_half = jnp.sum(grad_half * branch_half, 1) * gate_half * (1.0 - gate_half)
    centre_part = matmul(grad_logit_half, expert_rows[:half_rows].astype(F32))
    gate_column = gate_value[:, None]
    grad_b, grad_pre_b, part_m = mlp_backward(
        [gate_column, grad_returned], expert_out_b[0], expert_in_b[0], slope_b, half_rows // 2
    )
    from_m = swap(part_m)
    grad_a, grad_pre_a, part_x = mlp_backward(
        [gate_column, grad_returned, part_m, from_m],
        expert_out_a[0],
        expert_in_a[0],
        slope_a,
        half_rows // 2,
    )
    grad_rows = (
        keep_rows(part_x)
        + part_m[:half_rows].astype(F32)
        + from_m[half_rows:].astype(F32)
        + grad_logit_half[:, None] * centre.astype(F32)[None, :]
    )
    grad_rows, came_back, act_a, grad_a, expert_rows, grad_pre_a = lax.optimization_barrier(
        (grad_rows.astype(BF16), came_back, act_a, grad_a, expert_rows, grad_pre_a)
    )
    grad_out_a = matmul_tn(act_a, grad_a)
    grad_in_a = matmul_tn(expert_rows, grad_pre_a)
    output = hidden_two + matmul(placer, came_back)
    grad_back = to_experts(grad_rows.reshape(experts, slots_per, width))
    grad_back, grad_out_a, grad_in_a = lax.optimization_barrier((grad_back, grad_out_a, grad_in_a))
    grad_back = grad_back.reshape(half_rows, width)
    grad_two = grad_out.astype(F32) + matmul(placer, grad_back)

    rows_down = with_other(grad_two.astype(BF16))
    grad_ffn_pre, ffn_part = mlp_backward(
        [rows_down], second_all, second_all, ffn_slope, rows, transposed=False, columns=(0, 1)
    )
    grad_ffn_out_t = matmul_tn(rows_down, ffn_act)
    grad_ffn_in = matmul_tn(rows_two, grad_ffn_pre)
    grad_norm_two = keep_rows(ffn_part)
    back_two = norm_backward(grad_norm_two, hat_two, inv_two, gain_two)[0]
    grad_one = grad_two + back_two

    grad_branch_one = grad_one.astype(BF16)
    grad_attn_t = lax.dot_general(
        attn_out_t, grad_branch_one, (((0,), (1,)), ((), ())), preferred_element_type=F32
    ).astype(BF16)
    grad_by_head = lax.all_to_all(
        grad_attn_t.reshape(heads, HEAD, rows), "dp", split_axis=0, concat_axis=0, tiled=True
    )
    grad_attn_out = lax.dot_general(
        grad_branch_one, attn_t, (((0,), (1,)), ((), ())), preferred_element_type=F32
    )
    half_width = width // 2
    part_own, part_other = both(grad_attn_out[:, :half_width], grad_attn_out[:, half_width:])
    grad_attn_half = part_own + swap(part_other.astype(BF16)).astype(F32)
    second_part = jnp.concatenate(
        [grad_ffn_in.astype(BF16), grad_ffn_out_t.astype(BF16), grad_attn_half.astype(BF16)], 1
    )
    grad_by_head, second_part = lax.optimization_barrier((grad_by_head, second_part))
    second_sum = lax.psum_scatter(second_part, "dp", scatter_dimension=0, tiled=True).astype(F32)
    grad_blocks = jnp.concatenate([grad_by_head, to_core_zero(grad_by_head[:lent])], 0)
    grad_own_blocks, grad_prompts = attn_backward(
        plan, own_blocks, prompt_kv, grad_blocks, attn_blocks, log_sums
    )
    lent_grad = to_core_one(grad_own_blocks[experts:])
    prompt_sum = grad_prompts.astype(F32) + to_core_zero(grad_prompts).astype(F32)
    prompt_part = jnp.concatenate(
        [
            grad_own_blocks[:experts, :HEAD],
            (grad_own_blocks[:experts, HEAD:].astype(F32) + prompt_sum).astype(BF16),
        ],
        1,
    )
    cont_part = jnp.concatenate([lent_grad, grad_own_blocks[lent:experts]], 0)
    grad_head, act_b, grad_b, middle, grad_pre_b = lax.optimization_barrier(
        (jnp.where(core_zero, prompt_part, cont_part), act_b, grad_b, middle, grad_pre_b)
    )
    grad_qkv = lax.all_to_all(grad_head, "dp", split_axis=0, concat_axis=0, tiled=True)
    grad_out_b = matmul_tn(act_b, grad_b)
    grad_in_b = matmul_tn(middle, grad_pre_b)
    grad_qkv, grad_out_b, grad_in_b = lax.optimization_barrier((grad_qkv, grad_out_b, grad_in_b))
    grad_qkv = grad_qkv.reshape(2, half_heads * triple, rows)
    keep_half, send_half = both(grad_qkv[0], grad_qkv[1])
    grad_qkv_t = jnp.concatenate([keep_half, swap(send_half)], 1)
    grad_qkv_w = lax.dot_general(
        rows_one, grad_qkv_t, (((0,), (1,)), ((), ())), preferred_element_type=F32
    ).astype(BF16)
    by_chip = grad_qkv_w.reshape(experts // 4, 2, 2, shard, half_heads * triple)
    half_columns = half_heads * triple // 2
    qkv_sum = scatter_chips(by_chip[..., :half_columns], by_chip[..., half_columns:])
    grad_norm_one = keep_rows(
        lax.dot_general(
            grad_qkv_t, qkv_full, (((0,), (1,)), ((), ())), preferred_element_type=F32
        )
    )
    back_one = norm_backward(grad_norm_one, hat_one, inv_one, gain_one)[0]
    grad_input = grad_one + back_one
    qkv_sum = qkv_sum.reshape(shard, half_heads, 3, HEAD)
    query_shard, key_shard, value_shard = (
        qkv_sum[:, :, part].reshape(shard, half_heads * HEAD) for part in range(3)
    )

    ffn_in_sum = second_sum[:, :hidden]
    gains = jnp.stack(
        [
            jnp.sum(query_shard * w_query + key_shard * w_key + value_shard * w_value, 1)
            / norm1_gain.astype(F32),
            jnp.sum(ffn_in_sum * w_ffn_in, 1) / norm2_gain.astype(F32),
        ]
    )
    gains = gains + swap(gains)
    centre_grad = centre_part + swap(centre_part)
    return (
        output.astype(BF16),
        grad_input.astype(BF16),
        gains[0],
        query_shard,
        key_shard,
        value_shard,
        second_sum[:, 2 * hidden :].T,
        gains[1],
        ffn_in_sum,
        second_sum[:, hidden : 2 * hidden].T,
        centre_grad[None, :],
        grad_in_a[None],
        grad_out_a[None],
        grad_in_b[None],
        grad_out_b[None],
    )


def solution(mesh):
    body = body_paired if fits_paired(mesh) else body_general
    return jax.shard_map(
        body,
        mesh=mesh,
        in_specs=(
            P(("dp", "tensor"), None),
            P(),
            P(("dp", "tensor"), None),
            P("dp"),
            P("dp", "tensor"),
            P("dp", "tensor"),
            P("dp", "tensor"),
            P("tensor", "dp"),
            P("dp"),
            P("dp", "tensor"),
            P("tensor", "dp"),
            P("dp", None),
            P("dp", None, "tensor"),
            P("dp", "tensor", None),
            P("dp", None, "tensor"),
            P("dp", "tensor", None),
            P(("dp", "tensor"), None),
        ),
        out_specs=(
            P(("dp", "tensor"), None),
            P(("dp", "tensor"), None),
            P("dp"),
            P("dp", "tensor"),
            P("dp", "tensor"),
            P("dp", "tensor"),
            P("tensor", "dp"),
            P("dp"),
            P("dp", "tensor"),
            P("tensor", "dp"),
            P("dp", None),
            P("dp", None, "tensor"),
            P("dp", "tensor", None),
            P("dp", None, "tensor"),
            P("dp", "tensor", None),
        ),
        check_vma=False,
    )
```

```python
import functools

import jax
import jax.numpy as jnp
import numpy as np
from jax import lax
from jax.experimental import pallas as pl
from jax.experimental.pallas import tpu as pltpu
from jax.sharding import PartitionSpec as P

HEAD = 64
PLEN = 4096
CONT = 512


def shortened(value):

    def short(part):
        return part.astype(jnp.bfloat16) if part.dtype == jnp.float32 else part

    return jax.tree.map(short, value)


def carried_in(value, axis, combine, identity):
    peers, place = (lax.axis_size(axis), lax.axis_index(axis))
    everything = lax.all_gather(value, axis)
    start = jnp.broadcast_to(jnp.asarray(identity, value.dtype), value.shape)

    def turn(k, before):
        reached = k < place
        new = combine(before, everything[k])
        return jnp.where(reached, new, before)

    return lax.fori_loop(0, peers, turn, start)


def rows_gather(value):
    return lax.all_gather(value, "tensor", axis=0, tiled=True)


def rows_scatter(value):
    return lax.psum_scatter(
        value.astype(jnp.bfloat16), "tensor", scatter_dimension=0, tiled=True
    ).astype(jnp.float32)


def pair_total(value):
    return jax.tree.map(lambda part: part.astype(jnp.float32), lax.psum(shortened(value), "tensor"))


def to_experts(value):
    return lax.all_to_all(value, "dp", split_axis=0, concat_axis=0, tiled=True)


def matmul(left, right):
    return jnp.dot(left, right, preferred_element_type=jnp.float32)


def matmul_tn(left, right):
    return lax.dot_general(
        left, right, (((0,), (0,)), ((), ())), preferred_element_type=jnp.float32
    )


def matmul_nt(left, right):
    return lax.dot_general(
        left, right, (((1,), (1,)), ((), ())), preferred_element_type=jnp.float32
    )


def norm_forward(hidden, gain):
    mean_row = jnp.mean(hidden, -1, keepdims=True)
    centred = hidden - mean_row
    scale_inv = lax.rsqrt(jnp.mean(centred * centred, -1, keepdims=True) + 1e-05)
    normed = centred * scale_inv
    return (normed * gain, normed, scale_inv)


def norm_backward(grad_m, normed, scale_inv, gain):
    grad_hat = grad_m * gain
    inner = (
        grad_hat
        - jnp.mean(grad_hat, -1, keepdims=True)
        - normed * jnp.mean(grad_hat * normed, -1, keepdims=True)
    )
    return (inner * scale_inv, jnp.sum(grad_m * normed, 0))


def gelu_grad(preact, grad):
    unused, pull = jax.vjp(jax.nn.gelu, preact)
    return pull(grad)[0]


def add_counts(first, second):
    return first + second


def attend(queries, keys, values, allowed, heads):
    scale = HEAD ** (-0.5)

    def head_step(head, carry):
        outputs, log_sums = carry
        query_h = lax.dynamic_slice_in_dim(queries, head * HEAD, HEAD, 1)
        key_h = lax.dynamic_slice_in_dim(keys, head * HEAD, HEAD, 1)
        value_h = lax.dynamic_slice_in_dim(values, head * HEAD, HEAD, 1)
        scores = jnp.where(allowed, matmul_nt(query_h, key_h) * scale, -1e30)
        top_score = jnp.max(scores, 1, keepdims=True)
        expo = jnp.exp(scores - top_score)
        total = jnp.sum(expo, 1, keepdims=True)
        probs = (expo / total).astype(jnp.bfloat16)
        outputs = lax.dynamic_update_slice_in_dim(outputs, matmul(probs, value_h), head * HEAD, 1)
        log_sums = lax.dynamic_update_index_in_dim(
            log_sums, top_score[:, 0] + jnp.log(total[:, 0]), head, 0
        )
        return (outputs, log_sums)

    start_state = (
        jnp.zeros((queries.shape[0], heads * HEAD), jnp.float32),
        jnp.zeros((heads, queries.shape[0]), jnp.float32),
    )
    return lax.fori_loop(0, heads, head_step, start_state)


def attend_back(queries, keys, values, allowed, log_sums, grad_attended, heads):
    scale = HEAD ** (-0.5)

    def head_step(head, carry):
        grad_q, grad_k, grad_v = carry
        query_h = lax.dynamic_slice_in_dim(queries, head * HEAD, HEAD, 1)
        key_h = lax.dynamic_slice_in_dim(keys, head * HEAD, HEAD, 1)
        value_h = lax.dynamic_slice_in_dim(values, head * HEAD, HEAD, 1)
        grad_o = lax.dynamic_slice_in_dim(grad_attended, head * HEAD, HEAD, 1)
        scores = jnp.where(allowed, matmul_nt(query_h, key_h) * scale, -1e30)
        probs = jnp.exp(
            scores - lax.dynamic_index_in_dim(log_sums, head, 0, keepdims=False)[:, None]
        )
        grad_p = matmul_nt(grad_o, value_h)
        grad_s = (probs * (grad_p - jnp.sum(probs * grad_p, 1, keepdims=True))).astype(jnp.bfloat16)
        grad_q = lax.dynamic_update_slice_in_dim(
            grad_q, matmul(grad_s, key_h) * scale, head * HEAD, 1
        )
        grad_k = lax.dynamic_update_slice_in_dim(
            grad_k, matmul_tn(grad_s, query_h) * scale, head * HEAD, 1
        )
        grad_v = lax.dynamic_update_slice_in_dim(
            grad_v, matmul_tn(probs.astype(jnp.bfloat16), grad_o), head * HEAD, 1
        )
        return (grad_q, grad_k, grad_v)

    start_state = (
        jnp.zeros(queries.shape, jnp.float32),
        jnp.zeros(keys.shape, jnp.float32),
        jnp.zeros(values.shape, jnp.float32),
    )
    return lax.fori_loop(0, heads, head_step, start_state)


def add_block(buffer, block, start):
    length = block.shape[0]
    current = lax.dynamic_slice_in_dim(buffer, start, length, 0)
    return lax.dynamic_update_slice_in_dim(buffer, current + block, start, 0)


def body_general(
    tokens,
    cont_prompt,
    routes,
    norm1_gain,
    w_query,
    w_key,
    w_value,
    w_attn_out,
    norm2_gain,
    w_ffn_in,
    w_ffn_out,
    centroids,
    expert_in_a,
    expert_out_a,
    expert_in_b,
    expert_out_b,
    grad_out,
):
    experts = lax.axis_size("dp")
    pair_size = lax.axis_size("tensor")
    dp_index = lax.axis_index("dp")
    tensor_index = lax.axis_index("tensor")
    rows_dev = tokens.shape[0]
    rows_dp = rows_dev * pair_size
    prm_dev = rows_dp - CONT
    pkeys = experts * prm_dev
    heads = w_query.shape[1] // HEAD
    width = tokens.shape[1]
    span = PLEN // prm_dev
    owner_start = dp_index // span * PLEN
    mapped_start = cont_prompt[dp_index] * PLEN
    gain_one, query_full, key_full, value_full, attn_full, gain_two, ffn_in_full, ffn_out_full = (
        lax.all_gather(norm1_gain, "dp", axis=0, tiled=True),
        lax.all_gather(w_query, "dp", axis=0, tiled=True),
        lax.all_gather(w_key, "dp", axis=0, tiled=True),
        lax.all_gather(w_value, "dp", axis=0, tiled=True),
        lax.all_gather(w_attn_out, "dp", axis=1, tiled=True),
        lax.all_gather(norm2_gain, "dp", axis=0, tiled=True),
        lax.all_gather(w_ffn_in, "dp", axis=0, tiled=True),
        lax.all_gather(w_ffn_out, "dp", axis=1, tiled=True),
    )
    inputs = tokens.astype(jnp.float32)
    normed_one, hat_one, inv_one = norm_forward(inputs, gain_one.astype(jnp.float32))
    rows_one = rows_gather(normed_one.astype(jnp.bfloat16))
    queries = matmul(rows_one, query_full).astype(jnp.bfloat16)
    keys_own = matmul(rows_one, key_full).astype(jnp.bfloat16)
    values_own = matmul(rows_one, value_full).astype(jnp.bfloat16)
    prompt_keys, prompt_values = (
        lax.all_gather(keys_own[:prm_dev], "dp", axis=0, tiled=True),
        lax.all_gather(values_own[:prm_dev], "dp", axis=0, tiled=True),
    )
    keys_first = lax.dynamic_slice_in_dim(prompt_keys, owner_start, PLEN, 0)
    values_first = lax.dynamic_slice_in_dim(prompt_values, owner_start, PLEN, 0)
    first_row = lax.broadcasted_iota(jnp.int32, (prm_dev, 1), 0)
    first_column = lax.broadcasted_iota(jnp.int32, (1, PLEN), 1)
    allowed_first = first_column <= dp_index % span * prm_dev + first_row
    keys_second = jnp.concatenate(
        [lax.dynamic_slice_in_dim(prompt_keys, mapped_start, PLEN, 0), keys_own[prm_dev:]], 0
    )
    values_second = jnp.concatenate(
        [lax.dynamic_slice_in_dim(prompt_values, mapped_start, PLEN, 0), values_own[prm_dev:]], 0
    )
    second_row = lax.broadcasted_iota(jnp.int32, (CONT, 1), 0)
    second_column = lax.broadcasted_iota(jnp.int32, (1, PLEN + CONT), 1)
    allowed_second = (second_column < PLEN) | (second_column - PLEN <= second_row)
    attn_first, sums_first = attend(
        queries[:prm_dev], keys_first, values_first, allowed_first, heads
    )
    attn_second, sums_second = attend(
        queries[prm_dev:], keys_second, values_second, allowed_second, heads
    )
    attn_low = jnp.concatenate([attn_first, attn_second], 0).astype(jnp.bfloat16)
    hidden_one = inputs + rows_scatter(matmul(attn_low, attn_full))
    normed_two, hat_two, inv_two = norm_forward(hidden_one, gain_two.astype(jnp.float32))
    rows_two = rows_gather(normed_two.astype(jnp.bfloat16))
    ffn_pre = matmul(rows_two, ffn_in_full)
    ffn_act = jax.nn.gelu(ffn_pre).astype(jnp.bfloat16)
    hidden_two = hidden_one + rows_scatter(matmul(ffn_act, ffn_out_full))
    route = routes[:, 0]
    slots_per = max(2, (3 * rows_dev + 2 * experts - 1) // (2 * experts))
    capacity = 5 * rows_dp // 4
    expert_ids = lax.broadcasted_iota(jnp.int32, (1, experts), 1)
    onehot = (route[:, None] == expert_ids).astype(jnp.int32)
    offsets = carried_in(
        jnp.sum(onehot, 0), ("dp", "tensor"), add_counts, jnp.zeros((experts,), jnp.int32)
    )
    local_rank = jnp.sum((jnp.cumsum(onehot, 0) - 1) * onehot, 1)
    global_slot = local_rank + jnp.sum(onehot * offsets[None, :], 1)
    kept = global_slot < capacity
    target = route * slots_per + local_rank
    columns = lax.broadcasted_iota(jnp.int32, (1, experts * slots_per), 1)
    placer = ((columns == target[:, None]) & kept[:, None]).astype(jnp.bfloat16)
    sent_rows = (
        matmul_tn(placer, hidden_two.astype(jnp.bfloat16))
        .astype(jnp.bfloat16)
        .reshape(experts, slots_per, width)
    )
    expert_rows = rows_gather(to_experts(sent_rows)).reshape(-1, width)
    centre = centroids[0]
    gate_value = jax.nn.sigmoid(matmul(expert_rows, centre))
    pre_a = matmul(expert_rows, expert_in_a[0])
    act_a = jax.nn.gelu(pre_a).astype(jnp.bfloat16)
    branch_a = pair_total(matmul(act_a, expert_out_a[0]))
    middle = (expert_rows.astype(jnp.float32) + branch_a).astype(jnp.bfloat16)
    pre_b = matmul(middle, expert_in_b[0])
    act_b = jax.nn.gelu(pre_b).astype(jnp.bfloat16)
    branch_b = rows_scatter(matmul(act_b, expert_out_b[0]))
    half_rows = expert_rows.shape[0] // pair_size
    start_row = tensor_index * half_rows
    branch_half = lax.dynamic_slice_in_dim(branch_a, start_row, half_rows, 0) + branch_b
    gate_half = lax.dynamic_slice_in_dim(gate_value, start_row, half_rows, 0)
    returned = (
        (gate_half[:, None] * branch_half).astype(jnp.bfloat16).reshape(experts, slots_per, width)
    )
    came_back = to_experts(returned).reshape(experts * slots_per, width)
    output = hidden_two + matmul(placer, came_back)
    cotangent = grad_out.astype(jnp.float32)
    sent_grad = matmul_tn(placer, grad_out).astype(jnp.bfloat16).reshape(experts, slots_per, width)
    grad_half = to_experts(sent_grad).reshape(half_rows, width)
    grad_returned = rows_gather(grad_half).astype(jnp.float32)
    grad_gate_half = jnp.sum(grad_half.astype(jnp.float32) * branch_half, 1)
    grad_logit_half = grad_gate_half * gate_half * (1.0 - gate_half)
    rows_half = lax.dynamic_slice_in_dim(expert_rows, start_row, half_rows, 0)
    centre_part = matmul(grad_logit_half, rows_half.astype(jnp.float32))
    grad_branch = gate_value[:, None] * grad_returned
    grad_b = grad_branch.astype(jnp.bfloat16)
    grad_pre_b = gelu_grad(pre_b, matmul_nt(grad_b, expert_out_b[0])).astype(jnp.bfloat16)
    grad_out_b = matmul_tn(act_b, grad_b)
    grad_in_b = matmul_tn(middle, grad_pre_b)
    grad_middle = pair_total(matmul_nt(grad_pre_b, expert_in_b[0]))
    grad_a = (grad_branch + grad_middle).astype(jnp.bfloat16)
    grad_pre_a = gelu_grad(pre_a, matmul_nt(grad_a, expert_out_a[0])).astype(jnp.bfloat16)
    grad_out_a = matmul_tn(act_a, grad_a)
    grad_in_a = matmul_tn(expert_rows, grad_pre_a)
    grad_rows = (
        rows_scatter(matmul_nt(grad_pre_a, expert_in_a[0]))
        + lax.dynamic_slice_in_dim(grad_middle, start_row, half_rows, 0)
        + grad_logit_half[:, None] * centre.astype(jnp.float32)[None, :]
    )
    grad_back = to_experts(
        grad_rows.astype(jnp.bfloat16).reshape(experts, slots_per, width)
    ).reshape(experts * slots_per, width)
    grad_two = cotangent + matmul(placer, grad_back)
    gain_one, query_full, key_full, value_full, attn_full, gain_two, ffn_in_full, ffn_out_full = (
        lax.all_gather(norm1_gain, "dp", axis=0, tiled=True),
        lax.all_gather(w_query, "dp", axis=0, tiled=True),
        lax.all_gather(w_key, "dp", axis=0, tiled=True),
        lax.all_gather(w_value, "dp", axis=0, tiled=True),
        lax.all_gather(w_attn_out, "dp", axis=1, tiled=True),
        lax.all_gather(norm2_gain, "dp", axis=0, tiled=True),
        lax.all_gather(w_ffn_in, "dp", axis=0, tiled=True),
        lax.all_gather(w_ffn_out, "dp", axis=1, tiled=True),
    )
    rows_down = rows_gather(grad_two.astype(jnp.bfloat16))
    grad_ffn_pre = gelu_grad(ffn_pre, matmul_nt(rows_down, ffn_out_full)).astype(jnp.bfloat16)
    grad_ffn_out = matmul_tn(ffn_act, rows_down)
    grad_ffn_in = matmul_tn(rows_two, grad_ffn_pre)
    grad_norm_two = rows_scatter(matmul_nt(grad_ffn_pre, ffn_in_full))
    back_two, grad_gain_two = norm_backward(
        grad_norm_two, hat_two, inv_two, gain_two.astype(jnp.float32)
    )
    grad_one = grad_two + back_two
    rows_attn = rows_gather(grad_one.astype(jnp.bfloat16))
    grad_attn_out = matmul_tn(attn_low, rows_attn)
    grad_attended = matmul_nt(rows_attn, attn_full).astype(jnp.bfloat16)
    grad_q_first, grad_k_first, grad_v_first = attend_back(
        queries[:prm_dev],
        keys_first,
        values_first,
        allowed_first,
        sums_first,
        grad_attended[:prm_dev],
        heads,
    )
    grad_q_second, grad_k_second, grad_v_second = attend_back(
        queries[prm_dev:],
        keys_second,
        values_second,
        allowed_second,
        sums_second,
        grad_attended[prm_dev:],
        heads,
    )
    local_width = keys_own.shape[1]
    buffer_k = jnp.zeros((pkeys, local_width), jnp.float32)
    buffer_v = jnp.zeros((pkeys, local_width), jnp.float32)
    buffer_k = add_block(
        add_block(buffer_k, grad_k_first, owner_start), grad_k_second[:PLEN], mapped_start
    )
    buffer_v = add_block(
        add_block(buffer_v, grad_v_first, owner_start), grad_v_second[:PLEN], mapped_start
    )
    prompt_grad_k, prompt_grad_v = (
        lax.psum_scatter(buffer_k, "dp", scatter_dimension=0, tiled=True),
        lax.psum_scatter(buffer_v, "dp", scatter_dimension=0, tiled=True),
    )
    grad_keys = jnp.concatenate([prompt_grad_k, grad_k_second[PLEN:]], 0).astype(jnp.bfloat16)
    grad_values = jnp.concatenate([prompt_grad_v, grad_v_second[PLEN:]], 0).astype(jnp.bfloat16)
    grad_queries = jnp.concatenate([grad_q_first, grad_q_second], 0).astype(jnp.bfloat16)
    grad_query = matmul_tn(rows_one, grad_queries)
    grad_key = matmul_tn(rows_one, grad_keys)
    grad_value = matmul_tn(rows_one, grad_values)
    grad_norm_one = rows_scatter(
        matmul_nt(grad_queries, query_full)
        + matmul_nt(grad_keys, key_full)
        + matmul_nt(grad_values, value_full)
    )
    back_one, grad_gain_one = norm_backward(
        grad_norm_one, hat_one, inv_one, gain_one.astype(jnp.float32)
    )
    grad_input = grad_one + back_one
    (
        gain_one_part,
        query_shard,
        key_shard,
        value_shard,
        attn_shard,
        gain_two_part,
        ffn_in_shard,
        ffn_out_shard,
    ) = (
        lax.psum_scatter(grad_gain_one, "dp", scatter_dimension=0, tiled=True),
        lax.psum_scatter(grad_query, "dp", scatter_dimension=0, tiled=True),
        lax.psum_scatter(grad_key, "dp", scatter_dimension=0, tiled=True),
        lax.psum_scatter(grad_value, "dp", scatter_dimension=0, tiled=True),
        lax.psum_scatter(grad_attn_out, "dp", scatter_dimension=1, tiled=True),
        lax.psum_scatter(grad_gain_two, "dp", scatter_dimension=0, tiled=True),
        lax.psum_scatter(grad_ffn_in, "dp", scatter_dimension=0, tiled=True),
        lax.psum_scatter(grad_ffn_out, "dp", scatter_dimension=1, tiled=True),
    )
    gain_one_shard, gain_two_shard, centre_grad = pair_total(
        (gain_one_part, gain_two_part, centre_part)
    )
    return (
        output.astype(jnp.bfloat16),
        grad_input.astype(jnp.bfloat16),
        gain_one_shard,
        query_shard,
        key_shard,
        value_shard,
        attn_shard,
        gain_two_shard,
        ffn_in_shard,
        ffn_out_shard,
        centre_grad[None, :],
        grad_in_a[None],
        grad_out_a[None],
        grad_in_b[None],
        grad_out_b[None],
    )


LOG2E = 1.4426950408889634
GELU_A = 0.7978845608028654
GELU_B = 0.044715
BF16 = jnp.bfloat16
F32 = jnp.float32


def dot_tt(left, right):
    return lax.dot_general(left, right, (((0,), (0,)), ((), ())), preferred_element_type=F32)


def beside(blocks, at, count, start, stop):
    return jnp.concatenate([blocks[at + j, start:stop, :] for j in range(count)], 1)


def in_groups(sizes, first, count, take, carry):
    for size in sizes:
        groups = count // size
        step = take(size)
        carry = lax.fori_loop(
            0, groups, lambda k, value, at=first, n=size, f=step: f(at + k * n, value), carry
        )
        first, count = first + groups * size, count - groups * size
    return carry


def attn_fwd_kernel(plan, own, prompts, out, log_sums, values, *, head, factor):
    step_id = pl.program_id(0)
    block, full, first = plan[0, step_id], plan[1, step_id], plan[2, step_id]

    def with_ones(value):
        return jnp.concatenate([value.T, jnp.ones((value.shape[1], head), BF16)], 1)

    @pl.when(step_id == 0)
    def _():
        def turn(k, carry):
            values[k] = with_ones(prompts[k, head : 2 * head, :])
            return carry

        lax.fori_loop(0, prompts.shape[0], turn, 0)

    @pl.when(plan[3, step_id] > 0)
    def _():
        query = own[block, 0:head, :].T
        scores = matmul(query, own[block, head : 2 * head, :])
        query_at = lax.broadcasted_iota(jnp.int32, scores.shape, 0)
        key_at = lax.broadcasted_iota(jnp.int32, scores.shape, 1)
        scores = jnp.where(key_at <= query_at, scores, -1e30)
        top = jnp.max(scores, 1, keepdims=True) * factor
        expo = jnp.exp2(scores * factor - top)
        result = matmul(expo.astype(BF16), with_ones(own[block, 2 * head : 3 * head, :]))

        def take(count):
            def step(at, carry):
                before, result = carry
                scores = matmul(query, beside(prompts, at, count, 0, head))
                top = jnp.maximum(before, jnp.max(scores, 1, keepdims=True) * factor)
                expo = jnp.exp2(scores * factor - top).astype(BF16)
                rows = jnp.concatenate([values[at + j] for j in range(count)], 0)
                return top, result * jnp.exp2(before - top) + matmul(expo, rows)

            return step

        top, result = in_groups((4, 2, 1), first, full, take, (top, result))
        result = result.T
        total = result[head : head + 1]
        out[block] = (result[:head] / total).astype(BF16)
        top = jnp.broadcast_to(top, (top.shape[0], 128)).T[0:1]
        log_sums[block] = top + jnp.log2(total)


def attn_bwd_kernel(
    plan, own, prompts, grad, out, log_sums, grad_own, grad_prompts, sum_k, sum_v, *, head, factor, scale
):
    step_id = pl.program_id(0)
    block, full, first = plan[0, step_id], plan[1, step_id], plan[2, step_id]

    @pl.when(step_id == 0)
    def _():
        sum_k[...] = jnp.zeros_like(sum_k)
        sum_v[...] = jnp.zeros_like(sum_v)

    @pl.when(plan[3, step_id] > 0)
    def _():
        query_t, grad_t, log_sum = own[block, 0:head, :], grad[block], log_sums[block]
        inner = jnp.sum(grad_t.astype(F32) * out[block].astype(F32), 0, keepdims=True)
        query, grad_o = query_t.T, grad_t.T

        def tile(key, value, diagonal):
            probs = jnp.exp2(dot_tt(key, query_t) * factor - log_sum)
            if diagonal:
                key_at = lax.broadcasted_iota(jnp.int32, probs.shape, 0)
                query_at = lax.broadcasted_iota(jnp.int32, probs.shape, 1)
                probs = jnp.where(key_at <= query_at, probs, 0.0)
            grad_s = (probs * (dot_tt(value, grad_t) - inner)).astype(BF16)
            return matmul(grad_s, query), matmul(probs.astype(BF16), grad_o), matmul(key, grad_s)

        grad_k, grad_v, grad_q = tile(
            own[block, head : 2 * head, :], own[block, 2 * head : 3 * head, :], True
        )
        grad_own[block, head : 2 * head, :] = (grad_k * scale).T.astype(BF16)
        grad_own[block, 2 * head : 3 * head, :] = grad_v.T.astype(BF16)

        def take(count):
            def step(at, grad_q):
                more_k, more_v, more_q = tile(
                    beside(prompts, at, count, 0, head),
                    beside(prompts, at, count, head, 2 * head),
                    False,
                )
                length = more_k.shape[0] // count
                for j in range(count):
                    sum_k[at + j] += more_k[j * length : (j + 1) * length]
                    sum_v[at + j] += more_v[j * length : (j + 1) * length]
                return grad_q + more_q

            return step

        grad_q = in_groups((4, 2, 1), first, full, take, grad_q)
        grad_own[block, 0:head, :] = (grad_q * scale).astype(BF16)

    @pl.when(step_id == pl.num_programs(0) - 1)
    def _():
        def finish(k, carry):
            grad_prompts[k, 0:head, :] = (sum_k[k] * scale).T.astype(BF16)
            grad_prompts[k, head : 2 * head, :] = sum_v[k].T.astype(BF16)
            return carry

        lax.fori_loop(0, sum_k.shape[0], finish, 0)


def attn_forward(plan, own, prompts):
    blocks, triple, length = own.shape
    head = triple // 3
    whole = pl.BlockSpec(memory_space=pltpu.VMEM)
    return pl.pallas_call(
        functools.partial(attn_fwd_kernel, head=head, factor=head**-0.5 * LOG2E),
        grid_spec=pltpu.PrefetchScalarGridSpec(
            num_scalar_prefetch=1,
            grid=(plan.shape[1],),
            in_specs=[whole, whole],
            out_specs=[whole, whole],
            scratch_shapes=[pltpu.VMEM((prompts.shape[0], length, 2 * head), BF16)],
        ),
        out_shape=[
            jax.ShapeDtypeStruct((blocks, head, length), BF16),
            jax.ShapeDtypeStruct((blocks, 1, length), F32),
        ],
        compiler_params=pltpu.CompilerParams(vmem_limit_bytes=40 * 2**20),
        cost_estimate=pl.CostEstimate(
            flops=100 * length * length * 256 * 4,
            bytes_accessed=8 * 2**20,
            transcendentals=100 * length * length,
        ),
        name="attn_fwd",
    )(plan, own, prompts)


def attn_backward(plan, own, prompts, grad, out, log_sums):
    blocks, triple, length = own.shape
    head = triple // 3
    whole = pl.BlockSpec(memory_space=pltpu.VMEM)
    return pl.pallas_call(
        functools.partial(
            attn_bwd_kernel, head=head, factor=head**-0.5 * LOG2E, scale=head**-0.5
        ),
        grid_spec=pltpu.PrefetchScalarGridSpec(
            num_scalar_prefetch=1,
            grid=(plan.shape[1],),
            in_specs=[whole] * 5,
            out_specs=[whole, whole],
            scratch_shapes=[pltpu.VMEM((prompts.shape[0], length, head), F32)] * 2,
        ),
        out_shape=[
            jax.ShapeDtypeStruct(own.shape, BF16),
            jax.ShapeDtypeStruct(prompts.shape, BF16),
        ],
        compiler_params=pltpu.CompilerParams(vmem_limit_bytes=48 * 2**20),
        cost_estimate=pl.CostEstimate(
            flops=100 * length * length * 256 * 10,
            bytes_accessed=16 * 2**20,
            transcendentals=100 * length * length,
        ),
        name="attn_bwd",
    )(plan, own, prompts, grad, out, log_sums)


def swap(value):
    return lax.ppermute(value, "tensor", [(0, 1), (1, 0)])


def to_core_one(value):
    return lax.ppermute(value, "tensor", [(0, 1)])


def to_core_zero(value):
    return lax.ppermute(value, "tensor", [(1, 0)])


def with_other(value):
    return jnp.concatenate([value, swap(value)], 0)


def keep_rows(value):
    half = value.shape[0] // 2
    return value[:half].astype(F32) + swap(value[half:].astype(BF16)).astype(F32)


def gelu_pair(preact):
    square = preact * preact
    gate = 0.5 + 0.5 * jnp.tanh(preact * (GELU_A + GELU_A * GELU_B * square))
    act = preact * gate
    slope = gate + act * (1.0 - gate) * (2.0 * GELU_A + 6.0 * GELU_A * GELU_B * square)
    return act.astype(BF16), slope.astype(BF16)


def take_terms(refs, kinds):
    early = pl.program_id(0) < pl.num_programs(0) // 2
    values, at = [], 0
    for paired in kinds:
        if paired:
            values.append(jnp.where(early, refs[at][...], refs[at + 1][...]))
        else:
            values.append(refs[at][...])
        at += 1 + paired
    return values, refs[at:]


def give_halves(refs, value):
    early = pl.program_id(0) < pl.num_programs(0) // 2

    @pl.when(early)
    def _():
        refs[0][...] = value

    @pl.when(jnp.logical_not(early))
    def _():
        refs[1][...] = value


def mlp_kernel(*refs, kinds, transposed, gated):
    terms, refs = take_terms(refs, kinds)
    rows = terms[0]
    if len(terms) > 1:
        total = rows.astype(F32)
        for term in terms[1:]:
            total = total + term.astype(F32)
        rows = total.astype(BF16)
    if gated:
        centre, refs = refs[0], refs[1:]
        logit = jnp.sum(rows.astype(F32) * centre[...].astype(F32), 1, keepdims=True)
        refs[-1][...] = 1.0 / (1.0 + jnp.exp(-logit))
    w_in, w_out, kept_rows, kept_act, kept_slope, first, second = refs[:7]
    kept_rows[...] = rows
    act, slope = gelu_pair(matmul(rows, w_in[...]))
    kept_act[...] = act
    kept_slope[...] = slope
    result = (matmul_nt if transposed else matmul)(act, w_out[...])
    give_halves((first, second), result.astype(BF16))


def mlp_back_kernel(*refs, kinds, transposed, scaled):
    factor, refs = (refs[0], refs[1:]) if scaled else (None, refs)
    terms, refs = take_terms(refs, kinds)
    grad = terms[0]
    if scaled:
        total = factor[...] * grad.astype(F32)
        for term in terms[1:]:
            total = total + term.astype(F32)
        grad = total.astype(BF16)
    w_out, w_in, slope, kept_grad, kept_pre, first, second = refs
    kept_grad[...] = grad
    grad = (matmul_nt if transposed else matmul)(grad, w_out[...])
    grad_pre = (grad * slope[...].astype(F32)).astype(BF16)
    kept_pre[...] = grad_pre
    give_halves((first, second), matmul_nt(grad_pre, w_in[...]).astype(BF16))


def mlp_blocks(terms, length):
    paired = [isinstance(term, tuple) for term in terms]
    arrays = [part for term in terms for part in (term if isinstance(term, tuple) else (term,))]
    half = max(part.shape[0] // length // (1 + (not pair)) for term, pair in zip(terms, paired) for part in (term if pair else (term,)))
    width = arrays[0].shape[1]
    block = pl.BlockSpec((length, width), lambda m: (m, 0))
    halves = [
        pl.BlockSpec((length, width), lambda m: (jnp.minimum(m, half - 1), 0)),
        pl.BlockSpec((length, width), lambda m: (jnp.maximum(m - half, 0), 0)),
    ]
    specs = [spec for pair in paired for spec in (halves if pair else [block])]
    return tuple(paired), arrays, specs, block, halves, 2 * half


def mlp_forward(terms, w_in, w_out, hidden, length, transposed=False, columns=(0, 0), centre=None):
    kinds, arrays, specs, block, halves, steps = mlp_blocks(terms, length)
    rows, width = steps * length, arrays[0].shape[1]
    hidden_block = pl.BlockSpec((length, hidden), lambda m: (m, 0))
    once = dict(pipeline_mode=pl.Buffered(1))
    in_block = pl.BlockSpec((width, hidden), lambda m: (0, columns[0]), **once)
    out_block = (
        pl.BlockSpec((width, hidden), lambda m: (0, columns[1]), **once)
        if transposed
        else pl.BlockSpec((hidden, width), lambda m: (0, 0), **once)
    )
    gated = centre is not None
    return pl.pallas_call(
        functools.partial(mlp_kernel, kinds=kinds, transposed=transposed, gated=gated),
        grid=(steps,),
        in_specs=specs + [pl.BlockSpec((1, width), lambda m: (0, 0))] * gated + [in_block, out_block],
        out_specs=[block, hidden_block, hidden_block]
        + halves
        + [pl.BlockSpec((length, 1), lambda m: (m, 0))] * gated,
        out_shape=[jax.ShapeDtypeStruct((rows, width), BF16)]
        + [jax.ShapeDtypeStruct((rows, hidden), BF16)] * 2
        + [jax.ShapeDtypeStruct((rows // 2, width), BF16)] * 2
        + [jax.ShapeDtypeStruct((rows, 1), F32)] * gated,
        compiler_params=pltpu.CompilerParams(vmem_limit_bytes=54 * 2**20),
        cost_estimate=pl.CostEstimate(
            flops=4 * rows * width * hidden,
            bytes_accessed=4 * width * hidden + 4 * rows * hidden + 4 * rows * width,
            transcendentals=rows * hidden,
        ),
        name="mlp_fwd",
    )(*arrays, *([centre] * gated), w_in, w_out)


def mlp_backward(terms, w_out, w_in, slope, length, transposed=True, columns=(0, 0), factor=None):
    kinds, arrays, specs, block, halves, steps = mlp_blocks(terms, length)
    rows, width = steps * length, arrays[0].shape[1]
    hidden = slope.shape[1]
    hidden_block = pl.BlockSpec((length, hidden), lambda m: (m, 0))
    once = dict(pipeline_mode=pl.Buffered(1))
    out_block = (
        pl.BlockSpec((hidden, width), lambda m: (0, 0), **once)
        if transposed
        else pl.BlockSpec((width, hidden), lambda m: (0, columns[1]), **once)
    )
    in_block = pl.BlockSpec((width, hidden), lambda m: (0, columns[0]), **once)
    scaled = factor is not None
    return pl.pallas_call(
        functools.partial(mlp_back_kernel, kinds=kinds, transposed=transposed, scaled=scaled),
        grid=(steps,),
        in_specs=[pl.BlockSpec((length, 1), lambda m: (m, 0))] * scaled
        + specs
        + [out_block, in_block, hidden_block],
        out_specs=[block, hidden_block] + halves,
        out_shape=[
            jax.ShapeDtypeStruct((rows, width), BF16),
            jax.ShapeDtypeStruct((rows, hidden), BF16),
        ]
        + [jax.ShapeDtypeStruct((rows // 2, width), BF16)] * 2,
        compiler_params=pltpu.CompilerParams(vmem_limit_bytes=54 * 2**20),
        cost_estimate=pl.CostEstimate(
            flops=4 * rows * width * hidden,
            bytes_accessed=4 * width * hidden + 4 * rows * hidden + 4 * rows * width,
            transcendentals=0,
        ),
        name="mlp_bwd",
    )(*([factor] * scaled), *arrays, w_out, w_in, slope)


def from_bit(value, bit):
    return lax.ppermute(value, "dp", [(i, i ^ bit) for i in range(lax.axis_size("dp"))])


def chip_place():
    place = lax.axis_index("dp")
    return place // 4, place // 2 % 2, place % 2


def ordered(bit, own, other, axis):
    return jnp.where(
        bit == 0, jnp.stack([own, other], axis), jnp.stack([other, own], axis)
    )


def gather_line(value):
    planes = lax.axis_size("dp") // 4
    z = chip_place()[0]
    blocks = jnp.stack([value] + [from_bit(value, 4 * k) for k in range(1, planes)])
    return jnp.stack(
        [lax.dynamic_index_in_dim(blocks, z ^ k, 0, keepdims=False) for k in range(planes)]
    )


def gather_second(line):
    half = line.shape[-1] // 2
    y, x = chip_place()[1:]
    first, second = line[..., :half], line[..., half:]
    first = ordered(y, first, from_bit(first, 2), 1)
    second = ordered(x, second, from_bit(second, 1), 1)
    return first, second


def gather_third(first, second, cuts):
    y, x = chip_place()[1:]
    first_other, second_other = from_bit(first, 1), from_bit(second, 2)
    return (
        [ordered(x, first[at], first_other[at], 2) for at in cuts],
        [ordered(y, second[at], second_other[at], 1) for at in cuts],
    )


def halve(value, bit, axis, partner):
    lower = lax.index_in_dim(value, 0, axis, keepdims=False)
    upper = lax.index_in_dim(value, 1, axis, keepdims=False)
    keep, send = jnp.where(bit == 0, lower, upper), jnp.where(bit == 0, upper, lower)
    return keep.astype(F32) + from_bit(send, partner).astype(F32)


def scatter_chips(first, second):
    planes = first.shape[0]
    z, y, x = chip_place()
    first = halve(first, x, 2, 1).astype(BF16)
    second = halve(second, y, 1, 2).astype(BF16)
    line = jnp.concatenate([halve(first, y, 1, 2), halve(second, x, 1, 1)], -1).astype(BF16)
    total = lax.dynamic_index_in_dim(line, z, 0, keepdims=False).astype(F32)
    for k in range(1, planes):
        part = lax.dynamic_index_in_dim(line, z ^ k, 0, keepdims=False)
        total = total + from_bit(part, 4 * k).astype(F32)
    return total


def fits_paired(mesh):
    return mesh.shape["tensor"] == 2 and mesh.shape["dp"] == 16


def body_paired(
    tokens,
    cont_prompt,
    routes,
    norm1_gain,
    w_query,
    w_key,
    w_value,
    w_attn_out,
    norm2_gain,
    w_ffn_in,
    w_ffn_out,
    centroids,
    expert_in_a,
    expert_out_a,
    expert_in_b,
    expert_out_b,
    grad_out,
):
    experts = lax.axis_size("dp")
    dp_index = lax.axis_index("dp")
    core_zero = lax.axis_index("tensor") == 0
    rows, width = tokens.shape
    rows_dp = 2 * rows
    shard = w_query.shape[0]
    half_heads = w_query.shape[1] // HEAD
    hidden = w_ffn_in.shape[1]
    assert expert_in_a.shape[2] == hidden
    triple = 3 * HEAD
    heads = 2 * half_heads
    both = lambda lower, upper: (jnp.where(core_zero, lower, upper), jnp.where(core_zero, upper, lower))

    route = routes[:, 0]
    slots_per = max(2, (3 * rows + 2 * experts - 1) // (2 * experts))
    capacity = 5 * rows_dp // 4
    onehot = route[:, None] == lax.broadcasted_iota(jnp.int32, (1, experts), 1)
    onehot_low = onehot.astype(BF16)
    below = lax.broadcasted_iota(jnp.int32, (rows, rows), 0) > lax.broadcasted_iota(
        jnp.int32, (rows, rows), 1
    )
    earlier = matmul(below.astype(BF16), onehot_low)
    local_rank = jnp.sum(jnp.where(onehot, earlier, 0.0), 1).astype(jnp.int32)
    target = route * slots_per + local_rank
    columns = lax.broadcasted_iota(jnp.int32, (1, experts * slots_per), 1)
    placer = (columns == target[:, None]).astype(BF16)
    counts = jnp.sum(onehot_low.astype(F32), 0).astype(BF16)
    counts_pair = jnp.concatenate(both(counts, swap(counts)), 0)

    qkv_shard = jnp.stack(
        [part.reshape(shard, half_heads, HEAD) for part in (w_query, w_key, w_value)], 2
    ).reshape(shard, half_heads * triple)
    extra = jnp.concatenate([norm1_gain, norm2_gain, counts_pair], 0)
    extra = jnp.pad(extra[None, :], ((0, 7), (0, half_heads * triple - extra.shape[0])))
    planes = experts // 4
    first_shard, second_shard = lax.optimization_barrier(
        (
            jnp.concatenate([qkv_shard, extra], 0),
            jnp.concatenate([w_ffn_in, w_ffn_out.T, w_attn_out.T], 1),
        )
    )
    second_line = lax.all_gather(
        second_shard,
        "dp",
        axis_index_groups=[[4 * z + k for z in range(planes)] for k in range(4)],
    )
    line_one = gather_line(first_shard)
    weight_rows, extra_row = np.s_[..., :shard, :], np.s_[..., shard, :]
    (first_all, extra_all), (last_all, unused) = gather_third(
        *gather_second(line_one), (weight_rows, extra_row)
    )
    qkv_full = jnp.concatenate([first_all, last_all], -1).reshape(width, half_heads * triple)
    extra_all = extra_all.reshape(experts, -1)
    gain_one = extra_all[:, :shard].reshape(width).astype(F32)
    gain_two = extra_all[:, shard : 2 * shard].reshape(width).astype(F32)
    counts_all = extra_all[:, 2 * shard : 2 * shard + 2 * experts].reshape(experts, 2, experts)

    mine = jnp.sum(
        jnp.where(lax.broadcasted_iota(jnp.int32, (1, 1, experts), 2) == dp_index, counts_all.astype(F32), 0.0),
        2,
    )
    per_chip = jnp.sum(mine, 1)
    chip_before = jnp.sum(
        jnp.where(
            lax.broadcasted_iota(jnp.int32, (experts, experts), 1)
            < lax.broadcasted_iota(jnp.int32, (experts, experts), 0),
            per_chip[None, :],
            0.0,
        ),
        1,
    )
    starts = both(chip_before, chip_before + mine[:, 0])
    slot_at = lax.broadcasted_iota(jnp.int32, (1, slots_per), 1).astype(F32)
    kept = jnp.concatenate(
        [(start[:, None] + slot_at < capacity).reshape(-1, 1) for start in starts], 0
    )
    half_rows = experts * slots_per

    pair_tokens = with_other(tokens).astype(F32)
    normed_one, hat_pair, inv_pair = norm_forward(pair_tokens, gain_one)
    inputs, hat_one, inv_one = pair_tokens[:rows], hat_pair[:rows], inv_pair[:rows]
    rows_one = normed_one.astype(BF16)
    other_t = lax.dot_general(
        qkv_full, rows_one[rows:], (((0,), (1,)), ((), ())), preferred_element_type=F32
    ).astype(BF16)
    own_t = lax.dot_general(
        qkv_full, rows_one[:rows], (((0,), (1,)), ((), ())), preferred_element_type=F32
    ).astype(BF16)
    qkv_t = jnp.concatenate(both(own_t, swap(other_t)), 0).reshape(heads, triple, rows)
    qkv_t, second_line = lax.optimization_barrier((qkv_t, second_line))
    by_head = lax.all_to_all(qkv_t, "dp", split_axis=0, concat_axis=0, tiled=True)

    by_head, second_line = lax.optimization_barrier((by_head, second_line))
    second_all = lax.all_gather(
        second_line, "dp", axis_index_groups=[[4 * z + k for k in range(4)] for z in range(planes)]
    )
    second_all = second_all.transpose(1, 0, 2, 3).reshape(width, -1)
    attn_half = second_all[:, 2 * hidden :]

    lent = experts // 4
    span = PLEN // rows
    own_blocks = jnp.concatenate([by_head, to_core_zero(by_head[:lent])], 0)
    prompt_kv = jnp.where(core_zero, by_head[:, HEAD:], to_core_one(by_head[:, HEAD:]))
    places = jnp.arange(experts + lent, dtype=jnp.int32)
    follows = cont_prompt * span
    plan_zero = jnp.stack(
        [
            places,
            jnp.where(places < experts, places % span, span),
            jnp.concatenate([places[:experts] // span * span, follows[:lent]], 0),
            jnp.ones_like(places),
        ]
    )
    plan_one = jnp.stack(
        [
            jnp.minimum(places + lent, experts - 1),
            jnp.full_like(places, span),
            jnp.concatenate([follows[lent:], jnp.zeros((2 * lent,), jnp.int32)], 0),
            (places < experts - lent).astype(jnp.int32),
        ]
    )
    plan = jnp.where(core_zero, plan_zero, plan_one)
    attn_blocks, log_sums = attn_forward(plan, own_blocks, prompt_kv)
    lent_back = to_core_one(attn_blocks[experts:])
    attn_own = jnp.concatenate(
        [jnp.where(core_zero, attn_blocks[:lent], lent_back), attn_blocks[lent:experts]], 0
    )
    attn_t = lax.all_to_all(attn_own, "dp", split_axis=0, concat_axis=0, tiled=True).reshape(
        width, rows
    )

    sent_grad = matmul_tn(placer, grad_out).astype(BF16).reshape(experts, slots_per, width)
    attn_t, sent_grad = lax.optimization_barrier((attn_t, sent_grad))
    grad_own = to_experts(sent_grad).reshape(-1, width)
    half_width = width // 2
    own_heads, other_heads = both(attn_t[:half_width], attn_t[half_width:])
    attn_other = swap(attn_half)
    hidden_one = (
        inputs
        + lax.dot_general(
            own_heads, attn_half, (((0,), (1,)), ((), ())), preferred_element_type=F32
        )
        + lax.dot_general(
            other_heads, attn_other, (((0,), (1,)), ((), ())), preferred_element_type=F32
        )
    )
    normed_two, hat_two, inv_two = norm_forward(hidden_one, gain_two)
    normed_two = normed_two.astype(BF16)
    rows_two, ffn_act, ffn_slope, ffn_own, ffn_other = mlp_forward(
        [(normed_two, swap(normed_two))],
        second_all,
        second_all,
        hidden,
        rows,
        transposed=True,
        columns=(0, 1),
    )
    hidden_two = hidden_one + ffn_own.astype(F32) + swap(ffn_other).astype(F32)

    sent_rows = (
        matmul_tn(placer, hidden_two.astype(BF16)).astype(BF16).reshape(experts, slots_per, width)
    )
    sent_rows, grad_own = lax.optimization_barrier((sent_rows, grad_own))
    own_rows = to_experts(sent_rows).reshape(half_rows, width)
    centre = centroids[0]
    length = half_rows // 2
    expert_rows, act_a, slope_a, own_a, other_a, gate_column = mlp_forward(
        [(own_rows, swap(own_rows))],
        expert_in_a[0],
        expert_out_a[0],
        hidden,
        length,
        centre=centroids,
    )
    from_a = (swap(other_a), swap(own_a))
    middle, act_b, slope_b, own_b, other_b = mlp_forward(
        [expert_rows, (own_a, other_a), from_a], expert_in_b[0], expert_out_b[0], hidden, length
    )
    branch_half = (
        own_a.astype(F32) + from_a[0].astype(F32) + own_b.astype(F32) + swap(other_b).astype(F32)
    )
    gate_value = gate_column[:, 0]
    gate_half = gate_value[:half_rows]
    returned = (
        jnp.where(kept[:half_rows], gate_half[:, None] * branch_half, 0.0)
        .astype(BF16)
        .reshape(experts, slots_per, width)
    )
    came_back = to_experts(returned).reshape(half_rows, width)

    kept_half = kept[:half_rows, 0]
    grad_logit_half = jnp.where(
        kept_half,
        jnp.sum(grad_own.astype(F32) * branch_half, 1) * gate_half * (1.0 - gate_half),
        0.0,
    )
    centre_part = matmul(grad_logit_half, own_rows.astype(F32))
    kept_gate = jnp.where(kept, gate_column, 0.0)
    grad_pair = (grad_own, swap(grad_own))
    grad_b, grad_pre_b, own_m, other_m = mlp_backward(
        [grad_pair], expert_out_b[0], expert_in_b[0], slope_b, length, factor=kept_gate
    )
    from_m = (swap(other_m), swap(own_m))
    grad_a, grad_pre_a, own_x, other_x = mlp_backward(
        [grad_pair, (own_m, other_m), from_m],
        expert_out_a[0],
        expert_in_a[0],
        slope_a,
        length,
        factor=kept_gate,
    )
    grad_rows = (
        own_x.astype(F32)
        + swap(other_x).astype(F32)
        + own_m.astype(F32)
        + from_m[0].astype(F32)
        + grad_logit_half[:, None] * centre.astype(F32)[None, :]
    )
    grad_rows, came_back, act_a, grad_a, expert_rows, grad_pre_a = lax.optimization_barrier(
        (grad_rows.astype(BF16), came_back, act_a, grad_a, expert_rows, grad_pre_a)
    )
    grad_out_a = matmul_tn(act_a, grad_a)
    grad_in_a = matmul_tn(expert_rows, grad_pre_a)
    output = hidden_two + matmul(placer, came_back)
    grad_back = to_experts(grad_rows.reshape(experts, slots_per, width))
    grad_back, grad_out_a, grad_in_a = lax.optimization_barrier((grad_back, grad_out_a, grad_in_a))
    grad_back = grad_back.reshape(half_rows, width)
    grad_two = grad_out.astype(F32) + matmul(placer, grad_back)

    grad_down = grad_two.astype(BF16)
    rows_down, grad_ffn_pre, down_own, down_other = mlp_backward(
        [(grad_down, swap(grad_down))],
        second_all,
        second_all,
        ffn_slope,
        rows,
        transposed=False,
        columns=(0, 1),
    )
    grad_norm_two = down_own.astype(F32) + swap(down_other).astype(F32)
    back_two = norm_backward(grad_norm_two, hat_two, inv_two, gain_two)[0]
    grad_one = grad_two + back_two

    grad_branch_one = grad_one.astype(BF16)
    grad_halves = both(
        *(
            lax.dot_general(
                part, grad_branch_one, (((0,), (1,)), ((), ())), preferred_element_type=F32
            ).astype(BF16)
            for part in (attn_half, attn_other)
        )
    )
    grad_attn, rows_down, ffn_act, rows_two, grad_ffn_pre = lax.optimization_barrier(
        (
            jnp.concatenate(grad_halves, 0).reshape(heads, HEAD, rows),
            rows_down,
            ffn_act,
            rows_two,
            grad_ffn_pre,
        )
    )
    grad_by_head = lax.all_to_all(grad_attn, "dp", split_axis=0, concat_axis=0, tiled=True)
    grad_ffn_out_t = matmul_tn(rows_down, ffn_act)
    grad_ffn_in = matmul_tn(rows_two, grad_ffn_pre)
    part_own, part_other = (
        lax.dot_general(
            grad_branch_one, part, (((0,), (1,)), ((), ())), preferred_element_type=F32
        )
        for part in (own_heads, other_heads)
    )
    grad_attn_half = part_own + swap(part_other.astype(BF16)).astype(F32)
    second_part = jnp.concatenate(
        [grad_ffn_in.astype(BF16), grad_ffn_out_t.astype(BF16), grad_attn_half.astype(BF16)], 1
    )
    grad_by_head, second_part = lax.optimization_barrier((grad_by_head, second_part))
    second_sum = lax.psum_scatter(second_part, "dp", scatter_dimension=0, tiled=True).astype(F32)
    grad_blocks = jnp.concatenate([grad_by_head, to_core_zero(grad_by_head[:lent])], 0)
    grad_own_blocks, grad_prompts = attn_backward(
        plan, own_blocks, prompt_kv, grad_blocks, attn_blocks, log_sums
    )
    lent_grad = to_core_one(grad_own_blocks[experts:])
    prompt_sum = grad_prompts.astype(F32) + to_core_zero(grad_prompts).astype(F32)
    prompt_part = jnp.concatenate(
        [
            grad_own_blocks[:experts, :HEAD],
            (grad_own_blocks[:experts, HEAD:].astype(F32) + prompt_sum).astype(BF16),
        ],
        1,
    )
    cont_part = jnp.concatenate([lent_grad, grad_own_blocks[lent:experts]], 0)
    grad_head, act_b, grad_b, middle, grad_pre_b = lax.optimization_barrier(
        (jnp.where(core_zero, prompt_part, cont_part), act_b, grad_b, middle, grad_pre_b)
    )
    grad_qkv = lax.all_to_all(grad_head, "dp", split_axis=0, concat_axis=0, tiled=True)
    grad_out_b = matmul_tn(act_b, grad_b)
    grad_in_b = matmul_tn(middle, grad_pre_b)
    grad_qkv, grad_out_b, grad_in_b = lax.optimization_barrier((grad_qkv, grad_out_b, grad_in_b))
    grad_qkv = grad_qkv.reshape(2, half_heads * triple, rows)
    keep_half, send_half = both(grad_qkv[0], grad_qkv[1])
    grad_qkv_t = jnp.concatenate([keep_half, swap(send_half)], 1)
    grad_qkv_w = lax.dot_general(
        rows_one, grad_qkv_t, (((0,), (1,)), ((), ())), preferred_element_type=F32
    ).astype(BF16)
    by_chip = grad_qkv_w.reshape(experts // 4, 2, 2, shard, half_heads * triple)
    half_columns = half_heads * triple // 2
    qkv_sum = scatter_chips(by_chip[..., :half_columns], by_chip[..., half_columns:])
    grad_norm_one = keep_rows(
        lax.dot_general(
            grad_qkv_t, qkv_full, (((0,), (1,)), ((), ())), preferred_element_type=F32
        )
    )
    back_one = norm_backward(grad_norm_one, hat_one, inv_one, gain_one)[0]
    grad_input = grad_one + back_one
    qkv_sum = qkv_sum.reshape(shard, half_heads, 3, HEAD)
    query_shard, key_shard, value_shard = (
        qkv_sum[:, :, part].reshape(shard, half_heads * HEAD) for part in range(3)
    )

    ffn_in_sum = second_sum[:, :hidden]
    gains = jnp.stack(
        [
            jnp.sum(query_shard * w_query + key_shard * w_key + value_shard * w_value, 1)
            / norm1_gain.astype(F32),
            jnp.sum(ffn_in_sum * w_ffn_in, 1) / norm2_gain.astype(F32),
        ]
    )
    gains = gains + swap(gains)
    centre_grad = centre_part + swap(centre_part)
    return (
        output.astype(BF16),
        grad_input.astype(BF16),
        gains[0],
        query_shard,
        key_shard,
        value_shard,
        second_sum[:, 2 * hidden :].T,
        gains[1],
        ffn_in_sum,
        second_sum[:, hidden : 2 * hidden].T,
        centre_grad[None, :],
        grad_in_a[None],
        grad_out_a[None],
        grad_in_b[None],
        grad_out_b[None],
    )


def solution(mesh):
    body = body_paired if fits_paired(mesh) else body_general
    return jax.shard_map(
        body,
        mesh=mesh,
        in_specs=(
            P(("dp", "tensor"), None),
            P(),
            P(("dp", "tensor"), None),
            P("dp"),
            P("dp", "tensor"),
            P("dp", "tensor"),
            P("dp", "tensor"),
            P("tensor", "dp"),
            P("dp"),
            P("dp", "tensor"),
            P("tensor", "dp"),
            P("dp", None),
            P("dp", None, "tensor"),
            P("dp", "tensor", None),
            P("dp", None, "tensor"),
            P("dp", "tensor", None),
            P(("dp", "tensor"), None),
        ),
        out_specs=(
            P(("dp", "tensor"), None),
            P(("dp", "tensor"), None),
            P("dp"),
            P("dp", "tensor"),
            P("dp", "tensor"),
            P("dp", "tensor"),
            P("tensor", "dp"),
            P("dp"),
            P("dp", "tensor"),
            P("tensor", "dp"),
            P("dp", None),
            P("dp", None, "tensor"),
            P("dp", "tensor", None),
            P("dp", None, "tensor"),
            P("dp", "tensor", None),
        ),
        check_vma=False,
    )
```

```python
import functools

import jax
import jax.numpy as jnp
import numpy as np
from jax import lax
from jax.experimental import pallas as pl
from jax.experimental.pallas import tpu as pltpu
from jax.sharding import PartitionSpec as P

HEAD = 64
PLEN = 4096
CONT = 512


def shortened(value):

    def short(part):
        return part.astype(jnp.bfloat16) if part.dtype == jnp.float32 else part

    return jax.tree.map(short, value)


def carried_in(value, axis, combine, identity):
    peers, place = (lax.axis_size(axis), lax.axis_index(axis))
    everything = lax.all_gather(value, axis)
    start = jnp.broadcast_to(jnp.asarray(identity, value.dtype), value.shape)

    def turn(k, before):
        reached = k < place
        new = combine(before, everything[k])
        return jnp.where(reached, new, before)

    return lax.fori_loop(0, peers, turn, start)


def rows_gather(value):
    return lax.all_gather(value, "tensor", axis=0, tiled=True)


def rows_scatter(value):
    return lax.psum_scatter(
        value.astype(jnp.bfloat16), "tensor", scatter_dimension=0, tiled=True
    ).astype(jnp.float32)


def pair_total(value):
    return jax.tree.map(lambda part: part.astype(jnp.float32), lax.psum(shortened(value), "tensor"))


def to_experts(value):
    return lax.all_to_all(value, "dp", split_axis=0, concat_axis=0, tiled=True)


def matmul(left, right):
    return jnp.dot(left, right, preferred_element_type=jnp.float32)


def matmul_tn(left, right):
    return lax.dot_general(
        left, right, (((0,), (0,)), ((), ())), preferred_element_type=jnp.float32
    )


def matmul_nt(left, right):
    return lax.dot_general(
        left, right, (((1,), (1,)), ((), ())), preferred_element_type=jnp.float32
    )


def norm_forward(hidden, gain):
    mean_row = jnp.mean(hidden, -1, keepdims=True)
    centred = hidden - mean_row
    scale_inv = lax.rsqrt(jnp.mean(centred * centred, -1, keepdims=True) + 1e-05)
    normed = centred * scale_inv
    return (normed * gain, normed, scale_inv)


def norm_backward(grad_m, normed, scale_inv, gain):
    grad_hat = grad_m * gain
    inner = (
        grad_hat
        - jnp.mean(grad_hat, -1, keepdims=True)
        - normed * jnp.mean(grad_hat * normed, -1, keepdims=True)
    )
    return (inner * scale_inv, jnp.sum(grad_m * normed, 0))


def gelu_grad(preact, grad):
    unused, pull = jax.vjp(jax.nn.gelu, preact)
    return pull(grad)[0]


def add_counts(first, second):
    return first + second


def attend(queries, keys, values, allowed, heads):
    scale = HEAD ** (-0.5)

    def head_step(head, carry):
        outputs, log_sums = carry
        query_h = lax.dynamic_slice_in_dim(queries, head * HEAD, HEAD, 1)
        key_h = lax.dynamic_slice_in_dim(keys, head * HEAD, HEAD, 1)
        value_h = lax.dynamic_slice_in_dim(values, head * HEAD, HEAD, 1)
        scores = jnp.where(allowed, matmul_nt(query_h, key_h) * scale, -1e30)
        top_score = jnp.max(scores, 1, keepdims=True)
        expo = jnp.exp(scores - top_score)
        total = jnp.sum(expo, 1, keepdims=True)
        probs = (expo / total).astype(jnp.bfloat16)
        outputs = lax.dynamic_update_slice_in_dim(outputs, matmul(probs, value_h), head * HEAD, 1)
        log_sums = lax.dynamic_update_index_in_dim(
            log_sums, top_score[:, 0] + jnp.log(total[:, 0]), head, 0
        )
        return (outputs, log_sums)

    start_state = (
        jnp.zeros((queries.shape[0], heads * HEAD), jnp.float32),
        jnp.zeros((heads, queries.shape[0]), jnp.float32),
    )
    return lax.fori_loop(0, heads, head_step, start_state)


def attend_back(queries, keys, values, allowed, log_sums, grad_attended, heads):
    scale = HEAD ** (-0.5)

    def head_step(head, carry):
        grad_q, grad_k, grad_v = carry
        query_h = lax.dynamic_slice_in_dim(queries, head * HEAD, HEAD, 1)
        key_h = lax.dynamic_slice_in_dim(keys, head * HEAD, HEAD, 1)
        value_h = lax.dynamic_slice_in_dim(values, head * HEAD, HEAD, 1)
        grad_o = lax.dynamic_slice_in_dim(grad_attended, head * HEAD, HEAD, 1)
        scores = jnp.where(allowed, matmul_nt(query_h, key_h) * scale, -1e30)
        probs = jnp.exp(
            scores - lax.dynamic_index_in_dim(log_sums, head, 0, keepdims=False)[:, None]
        )
        grad_p = matmul_nt(grad_o, value_h)
        grad_s = (probs * (grad_p - jnp.sum(probs * grad_p, 1, keepdims=True))).astype(jnp.bfloat16)
        grad_q = lax.dynamic_update_slice_in_dim(
            grad_q, matmul(grad_s, key_h) * scale, head * HEAD, 1
        )
        grad_k = lax.dynamic_update_slice_in_dim(
            grad_k, matmul_tn(grad_s, query_h) * scale, head * HEAD, 1
        )
        grad_v = lax.dynamic_update_slice_in_dim(
            grad_v, matmul_tn(probs.astype(jnp.bfloat16), grad_o), head * HEAD, 1
        )
        return (grad_q, grad_k, grad_v)

    start_state = (
        jnp.zeros(queries.shape, jnp.float32),
        jnp.zeros(keys.shape, jnp.float32),
        jnp.zeros(values.shape, jnp.float32),
    )
    return lax.fori_loop(0, heads, head_step, start_state)


def add_block(buffer, block, start):
    length = block.shape[0]
    current = lax.dynamic_slice_in_dim(buffer, start, length, 0)
    return lax.dynamic_update_slice_in_dim(buffer, current + block, start, 0)


def body_general(
    tokens,
    cont_prompt,
    routes,
    norm1_gain,
    w_query,
    w_key,
    w_value,
    w_attn_out,
    norm2_gain,
    w_ffn_in,
    w_ffn_out,
    centroids,
    expert_in_a,
    expert_out_a,
    expert_in_b,
    expert_out_b,
    grad_out,
):
    experts = lax.axis_size("dp")
    pair_size = lax.axis_size("tensor")
    dp_index = lax.axis_index("dp")
    tensor_index = lax.axis_index("tensor")
    rows_dev = tokens.shape[0]
    rows_dp = rows_dev * pair_size
    prm_dev = rows_dp - CONT
    pkeys = experts * prm_dev
    heads = w_query.shape[1] // HEAD
    width = tokens.shape[1]
    span = PLEN // prm_dev
    owner_start = dp_index // span * PLEN
    mapped_start = cont_prompt[dp_index] * PLEN
    gain_one, query_full, key_full, value_full, attn_full, gain_two, ffn_in_full, ffn_out_full = (
        lax.all_gather(norm1_gain, "dp", axis=0, tiled=True),
        lax.all_gather(w_query, "dp", axis=0, tiled=True),
        lax.all_gather(w_key, "dp", axis=0, tiled=True),
        lax.all_gather(w_value, "dp", axis=0, tiled=True),
        lax.all_gather(w_attn_out, "dp", axis=1, tiled=True),
        lax.all_gather(norm2_gain, "dp", axis=0, tiled=True),
        lax.all_gather(w_ffn_in, "dp", axis=0, tiled=True),
        lax.all_gather(w_ffn_out, "dp", axis=1, tiled=True),
    )
    inputs = tokens.astype(jnp.float32)
    normed_one, hat_one, inv_one = norm_forward(inputs, gain_one.astype(jnp.float32))
    rows_one = rows_gather(normed_one.astype(jnp.bfloat16))
    queries = matmul(rows_one, query_full).astype(jnp.bfloat16)
    keys_own = matmul(rows_one, key_full).astype(jnp.bfloat16)
    values_own = matmul(rows_one, value_full).astype(jnp.bfloat16)
    prompt_keys, prompt_values = (
        lax.all_gather(keys_own[:prm_dev], "dp", axis=0, tiled=True),
        lax.all_gather(values_own[:prm_dev], "dp", axis=0, tiled=True),
    )
    keys_first = lax.dynamic_slice_in_dim(prompt_keys, owner_start, PLEN, 0)
    values_first = lax.dynamic_slice_in_dim(prompt_values, owner_start, PLEN, 0)
    first_row = lax.broadcasted_iota(jnp.int32, (prm_dev, 1), 0)
    first_column = lax.broadcasted_iota(jnp.int32, (1, PLEN), 1)
    allowed_first = first_column <= dp_index % span * prm_dev + first_row
    keys_second = jnp.concatenate(
        [lax.dynamic_slice_in_dim(prompt_keys, mapped_start, PLEN, 0), keys_own[prm_dev:]], 0
    )
    values_second = jnp.concatenate(
        [lax.dynamic_slice_in_dim(prompt_values, mapped_start, PLEN, 0), values_own[prm_dev:]], 0
    )
    second_row = lax.broadcasted_iota(jnp.int32, (CONT, 1), 0)
    second_column = lax.broadcasted_iota(jnp.int32, (1, PLEN + CONT), 1)
    allowed_second = (second_column < PLEN) | (second_column - PLEN <= second_row)
    attn_first, sums_first = attend(
        queries[:prm_dev], keys_first, values_first, allowed_first, heads
    )
    attn_second, sums_second = attend(
        queries[prm_dev:], keys_second, values_second, allowed_second, heads
    )
    attn_low = jnp.concatenate([attn_first, attn_second], 0).astype(jnp.bfloat16)
    hidden_one = inputs + rows_scatter(matmul(attn_low, attn_full))
    normed_two, hat_two, inv_two = norm_forward(hidden_one, gain_two.astype(jnp.float32))
    rows_two = rows_gather(normed_two.astype(jnp.bfloat16))
    ffn_pre = matmul(rows_two, ffn_in_full)
    ffn_act = jax.nn.gelu(ffn_pre).astype(jnp.bfloat16)
    hidden_two = hidden_one + rows_scatter(matmul(ffn_act, ffn_out_full))
    route = routes[:, 0]
    slots_per = max(2, (3 * rows_dev + 2 * experts - 1) // (2 * experts))
    capacity = 5 * rows_dp // 4
    expert_ids = lax.broadcasted_iota(jnp.int32, (1, experts), 1)
    onehot = (route[:, None] == expert_ids).astype(jnp.int32)
    offsets = carried_in(
        jnp.sum(onehot, 0), ("dp", "tensor"), add_counts, jnp.zeros((experts,), jnp.int32)
    )
    local_rank = jnp.sum((jnp.cumsum(onehot, 0) - 1) * onehot, 1)
    global_slot = local_rank + jnp.sum(onehot * offsets[None, :], 1)
    kept = global_slot < capacity
    target = route * slots_per + local_rank
    columns = lax.broadcasted_iota(jnp.int32, (1, experts * slots_per), 1)
    placer = ((columns == target[:, None]) & kept[:, None]).astype(jnp.bfloat16)
    sent_rows = (
        matmul_tn(placer, hidden_two.astype(jnp.bfloat16))
        .astype(jnp.bfloat16)
        .reshape(experts, slots_per, width)
    )
    expert_rows = rows_gather(to_experts(sent_rows)).reshape(-1, width)
    centre = centroids[0]
    gate_value = jax.nn.sigmoid(matmul(expert_rows, centre))
    pre_a = matmul(expert_rows, expert_in_a[0])
    act_a = jax.nn.gelu(pre_a).astype(jnp.bfloat16)
    branch_a = pair_total(matmul(act_a, expert_out_a[0]))
    middle = (expert_rows.astype(jnp.float32) + branch_a).astype(jnp.bfloat16)
    pre_b = matmul(middle, expert_in_b[0])
    act_b = jax.nn.gelu(pre_b).astype(jnp.bfloat16)
    branch_b = rows_scatter(matmul(act_b, expert_out_b[0]))
    half_rows = expert_rows.shape[0] // pair_size
    start_row = tensor_index * half_rows
    branch_half = lax.dynamic_slice_in_dim(branch_a, start_row, half_rows, 0) + branch_b
    gate_half = lax.dynamic_slice_in_dim(gate_value, start_row, half_rows, 0)
    returned = (
        (gate_half[:, None] * branch_half).astype(jnp.bfloat16).reshape(experts, slots_per, width)
    )
    came_back = to_experts(returned).reshape(experts * slots_per, width)
    output = hidden_two + matmul(placer, came_back)
    cotangent = grad_out.astype(jnp.float32)
    sent_grad = matmul_tn(placer, grad_out).astype(jnp.bfloat16).reshape(experts, slots_per, width)
    grad_half = to_experts(sent_grad).reshape(half_rows, width)
    grad_returned = rows_gather(grad_half).astype(jnp.float32)
    grad_gate_half = jnp.sum(grad_half.astype(jnp.float32) * branch_half, 1)
    grad_logit_half = grad_gate_half * gate_half * (1.0 - gate_half)
    rows_half = lax.dynamic_slice_in_dim(expert_rows, start_row, half_rows, 0)
    centre_part = matmul(grad_logit_half, rows_half.astype(jnp.float32))
    grad_branch = gate_value[:, None] * grad_returned
    grad_b = grad_branch.astype(jnp.bfloat16)
    grad_pre_b = gelu_grad(pre_b, matmul_nt(grad_b, expert_out_b[0])).astype(jnp.bfloat16)
    grad_out_b = matmul_tn(act_b, grad_b)
    grad_in_b = matmul_tn(middle, grad_pre_b)
    grad_middle = pair_total(matmul_nt(grad_pre_b, expert_in_b[0]))
    grad_a = (grad_branch + grad_middle).astype(jnp.bfloat16)
    grad_pre_a = gelu_grad(pre_a, matmul_nt(grad_a, expert_out_a[0])).astype(jnp.bfloat16)
    grad_out_a = matmul_tn(act_a, grad_a)
    grad_in_a = matmul_tn(expert_rows, grad_pre_a)
    grad_rows = (
        rows_scatter(matmul_nt(grad_pre_a, expert_in_a[0]))
        + lax.dynamic_slice_in_dim(grad_middle, start_row, half_rows, 0)
        + grad_logit_half[:, None] * centre.astype(jnp.float32)[None, :]
    )
    grad_back = to_experts(
        grad_rows.astype(jnp.bfloat16).reshape(experts, slots_per, width)
    ).reshape(experts * slots_per, width)
    grad_two = cotangent + matmul(placer, grad_back)
    gain_one, query_full, key_full, value_full, attn_full, gain_two, ffn_in_full, ffn_out_full = (
        lax.all_gather(norm1_gain, "dp", axis=0, tiled=True),
        lax.all_gather(w_query, "dp", axis=0, tiled=True),
        lax.all_gather(w_key, "dp", axis=0, tiled=True),
        lax.all_gather(w_value, "dp", axis=0, tiled=True),
        lax.all_gather(w_attn_out, "dp", axis=1, tiled=True),
        lax.all_gather(norm2_gain, "dp", axis=0, tiled=True),
        lax.all_gather(w_ffn_in, "dp", axis=0, tiled=True),
        lax.all_gather(w_ffn_out, "dp", axis=1, tiled=True),
    )
    rows_down = rows_gather(grad_two.astype(jnp.bfloat16))
    grad_ffn_pre = gelu_grad(ffn_pre, matmul_nt(rows_down, ffn_out_full)).astype(jnp.bfloat16)
    grad_ffn_out = matmul_tn(ffn_act, rows_down)
    grad_ffn_in = matmul_tn(rows_two, grad_ffn_pre)
    grad_norm_two = rows_scatter(matmul_nt(grad_ffn_pre, ffn_in_full))
    back_two, grad_gain_two = norm_backward(
        grad_norm_two, hat_two, inv_two, gain_two.astype(jnp.float32)
    )
    grad_one = grad_two + back_two
    rows_attn = rows_gather(grad_one.astype(jnp.bfloat16))
    grad_attn_out = matmul_tn(attn_low, rows_attn)
    grad_attended = matmul_nt(rows_attn, attn_full).astype(jnp.bfloat16)
    grad_q_first, grad_k_first, grad_v_first = attend_back(
        queries[:prm_dev],
        keys_first,
        values_first,
        allowed_first,
        sums_first,
        grad_attended[:prm_dev],
        heads,
    )
    grad_q_second, grad_k_second, grad_v_second = attend_back(
        queries[prm_dev:],
        keys_second,
        values_second,
        allowed_second,
        sums_second,
        grad_attended[prm_dev:],
        heads,
    )
    local_width = keys_own.shape[1]
    buffer_k = jnp.zeros((pkeys, local_width), jnp.float32)
    buffer_v = jnp.zeros((pkeys, local_width), jnp.float32)
    buffer_k = add_block(
        add_block(buffer_k, grad_k_first, owner_start), grad_k_second[:PLEN], mapped_start
    )
    buffer_v = add_block(
        add_block(buffer_v, grad_v_first, owner_start), grad_v_second[:PLEN], mapped_start
    )
    prompt_grad_k, prompt_grad_v = (
        lax.psum_scatter(buffer_k, "dp", scatter_dimension=0, tiled=True),
        lax.psum_scatter(buffer_v, "dp", scatter_dimension=0, tiled=True),
    )
    grad_keys = jnp.concatenate([prompt_grad_k, grad_k_second[PLEN:]], 0).astype(jnp.bfloat16)
    grad_values = jnp.concatenate([prompt_grad_v, grad_v_second[PLEN:]], 0).astype(jnp.bfloat16)
    grad_queries = jnp.concatenate([grad_q_first, grad_q_second], 0).astype(jnp.bfloat16)
    grad_query = matmul_tn(rows_one, grad_queries)
    grad_key = matmul_tn(rows_one, grad_keys)
    grad_value = matmul_tn(rows_one, grad_values)
    grad_norm_one = rows_scatter(
        matmul_nt(grad_queries, query_full)
        + matmul_nt(grad_keys, key_full)
        + matmul_nt(grad_values, value_full)
    )
    back_one, grad_gain_one = norm_backward(
        grad_norm_one, hat_one, inv_one, gain_one.astype(jnp.float32)
    )
    grad_input = grad_one + back_one
    (
        gain_one_part,
        query_shard,
        key_shard,
        value_shard,
        attn_shard,
        gain_two_part,
        ffn_in_shard,
        ffn_out_shard,
    ) = (
        lax.psum_scatter(grad_gain_one, "dp", scatter_dimension=0, tiled=True),
        lax.psum_scatter(grad_query, "dp", scatter_dimension=0, tiled=True),
        lax.psum_scatter(grad_key, "dp", scatter_dimension=0, tiled=True),
        lax.psum_scatter(grad_value, "dp", scatter_dimension=0, tiled=True),
        lax.psum_scatter(grad_attn_out, "dp", scatter_dimension=1, tiled=True),
        lax.psum_scatter(grad_gain_two, "dp", scatter_dimension=0, tiled=True),
        lax.psum_scatter(grad_ffn_in, "dp", scatter_dimension=0, tiled=True),
        lax.psum_scatter(grad_ffn_out, "dp", scatter_dimension=1, tiled=True),
    )
    gain_one_shard, gain_two_shard, centre_grad = pair_total(
        (gain_one_part, gain_two_part, centre_part)
    )
    return (
        output.astype(jnp.bfloat16),
        grad_input.astype(jnp.bfloat16),
        gain_one_shard,
        query_shard,
        key_shard,
        value_shard,
        attn_shard,
        gain_two_shard,
        ffn_in_shard,
        ffn_out_shard,
        centre_grad[None, :],
        grad_in_a[None],
        grad_out_a[None],
        grad_in_b[None],
        grad_out_b[None],
    )


LOG2E = 1.4426950408889634
GELU_A = 0.7978845608028654
GELU_B = 0.044715
BF16 = jnp.bfloat16
F32 = jnp.float32


def dot_tt(left, right):
    return lax.dot_general(left, right, (((0,), (0,)), ((), ())), preferred_element_type=F32)


def beside(blocks, at, count, start, stop):
    return jnp.concatenate([blocks[at + j, start:stop, :] for j in range(count)], 1)


def in_groups(sizes, first, count, take, carry):
    for size in sizes:
        groups = count // size
        step = take(size)
        carry = lax.fori_loop(
            0, groups, lambda k, value, at=first, n=size, f=step: f(at + k * n, value), carry
        )
        first, count = first + groups * size, count - groups * size
    return carry


def attn_fwd_kernel(plan, own, prompts, out, log_sums, values, *, head, factor):
    step_id = pl.program_id(0)
    block, full, first = plan[0, step_id], plan[1, step_id], plan[2, step_id]

    def with_ones(value):
        return jnp.concatenate([value.T, jnp.ones((value.shape[1], head), BF16)], 1)

    @pl.when(step_id == 0)
    def _():
        def turn(k, carry):
            values[k] = with_ones(prompts[k, head : 2 * head, :])
            return carry

        lax.fori_loop(0, prompts.shape[0], turn, 0)

    @pl.when(plan[3, step_id] > 0)
    def _():
        query = own[block, 0:head, :].T
        scores = matmul(query, own[block, head : 2 * head, :])
        query_at = lax.broadcasted_iota(jnp.int32, scores.shape, 0)
        key_at = lax.broadcasted_iota(jnp.int32, scores.shape, 1)
        scores = jnp.where(key_at <= query_at, scores, -1e30)
        top = jnp.max(scores, 1, keepdims=True) * factor
        expo = jnp.exp2(scores * factor - top)
        result = matmul(expo.astype(BF16), with_ones(own[block, 2 * head : 3 * head, :]))

        def take(count):
            def step(at, carry):
                before, result = carry
                scores = matmul(query, beside(prompts, at, count, 0, head))
                top = jnp.maximum(before, jnp.max(scores, 1, keepdims=True) * factor)
                expo = jnp.exp2(scores * factor - top).astype(BF16)
                rows = jnp.concatenate([values[at + j] for j in range(count)], 0)
                return top, result * jnp.exp2(before - top) + matmul(expo, rows)

            return step

        top, result = in_groups((4, 2, 1), first, full, take, (top, result))
        result = result.T
        total = result[head : head + 1]
        out[block] = (result[:head] / total).astype(BF16)
        top = jnp.broadcast_to(top, (top.shape[0], 128)).T[0:1]
        log_sums[block] = top + jnp.log2(total)


def attn_bwd_kernel(
    plan, own, prompts, grad, out, log_sums, grad_own, grad_prompts, sum_k, sum_v, *, head, factor, scale
):
    step_id = pl.program_id(0)
    block, full, first = plan[0, step_id], plan[1, step_id], plan[2, step_id]

    @pl.when(step_id == 0)
    def _():
        sum_k[...] = jnp.zeros_like(sum_k)
        sum_v[...] = jnp.zeros_like(sum_v)

    @pl.when(plan[3, step_id] > 0)
    def _():
        query_t, grad_t, log_sum = own[block, 0:head, :], grad[block], log_sums[block]
        inner = jnp.sum(grad_t.astype(F32) * out[block].astype(F32), 0, keepdims=True)
        query, grad_o = query_t.T, grad_t.T

        def tile(key, value, diagonal):
            probs = jnp.exp2(dot_tt(key, query_t) * factor - log_sum)
            if diagonal:
                key_at = lax.broadcasted_iota(jnp.int32, probs.shape, 0)
                query_at = lax.broadcasted_iota(jnp.int32, probs.shape, 1)
                probs = jnp.where(key_at <= query_at, probs, 0.0)
            grad_s = (probs * (dot_tt(value, grad_t) - inner)).astype(BF16)
            return matmul(grad_s, query), matmul(probs.astype(BF16), grad_o), matmul(key, grad_s)

        grad_k, grad_v, grad_q = tile(
            own[block, head : 2 * head, :], own[block, 2 * head : 3 * head, :], True
        )
        grad_own[block, head : 2 * head, :] = (grad_k * scale).T.astype(BF16)
        grad_own[block, 2 * head : 3 * head, :] = grad_v.T.astype(BF16)

        def take(count):
            def step(at, grad_q):
                more_k, more_v, more_q = tile(
                    beside(prompts, at, count, 0, head),
                    beside(prompts, at, count, head, 2 * head),
                    False,
                )
                length = more_k.shape[0] // count
                for j in range(count):
                    sum_k[at + j] += more_k[j * length : (j + 1) * length]
                    sum_v[at + j] += more_v[j * length : (j + 1) * length]
                return grad_q + more_q

            return step

        grad_q = in_groups((4, 2, 1), first, full, take, grad_q)
        grad_own[block, 0:head, :] = (grad_q * scale).astype(BF16)

    @pl.when(step_id == pl.num_programs(0) - 1)
    def _():
        def finish(k, carry):
            grad_prompts[k, 0:head, :] = (sum_k[k] * scale).T.astype(BF16)
            grad_prompts[k, head : 2 * head, :] = sum_v[k].T.astype(BF16)
            return carry

        lax.fori_loop(0, sum_k.shape[0], finish, 0)


def attn_forward(plan, own, prompts):
    blocks, triple, length = own.shape
    head = triple // 3
    whole = pl.BlockSpec(memory_space=pltpu.VMEM)
    return pl.pallas_call(
        functools.partial(attn_fwd_kernel, head=head, factor=head**-0.5 * LOG2E),
        grid_spec=pltpu.PrefetchScalarGridSpec(
            num_scalar_prefetch=1,
            grid=(plan.shape[1],),
            in_specs=[whole, whole],
            out_specs=[whole, whole],
            scratch_shapes=[pltpu.VMEM((prompts.shape[0], length, 2 * head), BF16)],
        ),
        out_shape=[
            jax.ShapeDtypeStruct((blocks, head, length), BF16),
            jax.ShapeDtypeStruct((blocks, 1, length), F32),
        ],
        compiler_params=pltpu.CompilerParams(vmem_limit_bytes=40 * 2**20),
        cost_estimate=pl.CostEstimate(
            flops=100 * length * length * 256 * 4,
            bytes_accessed=8 * 2**20,
            transcendentals=100 * length * length,
        ),
        name="attn_fwd",
    )(plan, own, prompts)


def attn_backward(plan, own, prompts, grad, out, log_sums):
    blocks, triple, length = own.shape
    head = triple // 3
    whole = pl.BlockSpec(memory_space=pltpu.VMEM)
    return pl.pallas_call(
        functools.partial(
            attn_bwd_kernel, head=head, factor=head**-0.5 * LOG2E, scale=head**-0.5
        ),
        grid_spec=pltpu.PrefetchScalarGridSpec(
            num_scalar_prefetch=1,
            grid=(plan.shape[1],),
            in_specs=[whole] * 5,
            out_specs=[whole, whole],
            scratch_shapes=[pltpu.VMEM((prompts.shape[0], length, head), F32)] * 2,
        ),
        out_shape=[
            jax.ShapeDtypeStruct(own.shape, BF16),
            jax.ShapeDtypeStruct(prompts.shape, BF16),
        ],
        compiler_params=pltpu.CompilerParams(vmem_limit_bytes=48 * 2**20),
        cost_estimate=pl.CostEstimate(
            flops=100 * length * length * 256 * 10,
            bytes_accessed=16 * 2**20,
            transcendentals=100 * length * length,
        ),
        name="attn_bwd",
    )(plan, own, prompts, grad, out, log_sums)


def swap(value):
    return lax.ppermute(value, "tensor", [(0, 1), (1, 0)])


def to_core_one(value):
    return lax.ppermute(value, "tensor", [(0, 1)])


def to_core_zero(value):
    return lax.ppermute(value, "tensor", [(1, 0)])


def with_other(value):
    return jnp.concatenate([value, swap(value)], 0)


def keep_rows(value):
    half = value.shape[0] // 2
    return value[:half].astype(F32) + swap(value[half:].astype(BF16)).astype(F32)


def gelu_pair(preact):
    square = preact * preact
    gate = 0.5 + 0.5 * jnp.tanh(preact * (GELU_A + GELU_A * GELU_B * square))
    act = preact * gate
    slope = gate + act * (1.0 - gate) * (2.0 * GELU_A + 6.0 * GELU_A * GELU_B * square)
    return act.astype(BF16), slope.astype(BF16)


def take_terms(refs, kinds):
    early = pl.program_id(0) < pl.num_programs(0) // 2
    values, at = [], 0
    for paired in kinds:
        if paired:
            values.append(jnp.where(early, refs[at][...], refs[at + 1][...]))
        else:
            values.append(refs[at][...])
        at += 1 + paired
    return values, refs[at:]


def give_halves(refs, value):
    early = pl.program_id(0) < pl.num_programs(0) // 2

    @pl.when(early)
    def _():
        refs[0][...] = value

    @pl.when(jnp.logical_not(early))
    def _():
        refs[1][...] = value


def copy_in(source, target, semaphore, at):
    if at is not None:
        source = source.at[:, at : at + target.shape[1]]
    return pltpu.make_async_copy(source, target, semaphore)


def mlp_kernel(*refs, kinds, transposed, gated, at):
    *refs, held, semaphore = refs
    w_out = refs[sum(kinds) + len(kinds) + gated + 1]

    @pl.when(pl.program_id(0) == 0)
    def _():
        copy_in(w_out, held, semaphore, at).start()

    terms, refs = take_terms(refs, kinds)
    rows = terms[0]
    if len(terms) > 1:
        total = rows.astype(F32)
        for term in terms[1:]:
            total = total + term.astype(F32)
        rows = total.astype(BF16)
    if gated:
        centre, refs = refs[0], refs[1:]
        logit = jnp.sum(rows.astype(F32) * centre[...].astype(F32), 1, keepdims=True)
        refs[-1][...] = 1.0 / (1.0 + jnp.exp(-logit))
    w_in, w_out, kept_rows, kept_act, kept_slope, first, second = refs[:7]
    kept_rows[...] = rows
    act, slope = gelu_pair(matmul(rows, w_in[...]))
    kept_act[...] = act
    kept_slope[...] = slope

    @pl.when(pl.program_id(0) == 0)
    def _():
        copy_in(w_out, held, semaphore, at).wait()

    result = (matmul_nt if transposed else matmul)(act, held[...])
    give_halves((first, second), result.astype(BF16))


def mlp_back_kernel(*refs, kinds, transposed, scaled, at):
    *refs, held, semaphore = refs
    w_in = refs[scaled + sum(kinds) + len(kinds) + 1]

    @pl.when(pl.program_id(0) == 0)
    def _():
        copy_in(w_in, held, semaphore, at).start()

    factor, refs = (refs[0], refs[1:]) if scaled else (None, refs)
    terms, refs = take_terms(refs, kinds)
    grad = terms[0]
    if scaled:
        total = factor[...] * grad.astype(F32)
        for term in terms[1:]:
            total = total + term.astype(F32)
        grad = total.astype(BF16)
    w_out, w_in, slope, kept_grad, kept_pre, first, second = refs
    kept_grad[...] = grad
    grad = (matmul_nt if transposed else matmul)(grad, w_out[...])
    grad_pre = (grad * slope[...].astype(F32)).astype(BF16)
    kept_pre[...] = grad_pre

    @pl.when(pl.program_id(0) == 0)
    def _():
        copy_in(w_in, held, semaphore, at).wait()

    give_halves((first, second), matmul_nt(grad_pre, held[...]).astype(BF16))


def mlp_blocks(terms, length):
    paired = [isinstance(term, tuple) for term in terms]
    arrays = [part for term in terms for part in (term if isinstance(term, tuple) else (term,))]
    half = max(part.shape[0] // length // (1 + (not pair)) for term, pair in zip(terms, paired) for part in (term if pair else (term,)))
    width = arrays[0].shape[1]
    block = pl.BlockSpec((length, width), lambda m: (m, 0))
    halves = [
        pl.BlockSpec((length, width), lambda m: (jnp.minimum(m, half - 1), 0)),
        pl.BlockSpec((length, width), lambda m: (jnp.maximum(m - half, 0), 0)),
    ]
    specs = [spec for pair in paired for spec in (halves if pair else [block])]
    return tuple(paired), arrays, specs, block, halves, 2 * half


def mlp_forward(terms, w_in, w_out, hidden, length, transposed=False, columns=(0, 0), centre=None):
    kinds, arrays, specs, block, halves, steps = mlp_blocks(terms, length)
    rows, width = steps * length, arrays[0].shape[1]
    hidden_block = pl.BlockSpec((length, hidden), lambda m: (m, 0))
    once = dict(pipeline_mode=pl.Buffered(1))
    in_block = pl.BlockSpec((width, hidden), lambda m: (0, columns[0]), **once)
    out_shape = (width, hidden) if transposed else (hidden, width)
    gated = centre is not None
    return pl.pallas_call(
        functools.partial(
            mlp_kernel,
            kinds=kinds,
            transposed=transposed,
            gated=gated,
            at=columns[1] * hidden if transposed else None,
        ),
        grid=(steps,),
        in_specs=specs + [pl.BlockSpec((1, width), lambda m: (0, 0))] * gated + [in_block, pl.BlockSpec(memory_space=pl.ANY)],
        out_specs=[block, hidden_block, hidden_block]
        + halves
        + [pl.BlockSpec((length, 1), lambda m: (m, 0))] * gated,
        out_shape=[jax.ShapeDtypeStruct((rows, width), BF16)]
        + [jax.ShapeDtypeStruct((rows, hidden), BF16)] * 2
        + [jax.ShapeDtypeStruct((rows // 2, width), BF16)] * 2
        + [jax.ShapeDtypeStruct((rows, 1), F32)] * gated,
        scratch_shapes=[pltpu.VMEM(out_shape, BF16), pltpu.SemaphoreType.DMA],
        compiler_params=pltpu.CompilerParams(vmem_limit_bytes=54 * 2**20),
        cost_estimate=pl.CostEstimate(
            flops=rows * width * hidden,
            bytes_accessed=width * hidden + rows * hidden + rows * width,
            transcendentals=0,
        ),
        name="mlp_fwd",
    )(*arrays, *([centre] * gated), w_in, w_out)


def mlp_backward(terms, w_out, w_in, slope, length, transposed=True, columns=(0, 0), factor=None):
    kinds, arrays, specs, block, halves, steps = mlp_blocks(terms, length)
    rows, width = steps * length, arrays[0].shape[1]
    hidden = slope.shape[1]
    hidden_block = pl.BlockSpec((length, hidden), lambda m: (m, 0))
    once = dict(pipeline_mode=pl.Buffered(1))
    out_block = (
        pl.BlockSpec((hidden, width), lambda m: (0, 0), **once)
        if transposed
        else pl.BlockSpec((width, hidden), lambda m: (0, columns[1]), **once)
    )
    scaled = factor is not None
    return pl.pallas_call(
        functools.partial(
            mlp_back_kernel,
            kinds=kinds,
            transposed=transposed,
            scaled=scaled,
            at=None if transposed else columns[0] * hidden,
        ),
        grid=(steps,),
        in_specs=[pl.BlockSpec((length, 1), lambda m: (m, 0))] * scaled
        + specs
        + [out_block, pl.BlockSpec(memory_space=pl.ANY), hidden_block],
        out_specs=[block, hidden_block] + halves,
        out_shape=[
            jax.ShapeDtypeStruct((rows, width), BF16),
            jax.ShapeDtypeStruct((rows, hidden), BF16),
        ]
        + [jax.ShapeDtypeStruct((rows // 2, width), BF16)] * 2,
        scratch_shapes=[pltpu.VMEM((width, hidden), BF16), pltpu.SemaphoreType.DMA],
        compiler_params=pltpu.CompilerParams(vmem_limit_bytes=54 * 2**20),
        cost_estimate=pl.CostEstimate(
            flops=4 * rows * width * hidden,
            bytes_accessed=4 * width * hidden + 4 * rows * hidden + 4 * rows * width,
            transcendentals=0,
        ),
        name="mlp_bwd",
    )(*([factor] * scaled), *arrays, w_out, w_in, slope)


def from_bit(value, bit):
    return lax.ppermute(value, "dp", [(i, i ^ bit) for i in range(lax.axis_size("dp"))])


def chip_place():
    place = lax.axis_index("dp")
    return place // 4, place // 2 % 2, place % 2


def ordered(bit, own, other, axis):
    return jnp.where(
        bit == 0, jnp.stack([own, other], axis), jnp.stack([other, own], axis)
    )


def gather_line(value):
    planes = lax.axis_size("dp") // 4
    z = chip_place()[0]
    blocks = jnp.stack([value] + [from_bit(value, 4 * k) for k in range(1, planes)])
    return jnp.stack(
        [lax.dynamic_index_in_dim(blocks, z ^ k, 0, keepdims=False) for k in range(planes)]
    )


def gather_second(line):
    half = line.shape[-1] // 2
    y, x = chip_place()[1:]
    first, second = line[..., :half], line[..., half:]
    first = ordered(y, first, from_bit(first, 2), 1)
    second = ordered(x, second, from_bit(second, 1), 1)
    return first, second


def gather_third(first, second, cuts):
    y, x = chip_place()[1:]
    first_other, second_other = from_bit(first, 1), from_bit(second, 2)
    return (
        [ordered(x, first[at], first_other[at], 2) for at in cuts],
        [ordered(y, second[at], second_other[at], 1) for at in cuts],
    )


def halve(value, bit, axis, partner):
    lower = lax.index_in_dim(value, 0, axis, keepdims=False)
    upper = lax.index_in_dim(value, 1, axis, keepdims=False)
    keep, send = jnp.where(bit == 0, lower, upper), jnp.where(bit == 0, upper, lower)
    return keep.astype(F32) + from_bit(send, partner).astype(F32)


def scatter_chips(first, second):
    planes = first.shape[0]
    z, y, x = chip_place()
    first = halve(first, x, 2, 1).astype(BF16)
    second = halve(second, y, 1, 2).astype(BF16)
    line = jnp.concatenate([halve(first, y, 1, 2), halve(second, x, 1, 1)], -1).astype(BF16)
    total = lax.dynamic_index_in_dim(line, z, 0, keepdims=False).astype(F32)
    for k in range(1, planes):
        part = lax.dynamic_index_in_dim(line, z ^ k, 0, keepdims=False)
        total = total + from_bit(part, 4 * k).astype(F32)
    return total


def fits_paired(mesh):
    return mesh.shape["tensor"] == 2 and mesh.shape["dp"] == 16


def body_paired(
    tokens,
    cont_prompt,
    routes,
    norm1_gain,
    w_query,
    w_key,
    w_value,
    w_attn_out,
    norm2_gain,
    w_ffn_in,
    w_ffn_out,
    centroids,
    expert_in_a,
    expert_out_a,
    expert_in_b,
    expert_out_b,
    grad_out,
):
    experts = lax.axis_size("dp")
    dp_index = lax.axis_index("dp")
    core_zero = lax.axis_index("tensor") == 0
    rows, width = tokens.shape
    rows_dp = 2 * rows
    shard = w_query.shape[0]
    half_heads = w_query.shape[1] // HEAD
    hidden = w_ffn_in.shape[1]
    assert expert_in_a.shape[2] == hidden
    triple = 3 * HEAD
    heads = 2 * half_heads
    both = lambda lower, upper: (jnp.where(core_zero, lower, upper), jnp.where(core_zero, upper, lower))

    route = routes[:, 0]
    slots_per = max(2, (3 * rows + 2 * experts - 1) // (2 * experts))
    capacity = 5 * rows_dp // 4
    onehot = route[:, None] == lax.broadcasted_iota(jnp.int32, (1, experts), 1)
    onehot_low = onehot.astype(BF16)
    below = lax.broadcasted_iota(jnp.int32, (rows, rows), 0) > lax.broadcasted_iota(
        jnp.int32, (rows, rows), 1
    )
    earlier = matmul(below.astype(BF16), onehot_low)
    local_rank = jnp.sum(jnp.where(onehot, earlier, 0.0), 1).astype(jnp.int32)
    target = route * slots_per + local_rank
    columns = lax.broadcasted_iota(jnp.int32, (1, experts * slots_per), 1)
    placer = (columns == target[:, None]).astype(BF16)
    counts = jnp.sum(onehot_low.astype(F32), 0).astype(BF16)
    counts_pair = jnp.concatenate(both(counts, swap(counts)), 0)

    qkv_shard = jnp.stack(
        [part.reshape(shard, half_heads, HEAD) for part in (w_query, w_key, w_value)], 2
    ).reshape(shard, half_heads * triple)
    extra = jnp.concatenate([norm1_gain, norm2_gain, counts_pair], 0)
    extra = jnp.pad(extra[None, :], ((0, 7), (0, half_heads * triple - extra.shape[0])))
    planes = experts // 4
    first_shard, second_shard = lax.optimization_barrier(
        (
            jnp.concatenate([qkv_shard, extra], 0),
            jnp.concatenate([w_ffn_in, w_ffn_out.T, w_attn_out.T], 1),
        )
    )
    second_line = lax.all_gather(
        second_shard,
        "dp",
        axis_index_groups=[[4 * z + k for z in range(planes)] for k in range(4)],
    )
    line_one = gather_line(first_shard)
    weight_rows, extra_row = np.s_[..., :shard, :], np.s_[..., shard, :]
    (first_all, extra_all), (last_all, unused) = gather_third(
        *gather_second(line_one), (weight_rows, extra_row)
    )
    qkv_full = jnp.concatenate([first_all, last_all], -1).reshape(width, half_heads * triple)
    extra_all = extra_all.reshape(experts, -1)
    gain_one = extra_all[:, :shard].reshape(width).astype(F32)
    gain_two = extra_all[:, shard : 2 * shard].reshape(width).astype(F32)
    counts_all = extra_all[:, 2 * shard : 2 * shard + 2 * experts].reshape(experts, 2, experts)

    mine = jnp.sum(
        jnp.where(lax.broadcasted_iota(jnp.int32, (1, 1, experts), 2) == dp_index, counts_all.astype(F32), 0.0),
        2,
    )
    per_chip = jnp.sum(mine, 1)
    chip_before = jnp.sum(
        jnp.where(
            lax.broadcasted_iota(jnp.int32, (experts, experts), 1)
            < lax.broadcasted_iota(jnp.int32, (experts, experts), 0),
            per_chip[None, :],
            0.0,
        ),
        1,
    )
    starts = both(chip_before, chip_before + mine[:, 0])
    slot_at = lax.broadcasted_iota(jnp.int32, (1, slots_per), 1).astype(F32)
    kept = jnp.concatenate(
        [(start[:, None] + slot_at < capacity).reshape(-1, 1) for start in starts], 0
    )
    half_rows = experts * slots_per

    pair_tokens = with_other(tokens).astype(F32)
    normed_one, hat_pair, inv_pair = norm_forward(pair_tokens, gain_one)
    inputs, hat_one, inv_one = pair_tokens[:rows], hat_pair[:rows], inv_pair[:rows]
    rows_one = normed_one.astype(BF16)
    other_t = lax.dot_general(
        qkv_full, rows_one[rows:], (((0,), (1,)), ((), ())), preferred_element_type=F32
    ).astype(BF16)
    own_t = lax.dot_general(
        qkv_full, rows_one[:rows], (((0,), (1,)), ((), ())), preferred_element_type=F32
    ).astype(BF16)
    qkv_t = jnp.concatenate(both(own_t, swap(other_t)), 0).reshape(heads, triple, rows)
    qkv_t, second_line, late_grad = lax.optimization_barrier((qkv_t, second_line, grad_out))
    sent_grad = matmul_tn(placer, late_grad).astype(BF16).reshape(experts, slots_per, width)
    by_head = lax.all_to_all(qkv_t, "dp", split_axis=0, concat_axis=0, tiled=True)

    by_head, second_line, sent_grad = lax.optimization_barrier((by_head, second_line, sent_grad))
    second_all = lax.all_gather(
        second_line, "dp", axis_index_groups=[[4 * z + k for k in range(4)] for z in range(planes)]
    )
    second_all = second_all.transpose(1, 0, 2, 3).reshape(width, -1)
    attn_half = second_all[:, 2 * hidden :]

    lent = experts // 4
    span = PLEN // rows
    own_blocks = jnp.concatenate([by_head, to_core_zero(by_head[:lent])], 0)
    prompt_kv = jnp.where(core_zero, by_head[:, HEAD:], to_core_one(by_head[:, HEAD:]))
    places = jnp.arange(experts + lent, dtype=jnp.int32)
    follows = cont_prompt * span
    plan_zero = jnp.stack(
        [
            places,
            jnp.where(places < experts, places % span, span),
            jnp.concatenate([places[:experts] // span * span, follows[:lent]], 0),
            jnp.ones_like(places),
        ]
    )
    plan_one = jnp.stack(
        [
            jnp.minimum(places + lent, experts - 1),
            jnp.full_like(places, span),
            jnp.concatenate([follows[lent:], jnp.zeros((2 * lent,), jnp.int32)], 0),
            (places < experts - lent).astype(jnp.int32),
        ]
    )
    plan = jnp.where(core_zero, plan_zero, plan_one)
    attn_blocks, log_sums = attn_forward(plan, own_blocks, prompt_kv)
    lent_back = to_core_one(attn_blocks[experts:])
    attn_own = jnp.concatenate(
        [jnp.where(core_zero, attn_blocks[:lent], lent_back), attn_blocks[lent:experts]], 0
    )
    attn_t = lax.all_to_all(attn_own, "dp", split_axis=0, concat_axis=0, tiled=True).reshape(
        width, rows
    )

    half_width = width // 2
    own_heads, other_heads = both(attn_t[:half_width], attn_t[half_width:])
    attn_other = swap(attn_half)
    hidden_one = (
        inputs
        + lax.dot_general(
            own_heads, attn_half, (((0,), (1,)), ((), ())), preferred_element_type=F32
        )
        + lax.dot_general(
            other_heads, attn_other, (((0,), (1,)), ((), ())), preferred_element_type=F32
        )
    )
    normed_two, hat_two, inv_two = norm_forward(hidden_one, gain_two)
    normed_two = normed_two.astype(BF16)
    rows_two, ffn_act, ffn_slope, ffn_own, ffn_other = mlp_forward(
        [(normed_two, swap(normed_two))],
        second_all,
        second_all,
        hidden,
        rows,
        transposed=True,
        columns=(0, 1),
    )
    hidden_two = hidden_one + ffn_own.astype(F32) + swap(ffn_other).astype(F32)

    sent_rows = (
        matmul_tn(placer, hidden_two.astype(BF16)).astype(BF16).reshape(experts, slots_per, width)
    )
    own_rows, sent_grad = lax.optimization_barrier((to_experts(sent_rows), sent_grad))
    own_rows = own_rows.reshape(half_rows, width)
    grad_own = to_experts(sent_grad).reshape(half_rows, width)
    centre = centroids[0]
    length = half_rows // 2
    expert_rows, act_a, slope_a, own_a, other_a, gate_column = mlp_forward(
        [(own_rows, swap(own_rows))],
        expert_in_a[0],
        expert_out_a[0],
        hidden,
        length,
        centre=centroids,
    )
    from_a = (swap(other_a), swap(own_a))
    middle, act_b, slope_b, own_b, other_b = mlp_forward(
        [expert_rows, (own_a, other_a), from_a], expert_in_b[0], expert_out_b[0], hidden, length
    )
    own_b, grad_own = lax.optimization_barrier((own_b, grad_own))
    branch_half = (
        own_a.astype(F32) + from_a[0].astype(F32) + own_b.astype(F32) + swap(other_b).astype(F32)
    )
    gate_value = gate_column[:, 0]
    gate_half = gate_value[:half_rows]
    returned = (
        jnp.where(kept[:half_rows], gate_half[:, None] * branch_half, 0.0)
        .astype(BF16)
        .reshape(experts, slots_per, width)
    )
    came_back = to_experts(returned).reshape(half_rows, width)

    kept_half = kept[:half_rows, 0]
    grad_logit_half = jnp.where(
        kept_half,
        jnp.sum(grad_own.astype(F32) * branch_half, 1) * gate_half * (1.0 - gate_half),
        0.0,
    )
    centre_part = matmul(grad_logit_half, own_rows.astype(F32))
    kept_gate = jnp.where(kept, gate_column, 0.0)
    grad_pair = (grad_own, swap(grad_own))
    grad_b, grad_pre_b, own_m, other_m = mlp_backward(
        [grad_pair], expert_out_b[0], expert_in_b[0], slope_b, length, factor=kept_gate
    )
    from_m = (swap(other_m), swap(own_m))
    grad_a, grad_pre_a, own_x, other_x = mlp_backward(
        [grad_pair, (own_m, other_m), from_m],
        expert_out_a[0],
        expert_in_a[0],
        slope_a,
        length,
        factor=kept_gate,
    )
    grad_rows = (
        own_x.astype(F32)
        + swap(other_x).astype(F32)
        + own_m.astype(F32)
        + from_m[0].astype(F32)
        + grad_logit_half[:, None] * centre.astype(F32)[None, :]
    )
    grad_rows, came_back, act_a, grad_a, expert_rows, grad_pre_a = lax.optimization_barrier(
        (grad_rows.astype(BF16), came_back, act_a, grad_a, expert_rows, grad_pre_a)
    )
    grad_out_a = matmul_tn(act_a, grad_a)
    grad_in_a = matmul_tn(expert_rows, grad_pre_a)
    output = hidden_two + matmul(placer, came_back)
    grad_back = to_experts(grad_rows.reshape(experts, slots_per, width))
    grad_back, grad_out_a, grad_in_a = lax.optimization_barrier((grad_back, grad_out_a, grad_in_a))
    grad_back = grad_back.reshape(half_rows, width)
    grad_two = grad_out.astype(F32) + matmul(placer, grad_back)

    grad_down = grad_two.astype(BF16)
    rows_down, grad_ffn_pre, down_own, down_other = mlp_backward(
        [(grad_down, swap(grad_down))],
        second_all,
        second_all,
        ffn_slope,
        rows,
        transposed=False,
        columns=(0, 1),
    )
    grad_norm_two = down_own.astype(F32) + swap(down_other).astype(F32)
    back_two = norm_backward(grad_norm_two, hat_two, inv_two, gain_two)[0]
    grad_one = grad_two + back_two

    grad_branch_one = grad_one.astype(BF16)
    grad_halves = both(
        *(
            lax.dot_general(
                part, grad_branch_one, (((0,), (1,)), ((), ())), preferred_element_type=F32
            ).astype(BF16)
            for part in (attn_half, attn_other)
        )
    )
    grad_attn, rows_down, ffn_act, rows_two, grad_ffn_pre = lax.optimization_barrier(
        (
            jnp.concatenate(grad_halves, 0).reshape(heads, HEAD, rows),
            rows_down,
            ffn_act,
            rows_two,
            grad_ffn_pre,
        )
    )
    grad_by_head = lax.all_to_all(grad_attn, "dp", split_axis=0, concat_axis=0, tiled=True)
    grad_ffn_out_t = matmul_tn(rows_down, ffn_act)
    grad_ffn_in = matmul_tn(rows_two, grad_ffn_pre)
    part_own, part_other = (
        lax.dot_general(
            grad_branch_one, part, (((0,), (1,)), ((), ())), preferred_element_type=F32
        )
        for part in (own_heads, other_heads)
    )
    grad_attn_half = part_own + swap(part_other.astype(BF16)).astype(F32)
    second_part = jnp.concatenate(
        [grad_ffn_in.astype(BF16), grad_ffn_out_t.astype(BF16), grad_attn_half.astype(BF16)], 1
    )
    grad_by_head, second_part = lax.optimization_barrier((grad_by_head, second_part))
    second_sum = lax.psum_scatter(second_part, "dp", scatter_dimension=0, tiled=True).astype(F32)
    grad_blocks = jnp.concatenate([grad_by_head, to_core_zero(grad_by_head[:lent])], 0)
    grad_own_blocks, grad_prompts = attn_backward(
        plan, own_blocks, prompt_kv, grad_blocks, attn_blocks, log_sums
    )
    lent_grad = to_core_one(grad_own_blocks[experts:])
    prompt_sum = grad_prompts.astype(F32) + to_core_zero(grad_prompts).astype(F32)
    prompt_part = jnp.concatenate(
        [
            grad_own_blocks[:experts, :HEAD],
            (grad_own_blocks[:experts, HEAD:].astype(F32) + prompt_sum).astype(BF16),
        ],
        1,
    )
    cont_part = jnp.concatenate([lent_grad, grad_own_blocks[lent:experts]], 0)
    grad_head, act_b, grad_b, middle, grad_pre_b = lax.optimization_barrier(
        (jnp.where(core_zero, prompt_part, cont_part), act_b, grad_b, middle, grad_pre_b)
    )
    grad_qkv = lax.all_to_all(grad_head, "dp", split_axis=0, concat_axis=0, tiled=True)
    grad_out_b = matmul_tn(act_b, grad_b)
    grad_in_b = matmul_tn(middle, grad_pre_b)
    grad_qkv, grad_out_b, grad_in_b = lax.optimization_barrier((grad_qkv, grad_out_b, grad_in_b))
    grad_qkv = grad_qkv.reshape(2, half_heads * triple, rows)
    keep_half, send_half = both(grad_qkv[0], grad_qkv[1])
    grad_qkv_t = jnp.concatenate([keep_half, swap(send_half)], 1)
    grad_qkv_w = lax.dot_general(
        rows_one, grad_qkv_t, (((0,), (1,)), ((), ())), preferred_element_type=F32
    ).astype(BF16)
    by_chip = grad_qkv_w.reshape(experts // 4, 2, 2, shard, half_heads * triple)
    half_columns = half_heads * triple // 2
    qkv_sum = scatter_chips(by_chip[..., :half_columns], by_chip[..., half_columns:])
    grad_norm_one = keep_rows(
        lax.dot_general(
            grad_qkv_t, qkv_full, (((0,), (1,)), ((), ())), preferred_element_type=F32
        )
    )
    back_one = norm_backward(grad_norm_one, hat_one, inv_one, gain_one)[0]
    grad_input = grad_one + back_one
    qkv_sum = qkv_sum.reshape(shard, half_heads, 3, HEAD)
    query_shard, key_shard, value_shard = (
        qkv_sum[:, :, part].reshape(shard, half_heads * HEAD) for part in range(3)
    )

    ffn_in_sum = second_sum[:, :hidden]
    gains = jnp.stack(
        [
            jnp.sum(query_shard * w_query + key_shard * w_key + value_shard * w_value, 1)
            / norm1_gain.astype(F32),
            jnp.sum(ffn_in_sum * w_ffn_in, 1) / norm2_gain.astype(F32),
        ]
    )
    gains = gains + swap(gains)
    centre_grad = centre_part + swap(centre_part)
    return (
        output.astype(BF16),
        grad_input.astype(BF16),
        gains[0],
        query_shard,
        key_shard,
        value_shard,
        second_sum[:, 2 * hidden :].T,
        gains[1],
        ffn_in_sum,
        second_sum[:, hidden : 2 * hidden].T,
        centre_grad[None, :],
        grad_in_a[None],
        grad_out_a[None],
        grad_in_b[None],
        grad_out_b[None],
    )


def solution(mesh):
    body = body_paired if fits_paired(mesh) else body_general
    return jax.shard_map(
        body,
        mesh=mesh,
        in_specs=(
            P(("dp", "tensor"), None),
            P(),
            P(("dp", "tensor"), None),
            P("dp"),
            P("dp", "tensor"),
            P("dp", "tensor"),
            P("dp", "tensor"),
            P("tensor", "dp"),
            P("dp"),
            P("dp", "tensor"),
            P("tensor", "dp"),
            P("dp", None),
            P("dp", None, "tensor"),
            P("dp", "tensor", None),
            P("dp", None, "tensor"),
            P("dp", "tensor", None),
            P(("dp", "tensor"), None),
        ),
        out_specs=(
            P(("dp", "tensor"), None),
            P(("dp", "tensor"), None),
            P("dp"),
            P("dp", "tensor"),
            P("dp", "tensor"),
            P("dp", "tensor"),
            P("tensor", "dp"),
            P("dp"),
            P("dp", "tensor"),
            P("tensor", "dp"),
            P("dp", None),
            P("dp", None, "tensor"),
            P("dp", "tensor", None),
            P("dp", None, "tensor"),
            P("dp", "tensor", None),
        ),
        check_vma=False,
    )
```

```python
import functools

import jax
import jax.numpy as jnp
import numpy as np
from jax import lax
from jax.experimental import pallas as pl
from jax.experimental.pallas import tpu as pltpu
from jax.sharding import PartitionSpec as P

HEAD = 64
PLEN = 4096
CONT = 512


def shortened(value):

    def short(part):
        return part.astype(jnp.bfloat16) if part.dtype == jnp.float32 else part

    return jax.tree.map(short, value)


def carried_in(value, axis, combine, identity):
    peers, place = (lax.axis_size(axis), lax.axis_index(axis))
    everything = lax.all_gather(value, axis)
    start = jnp.broadcast_to(jnp.asarray(identity, value.dtype), value.shape)

    def turn(k, before):
        reached = k < place
        new = combine(before, everything[k])
        return jnp.where(reached, new, before)

    return lax.fori_loop(0, peers, turn, start)


def rows_gather(value):
    return lax.all_gather(value, "tensor", axis=0, tiled=True)


def rows_scatter(value):
    return lax.psum_scatter(
        value.astype(jnp.bfloat16), "tensor", scatter_dimension=0, tiled=True
    ).astype(jnp.float32)


def pair_total(value):
    return jax.tree.map(lambda part: part.astype(jnp.float32), lax.psum(shortened(value), "tensor"))


def to_experts(value):
    return lax.all_to_all(value, "dp", split_axis=0, concat_axis=0, tiled=True)


def matmul(left, right):
    return jnp.dot(left, right, preferred_element_type=jnp.float32)


def matmul_tn(left, right):
    return lax.dot_general(
        left, right, (((0,), (0,)), ((), ())), preferred_element_type=jnp.float32
    )


def matmul_nt(left, right):
    return lax.dot_general(
        left, right, (((1,), (1,)), ((), ())), preferred_element_type=jnp.float32
    )


def norm_forward(hidden, gain):
    mean_row = jnp.mean(hidden, -1, keepdims=True)
    centred = hidden - mean_row
    scale_inv = lax.rsqrt(jnp.mean(centred * centred, -1, keepdims=True) + 1e-05)
    normed = centred * scale_inv
    return (normed * gain, normed, scale_inv)


def norm_backward(grad_m, normed, scale_inv, gain):
    grad_hat = grad_m * gain
    inner = (
        grad_hat
        - jnp.mean(grad_hat, -1, keepdims=True)
        - normed * jnp.mean(grad_hat * normed, -1, keepdims=True)
    )
    return (inner * scale_inv, jnp.sum(grad_m * normed, 0))


def gelu_grad(preact, grad):
    unused, pull = jax.vjp(jax.nn.gelu, preact)
    return pull(grad)[0]


def add_counts(first, second):
    return first + second


def attend(queries, keys, values, allowed, heads):
    scale = HEAD ** (-0.5)

    def head_step(head, carry):
        outputs, log_sums = carry
        query_h = lax.dynamic_slice_in_dim(queries, head * HEAD, HEAD, 1)
        key_h = lax.dynamic_slice_in_dim(keys, head * HEAD, HEAD, 1)
        value_h = lax.dynamic_slice_in_dim(values, head * HEAD, HEAD, 1)
        scores = jnp.where(allowed, matmul_nt(query_h, key_h) * scale, -1e30)
        top_score = jnp.max(scores, 1, keepdims=True)
        expo = jnp.exp(scores - top_score)
        total = jnp.sum(expo, 1, keepdims=True)
        probs = (expo / total).astype(jnp.bfloat16)
        outputs = lax.dynamic_update_slice_in_dim(outputs, matmul(probs, value_h), head * HEAD, 1)
        log_sums = lax.dynamic_update_index_in_dim(
            log_sums, top_score[:, 0] + jnp.log(total[:, 0]), head, 0
        )
        return (outputs, log_sums)

    start_state = (
        jnp.zeros((queries.shape[0], heads * HEAD), jnp.float32),
        jnp.zeros((heads, queries.shape[0]), jnp.float32),
    )
    return lax.fori_loop(0, heads, head_step, start_state)


def attend_back(queries, keys, values, allowed, log_sums, grad_attended, heads):
    scale = HEAD ** (-0.5)

    def head_step(head, carry):
        grad_q, grad_k, grad_v = carry
        query_h = lax.dynamic_slice_in_dim(queries, head * HEAD, HEAD, 1)
        key_h = lax.dynamic_slice_in_dim(keys, head * HEAD, HEAD, 1)
        value_h = lax.dynamic_slice_in_dim(values, head * HEAD, HEAD, 1)
        grad_o = lax.dynamic_slice_in_dim(grad_attended, head * HEAD, HEAD, 1)
        scores = jnp.where(allowed, matmul_nt(query_h, key_h) * scale, -1e30)
        probs = jnp.exp(
            scores - lax.dynamic_index_in_dim(log_sums, head, 0, keepdims=False)[:, None]
        )
        grad_p = matmul_nt(grad_o, value_h)
        grad_s = (probs * (grad_p - jnp.sum(probs * grad_p, 1, keepdims=True))).astype(jnp.bfloat16)
        grad_q = lax.dynamic_update_slice_in_dim(
            grad_q, matmul(grad_s, key_h) * scale, head * HEAD, 1
        )
        grad_k = lax.dynamic_update_slice_in_dim(
            grad_k, matmul_tn(grad_s, query_h) * scale, head * HEAD, 1
        )
        grad_v = lax.dynamic_update_slice_in_dim(
            grad_v, matmul_tn(probs.astype(jnp.bfloat16), grad_o), head * HEAD, 1
        )
        return (grad_q, grad_k, grad_v)

    start_state = (
        jnp.zeros(queries.shape, jnp.float32),
        jnp.zeros(keys.shape, jnp.float32),
        jnp.zeros(values.shape, jnp.float32),
    )
    return lax.fori_loop(0, heads, head_step, start_state)


def add_block(buffer, block, start):
    length = block.shape[0]
    current = lax.dynamic_slice_in_dim(buffer, start, length, 0)
    return lax.dynamic_update_slice_in_dim(buffer, current + block, start, 0)


def body_general(
    tokens,
    cont_prompt,
    routes,
    norm1_gain,
    w_query,
    w_key,
    w_value,
    w_attn_out,
    norm2_gain,
    w_ffn_in,
    w_ffn_out,
    centroids,
    expert_in_a,
    expert_out_a,
    expert_in_b,
    expert_out_b,
    grad_out,
):
    experts = lax.axis_size("dp")
    pair_size = lax.axis_size("tensor")
    dp_index = lax.axis_index("dp")
    tensor_index = lax.axis_index("tensor")
    rows_dev = tokens.shape[0]
    rows_dp = rows_dev * pair_size
    prm_dev = rows_dp - CONT
    pkeys = experts * prm_dev
    heads = w_query.shape[1] // HEAD
    width = tokens.shape[1]
    span = PLEN // prm_dev
    owner_start = dp_index // span * PLEN
    mapped_start = cont_prompt[dp_index] * PLEN
    gain_one, query_full, key_full, value_full, attn_full, gain_two, ffn_in_full, ffn_out_full = (
        lax.all_gather(norm1_gain, "dp", axis=0, tiled=True),
        lax.all_gather(w_query, "dp", axis=0, tiled=True),
        lax.all_gather(w_key, "dp", axis=0, tiled=True),
        lax.all_gather(w_value, "dp", axis=0, tiled=True),
        lax.all_gather(w_attn_out, "dp", axis=1, tiled=True),
        lax.all_gather(norm2_gain, "dp", axis=0, tiled=True),
        lax.all_gather(w_ffn_in, "dp", axis=0, tiled=True),
        lax.all_gather(w_ffn_out, "dp", axis=1, tiled=True),
    )
    inputs = tokens.astype(jnp.float32)
    normed_one, hat_one, inv_one = norm_forward(inputs, gain_one.astype(jnp.float32))
    rows_one = rows_gather(normed_one.astype(jnp.bfloat16))
    queries = matmul(rows_one, query_full).astype(jnp.bfloat16)
    keys_own = matmul(rows_one, key_full).astype(jnp.bfloat16)
    values_own = matmul(rows_one, value_full).astype(jnp.bfloat16)
    prompt_keys, prompt_values = (
        lax.all_gather(keys_own[:prm_dev], "dp", axis=0, tiled=True),
        lax.all_gather(values_own[:prm_dev], "dp", axis=0, tiled=True),
    )
    keys_first = lax.dynamic_slice_in_dim(prompt_keys, owner_start, PLEN, 0)
    values_first = lax.dynamic_slice_in_dim(prompt_values, owner_start, PLEN, 0)
    first_row = lax.broadcasted_iota(jnp.int32, (prm_dev, 1), 0)
    first_column = lax.broadcasted_iota(jnp.int32, (1, PLEN), 1)
    allowed_first = first_column <= dp_index % span * prm_dev + first_row
    keys_second = jnp.concatenate(
        [lax.dynamic_slice_in_dim(prompt_keys, mapped_start, PLEN, 0), keys_own[prm_dev:]], 0
    )
    values_second = jnp.concatenate(
        [lax.dynamic_slice_in_dim(prompt_values, mapped_start, PLEN, 0), values_own[prm_dev:]], 0
    )
    second_row = lax.broadcasted_iota(jnp.int32, (CONT, 1), 0)
    second_column = lax.broadcasted_iota(jnp.int32, (1, PLEN + CONT), 1)
    allowed_second = (second_column < PLEN) | (second_column - PLEN <= second_row)
    attn_first, sums_first = attend(
        queries[:prm_dev], keys_first, values_first, allowed_first, heads
    )
    attn_second, sums_second = attend(
        queries[prm_dev:], keys_second, values_second, allowed_second, heads
    )
    attn_low = jnp.concatenate([attn_first, attn_second], 0).astype(jnp.bfloat16)
    hidden_one = inputs + rows_scatter(matmul(attn_low, attn_full))
    normed_two, hat_two, inv_two = norm_forward(hidden_one, gain_two.astype(jnp.float32))
    rows_two = rows_gather(normed_two.astype(jnp.bfloat16))
    ffn_pre = matmul(rows_two, ffn_in_full)
    ffn_act = jax.nn.gelu(ffn_pre).astype(jnp.bfloat16)
    hidden_two = hidden_one + rows_scatter(matmul(ffn_act, ffn_out_full))
    route = routes[:, 0]
    slots_per = max(2, (3 * rows_dev + 2 * experts - 1) // (2 * experts))
    capacity = 5 * rows_dp // 4
    expert_ids = lax.broadcasted_iota(jnp.int32, (1, experts), 1)
    onehot = (route[:, None] == expert_ids).astype(jnp.int32)
    offsets = carried_in(
        jnp.sum(onehot, 0), ("dp", "tensor"), add_counts, jnp.zeros((experts,), jnp.int32)
    )
    local_rank = jnp.sum((jnp.cumsum(onehot, 0) - 1) * onehot, 1)
    global_slot = local_rank + jnp.sum(onehot * offsets[None, :], 1)
    kept = global_slot < capacity
    target = route * slots_per + local_rank
    columns = lax.broadcasted_iota(jnp.int32, (1, experts * slots_per), 1)
    placer = ((columns == target[:, None]) & kept[:, None]).astype(jnp.bfloat16)
    sent_rows = (
        matmul_tn(placer, hidden_two.astype(jnp.bfloat16))
        .astype(jnp.bfloat16)
        .reshape(experts, slots_per, width)
    )
    expert_rows = rows_gather(to_experts(sent_rows)).reshape(-1, width)
    centre = centroids[0]
    gate_value = jax.nn.sigmoid(matmul(expert_rows, centre))
    pre_a = matmul(expert_rows, expert_in_a[0])
    act_a = jax.nn.gelu(pre_a).astype(jnp.bfloat16)
    branch_a = pair_total(matmul(act_a, expert_out_a[0]))
    middle = (expert_rows.astype(jnp.float32) + branch_a).astype(jnp.bfloat16)
    pre_b = matmul(middle, expert_in_b[0])
    act_b = jax.nn.gelu(pre_b).astype(jnp.bfloat16)
    branch_b = rows_scatter(matmul(act_b, expert_out_b[0]))
    half_rows = expert_rows.shape[0] // pair_size
    start_row = tensor_index * half_rows
    branch_half = lax.dynamic_slice_in_dim(branch_a, start_row, half_rows, 0) + branch_b
    gate_half = lax.dynamic_slice_in_dim(gate_value, start_row, half_rows, 0)
    returned = (
        (gate_half[:, None] * branch_half).astype(jnp.bfloat16).reshape(experts, slots_per, width)
    )
    came_back = to_experts(returned).reshape(experts * slots_per, width)
    output = hidden_two + matmul(placer, came_back)
    cotangent = grad_out.astype(jnp.float32)
    sent_grad = matmul_tn(placer, grad_out).astype(jnp.bfloat16).reshape(experts, slots_per, width)
    grad_half = to_experts(sent_grad).reshape(half_rows, width)
    grad_returned = rows_gather(grad_half).astype(jnp.float32)
    grad_gate_half = jnp.sum(grad_half.astype(jnp.float32) * branch_half, 1)
    grad_logit_half = grad_gate_half * gate_half * (1.0 - gate_half)
    rows_half = lax.dynamic_slice_in_dim(expert_rows, start_row, half_rows, 0)
    centre_part = matmul(grad_logit_half, rows_half.astype(jnp.float32))
    grad_branch = gate_value[:, None] * grad_returned
    grad_b = grad_branch.astype(jnp.bfloat16)
    grad_pre_b = gelu_grad(pre_b, matmul_nt(grad_b, expert_out_b[0])).astype(jnp.bfloat16)
    grad_out_b = matmul_tn(act_b, grad_b)
    grad_in_b = matmul_tn(middle, grad_pre_b)
    grad_middle = pair_total(matmul_nt(grad_pre_b, expert_in_b[0]))
    grad_a = (grad_branch + grad_middle).astype(jnp.bfloat16)
    grad_pre_a = gelu_grad(pre_a, matmul_nt(grad_a, expert_out_a[0])).astype(jnp.bfloat16)
    grad_out_a = matmul_tn(act_a, grad_a)
    grad_in_a = matmul_tn(expert_rows, grad_pre_a)
    grad_rows = (
        rows_scatter(matmul_nt(grad_pre_a, expert_in_a[0]))
        + lax.dynamic_slice_in_dim(grad_middle, start_row, half_rows, 0)
        + grad_logit_half[:, None] * centre.astype(jnp.float32)[None, :]
    )
    grad_back = to_experts(
        grad_rows.astype(jnp.bfloat16).reshape(experts, slots_per, width)
    ).reshape(experts * slots_per, width)
    grad_two = cotangent + matmul(placer, grad_back)
    gain_one, query_full, key_full, value_full, attn_full, gain_two, ffn_in_full, ffn_out_full = (
        lax.all_gather(norm1_gain, "dp", axis=0, tiled=True),
        lax.all_gather(w_query, "dp", axis=0, tiled=True),
        lax.all_gather(w_key, "dp", axis=0, tiled=True),
        lax.all_gather(w_value, "dp", axis=0, tiled=True),
        lax.all_gather(w_attn_out, "dp", axis=1, tiled=True),
        lax.all_gather(norm2_gain, "dp", axis=0, tiled=True),
        lax.all_gather(w_ffn_in, "dp", axis=0, tiled=True),
        lax.all_gather(w_ffn_out, "dp", axis=1, tiled=True),
    )
    rows_down = rows_gather(grad_two.astype(jnp.bfloat16))
    grad_ffn_pre = gelu_grad(ffn_pre, matmul_nt(rows_down, ffn_out_full)).astype(jnp.bfloat16)
    grad_ffn_out = matmul_tn(ffn_act, rows_down)
    grad_ffn_in = matmul_tn(rows_two, grad_ffn_pre)
    grad_norm_two = rows_scatter(matmul_nt(grad_ffn_pre, ffn_in_full))
    back_two, grad_gain_two = norm_backward(
        grad_norm_two, hat_two, inv_two, gain_two.astype(jnp.float32)
    )
    grad_one = grad_two + back_two
    rows_attn = rows_gather(grad_one.astype(jnp.bfloat16))
    grad_attn_out = matmul_tn(attn_low, rows_attn)
    grad_attended = matmul_nt(rows_attn, attn_full).astype(jnp.bfloat16)
    grad_q_first, grad_k_first, grad_v_first = attend_back(
        queries[:prm_dev],
        keys_first,
        values_first,
        allowed_first,
        sums_first,
        grad_attended[:prm_dev],
        heads,
    )
    grad_q_second, grad_k_second, grad_v_second = attend_back(
        queries[prm_dev:],
        keys_second,
        values_second,
        allowed_second,
        sums_second,
        grad_attended[prm_dev:],
        heads,
    )
    local_width = keys_own.shape[1]
    buffer_k = jnp.zeros((pkeys, local_width), jnp.float32)
    buffer_v = jnp.zeros((pkeys, local_width), jnp.float32)
    buffer_k = add_block(
        add_block(buffer_k, grad_k_first, owner_start), grad_k_second[:PLEN], mapped_start
    )
    buffer_v = add_block(
        add_block(buffer_v, grad_v_first, owner_start), grad_v_second[:PLEN], mapped_start
    )
    prompt_grad_k, prompt_grad_v = (
        lax.psum_scatter(buffer_k, "dp", scatter_dimension=0, tiled=True),
        lax.psum_scatter(buffer_v, "dp", scatter_dimension=0, tiled=True),
    )
    grad_keys = jnp.concatenate([prompt_grad_k, grad_k_second[PLEN:]], 0).astype(jnp.bfloat16)
    grad_values = jnp.concatenate([prompt_grad_v, grad_v_second[PLEN:]], 0).astype(jnp.bfloat16)
    grad_queries = jnp.concatenate([grad_q_first, grad_q_second], 0).astype(jnp.bfloat16)
    grad_query = matmul_tn(rows_one, grad_queries)
    grad_key = matmul_tn(rows_one, grad_keys)
    grad_value = matmul_tn(rows_one, grad_values)
    grad_norm_one = rows_scatter(
        matmul_nt(grad_queries, query_full)
        + matmul_nt(grad_keys, key_full)
        + matmul_nt(grad_values, value_full)
    )
    back_one, grad_gain_one = norm_backward(
        grad_norm_one, hat_one, inv_one, gain_one.astype(jnp.float32)
    )
    grad_input = grad_one + back_one
    (
        gain_one_part,
        query_shard,
        key_shard,
        value_shard,
        attn_shard,
        gain_two_part,
        ffn_in_shard,
        ffn_out_shard,
    ) = (
        lax.psum_scatter(grad_gain_one, "dp", scatter_dimension=0, tiled=True),
        lax.psum_scatter(grad_query, "dp", scatter_dimension=0, tiled=True),
        lax.psum_scatter(grad_key, "dp", scatter_dimension=0, tiled=True),
        lax.psum_scatter(grad_value, "dp", scatter_dimension=0, tiled=True),
        lax.psum_scatter(grad_attn_out, "dp", scatter_dimension=1, tiled=True),
        lax.psum_scatter(grad_gain_two, "dp", scatter_dimension=0, tiled=True),
        lax.psum_scatter(grad_ffn_in, "dp", scatter_dimension=0, tiled=True),
        lax.psum_scatter(grad_ffn_out, "dp", scatter_dimension=1, tiled=True),
    )
    gain_one_shard, gain_two_shard, centre_grad = pair_total(
        (gain_one_part, gain_two_part, centre_part)
    )
    return (
        output.astype(jnp.bfloat16),
        grad_input.astype(jnp.bfloat16),
        gain_one_shard,
        query_shard,
        key_shard,
        value_shard,
        attn_shard,
        gain_two_shard,
        ffn_in_shard,
        ffn_out_shard,
        centre_grad[None, :],
        grad_in_a[None],
        grad_out_a[None],
        grad_in_b[None],
        grad_out_b[None],
    )


LOG2E = 1.4426950408889634
GELU_A = 0.7978845608028654
GELU_B = 0.044715
BF16 = jnp.bfloat16
F32 = jnp.float32


def dot_tt(left, right):
    return lax.dot_general(left, right, (((0,), (0,)), ((), ())), preferred_element_type=F32)


def beside(blocks, at, count, start, stop):
    return jnp.concatenate([blocks[at + j, start:stop, :] for j in range(count)], 1)


def in_groups(sizes, first, count, take, carry):
    for size in sizes:
        groups = count // size
        step = take(size)
        carry = lax.fori_loop(
            0, groups, lambda k, value, at=first, n=size, f=step: f(at + k * n, value), carry
        )
        first, count = first + groups * size, count - groups * size
    return carry


def attn_fwd_kernel(plan, own, prompts, out, log_sums, values, *, head, factor):
    step_id = pl.program_id(0)
    block, full, first = plan[0, step_id], plan[1, step_id], plan[2, step_id]

    def with_ones(value):
        return jnp.concatenate([value.T, jnp.ones((value.shape[1], head), BF16)], 1)

    @pl.when(step_id == 0)
    def _():
        def turn(k, carry):
            values[k] = with_ones(prompts[k, head : 2 * head, :])
            return carry

        lax.fori_loop(0, prompts.shape[0], turn, 0)

    @pl.when(plan[3, step_id] > 0)
    def _():
        query = own[block, 0:head, :].T
        scores = matmul(query, own[block, head : 2 * head, :])
        query_at = lax.broadcasted_iota(jnp.int32, scores.shape, 0)
        key_at = lax.broadcasted_iota(jnp.int32, scores.shape, 1)
        scores = jnp.where(key_at <= query_at, scores, -1e30)
        top = jnp.max(scores, 1, keepdims=True) * factor
        expo = jnp.exp2(scores * factor - top)
        result = matmul(expo.astype(BF16), with_ones(own[block, 2 * head : 3 * head, :]))

        def take(count):
            def step(at, carry):
                before, result = carry
                scores = matmul(query, beside(prompts, at, count, 0, head))
                top = jnp.maximum(before, jnp.max(scores, 1, keepdims=True) * factor)
                expo = jnp.exp2(scores * factor - top).astype(BF16)
                rows = jnp.concatenate([values[at + j] for j in range(count)], 0)
                return top, result * jnp.exp2(before - top) + matmul(expo, rows)

            return step

        top, result = in_groups((4, 2, 1), first, full, take, (top, result))
        result = result.T
        total = result[head : head + 1]
        out[block] = (result[:head] / total).astype(BF16)
        top = jnp.broadcast_to(top, (top.shape[0], 128)).T[0:1]
        log_sums[block] = top + jnp.log2(total)


def attn_bwd_kernel(
    plan, own, prompts, grad, out, log_sums, grad_own, grad_prompts, sum_k, sum_v, *, head, factor, scale
):
    step_id = pl.program_id(0)
    block, full, first = plan[0, step_id], plan[1, step_id], plan[2, step_id]

    @pl.when(step_id == 0)
    def _():
        sum_k[...] = jnp.zeros_like(sum_k)
        sum_v[...] = jnp.zeros_like(sum_v)

    @pl.when(plan[3, step_id] > 0)
    def _():
        query_t, grad_t, log_sum = own[block, 0:head, :], grad[block], log_sums[block]
        inner = jnp.sum(grad_t.astype(F32) * out[block].astype(F32), 0, keepdims=True)
        query, grad_o = query_t.T, grad_t.T

        def tile(key, value, diagonal):
            probs = jnp.exp2(dot_tt(key, query_t) * factor - log_sum)
            if diagonal:
                key_at = lax.broadcasted_iota(jnp.int32, probs.shape, 0)
                query_at = lax.broadcasted_iota(jnp.int32, probs.shape, 1)
                probs = jnp.where(key_at <= query_at, probs, 0.0)
            grad_s = (probs * (dot_tt(value, grad_t) - inner)).astype(BF16)
            return matmul(grad_s, query), matmul(probs.astype(BF16), grad_o), matmul(key, grad_s)

        grad_k, grad_v, grad_q = tile(
            own[block, head : 2 * head, :], own[block, 2 * head : 3 * head, :], True
        )
        grad_own[block, head : 2 * head, :] = (grad_k * scale).T.astype(BF16)
        grad_own[block, 2 * head : 3 * head, :] = grad_v.T.astype(BF16)

        def take(count):
            def step(at, grad_q):
                more_k, more_v, more_q = tile(
                    beside(prompts, at, count, 0, head),
                    beside(prompts, at, count, head, 2 * head),
                    False,
                )
                length = more_k.shape[0] // count
                for j in range(count):
                    sum_k[at + j] += more_k[j * length : (j + 1) * length]
                    sum_v[at + j] += more_v[j * length : (j + 1) * length]
                return grad_q + more_q

            return step

        grad_q = in_groups((4, 2, 1), first, full, take, grad_q)
        grad_own[block, 0:head, :] = (grad_q * scale).astype(BF16)

    @pl.when(step_id == pl.num_programs(0) - 1)
    def _():
        def finish(k, carry):
            grad_prompts[k, 0:head, :] = (sum_k[k] * scale).T.astype(BF16)
            grad_prompts[k, head : 2 * head, :] = sum_v[k].T.astype(BF16)
            return carry

        lax.fori_loop(0, sum_k.shape[0], finish, 0)


def attn_forward(plan, own, prompts):
    blocks, triple, length = own.shape
    head = triple // 3
    whole = pl.BlockSpec(memory_space=pltpu.VMEM)
    return pl.pallas_call(
        functools.partial(attn_fwd_kernel, head=head, factor=head**-0.5 * LOG2E),
        grid_spec=pltpu.PrefetchScalarGridSpec(
            num_scalar_prefetch=1,
            grid=(plan.shape[1],),
            in_specs=[whole, whole],
            out_specs=[whole, whole],
            scratch_shapes=[pltpu.VMEM((prompts.shape[0], length, 2 * head), BF16)],
        ),
        out_shape=[
            jax.ShapeDtypeStruct((blocks, head, length), BF16),
            jax.ShapeDtypeStruct((blocks, 1, length), F32),
        ],
        compiler_params=pltpu.CompilerParams(vmem_limit_bytes=40 * 2**20),
        cost_estimate=pl.CostEstimate(
            flops=100 * length * length * 256 * 4,
            bytes_accessed=8 * 2**20,
            transcendentals=100 * length * length,
        ),
        name="attn_fwd",
    )(plan, own, prompts)


def attn_backward(plan, own, prompts, grad, out, log_sums):
    blocks, triple, length = own.shape
    head = triple // 3
    whole = pl.BlockSpec(memory_space=pltpu.VMEM)
    return pl.pallas_call(
        functools.partial(
            attn_bwd_kernel, head=head, factor=head**-0.5 * LOG2E, scale=head**-0.5
        ),
        grid_spec=pltpu.PrefetchScalarGridSpec(
            num_scalar_prefetch=1,
            grid=(plan.shape[1],),
            in_specs=[whole] * 5,
            out_specs=[whole, whole],
            scratch_shapes=[pltpu.VMEM((prompts.shape[0], length, head), F32)] * 2,
        ),
        out_shape=[
            jax.ShapeDtypeStruct(own.shape, BF16),
            jax.ShapeDtypeStruct(prompts.shape, BF16),
        ],
        compiler_params=pltpu.CompilerParams(vmem_limit_bytes=48 * 2**20),
        cost_estimate=pl.CostEstimate(
            flops=100 * length * length * 256 * 10,
            bytes_accessed=16 * 2**20,
            transcendentals=100 * length * length,
        ),
        name="attn_bwd",
    )(plan, own, prompts, grad, out, log_sums)


def swap(value):
    return lax.ppermute(value, "tensor", [(0, 1), (1, 0)])


def to_core_one(value):
    return lax.ppermute(value, "tensor", [(0, 1)])


def to_core_zero(value):
    return lax.ppermute(value, "tensor", [(1, 0)])


def with_other(value):
    return jnp.concatenate([value, swap(value)], 0)


def keep_rows(value):
    half = value.shape[0] // 2
    return value[:half].astype(F32) + swap(value[half:].astype(BF16)).astype(F32)


def gelu_pair(preact):
    square = preact * preact
    gate = 0.5 + 0.5 * jnp.tanh(preact * (GELU_A + GELU_A * GELU_B * square))
    act = preact * gate
    slope = gate + act * (1.0 - gate) * (2.0 * GELU_A + 6.0 * GELU_A * GELU_B * square)
    return act.astype(BF16), slope.astype(BF16)


def by_halves(run):
    early = pl.program_id(0) < pl.num_programs(0) // 2
    pl.when(early)(functools.partial(run, 0))
    pl.when(jnp.logical_not(early))(functools.partial(run, 1))


def take_terms(refs, kinds, half):
    values, at = [], 0
    for paired in kinds:
        values.append(refs[at + half * paired][...])
        at += 1 + paired
    return values, refs[at:]


def mlp_kernel(*refs, kinds, transposed, gated):
    def run(half):
        terms, rest = take_terms(refs, kinds, half)
        rows = terms[0]
        if len(terms) > 1:
            total = rows.astype(F32)
            for term in terms[1:]:
                total = total + term.astype(F32)
            rows = total.astype(BF16)
        if gated:
            centre, rest = rest[0], rest[1:]
            logit = jnp.sum(rows.astype(F32) * centre[...].astype(F32), 1, keepdims=True)
            rest[-1][...] = 1.0 / (1.0 + jnp.exp(-logit))
        w_in, w_out, kept_rows, kept_act, kept_slope, *results = rest[:7]
        kept_rows[...] = rows
        act, slope = gelu_pair(matmul(rows, w_in[...]))
        kept_act[...] = act
        kept_slope[...] = slope
        product = matmul_nt if transposed else matmul
        results[half][...] = product(act, w_out[...]).astype(BF16)

    by_halves(run)


def mlp_back_kernel(*refs, kinds, transposed, scaled):
    def run(half):
        factor, rest = (refs[0], refs[1:]) if scaled else (None, refs)
        terms, rest = take_terms(rest, kinds, half)
        grad = terms[0]
        if scaled:
            total = factor[...] * grad.astype(F32)
            for term in terms[1:]:
                total = total + term.astype(F32)
            grad = total.astype(BF16)
        w_out, w_in, slope, kept_grad, kept_pre, *results = rest
        kept_grad[...] = grad
        grad = (matmul_nt if transposed else matmul)(grad, w_out[...])
        grad_pre = (grad * slope[...].astype(F32)).astype(BF16)
        kept_pre[...] = grad_pre
        results[half][...] = matmul_nt(grad_pre, w_in[...]).astype(BF16)

    by_halves(run)


def mlp_blocks(terms, length):
    paired = [isinstance(term, tuple) for term in terms]
    arrays = [part for term in terms for part in (term if isinstance(term, tuple) else (term,))]
    half = max(part.shape[0] // length // (1 + (not pair)) for term, pair in zip(terms, paired) for part in (term if pair else (term,)))
    width = arrays[0].shape[1]
    block = pl.BlockSpec((length, width), lambda m: (m, 0))
    halves = [
        pl.BlockSpec((length, width), lambda m: (jnp.minimum(m, half - 1), 0)),
        pl.BlockSpec((length, width), lambda m: (jnp.maximum(m - half, 0), 0)),
    ]
    specs = [spec for pair in paired for spec in (halves if pair else [block])]
    return tuple(paired), arrays, specs, block, halves, 2 * half


def mlp_forward(terms, w_in, w_out, hidden, length, transposed=False, columns=(0, 0), centre=None):
    kinds, arrays, specs, block, halves, steps = mlp_blocks(terms, length)
    rows, width = steps * length, arrays[0].shape[1]
    hidden_block = pl.BlockSpec((length, hidden), lambda m: (m, 0))
    once = dict(pipeline_mode=pl.Buffered(1))
    in_block = pl.BlockSpec((width, hidden), lambda m: (0, columns[0]), **once)
    out_block = (
        pl.BlockSpec((width, hidden), lambda m: (0, columns[1]), **once)
        if transposed
        else pl.BlockSpec((hidden, width), lambda m: (0, 0), **once)
    )
    gated = centre is not None
    return pl.pallas_call(
        functools.partial(mlp_kernel, kinds=kinds, transposed=transposed, gated=gated),
        grid=(steps,),
        in_specs=specs + [pl.BlockSpec((1, width), lambda m: (0, 0))] * gated + [in_block, out_block],
        out_specs=[block, hidden_block, hidden_block]
        + halves
        + [pl.BlockSpec((length, 1), lambda m: (m, 0))] * gated,
        out_shape=[jax.ShapeDtypeStruct((rows, width), BF16)]
        + [jax.ShapeDtypeStruct((rows, hidden), BF16)] * 2
        + [jax.ShapeDtypeStruct((rows // 2, width), BF16)] * 2
        + [jax.ShapeDtypeStruct((rows, 1), F32)] * gated,
        compiler_params=pltpu.CompilerParams(vmem_limit_bytes=54 * 2**20),
        cost_estimate=pl.CostEstimate(
            flops=rows * width * hidden,
            bytes_accessed=width * hidden + rows * hidden + rows * width,
            transcendentals=0,
        ),
        name="mlp_fwd",
    )(*arrays, *([centre] * gated), w_in, w_out)


def mlp_backward(terms, w_out, w_in, slope, length, transposed=True, columns=(0, 0), factor=None):
    kinds, arrays, specs, block, halves, steps = mlp_blocks(terms, length)
    rows, width = steps * length, arrays[0].shape[1]
    hidden = slope.shape[1]
    hidden_block = pl.BlockSpec((length, hidden), lambda m: (m, 0))
    once = dict(pipeline_mode=pl.Buffered(1))
    out_block = (
        pl.BlockSpec((hidden, width), lambda m: (0, 0), **once)
        if transposed
        else pl.BlockSpec((width, hidden), lambda m: (0, columns[1]), **once)
    )
    in_block = pl.BlockSpec((width, hidden), lambda m: (0, columns[0]), **once)
    scaled = factor is not None
    return pl.pallas_call(
        functools.partial(mlp_back_kernel, kinds=kinds, transposed=transposed, scaled=scaled),
        grid=(steps,),
        in_specs=[pl.BlockSpec((length, 1), lambda m: (m, 0))] * scaled
        + specs
        + [out_block, in_block, hidden_block],
        out_specs=[block, hidden_block] + halves,
        out_shape=[
            jax.ShapeDtypeStruct((rows, width), BF16),
            jax.ShapeDtypeStruct((rows, hidden), BF16),
        ]
        + [jax.ShapeDtypeStruct((rows // 2, width), BF16)] * 2,
        compiler_params=pltpu.CompilerParams(vmem_limit_bytes=54 * 2**20),
        cost_estimate=pl.CostEstimate(
            flops=4 * rows * width * hidden,
            bytes_accessed=4 * width * hidden + 4 * rows * hidden + 4 * rows * width,
            transcendentals=0,
        ),
        name="mlp_bwd",
    )(*([factor] * scaled), *arrays, w_out, w_in, slope)


def from_bit(value, bit):
    return lax.ppermute(value, "dp", [(i, i ^ bit) for i in range(lax.axis_size("dp"))])


def chip_place():
    place = lax.axis_index("dp")
    return place // 4, place // 2 % 2, place % 2


def ordered(bit, own, other, axis):
    return jnp.where(
        bit == 0, jnp.stack([own, other], axis), jnp.stack([other, own], axis)
    )


def gather_line(value):
    planes = lax.axis_size("dp") // 4
    z = chip_place()[0]
    blocks = jnp.stack([value] + [from_bit(value, 4 * k) for k in range(1, planes)])
    return jnp.stack(
        [lax.dynamic_index_in_dim(blocks, z ^ k, 0, keepdims=False) for k in range(planes)]
    )


def gather_second(line):
    half = line.shape[-1] // 2
    y, x = chip_place()[1:]
    first, second = line[..., :half], line[..., half:]
    first = ordered(y, first, from_bit(first, 2), 1)
    second = ordered(x, second, from_bit(second, 1), 1)
    return first, second


def gather_third(first, second, cuts):
    y, x = chip_place()[1:]
    first_other, second_other = from_bit(first, 1), from_bit(second, 2)
    return (
        [ordered(x, first[at], first_other[at], 2) for at in cuts],
        [ordered(y, second[at], second_other[at], 1) for at in cuts],
    )


def halve(value, bit, axis, partner):
    lower = lax.index_in_dim(value, 0, axis, keepdims=False)
    upper = lax.index_in_dim(value, 1, axis, keepdims=False)
    keep, send = jnp.where(bit == 0, lower, upper), jnp.where(bit == 0, upper, lower)
    return keep.astype(F32) + from_bit(send, partner).astype(F32)


def scatter_chips(first, second):
    planes = first.shape[0]
    z, y, x = chip_place()
    first = halve(first, x, 2, 1).astype(BF16)
    second = halve(second, y, 1, 2).astype(BF16)
    line = jnp.concatenate([halve(first, y, 1, 2), halve(second, x, 1, 1)], -1).astype(BF16)
    total = lax.dynamic_index_in_dim(line, z, 0, keepdims=False).astype(F32)
    for k in range(1, planes):
        part = lax.dynamic_index_in_dim(line, z ^ k, 0, keepdims=False)
        total = total + from_bit(part, 4 * k).astype(F32)
    return total


def fits_paired(mesh):
    return mesh.shape["tensor"] == 2 and mesh.shape["dp"] == 16


def body_paired(
    tokens,
    cont_prompt,
    routes,
    norm1_gain,
    w_query,
    w_key,
    w_value,
    w_attn_out,
    norm2_gain,
    w_ffn_in,
    w_ffn_out,
    centroids,
    expert_in_a,
    expert_out_a,
    expert_in_b,
    expert_out_b,
    grad_out,
):
    experts = lax.axis_size("dp")
    dp_index = lax.axis_index("dp")
    core_zero = lax.axis_index("tensor") == 0
    rows, width = tokens.shape
    rows_dp = 2 * rows
    shard = w_query.shape[0]
    half_heads = w_query.shape[1] // HEAD
    hidden = w_ffn_in.shape[1]
    assert expert_in_a.shape[2] == hidden
    triple = 3 * HEAD
    heads = 2 * half_heads
    both = lambda lower, upper: (jnp.where(core_zero, lower, upper), jnp.where(core_zero, upper, lower))

    route = routes[:, 0]
    slots_per = max(2, (3 * rows + 2 * experts - 1) // (2 * experts))
    capacity = 5 * rows_dp // 4
    onehot = route[:, None] == lax.broadcasted_iota(jnp.int32, (1, experts), 1)
    onehot_low = onehot.astype(BF16)
    below = lax.broadcasted_iota(jnp.int32, (rows, rows), 0) > lax.broadcasted_iota(
        jnp.int32, (rows, rows), 1
    )
    earlier = matmul(below.astype(BF16), onehot_low)
    local_rank = jnp.sum(jnp.where(onehot, earlier, 0.0), 1).astype(jnp.int32)
    target = route * slots_per + local_rank
    half_rows = experts * slots_per
    columns = lax.broadcasted_iota(jnp.int32, (1, half_rows), 1)
    placer = (columns == target[:, None]).astype(BF16)
    counts = jnp.sum(onehot_low.astype(F32), 0).astype(BF16)
    counts_pair = jnp.concatenate(both(counts, swap(counts)), 0)

    qkv_shard = jnp.stack(
        [part.reshape(shard, half_heads, HEAD) for part in (w_query, w_key, w_value)], 2
    ).reshape(shard, half_heads * triple)
    extra = jnp.concatenate([norm1_gain, norm2_gain, counts_pair], 0)
    extra = jnp.pad(extra[None, :], ((0, 7), (0, half_heads * triple - extra.shape[0])))
    planes = experts // 4
    first_shard, second_shard = lax.optimization_barrier(
        (
            jnp.concatenate([qkv_shard, extra], 0),
            jnp.concatenate([w_ffn_in, w_ffn_out.T, w_attn_out.T], 1),
        )
    )
    second_line = lax.all_gather(
        second_shard,
        "dp",
        axis_index_groups=[[4 * z + k for z in range(planes)] for k in range(4)],
    )
    line_one = gather_line(first_shard)
    weight_rows, extra_row = np.s_[..., :shard, :], np.s_[..., shard, :]
    (first_all, extra_all), (last_all, unused) = gather_third(
        *gather_second(line_one), (weight_rows, extra_row)
    )
    qkv_full = jnp.concatenate([first_all, last_all], -1).reshape(width, half_heads * triple)
    extra_all = extra_all.reshape(experts, -1)
    gain_one = extra_all[:, :shard].reshape(width).astype(F32)
    gain_two = extra_all[:, shard : 2 * shard].reshape(width).astype(F32)
    counts_all = extra_all[:, 2 * shard : 2 * shard + 2 * experts].reshape(experts, 2, experts)

    pair_tokens = with_other(tokens).astype(F32)
    normed_one, hat_pair, inv_pair = norm_forward(pair_tokens, gain_one)
    inputs, hat_one, inv_one = pair_tokens[:rows], hat_pair[:rows], inv_pair[:rows]
    rows_one = normed_one.astype(BF16)
    other_t = lax.dot_general(
        qkv_full, rows_one[rows:], (((0,), (1,)), ((), ())), preferred_element_type=F32
    ).astype(BF16)
    own_t = lax.dot_general(
        qkv_full, rows_one[:rows], (((0,), (1,)), ((), ())), preferred_element_type=F32
    ).astype(BF16)
    qkv_t = jnp.concatenate(both(own_t, swap(other_t)), 0).reshape(heads, triple, rows)
    qkv_t, second_line, late_grad = lax.optimization_barrier((qkv_t, second_line, grad_out))
    sent_grad = matmul_tn(placer, late_grad).astype(BF16).reshape(experts, slots_per, width)
    by_head = lax.all_to_all(qkv_t, "dp", split_axis=0, concat_axis=0, tiled=True)

    by_head, second_line, sent_grad = lax.optimization_barrier((by_head, second_line, sent_grad))
    second_all = lax.all_gather(
        second_line, "dp", axis_index_groups=[[4 * z + k for k in range(4)] for z in range(planes)]
    )
    second_all = second_all.transpose(1, 0, 2, 3).reshape(width, -1)
    attn_half = second_all[:, 2 * hidden :]

    lent = experts // 4
    span = PLEN // rows
    own_blocks = jnp.concatenate([by_head, to_core_zero(by_head[:lent])], 0)
    prompt_kv = jnp.where(core_zero, by_head[:, HEAD:], to_core_one(by_head[:, HEAD:]))
    places = jnp.arange(experts + lent, dtype=jnp.int32)
    follows = cont_prompt * span
    plan_zero = jnp.stack(
        [
            places,
            jnp.where(places < experts, places % span, span),
            jnp.concatenate([places[:experts] // span * span, follows[:lent]], 0),
            jnp.ones_like(places),
        ]
    )
    plan_one = jnp.stack(
        [
            jnp.minimum(places + lent, experts - 1),
            jnp.full_like(places, span),
            jnp.concatenate([follows[lent:], jnp.zeros((2 * lent,), jnp.int32)], 0),
            (places < experts - lent).astype(jnp.int32),
        ]
    )
    plan = jnp.where(core_zero, plan_zero, plan_one)
    attn_blocks, log_sums = attn_forward(plan, own_blocks, prompt_kv)
    lent_back = to_core_one(attn_blocks[experts:])
    attn_own = jnp.concatenate(
        [jnp.where(core_zero, attn_blocks[:lent], lent_back), attn_blocks[lent:experts]], 0
    )
    attn_t = lax.all_to_all(attn_own, "dp", split_axis=0, concat_axis=0, tiled=True).reshape(
        width, rows
    )

    half_width = width // 2
    own_heads, other_heads = both(attn_t[:half_width], attn_t[half_width:])
    attn_other = swap(attn_half)
    hidden_one = (
        inputs
        + lax.dot_general(
            own_heads, attn_half, (((0,), (1,)), ((), ())), preferred_element_type=F32
        )
        + lax.dot_general(
            other_heads, attn_other, (((0,), (1,)), ((), ())), preferred_element_type=F32
        )
    )
    normed_two, hat_two, inv_two = norm_forward(hidden_one, gain_two)
    normed_two = normed_two.astype(BF16)
    rows_two, ffn_act, ffn_slope, ffn_own, ffn_other = mlp_forward(
        [(normed_two, swap(normed_two))],
        second_all,
        second_all,
        hidden,
        rows,
        transposed=True,
        columns=(0, 1),
    )
    hidden_two = hidden_one + ffn_own.astype(F32) + swap(ffn_other).astype(F32)

    sent_rows = (
        matmul_tn(placer, hidden_two.astype(BF16)).astype(BF16).reshape(experts, slots_per, width)
    )
    sent_rows, counts_all = lax.optimization_barrier((sent_rows, counts_all))
    mine = jnp.sum(
        jnp.where(lax.broadcasted_iota(jnp.int32, (1, 1, experts), 2) == dp_index, counts_all.astype(F32), 0.0),
        2,
    )
    per_chip = jnp.sum(mine, 1)
    chip_before = jnp.sum(
        jnp.where(
            lax.broadcasted_iota(jnp.int32, (experts, experts), 1)
            < lax.broadcasted_iota(jnp.int32, (experts, experts), 0),
            per_chip[None, :],
            0.0,
        ),
        1,
    )
    starts = both(chip_before, chip_before + mine[:, 0])
    slot_at = lax.broadcasted_iota(jnp.int32, (1, slots_per), 1).astype(F32)
    kept = jnp.concatenate(
        [(start[:, None] + slot_at < capacity).reshape(-1, 1) for start in starts], 0
    )
    own_rows, sent_grad, kept = lax.optimization_barrier((to_experts(sent_rows), sent_grad, kept))
    own_rows = own_rows.reshape(half_rows, width)
    grad_own = to_experts(sent_grad).reshape(half_rows, width)
    centre = centroids[0]
    length = half_rows // 2
    expert_rows, act_a, slope_a, own_a, other_a, gate_column = mlp_forward(
        [(own_rows, swap(own_rows))],
        expert_in_a[0],
        expert_out_a[0],
        hidden,
        length,
        centre=centroids,
    )
    from_a = (swap(other_a), swap(own_a))
    middle, act_b, slope_b, own_b, other_b = mlp_forward(
        [expert_rows, (own_a, other_a), from_a], expert_in_b[0], expert_out_b[0], hidden, length
    )
    own_b, grad_own = lax.optimization_barrier((own_b, grad_own))
    branch_half = (
        own_a.astype(F32) + from_a[0].astype(F32) + own_b.astype(F32) + swap(other_b).astype(F32)
    )
    gate_value = gate_column[:, 0]
    gate_half = gate_value[:half_rows]
    returned = (
        jnp.where(kept[:half_rows], gate_half[:, None] * branch_half, 0.0)
        .astype(BF16)
        .reshape(experts, slots_per, width)
    )
    came_back = to_experts(returned).reshape(half_rows, width)

    kept_half = kept[:half_rows, 0]
    grad_logit_half = jnp.where(
        kept_half,
        jnp.sum(grad_own.astype(F32) * branch_half, 1) * gate_half * (1.0 - gate_half),
        0.0,
    )
    centre_part = matmul(grad_logit_half, own_rows.astype(F32))
    kept_gate = jnp.where(kept, gate_column, 0.0)
    grad_pair = (grad_own, swap(grad_own))
    grad_b, grad_pre_b, own_m, other_m = mlp_backward(
        [grad_pair], expert_out_b[0], expert_in_b[0], slope_b, length, factor=kept_gate
    )
    from_m = (swap(other_m), swap(own_m))
    grad_a, grad_pre_a, own_x, other_x = mlp_backward(
        [grad_pair, (own_m, other_m), from_m],
        expert_out_a[0],
        expert_in_a[0],
        slope_a,
        length,
        factor=kept_gate,
    )
    grad_rows = (
        own_x.astype(F32)
        + swap(other_x).astype(F32)
        + own_m.astype(F32)
        + from_m[0].astype(F32)
        + grad_logit_half[:, None] * centre.astype(F32)[None, :]
    )
    grad_rows, came_back, act_a, grad_a, expert_rows, grad_pre_a = lax.optimization_barrier(
        (grad_rows.astype(BF16), came_back, act_a, grad_a, expert_rows, grad_pre_a)
    )
    grad_out_a = matmul_tn(act_a, grad_a)
    grad_in_a = matmul_tn(expert_rows, grad_pre_a)
    output = hidden_two + matmul(placer, came_back)
    grad_back = to_experts(grad_rows.reshape(experts, slots_per, width))
    grad_back, grad_out_a, grad_in_a = lax.optimization_barrier((grad_back, grad_out_a, grad_in_a))
    grad_back = grad_back.reshape(half_rows, width)
    grad_two = grad_out.astype(F32) + matmul(placer, grad_back)

    grad_down = grad_two.astype(BF16)
    rows_down, grad_ffn_pre, down_own, down_other = mlp_backward(
        [(grad_down, swap(grad_down))],
        second_all,
        second_all,
        ffn_slope,
        rows,
        transposed=False,
        columns=(0, 1),
    )
    grad_norm_two = down_own.astype(F32) + swap(down_other).astype(F32)
    back_two = norm_backward(grad_norm_two, hat_two, inv_two, gain_two)[0]
    grad_one = grad_two + back_two

    grad_branch_one = grad_one.astype(BF16)
    grad_halves = both(
        *(
            lax.dot_general(
                part, grad_branch_one, (((0,), (1,)), ((), ())), preferred_element_type=F32
            ).astype(BF16)
            for part in (attn_half, attn_other)
        )
    )
    grad_attn, rows_down, ffn_act, rows_two, grad_ffn_pre = lax.optimization_barrier(
        (
            jnp.concatenate(grad_halves, 0).reshape(heads, HEAD, rows),
            rows_down,
            ffn_act,
            rows_two,
            grad_ffn_pre,
        )
    )
    grad_by_head = lax.all_to_all(grad_attn, "dp", split_axis=0, concat_axis=0, tiled=True)
    grad_ffn_out_t = matmul_tn(rows_down, ffn_act)
    grad_ffn_in = matmul_tn(rows_two, grad_ffn_pre)
    part_own, part_other = (
        lax.dot_general(
            grad_branch_one, part, (((0,), (1,)), ((), ())), preferred_element_type=F32
        )
        for part in (own_heads, other_heads)
    )
    grad_attn_half = part_own + swap(part_other.astype(BF16)).astype(F32)
    second_part = jnp.concatenate(
        [grad_ffn_in.astype(BF16), grad_ffn_out_t.astype(BF16), grad_attn_half.astype(BF16)], 1
    )
    grad_by_head, second_part = lax.optimization_barrier((grad_by_head, second_part))
    second_sum = lax.psum_scatter(second_part, "dp", scatter_dimension=0, tiled=True).astype(F32)
    grad_blocks = jnp.concatenate([grad_by_head, to_core_zero(grad_by_head[:lent])], 0)
    grad_own_blocks, grad_prompts = attn_backward(
        plan, own_blocks, prompt_kv, grad_blocks, attn_blocks, log_sums
    )
    lent_grad = to_core_one(grad_own_blocks[experts:])
    prompt_sum = grad_prompts.astype(F32) + to_core_zero(grad_prompts).astype(F32)
    prompt_part = jnp.concatenate(
        [
            grad_own_blocks[:experts, :HEAD],
            (grad_own_blocks[:experts, HEAD:].astype(F32) + prompt_sum).astype(BF16),
        ],
        1,
    )
    cont_part = jnp.concatenate([lent_grad, grad_own_blocks[lent:experts]], 0)
    grad_head, act_b, grad_b, middle, grad_pre_b = lax.optimization_barrier(
        (jnp.where(core_zero, prompt_part, cont_part), act_b, grad_b, middle, grad_pre_b)
    )
    grad_qkv = lax.all_to_all(grad_head, "dp", split_axis=0, concat_axis=0, tiled=True)
    grad_out_b = matmul_tn(act_b, grad_b)
    grad_in_b = matmul_tn(middle, grad_pre_b)
    grad_qkv, grad_out_b, grad_in_b = lax.optimization_barrier((grad_qkv, grad_out_b, grad_in_b))
    grad_qkv = grad_qkv.reshape(2, half_heads * triple, rows)
    keep_half, send_half = both(grad_qkv[0], grad_qkv[1])
    grad_qkv_t = jnp.concatenate([keep_half, swap(send_half)], 1)
    grad_qkv_w = lax.dot_general(
        rows_one, grad_qkv_t, (((0,), (1,)), ((), ())), preferred_element_type=F32
    ).astype(BF16)
    by_chip = grad_qkv_w.reshape(experts // 4, 2, 2, shard, half_heads * triple)
    half_columns = half_heads * triple // 2
    qkv_sum = scatter_chips(by_chip[..., :half_columns], by_chip[..., half_columns:])
    grad_norm_one = keep_rows(
        lax.dot_general(
            grad_qkv_t, qkv_full, (((0,), (1,)), ((), ())), preferred_element_type=F32
        )
    )
    back_one = norm_backward(grad_norm_one, hat_one, inv_one, gain_one)[0]
    grad_input = grad_one + back_one
    qkv_sum = qkv_sum.reshape(shard, half_heads, 3, HEAD)
    query_shard, key_shard, value_shard = (
        qkv_sum[:, :, part].reshape(shard, half_heads * HEAD) for part in range(3)
    )

    ffn_in_sum = second_sum[:, :hidden]
    gains = jnp.stack(
        [
            jnp.sum(query_shard * w_query + key_shard * w_key + value_shard * w_value, 1)
            / norm1_gain.astype(F32),
            jnp.sum(ffn_in_sum * w_ffn_in, 1) / norm2_gain.astype(F32),
        ]
    )
    gains = gains + swap(gains)
    centre_grad = centre_part + swap(centre_part)
    return (
        output.astype(BF16),
        grad_input.astype(BF16),
        gains[0],
        query_shard,
        key_shard,
        value_shard,
        second_sum[:, 2 * hidden :].T,
        gains[1],
        ffn_in_sum,
        second_sum[:, hidden : 2 * hidden].T,
        centre_grad[None, :],
        grad_in_a[None],
        grad_out_a[None],
        grad_in_b[None],
        grad_out_b[None],
    )


def solution(mesh):
    body = body_paired if fits_paired(mesh) else body_general
    return jax.shard_map(
        body,
        mesh=mesh,
        in_specs=(
            P(("dp", "tensor"), None),
            P(),
            P(("dp", "tensor"), None),
            P("dp"),
            P("dp", "tensor"),
            P("dp", "tensor"),
            P("dp", "tensor"),
            P("tensor", "dp"),
            P("dp"),
            P("dp", "tensor"),
            P("tensor", "dp"),
            P("dp", None),
            P("dp", None, "tensor"),
            P("dp", "tensor", None),
            P("dp", None, "tensor"),
            P("dp", "tensor", None),
            P(("dp", "tensor"), None),
        ),
        out_specs=(
            P(("dp", "tensor"), None),
            P(("dp", "tensor"), None),
            P("dp"),
            P("dp", "tensor"),
            P("dp", "tensor"),
            P("dp", "tensor"),
            P("tensor", "dp"),
            P("dp"),
            P("dp", "tensor"),
            P("tensor", "dp"),
            P("dp", None),
            P("dp", None, "tensor"),
            P("dp", "tensor", None),
            P("dp", None, "tensor"),
            P("dp", "tensor", None),
        ),
        check_vma=False,
    )
```

```python
import functools

import jax
import jax.numpy as jnp
import numpy as np
from jax import lax
from jax.experimental import pallas as pl
from jax.experimental.pallas import tpu as pltpu
from jax.sharding import PartitionSpec as P

HEAD = 64
PLEN = 4096
CONT = 512


def shortened(value):

    def short(part):
        return part.astype(jnp.bfloat16) if part.dtype == jnp.float32 else part

    return jax.tree.map(short, value)


def carried_in(value, axis, combine, identity):
    peers, place = (lax.axis_size(axis), lax.axis_index(axis))
    everything = lax.all_gather(value, axis)
    start = jnp.broadcast_to(jnp.asarray(identity, value.dtype), value.shape)

    def turn(k, before):
        reached = k < place
        new = combine(before, everything[k])
        return jnp.where(reached, new, before)

    return lax.fori_loop(0, peers, turn, start)


def rows_gather(value):
    return lax.all_gather(value, "tensor", axis=0, tiled=True)


def rows_scatter(value):
    return lax.psum_scatter(
        value.astype(jnp.bfloat16), "tensor", scatter_dimension=0, tiled=True
    ).astype(jnp.float32)


def pair_total(value):
    return jax.tree.map(lambda part: part.astype(jnp.float32), lax.psum(shortened(value), "tensor"))


def to_experts(value):
    return lax.all_to_all(value, "dp", split_axis=0, concat_axis=0, tiled=True)


def matmul(left, right):
    return jnp.dot(left, right, preferred_element_type=jnp.float32)


def matmul_tn(left, right):
    return lax.dot_general(
        left, right, (((0,), (0,)), ((), ())), preferred_element_type=jnp.float32
    )


def matmul_nt(left, right):
    return lax.dot_general(
        left, right, (((1,), (1,)), ((), ())), preferred_element_type=jnp.float32
    )


def norm_forward(hidden, gain):
    mean_row = jnp.mean(hidden, -1, keepdims=True)
    centred = hidden - mean_row
    scale_inv = lax.rsqrt(jnp.mean(centred * centred, -1, keepdims=True) + 1e-05)
    normed = centred * scale_inv
    return (normed * gain, normed, scale_inv)


def norm_backward(grad_m, normed, scale_inv, gain):
    grad_hat = grad_m * gain
    inner = (
        grad_hat
        - jnp.mean(grad_hat, -1, keepdims=True)
        - normed * jnp.mean(grad_hat * normed, -1, keepdims=True)
    )
    return (inner * scale_inv, jnp.sum(grad_m * normed, 0))


def gelu_grad(preact, grad):
    unused, pull = jax.vjp(jax.nn.gelu, preact)
    return pull(grad)[0]


def add_counts(first, second):
    return first + second


def attend(queries, keys, values, allowed, heads):
    scale = HEAD ** (-0.5)

    def head_step(head, carry):
        outputs, log_sums = carry
        query_h = lax.dynamic_slice_in_dim(queries, head * HEAD, HEAD, 1)
        key_h = lax.dynamic_slice_in_dim(keys, head * HEAD, HEAD, 1)
        value_h = lax.dynamic_slice_in_dim(values, head * HEAD, HEAD, 1)
        scores = jnp.where(allowed, matmul_nt(query_h, key_h) * scale, -1e30)
        top_score = jnp.max(scores, 1, keepdims=True)
        expo = jnp.exp(scores - top_score)
        total = jnp.sum(expo, 1, keepdims=True)
        probs = (expo / total).astype(jnp.bfloat16)
        outputs = lax.dynamic_update_slice_in_dim(outputs, matmul(probs, value_h), head * HEAD, 1)
        log_sums = lax.dynamic_update_index_in_dim(
            log_sums, top_score[:, 0] + jnp.log(total[:, 0]), head, 0
        )
        return (outputs, log_sums)

    start_state = (
        jnp.zeros((queries.shape[0], heads * HEAD), jnp.float32),
        jnp.zeros((heads, queries.shape[0]), jnp.float32),
    )
    return lax.fori_loop(0, heads, head_step, start_state)


def attend_back(queries, keys, values, allowed, log_sums, grad_attended, heads):
    scale = HEAD ** (-0.5)

    def head_step(head, carry):
        grad_q, grad_k, grad_v = carry
        query_h = lax.dynamic_slice_in_dim(queries, head * HEAD, HEAD, 1)
        key_h = lax.dynamic_slice_in_dim(keys, head * HEAD, HEAD, 1)
        value_h = lax.dynamic_slice_in_dim(values, head * HEAD, HEAD, 1)
        grad_o = lax.dynamic_slice_in_dim(grad_attended, head * HEAD, HEAD, 1)
        scores = jnp.where(allowed, matmul_nt(query_h, key_h) * scale, -1e30)
        probs = jnp.exp(
            scores - lax.dynamic_index_in_dim(log_sums, head, 0, keepdims=False)[:, None]
        )
        grad_p = matmul_nt(grad_o, value_h)
        grad_s = (probs * (grad_p - jnp.sum(probs * grad_p, 1, keepdims=True))).astype(jnp.bfloat16)
        grad_q = lax.dynamic_update_slice_in_dim(
            grad_q, matmul(grad_s, key_h) * scale, head * HEAD, 1
        )
        grad_k = lax.dynamic_update_slice_in_dim(
            grad_k, matmul_tn(grad_s, query_h) * scale, head * HEAD, 1
        )
        grad_v = lax.dynamic_update_slice_in_dim(
            grad_v, matmul_tn(probs.astype(jnp.bfloat16), grad_o), head * HEAD, 1
        )
        return (grad_q, grad_k, grad_v)

    start_state = (
        jnp.zeros(queries.shape, jnp.float32),
        jnp.zeros(keys.shape, jnp.float32),
        jnp.zeros(values.shape, jnp.float32),
    )
    return lax.fori_loop(0, heads, head_step, start_state)


def add_block(buffer, block, start):
    length = block.shape[0]
    current = lax.dynamic_slice_in_dim(buffer, start, length, 0)
    return lax.dynamic_update_slice_in_dim(buffer, current + block, start, 0)


def body_general(
    tokens,
    cont_prompt,
    routes,
    norm1_gain,
    w_query,
    w_key,
    w_value,
    w_attn_out,
    norm2_gain,
    w_ffn_in,
    w_ffn_out,
    centroids,
    expert_in_a,
    expert_out_a,
    expert_in_b,
    expert_out_b,
    grad_out,
):
    experts = lax.axis_size("dp")
    pair_size = lax.axis_size("tensor")
    dp_index = lax.axis_index("dp")
    tensor_index = lax.axis_index("tensor")
    rows_dev = tokens.shape[0]
    rows_dp = rows_dev * pair_size
    prm_dev = rows_dp - CONT
    pkeys = experts * prm_dev
    heads = w_query.shape[1] // HEAD
    width = tokens.shape[1]
    span = PLEN // prm_dev
    owner_start = dp_index // span * PLEN
    mapped_start = cont_prompt[dp_index] * PLEN
    gain_one, query_full, key_full, value_full, attn_full, gain_two, ffn_in_full, ffn_out_full = (
        lax.all_gather(norm1_gain, "dp", axis=0, tiled=True),
        lax.all_gather(w_query, "dp", axis=0, tiled=True),
        lax.all_gather(w_key, "dp", axis=0, tiled=True),
        lax.all_gather(w_value, "dp", axis=0, tiled=True),
        lax.all_gather(w_attn_out, "dp", axis=1, tiled=True),
        lax.all_gather(norm2_gain, "dp", axis=0, tiled=True),
        lax.all_gather(w_ffn_in, "dp", axis=0, tiled=True),
        lax.all_gather(w_ffn_out, "dp", axis=1, tiled=True),
    )
    inputs = tokens.astype(jnp.float32)
    normed_one, hat_one, inv_one = norm_forward(inputs, gain_one.astype(jnp.float32))
    rows_one = rows_gather(normed_one.astype(jnp.bfloat16))
    queries = matmul(rows_one, query_full).astype(jnp.bfloat16)
    keys_own = matmul(rows_one, key_full).astype(jnp.bfloat16)
    values_own = matmul(rows_one, value_full).astype(jnp.bfloat16)
    prompt_keys, prompt_values = (
        lax.all_gather(keys_own[:prm_dev], "dp", axis=0, tiled=True),
        lax.all_gather(values_own[:prm_dev], "dp", axis=0, tiled=True),
    )
    keys_first = lax.dynamic_slice_in_dim(prompt_keys, owner_start, PLEN, 0)
    values_first = lax.dynamic_slice_in_dim(prompt_values, owner_start, PLEN, 0)
    first_row = lax.broadcasted_iota(jnp.int32, (prm_dev, 1), 0)
    first_column = lax.broadcasted_iota(jnp.int32, (1, PLEN), 1)
    allowed_first = first_column <= dp_index % span * prm_dev + first_row
    keys_second = jnp.concatenate(
        [lax.dynamic_slice_in_dim(prompt_keys, mapped_start, PLEN, 0), keys_own[prm_dev:]], 0
    )
    values_second = jnp.concatenate(
        [lax.dynamic_slice_in_dim(prompt_values, mapped_start, PLEN, 0), values_own[prm_dev:]], 0
    )
    second_row = lax.broadcasted_iota(jnp.int32, (CONT, 1), 0)
    second_column = lax.broadcasted_iota(jnp.int32, (1, PLEN + CONT), 1)
    allowed_second = (second_column < PLEN) | (second_column - PLEN <= second_row)
    attn_first, sums_first = attend(
        queries[:prm_dev], keys_first, values_first, allowed_first, heads
    )
    attn_second, sums_second = attend(
        queries[prm_dev:], keys_second, values_second, allowed_second, heads
    )
    attn_low = jnp.concatenate([attn_first, attn_second], 0).astype(jnp.bfloat16)
    hidden_one = inputs + rows_scatter(matmul(attn_low, attn_full))
    normed_two, hat_two, inv_two = norm_forward(hidden_one, gain_two.astype(jnp.float32))
    rows_two = rows_gather(normed_two.astype(jnp.bfloat16))
    ffn_pre = matmul(rows_two, ffn_in_full)
    ffn_act = jax.nn.gelu(ffn_pre).astype(jnp.bfloat16)
    hidden_two = hidden_one + rows_scatter(matmul(ffn_act, ffn_out_full))
    route = routes[:, 0]
    slots_per = max(2, (3 * rows_dev + 2 * experts - 1) // (2 * experts))
    capacity = 5 * rows_dp // 4
    expert_ids = lax.broadcasted_iota(jnp.int32, (1, experts), 1)
    onehot = (route[:, None] == expert_ids).astype(jnp.int32)
    offsets = carried_in(
        jnp.sum(onehot, 0), ("dp", "tensor"), add_counts, jnp.zeros((experts,), jnp.int32)
    )
    local_rank = jnp.sum((jnp.cumsum(onehot, 0) - 1) * onehot, 1)
    global_slot = local_rank + jnp.sum(onehot * offsets[None, :], 1)
    kept = global_slot < capacity
    target = route * slots_per + local_rank
    columns = lax.broadcasted_iota(jnp.int32, (1, experts * slots_per), 1)
    placer = ((columns == target[:, None]) & kept[:, None]).astype(jnp.bfloat16)
    sent_rows = (
        matmul_tn(placer, hidden_two.astype(jnp.bfloat16))
        .astype(jnp.bfloat16)
        .reshape(experts, slots_per, width)
    )
    expert_rows = rows_gather(to_experts(sent_rows)).reshape(-1, width)
    centre = centroids[0]
    gate_value = jax.nn.sigmoid(matmul(expert_rows, centre))
    pre_a = matmul(expert_rows, expert_in_a[0])
    act_a = jax.nn.gelu(pre_a).astype(jnp.bfloat16)
    branch_a = pair_total(matmul(act_a, expert_out_a[0]))
    middle = (expert_rows.astype(jnp.float32) + branch_a).astype(jnp.bfloat16)
    pre_b = matmul(middle, expert_in_b[0])
    act_b = jax.nn.gelu(pre_b).astype(jnp.bfloat16)
    branch_b = rows_scatter(matmul(act_b, expert_out_b[0]))
    half_rows = expert_rows.shape[0] // pair_size
    start_row = tensor_index * half_rows
    branch_half = lax.dynamic_slice_in_dim(branch_a, start_row, half_rows, 0) + branch_b
    gate_half = lax.dynamic_slice_in_dim(gate_value, start_row, half_rows, 0)
    returned = (
        (gate_half[:, None] * branch_half).astype(jnp.bfloat16).reshape(experts, slots_per, width)
    )
    came_back = to_experts(returned).reshape(experts * slots_per, width)
    output = hidden_two + matmul(placer, came_back)
    cotangent = grad_out.astype(jnp.float32)
    sent_grad = matmul_tn(placer, grad_out).astype(jnp.bfloat16).reshape(experts, slots_per, width)
    grad_half = to_experts(sent_grad).reshape(half_rows, width)
    grad_returned = rows_gather(grad_half).astype(jnp.float32)
    grad_gate_half = jnp.sum(grad_half.astype(jnp.float32) * branch_half, 1)
    grad_logit_half = grad_gate_half * gate_half * (1.0 - gate_half)
    rows_half = lax.dynamic_slice_in_dim(expert_rows, start_row, half_rows, 0)
    centre_part = matmul(grad_logit_half, rows_half.astype(jnp.float32))
    grad_branch = gate_value[:, None] * grad_returned
    grad_b = grad_branch.astype(jnp.bfloat16)
    grad_pre_b = gelu_grad(pre_b, matmul_nt(grad_b, expert_out_b[0])).astype(jnp.bfloat16)
    grad_out_b = matmul_tn(act_b, grad_b)
    grad_in_b = matmul_tn(middle, grad_pre_b)
    grad_middle = pair_total(matmul_nt(grad_pre_b, expert_in_b[0]))
    grad_a = (grad_branch + grad_middle).astype(jnp.bfloat16)
    grad_pre_a = gelu_grad(pre_a, matmul_nt(grad_a, expert_out_a[0])).astype(jnp.bfloat16)
    grad_out_a = matmul_tn(act_a, grad_a)
    grad_in_a = matmul_tn(expert_rows, grad_pre_a)
    grad_rows = (
        rows_scatter(matmul_nt(grad_pre_a, expert_in_a[0]))
        + lax.dynamic_slice_in_dim(grad_middle, start_row, half_rows, 0)
        + grad_logit_half[:, None] * centre.astype(jnp.float32)[None, :]
    )
    grad_back = to_experts(
        grad_rows.astype(jnp.bfloat16).reshape(experts, slots_per, width)
    ).reshape(experts * slots_per, width)
    grad_two = cotangent + matmul(placer, grad_back)
    gain_one, query_full, key_full, value_full, attn_full, gain_two, ffn_in_full, ffn_out_full = (
        lax.all_gather(norm1_gain, "dp", axis=0, tiled=True),
        lax.all_gather(w_query, "dp", axis=0, tiled=True),
        lax.all_gather(w_key, "dp", axis=0, tiled=True),
        lax.all_gather(w_value, "dp", axis=0, tiled=True),
        lax.all_gather(w_attn_out, "dp", axis=1, tiled=True),
        lax.all_gather(norm2_gain, "dp", axis=0, tiled=True),
        lax.all_gather(w_ffn_in, "dp", axis=0, tiled=True),
        lax.all_gather(w_ffn_out, "dp", axis=1, tiled=True),
    )
    rows_down = rows_gather(grad_two.astype(jnp.bfloat16))
    grad_ffn_pre = gelu_grad(ffn_pre, matmul_nt(rows_down, ffn_out_full)).astype(jnp.bfloat16)
    grad_ffn_out = matmul_tn(ffn_act, rows_down)
    grad_ffn_in = matmul_tn(rows_two, grad_ffn_pre)
    grad_norm_two = rows_scatter(matmul_nt(grad_ffn_pre, ffn_in_full))
    back_two, grad_gain_two = norm_backward(
        grad_norm_two, hat_two, inv_two, gain_two.astype(jnp.float32)
    )
    grad_one = grad_two + back_two
    rows_attn = rows_gather(grad_one.astype(jnp.bfloat16))
    grad_attn_out = matmul_tn(attn_low, rows_attn)
    grad_attended = matmul_nt(rows_attn, attn_full).astype(jnp.bfloat16)
    grad_q_first, grad_k_first, grad_v_first = attend_back(
        queries[:prm_dev],
        keys_first,
        values_first,
        allowed_first,
        sums_first,
        grad_attended[:prm_dev],
        heads,
    )
    grad_q_second, grad_k_second, grad_v_second = attend_back(
        queries[prm_dev:],
        keys_second,
        values_second,
        allowed_second,
        sums_second,
        grad_attended[prm_dev:],
        heads,
    )
    local_width = keys_own.shape[1]
    buffer_k = jnp.zeros((pkeys, local_width), jnp.float32)
    buffer_v = jnp.zeros((pkeys, local_width), jnp.float32)
    buffer_k = add_block(
        add_block(buffer_k, grad_k_first, owner_start), grad_k_second[:PLEN], mapped_start
    )
    buffer_v = add_block(
        add_block(buffer_v, grad_v_first, owner_start), grad_v_second[:PLEN], mapped_start
    )
    prompt_grad_k, prompt_grad_v = (
        lax.psum_scatter(buffer_k, "dp", scatter_dimension=0, tiled=True),
        lax.psum_scatter(buffer_v, "dp", scatter_dimension=0, tiled=True),
    )
    grad_keys = jnp.concatenate([prompt_grad_k, grad_k_second[PLEN:]], 0).astype(jnp.bfloat16)
    grad_values = jnp.concatenate([prompt_grad_v, grad_v_second[PLEN:]], 0).astype(jnp.bfloat16)
    grad_queries = jnp.concatenate([grad_q_first, grad_q_second], 0).astype(jnp.bfloat16)
    grad_query = matmul_tn(rows_one, grad_queries)
    grad_key = matmul_tn(rows_one, grad_keys)
    grad_value = matmul_tn(rows_one, grad_values)
    grad_norm_one = rows_scatter(
        matmul_nt(grad_queries, query_full)
        + matmul_nt(grad_keys, key_full)
        + matmul_nt(grad_values, value_full)
    )
    back_one, grad_gain_one = norm_backward(
        grad_norm_one, hat_one, inv_one, gain_one.astype(jnp.float32)
    )
    grad_input = grad_one + back_one
    (
        gain_one_part,
        query_shard,
        key_shard,
        value_shard,
        attn_shard,
        gain_two_part,
        ffn_in_shard,
        ffn_out_shard,
    ) = (
        lax.psum_scatter(grad_gain_one, "dp", scatter_dimension=0, tiled=True),
        lax.psum_scatter(grad_query, "dp", scatter_dimension=0, tiled=True),
        lax.psum_scatter(grad_key, "dp", scatter_dimension=0, tiled=True),
        lax.psum_scatter(grad_value, "dp", scatter_dimension=0, tiled=True),
        lax.psum_scatter(grad_attn_out, "dp", scatter_dimension=1, tiled=True),
        lax.psum_scatter(grad_gain_two, "dp", scatter_dimension=0, tiled=True),
        lax.psum_scatter(grad_ffn_in, "dp", scatter_dimension=0, tiled=True),
        lax.psum_scatter(grad_ffn_out, "dp", scatter_dimension=1, tiled=True),
    )
    gain_one_shard, gain_two_shard, centre_grad = pair_total(
        (gain_one_part, gain_two_part, centre_part)
    )
    return (
        output.astype(jnp.bfloat16),
        grad_input.astype(jnp.bfloat16),
        gain_one_shard,
        query_shard,
        key_shard,
        value_shard,
        attn_shard,
        gain_two_shard,
        ffn_in_shard,
        ffn_out_shard,
        centre_grad[None, :],
        grad_in_a[None],
        grad_out_a[None],
        grad_in_b[None],
        grad_out_b[None],
    )


LOG2E = 1.4426950408889634
GELU_A = 0.7978845608028654
GELU_B = 0.044715
BF16 = jnp.bfloat16
F32 = jnp.float32


def dot_tt(left, right):
    return lax.dot_general(left, right, (((0,), (0,)), ((), ())), preferred_element_type=F32)


def beside(blocks, at, count, start, stop):
    return jnp.concatenate([blocks[at + j, start:stop, :] for j in range(count)], 1)


def in_groups(sizes, first, count, take, carry):
    for size in sizes:
        groups = count // size
        step = take(size)
        carry = lax.fori_loop(
            0, groups, lambda k, value, at=first, n=size, f=step: f(at + k * n, value), carry
        )
        first, count = first + groups * size, count - groups * size
    return carry


def attn_fwd_kernel(plan, own, prompts, out, log_sums, values, *, head, factor):
    step_id = pl.program_id(0)
    block, full, first = plan[0, step_id], plan[1, step_id], plan[2, step_id]

    def with_ones(value):
        return jnp.concatenate([value.T, jnp.ones((value.shape[1], head), BF16)], 1)

    @pl.when(step_id == 0)
    def _():
        def turn(k, carry):
            values[k] = with_ones(prompts[k, head : 2 * head, :])
            return carry

        lax.fori_loop(0, prompts.shape[0], turn, 0)

    @pl.when(plan[3, step_id] > 0)
    def _():
        query = own[block, 0:head, :].T
        scores = matmul(query, own[block, head : 2 * head, :])
        query_at = lax.broadcasted_iota(jnp.int32, scores.shape, 0)
        key_at = lax.broadcasted_iota(jnp.int32, scores.shape, 1)
        scores = jnp.where(key_at <= query_at, scores, -1e30)
        top = jnp.max(scores, 1, keepdims=True) * factor
        expo = jnp.exp2(scores * factor - top)
        result = matmul(expo.astype(BF16), with_ones(own[block, 2 * head : 3 * head, :]))

        def take(count):
            def step(at, carry):
                before, result = carry
                scores = matmul(query, beside(prompts, at, count, 0, head))
                top = jnp.maximum(before, jnp.max(scores, 1, keepdims=True) * factor)
                expo = jnp.exp2(scores * factor - top).astype(BF16)
                rows = jnp.concatenate([values[at + j] for j in range(count)], 0)
                return top, result * jnp.exp2(before - top) + matmul(expo, rows)

            return step

        top, result = in_groups((4, 2, 1), first, full, take, (top, result))
        result = result.T
        total = result[head : head + 1]
        out[block] = (result[:head] / total).astype(BF16)
        top = jnp.broadcast_to(top, (top.shape[0], 128)).T[0:1]
        log_sums[block] = top + jnp.log2(total)


def attn_bwd_kernel(
    plan, own, prompts, grad, out, log_sums, grad_own, grad_prompts, sum_k, sum_v, *, head, factor, scale
):
    step_id = pl.program_id(0)
    block, full, first = plan[0, step_id], plan[1, step_id], plan[2, step_id]

    @pl.when(step_id == 0)
    def _():
        sum_k[...] = jnp.zeros_like(sum_k)
        sum_v[...] = jnp.zeros_like(sum_v)

    @pl.when(plan[3, step_id] > 0)
    def _():
        query_t, grad_t, log_sum = own[block, 0:head, :], grad[block], log_sums[block]
        inner = jnp.sum(grad_t.astype(F32) * out[block].astype(F32), 0, keepdims=True)
        query, grad_o = query_t.T, grad_t.T

        def tile(key, value, diagonal):
            probs = jnp.exp2(dot_tt(key, query_t) * factor - log_sum)
            if diagonal:
                key_at = lax.broadcasted_iota(jnp.int32, probs.shape, 0)
                query_at = lax.broadcasted_iota(jnp.int32, probs.shape, 1)
                probs = jnp.where(key_at <= query_at, probs, 0.0)
            grad_s = (probs * (dot_tt(value, grad_t) - inner)).astype(BF16)
            return matmul(grad_s, query), matmul(probs.astype(BF16), grad_o), matmul(key, grad_s)

        grad_k, grad_v, grad_q = tile(
            own[block, head : 2 * head, :], own[block, 2 * head : 3 * head, :], True
        )
        grad_own[block, head : 2 * head, :] = (grad_k * scale).T.astype(BF16)
        grad_own[block, 2 * head : 3 * head, :] = grad_v.T.astype(BF16)

        def take(count):
            def step(at, grad_q):
                more_k, more_v, more_q = tile(
                    beside(prompts, at, count, 0, head),
                    beside(prompts, at, count, head, 2 * head),
                    False,
                )
                length = more_k.shape[0] // count
                for j in range(count):
                    sum_k[at + j] += more_k[j * length : (j + 1) * length]
                    sum_v[at + j] += more_v[j * length : (j + 1) * length]
                return grad_q + more_q

            return step

        grad_q = in_groups((4, 2, 1), first, full, take, grad_q)
        grad_own[block, 0:head, :] = (grad_q * scale).astype(BF16)

    @pl.when(step_id == pl.num_programs(0) - 1)
    def _():
        def finish(k, carry):
            grad_prompts[k, 0:head, :] = (sum_k[k] * scale).T.astype(BF16)
            grad_prompts[k, head : 2 * head, :] = sum_v[k].T.astype(BF16)
            return carry

        lax.fori_loop(0, sum_k.shape[0], finish, 0)


def attn_forward(plan, own, prompts):
    blocks, triple, length = own.shape
    head = triple // 3
    whole = pl.BlockSpec(memory_space=pltpu.VMEM)
    return pl.pallas_call(
        functools.partial(attn_fwd_kernel, head=head, factor=head**-0.5 * LOG2E),
        grid_spec=pltpu.PrefetchScalarGridSpec(
            num_scalar_prefetch=1,
            grid=(plan.shape[1],),
            in_specs=[whole, whole],
            out_specs=[whole, whole],
            scratch_shapes=[pltpu.VMEM((prompts.shape[0], length, 2 * head), BF16)],
        ),
        out_shape=[
            jax.ShapeDtypeStruct((blocks, head, length), BF16),
            jax.ShapeDtypeStruct((blocks, 1, length), F32),
        ],
        compiler_params=pltpu.CompilerParams(vmem_limit_bytes=40 * 2**20),
        cost_estimate=pl.CostEstimate(
            flops=100 * length * length * 256 * 4,
            bytes_accessed=8 * 2**20,
            transcendentals=100 * length * length,
        ),
        name="attn_fwd",
    )(plan, own, prompts)


def attn_backward(plan, own, prompts, grad, out, log_sums):
    blocks, triple, length = own.shape
    head = triple // 3
    whole = pl.BlockSpec(memory_space=pltpu.VMEM)
    return pl.pallas_call(
        functools.partial(
            attn_bwd_kernel, head=head, factor=head**-0.5 * LOG2E, scale=head**-0.5
        ),
        grid_spec=pltpu.PrefetchScalarGridSpec(
            num_scalar_prefetch=1,
            grid=(plan.shape[1],),
            in_specs=[whole] * 5,
            out_specs=[whole, whole],
            scratch_shapes=[pltpu.VMEM((prompts.shape[0], length, head), F32)] * 2,
        ),
        out_shape=[
            jax.ShapeDtypeStruct(own.shape, BF16),
            jax.ShapeDtypeStruct(prompts.shape, BF16),
        ],
        compiler_params=pltpu.CompilerParams(vmem_limit_bytes=48 * 2**20),
        cost_estimate=pl.CostEstimate(
            flops=100 * length * length * 256 * 10,
            bytes_accessed=16 * 2**20,
            transcendentals=100 * length * length,
        ),
        name="attn_bwd",
    )(plan, own, prompts, grad, out, log_sums)


def swap(value):
    return lax.ppermute(value, "tensor", [(0, 1), (1, 0)])


def to_core_one(value):
    return lax.ppermute(value, "tensor", [(0, 1)])


def to_core_zero(value):
    return lax.ppermute(value, "tensor", [(1, 0)])


def with_other(value):
    return jnp.concatenate([value, swap(value)], 0)


def keep_rows(value):
    half = value.shape[0] // 2
    return value[:half].astype(F32) + swap(value[half:].astype(BF16)).astype(F32)


def gelu_pair(preact):
    square = preact * preact
    gate = 0.5 + 0.5 * jnp.tanh(preact * (GELU_A + GELU_A * GELU_B * square))
    act = preact * gate
    slope = gate + act * (1.0 - gate) * (2.0 * GELU_A + 6.0 * GELU_A * GELU_B * square)
    return act.astype(BF16), slope.astype(BF16)


def by_halves(run):
    early = pl.program_id(0) < pl.num_programs(0) // 2
    pl.when(early)(functools.partial(run, 0))
    pl.when(jnp.logical_not(early))(functools.partial(run, 1))


def take_terms(refs, kinds, half):
    values, at = [], 0
    for paired in kinds:
        values.append(refs[at + half * paired][...])
        at += 1 + paired
    return values, refs[at:]


def mlp_kernel(*refs, kinds, transposed, gated):
    def run(half):
        terms, rest = take_terms(refs, kinds, half)
        rows = terms[0]
        if len(terms) > 1:
            total = rows.astype(F32)
            for term in terms[1:]:
                total = total + term.astype(F32)
            rows = total.astype(BF16)
        if gated:
            centre, rest = rest[0], rest[1:]
            logit = jnp.sum(rows.astype(F32) * centre[...].astype(F32), 1, keepdims=True)
            rest[-1][...] = 1.0 / (1.0 + jnp.exp(-logit))
        w_in, w_out, kept_rows, kept_act, kept_slope, *results = rest[:7]
        kept_rows[...] = rows
        act, slope = gelu_pair(matmul(rows, w_in[...]))
        kept_act[...] = act
        kept_slope[...] = slope
        product = matmul_nt if transposed else matmul
        results[half][...] = product(act, w_out[...]).astype(BF16)

    by_halves(run)


def mlp_back_kernel(*refs, kinds, transposed, scaled):
    def run(half):
        factor, rest = (refs[0], refs[1:]) if scaled else (None, refs)
        terms, rest = take_terms(rest, kinds, half)
        grad = terms[0]
        if scaled:
            total = factor[...] * grad.astype(F32)
            for term in terms[1:]:
                total = total + term.astype(F32)
            grad = total.astype(BF16)
        w_out, w_in, slope, kept_grad, kept_pre, *results = rest
        kept_grad[...] = grad
        grad = (matmul_nt if transposed else matmul)(grad, w_out[...])
        grad_pre = (grad * slope[...].astype(F32)).astype(BF16)
        kept_pre[...] = grad_pre
        results[half][...] = matmul_nt(grad_pre, w_in[...]).astype(BF16)

    by_halves(run)


def mlp_blocks(terms, length):
    paired = [isinstance(term, tuple) for term in terms]
    arrays = [part for term in terms for part in (term if isinstance(term, tuple) else (term,))]
    half = max(part.shape[0] // length // (1 + (not pair)) for term, pair in zip(terms, paired) for part in (term if pair else (term,)))
    width = arrays[0].shape[1]
    block = pl.BlockSpec((length, width), lambda m: (m, 0))
    halves = [
        pl.BlockSpec((length, width), lambda m: (jnp.minimum(m, half - 1), 0)),
        pl.BlockSpec((length, width), lambda m: (jnp.maximum(m - half, 0), 0)),
    ]
    specs = [spec for pair in paired for spec in (halves if pair else [block])]
    return tuple(paired), arrays, specs, block, halves, 2 * half


def mlp_forward(terms, w_in, w_out, hidden, length, transposed=False, columns=(0, 0), centre=None):
    kinds, arrays, specs, block, halves, steps = mlp_blocks(terms, length)
    rows, width = steps * length, arrays[0].shape[1]
    hidden_block = pl.BlockSpec((length, hidden), lambda m: (m, 0))
    once = dict(pipeline_mode=pl.Buffered(1))
    in_block = pl.BlockSpec((width, hidden), lambda m: (0, columns[0]), **once)
    out_block = (
        pl.BlockSpec((width, hidden), lambda m: (0, columns[1]), **once)
        if transposed
        else pl.BlockSpec((hidden, width), lambda m: (0, 0), **once)
    )
    gated = centre is not None
    return pl.pallas_call(
        functools.partial(mlp_kernel, kinds=kinds, transposed=transposed, gated=gated),
        grid=(steps,),
        in_specs=specs + [pl.BlockSpec((1, width), lambda m: (0, 0))] * gated + [in_block, out_block],
        out_specs=[block, hidden_block, hidden_block]
        + halves
        + [pl.BlockSpec((length, 1), lambda m: (m, 0))] * gated,
        out_shape=[jax.ShapeDtypeStruct((rows, width), BF16)]
        + [jax.ShapeDtypeStruct((rows, hidden), BF16)] * 2
        + [jax.ShapeDtypeStruct((rows // 2, width), BF16)] * 2
        + [jax.ShapeDtypeStruct((rows, 1), F32)] * gated,
        compiler_params=pltpu.CompilerParams(vmem_limit_bytes=54 * 2**20),
        cost_estimate=pl.CostEstimate(
            flops=rows * width * hidden,
            bytes_accessed=width * hidden + rows * hidden + rows * width,
            transcendentals=0,
        ),
        name="mlp_fwd",
    )(*arrays, *([centre] * gated), w_in, w_out)


def mlp_backward(terms, w_out, w_in, slope, length, transposed=True, columns=(0, 0), factor=None):
    kinds, arrays, specs, block, halves, steps = mlp_blocks(terms, length)
    rows, width = steps * length, arrays[0].shape[1]
    hidden = slope.shape[1]
    hidden_block = pl.BlockSpec((length, hidden), lambda m: (m, 0))
    once = dict(pipeline_mode=pl.Buffered(1))
    out_block = (
        pl.BlockSpec((hidden, width), lambda m: (0, 0), **once)
        if transposed
        else pl.BlockSpec((width, hidden), lambda m: (0, columns[1]), **once)
    )
    in_block = pl.BlockSpec((width, hidden), lambda m: (0, columns[0]), **once)
    scaled = factor is not None
    return pl.pallas_call(
        functools.partial(mlp_back_kernel, kinds=kinds, transposed=transposed, scaled=scaled),
        grid=(steps,),
        in_specs=[pl.BlockSpec((length, 1), lambda m: (m, 0))] * scaled
        + specs
        + [out_block, in_block, hidden_block],
        out_specs=[block, hidden_block] + halves,
        out_shape=[
            jax.ShapeDtypeStruct((rows, width), BF16),
            jax.ShapeDtypeStruct((rows, hidden), BF16),
        ]
        + [jax.ShapeDtypeStruct((rows // 2, width), BF16)] * 2,
        compiler_params=pltpu.CompilerParams(vmem_limit_bytes=54 * 2**20),
        cost_estimate=pl.CostEstimate(
            flops=4 * rows * width * hidden,
            bytes_accessed=4 * width * hidden + 4 * rows * hidden + 4 * rows * width,
            transcendentals=0,
        ),
        name="mlp_bwd",
    )(*([factor] * scaled), *arrays, w_out, w_in, slope)


def from_bit(value, bit):
    return lax.ppermute(value, "dp", [(i, i ^ bit) for i in range(lax.axis_size("dp"))])


def chip_place():
    place = lax.axis_index("dp")
    return place // 4, place // 2 % 2, place % 2


def ordered(bit, own, other, axis):
    return jnp.where(
        bit == 0, jnp.stack([own, other], axis), jnp.stack([other, own], axis)
    )


def gather_line(value):
    planes = lax.axis_size("dp") // 4
    z = chip_place()[0]
    blocks = jnp.stack([value] + [from_bit(value, 4 * k) for k in range(1, planes)])
    return jnp.stack(
        [lax.dynamic_index_in_dim(blocks, z ^ k, 0, keepdims=False) for k in range(planes)]
    )


def gather_second(line):
    half = line.shape[-1] // 2
    y, x = chip_place()[1:]
    first, second = line[..., :half], line[..., half:]
    first = ordered(y, first, from_bit(first, 2), 1)
    second = ordered(x, second, from_bit(second, 1), 1)
    return first, second


def gather_third(first, second, cuts):
    y, x = chip_place()[1:]
    first_other, second_other = from_bit(first, 1), from_bit(second, 2)
    return (
        [ordered(x, first[at], first_other[at], 2) for at in cuts],
        [ordered(y, second[at], second_other[at], 1) for at in cuts],
    )


def halve(value, bit, axis, partner):
    lower = lax.index_in_dim(value, 0, axis, keepdims=False)
    upper = lax.index_in_dim(value, 1, axis, keepdims=False)
    keep, send = jnp.where(bit == 0, lower, upper), jnp.where(bit == 0, upper, lower)
    return keep.astype(F32) + from_bit(send, partner).astype(F32)


def scatter_chips(first, second):
    planes = first.shape[0]
    z, y, x = chip_place()
    first = halve(first, x, 2, 1).astype(BF16)
    second = halve(second, y, 1, 2).astype(BF16)
    line = jnp.concatenate([halve(first, y, 1, 2), halve(second, x, 1, 1)], -1).astype(BF16)
    total = lax.dynamic_index_in_dim(line, z, 0, keepdims=False).astype(F32)
    for k in range(1, planes):
        part = lax.dynamic_index_in_dim(line, z ^ k, 0, keepdims=False)
        total = total + from_bit(part, 4 * k).astype(F32)
    return total


def fits_paired(mesh):
    return mesh.shape["tensor"] == 2 and mesh.shape["dp"] == 16


def body_paired(
    tokens,
    cont_prompt,
    routes,
    norm1_gain,
    w_query,
    w_key,
    w_value,
    w_attn_out,
    norm2_gain,
    w_ffn_in,
    w_ffn_out,
    centroids,
    expert_in_a,
    expert_out_a,
    expert_in_b,
    expert_out_b,
    grad_out,
):
    experts = lax.axis_size("dp")
    dp_index = lax.axis_index("dp")
    core_zero = lax.axis_index("tensor") == 0
    rows, width = tokens.shape
    rows_dp = 2 * rows
    shard = w_query.shape[0]
    half_heads = w_query.shape[1] // HEAD
    hidden = w_ffn_in.shape[1]
    assert expert_in_a.shape[2] == hidden
    triple = 3 * HEAD
    heads = 2 * half_heads
    both = lambda lower, upper: (jnp.where(core_zero, lower, upper), jnp.where(core_zero, upper, lower))

    route = routes[:, 0]
    slots_per = max(2, (3 * rows + 2 * experts - 1) // (2 * experts))
    capacity = 5 * rows_dp // 4
    onehot = route[:, None] == lax.broadcasted_iota(jnp.int32, (1, experts), 1)
    onehot_low = onehot.astype(BF16)
    below = lax.broadcasted_iota(jnp.int32, (rows, rows), 0) > lax.broadcasted_iota(
        jnp.int32, (rows, rows), 1
    )
    earlier = matmul(below.astype(BF16), onehot_low)
    local_rank = jnp.sum(jnp.where(onehot, earlier, 0.0), 1).astype(jnp.int32)
    target = route * slots_per + local_rank
    half_rows = experts * slots_per
    columns = lax.broadcasted_iota(jnp.int32, (1, half_rows), 1)
    placer = (columns == target[:, None]).astype(BF16)
    counts = jnp.sum(onehot_low.astype(F32), 0).astype(BF16)
    counts_pair = jnp.concatenate(both(counts, swap(counts)), 0)

    qkv_shard = jnp.stack(
        [part.reshape(shard, half_heads, HEAD) for part in (w_query, w_key, w_value)], 2
    ).reshape(shard, half_heads * triple)
    extra = jnp.concatenate([norm1_gain, norm2_gain, counts_pair], 0)
    extra = jnp.pad(extra[None, :], ((0, 7), (0, half_heads * triple - extra.shape[0])))
    planes = experts // 4
    first_shard, second_shard = lax.optimization_barrier(
        (
            jnp.concatenate([qkv_shard, extra], 0),
            jnp.concatenate([w_ffn_in, w_ffn_out.T, w_attn_out.T], 1),
        )
    )
    second_line = lax.all_gather(
        second_shard,
        "dp",
        axis_index_groups=[[4 * z + k for z in range(planes)] for k in range(4)],
    )
    line_one = gather_line(first_shard)
    weight_rows, extra_row = np.s_[..., :shard, :], np.s_[..., shard, :]
    (first_all, extra_all), (last_all, unused) = gather_third(
        *gather_second(line_one), (weight_rows, extra_row)
    )
    qkv_full = jnp.concatenate([first_all, last_all], -1).reshape(width, half_heads * triple)
    extra_all = extra_all.reshape(experts, -1)
    gain_one = extra_all[:, :shard].reshape(width).astype(F32)
    gain_two = extra_all[:, shard : 2 * shard].reshape(width).astype(F32)
    counts_all = extra_all[:, 2 * shard : 2 * shard + 2 * experts].reshape(experts, 2, experts)

    pair_tokens = with_other(tokens).astype(F32)
    normed_one, hat_pair, inv_pair = norm_forward(pair_tokens, gain_one)
    inputs, hat_one, inv_one = pair_tokens[:rows], hat_pair[:rows], inv_pair[:rows]
    rows_one = normed_one.astype(BF16)
    other_t = lax.dot_general(
        qkv_full, rows_one[rows:], (((0,), (1,)), ((), ())), preferred_element_type=F32
    ).astype(BF16)
    own_t = lax.dot_general(
        qkv_full, rows_one[:rows], (((0,), (1,)), ((), ())), preferred_element_type=F32
    ).astype(BF16)
    qkv_t = jnp.concatenate(both(own_t, swap(other_t)), 0).reshape(heads, triple, rows)
    qkv_t, second_line, late_grad = lax.optimization_barrier((qkv_t, second_line, grad_out))
    sent_grad = matmul_tn(placer, late_grad).astype(BF16).reshape(experts, slots_per, width)
    by_head = lax.all_to_all(qkv_t, "dp", split_axis=0, concat_axis=0, tiled=True)

    by_head, sent_grad = lax.optimization_barrier((by_head, sent_grad))
    second_all = lax.all_gather(
        second_line, "dp", axis_index_groups=[[4 * z + k for k in range(4)] for z in range(planes)]
    )
    second_all = second_all.transpose(1, 0, 2, 3).reshape(width, -1)
    attn_half = second_all[:, 2 * hidden :]

    lent = experts // 4
    span = PLEN // rows
    own_blocks = jnp.concatenate([by_head, to_core_zero(by_head[:lent])], 0)
    prompt_kv = jnp.where(core_zero, by_head[:, HEAD:], to_core_one(by_head[:, HEAD:]))
    places = jnp.arange(experts + lent, dtype=jnp.int32)
    follows = cont_prompt * span
    plan_zero = jnp.stack(
        [
            places,
            jnp.where(places < experts, places % span, span),
            jnp.concatenate([places[:experts] // span * span, follows[:lent]], 0),
            jnp.ones_like(places),
        ]
    )
    plan_one = jnp.stack(
        [
            jnp.minimum(places + lent, experts - 1),
            jnp.full_like(places, span),
            jnp.concatenate([follows[lent:], jnp.zeros((2 * lent,), jnp.int32)], 0),
            (places < experts - lent).astype(jnp.int32),
        ]
    )
    plan = jnp.where(core_zero, plan_zero, plan_one)
    attn_blocks, log_sums = attn_forward(plan, own_blocks, prompt_kv)
    lent_back = to_core_one(attn_blocks[experts:])
    attn_own = jnp.concatenate(
        [jnp.where(core_zero, attn_blocks[:lent], lent_back), attn_blocks[lent:experts]], 0
    )
    attn_t = lax.all_to_all(attn_own, "dp", split_axis=0, concat_axis=0, tiled=True).reshape(
        width, rows
    )

    half_width = width // 2
    own_heads, other_heads = both(attn_t[:half_width], attn_t[half_width:])
    attn_other = swap(attn_half)
    hidden_one = (
        inputs
        + lax.dot_general(
            own_heads, attn_half, (((0,), (1,)), ((), ())), preferred_element_type=F32
        )
        + lax.dot_general(
            other_heads, attn_other, (((0,), (1,)), ((), ())), preferred_element_type=F32
        )
    )
    normed_two, hat_two, inv_two = norm_forward(hidden_one, gain_two)
    normed_two = normed_two.astype(BF16)
    rows_two, ffn_act, ffn_slope, ffn_own, ffn_other = mlp_forward(
        [(normed_two, swap(normed_two))],
        second_all,
        second_all,
        hidden,
        rows,
        transposed=True,
        columns=(0, 1),
    )
    hidden_two = hidden_one + ffn_own.astype(F32) + swap(ffn_other).astype(F32)

    sent_rows = (
        matmul_tn(placer, hidden_two.astype(BF16)).astype(BF16).reshape(experts, slots_per, width)
    )
    sent_rows, counts_all = lax.optimization_barrier((sent_rows, counts_all))
    mine = jnp.sum(
        jnp.where(lax.broadcasted_iota(jnp.int32, (1, 1, experts), 2) == dp_index, counts_all.astype(F32), 0.0),
        2,
    )
    per_chip = jnp.sum(mine, 1)
    chip_before = jnp.sum(
        jnp.where(
            lax.broadcasted_iota(jnp.int32, (experts, experts), 1)
            < lax.broadcasted_iota(jnp.int32, (experts, experts), 0),
            per_chip[None, :],
            0.0,
        ),
        1,
    )
    starts = both(chip_before, chip_before + mine[:, 0])
    slot_at = lax.broadcasted_iota(jnp.int32, (1, slots_per), 1).astype(F32)
    kept = jnp.concatenate(
        [(start[:, None] + slot_at < capacity).reshape(-1, 1) for start in starts], 0
    )
    own_rows, sent_grad, kept = lax.optimization_barrier((to_experts(sent_rows), sent_grad, kept))
    own_rows = own_rows.reshape(half_rows, width)
    grad_own = to_experts(sent_grad).reshape(half_rows, width)
    centre = centroids[0]
    length = half_rows // 2
    expert_rows, act_a, slope_a, own_a, other_a, gate_column = mlp_forward(
        [(own_rows, swap(own_rows))],
        expert_in_a[0],
        expert_out_a[0],
        hidden,
        length,
        centre=centroids,
    )
    from_a = (swap(other_a), swap(own_a))
    middle, act_b, slope_b, own_b, other_b = mlp_forward(
        [expert_rows, (own_a, other_a), from_a], expert_in_b[0], expert_out_b[0], hidden, length
    )
    own_b, grad_own = lax.optimization_barrier((own_b, grad_own))
    branch_half = (
        own_a.astype(F32) + from_a[0].astype(F32) + own_b.astype(F32) + swap(other_b).astype(F32)
    )
    gate_value = gate_column[:, 0]
    gate_half = gate_value[:half_rows]
    returned = (
        jnp.where(kept[:half_rows], gate_half[:, None] * branch_half, 0.0)
        .astype(BF16)
        .reshape(experts, slots_per, width)
    )
    came_back = to_experts(returned).reshape(half_rows, width)

    kept_half = kept[:half_rows, 0]
    grad_logit_half = jnp.where(
        kept_half,
        jnp.sum(grad_own.astype(F32) * branch_half, 1) * gate_half * (1.0 - gate_half),
        0.0,
    )
    centre_part = matmul(grad_logit_half, own_rows.astype(F32))
    kept_gate = jnp.where(kept, gate_column, 0.0)
    grad_pair = (grad_own, swap(grad_own))
    grad_b, grad_pre_b, own_m, other_m = mlp_backward(
        [grad_pair], expert_out_b[0], expert_in_b[0], slope_b, length, factor=kept_gate
    )
    from_m = (swap(other_m), swap(own_m))
    grad_a, grad_pre_a, own_x, other_x = mlp_backward(
        [grad_pair, (own_m, other_m), from_m],
        expert_out_a[0],
        expert_in_a[0],
        slope_a,
        length,
        factor=kept_gate,
    )
    grad_rows = (
        own_x.astype(F32)
        + swap(other_x).astype(F32)
        + own_m.astype(F32)
        + from_m[0].astype(F32)
        + grad_logit_half[:, None] * centre.astype(F32)[None, :]
    )
    grad_rows, came_back, act_a, grad_a, expert_rows, grad_pre_a = lax.optimization_barrier(
        (grad_rows.astype(BF16), came_back, act_a, grad_a, expert_rows, grad_pre_a)
    )
    grad_out_a = matmul_tn(act_a, grad_a)
    grad_in_a = matmul_tn(expert_rows, grad_pre_a)
    output = hidden_two + matmul(placer, came_back)
    grad_back = to_experts(grad_rows.reshape(experts, slots_per, width))
    grad_back, grad_out_a, grad_in_a = lax.optimization_barrier((grad_back, grad_out_a, grad_in_a))
    grad_back = grad_back.reshape(half_rows, width)
    grad_two = grad_out.astype(F32) + matmul(placer, grad_back)

    grad_down = grad_two.astype(BF16)
    rows_down, grad_ffn_pre, down_own, down_other = mlp_backward(
        [(grad_down, swap(grad_down))],
        second_all,
        second_all,
        ffn_slope,
        rows,
        transposed=False,
        columns=(0, 1),
    )
    grad_norm_two = down_own.astype(F32) + swap(down_other).astype(F32)
    back_two = norm_backward(grad_norm_two, hat_two, inv_two, gain_two)[0]
    grad_one = grad_two + back_two

    grad_branch_one = grad_one.astype(BF16)
    grad_halves = both(
        *(
            lax.dot_general(
                part, grad_branch_one, (((0,), (1,)), ((), ())), preferred_element_type=F32
            ).astype(BF16)
            for part in (attn_half, attn_other)
        )
    )
    grad_attn, rows_down, ffn_act, rows_two, grad_ffn_pre = lax.optimization_barrier(
        (
            jnp.concatenate(grad_halves, 0).reshape(heads, HEAD, rows),
            rows_down,
            ffn_act,
            rows_two,
            grad_ffn_pre,
        )
    )
    grad_by_head = lax.all_to_all(grad_attn, "dp", split_axis=0, concat_axis=0, tiled=True)
    grad_ffn_out_t = matmul_tn(rows_down, ffn_act)
    grad_ffn_in = matmul_tn(rows_two, grad_ffn_pre)
    part_own, part_other = (
        lax.dot_general(
            grad_branch_one, part, (((0,), (1,)), ((), ())), preferred_element_type=F32
        )
        for part in (own_heads, other_heads)
    )
    grad_attn_half = part_own + swap(part_other.astype(BF16)).astype(F32)
    second_part = jnp.concatenate(
        [grad_ffn_in.astype(BF16), grad_ffn_out_t.astype(BF16), grad_attn_half.astype(BF16)], 1
    )
    grad_by_head, second_part = lax.optimization_barrier((grad_by_head, second_part))
    second_sum = lax.psum_scatter(second_part, "dp", scatter_dimension=0, tiled=True).astype(F32)
    grad_blocks = jnp.concatenate([grad_by_head, to_core_zero(grad_by_head[:lent])], 0)
    grad_own_blocks, grad_prompts = attn_backward(
        plan, own_blocks, prompt_kv, grad_blocks, attn_blocks, log_sums
    )
    lent_grad = to_core_one(grad_own_blocks[experts:])
    prompt_sum = grad_prompts.astype(F32) + to_core_zero(grad_prompts).astype(F32)
    prompt_part = jnp.concatenate(
        [
            grad_own_blocks[:experts, :HEAD],
            (grad_own_blocks[:experts, HEAD:].astype(F32) + prompt_sum).astype(BF16),
        ],
        1,
    )
    cont_part = jnp.concatenate([lent_grad, grad_own_blocks[lent:experts]], 0)
    grad_head, act_b, grad_b, middle, grad_pre_b = lax.optimization_barrier(
        (jnp.where(core_zero, prompt_part, cont_part), act_b, grad_b, middle, grad_pre_b)
    )
    grad_qkv = lax.all_to_all(grad_head, "dp", split_axis=0, concat_axis=0, tiled=True)
    grad_out_b = matmul_tn(act_b, grad_b)
    grad_in_b = matmul_tn(middle, grad_pre_b)
    grad_qkv, grad_out_b, grad_in_b = lax.optimization_barrier((grad_qkv, grad_out_b, grad_in_b))
    grad_qkv = grad_qkv.reshape(2, half_heads * triple, rows)
    keep_half, send_half = both(grad_qkv[0], grad_qkv[1])
    grad_qkv_t = jnp.concatenate([keep_half, swap(send_half)], 1)
    grad_qkv_w = lax.dot_general(
        rows_one, grad_qkv_t, (((0,), (1,)), ((), ())), preferred_element_type=F32
    ).astype(BF16)
    by_chip = grad_qkv_w.reshape(experts // 4, 2, 2, shard, half_heads * triple)
    half_columns = half_heads * triple // 2
    qkv_sum = scatter_chips(by_chip[..., :half_columns], by_chip[..., half_columns:])
    grad_norm_one = keep_rows(
        lax.dot_general(
            grad_qkv_t, qkv_full, (((0,), (1,)), ((), ())), preferred_element_type=F32
        )
    )
    back_one = norm_backward(grad_norm_one, hat_one, inv_one, gain_one)[0]
    grad_input = grad_one + back_one
    qkv_sum = qkv_sum.reshape(shard, half_heads, 3, HEAD)
    query_shard, key_shard, value_shard = (
        qkv_sum[:, :, part].reshape(shard, half_heads * HEAD) for part in range(3)
    )

    ffn_in_sum = second_sum[:, :hidden]
    gains = jnp.stack(
        [
            jnp.sum(query_shard * w_query + key_shard * w_key + value_shard * w_value, 1)
            / norm1_gain.astype(F32),
            jnp.sum(ffn_in_sum * w_ffn_in, 1) / norm2_gain.astype(F32),
        ]
    )
    gains = gains + swap(gains)
    centre_grad = centre_part + swap(centre_part)
    return (
        output.astype(BF16),
        grad_input.astype(BF16),
        gains[0],
        query_shard,
        key_shard,
        value_shard,
        second_sum[:, 2 * hidden :].T,
        gains[1],
        ffn_in_sum,
        second_sum[:, hidden : 2 * hidden].T,
        centre_grad[None, :],
        grad_in_a[None],
        grad_out_a[None],
        grad_in_b[None],
        grad_out_b[None],
    )


def solution(mesh):
    body = body_paired if fits_paired(mesh) else body_general
    return jax.shard_map(
        body,
        mesh=mesh,
        in_specs=(
            P(("dp", "tensor"), None),
            P(),
            P(("dp", "tensor"), None),
            P("dp"),
            P("dp", "tensor"),
            P("dp", "tensor"),
            P("dp", "tensor"),
            P("tensor", "dp"),
            P("dp"),
            P("dp", "tensor"),
            P("tensor", "dp"),
            P("dp", None),
            P("dp", None, "tensor"),
            P("dp", "tensor", None),
            P("dp", None, "tensor"),
            P("dp", "tensor", None),
            P(("dp", "tensor"), None),
        ),
        out_specs=(
            P(("dp", "tensor"), None),
            P(("dp", "tensor"), None),
            P("dp"),
            P("dp", "tensor"),
            P("dp", "tensor"),
            P("dp", "tensor"),
            P("tensor", "dp"),
            P("dp"),
            P("dp", "tensor"),
            P("tensor", "dp"),
            P("dp", None),
            P("dp", None, "tensor"),
            P("dp", "tensor", None),
            P("dp", None, "tensor"),
            P("dp", "tensor", None),
        ),
        check_vma=False,
    )
```

```python
import functools

import jax
import jax.numpy as jnp
import numpy as np
from jax import lax
from jax.experimental import pallas as pl
from jax.experimental.pallas import tpu as pltpu
from jax.sharding import PartitionSpec as P

HEAD = 64
PLEN = 4096
CONT = 512


def shortened(value):

    def short(part):
        return part.astype(jnp.bfloat16) if part.dtype == jnp.float32 else part

    return jax.tree.map(short, value)


def carried_in(value, axis, combine, identity):
    peers, place = (lax.axis_size(axis), lax.axis_index(axis))
    everything = lax.all_gather(value, axis)
    start = jnp.broadcast_to(jnp.asarray(identity, value.dtype), value.shape)

    def turn(k, before):
        reached = k < place
        new = combine(before, everything[k])
        return jnp.where(reached, new, before)

    return lax.fori_loop(0, peers, turn, start)


def rows_gather(value):
    return lax.all_gather(value, "tensor", axis=0, tiled=True)


def rows_scatter(value):
    return lax.psum_scatter(
        value.astype(jnp.bfloat16), "tensor", scatter_dimension=0, tiled=True
    ).astype(jnp.float32)


def pair_total(value):
    return jax.tree.map(lambda part: part.astype(jnp.float32), lax.psum(shortened(value), "tensor"))


def to_experts(value):
    return lax.all_to_all(value, "dp", split_axis=0, concat_axis=0, tiled=True)


def matmul(left, right):
    return jnp.dot(left, right, preferred_element_type=jnp.float32)


def matmul_tn(left, right):
    return lax.dot_general(
        left, right, (((0,), (0,)), ((), ())), preferred_element_type=jnp.float32
    )


def matmul_nt(left, right):
    return lax.dot_general(
        left, right, (((1,), (1,)), ((), ())), preferred_element_type=jnp.float32
    )


def norm_forward(hidden, gain):
    mean_row = jnp.mean(hidden, -1, keepdims=True)
    centred = hidden - mean_row
    scale_inv = lax.rsqrt(jnp.mean(centred * centred, -1, keepdims=True) + 1e-05)
    normed = centred * scale_inv
    return (normed * gain, normed, scale_inv)


def norm_backward(grad_m, normed, scale_inv, gain):
    grad_hat = grad_m * gain
    inner = (
        grad_hat
        - jnp.mean(grad_hat, -1, keepdims=True)
        - normed * jnp.mean(grad_hat * normed, -1, keepdims=True)
    )
    return (inner * scale_inv, jnp.sum(grad_m * normed, 0))


def gelu_grad(preact, grad):
    unused, pull = jax.vjp(jax.nn.gelu, preact)
    return pull(grad)[0]


def add_counts(first, second):
    return first + second


def attend(queries, keys, values, allowed, heads):
    scale = HEAD ** (-0.5)

    def head_step(head, carry):
        outputs, log_sums = carry
        query_h = lax.dynamic_slice_in_dim(queries, head * HEAD, HEAD, 1)
        key_h = lax.dynamic_slice_in_dim(keys, head * HEAD, HEAD, 1)
        value_h = lax.dynamic_slice_in_dim(values, head * HEAD, HEAD, 1)
        scores = jnp.where(allowed, matmul_nt(query_h, key_h) * scale, -1e30)
        top_score = jnp.max(scores, 1, keepdims=True)
        expo = jnp.exp(scores - top_score)
        total = jnp.sum(expo, 1, keepdims=True)
        probs = (expo / total).astype(jnp.bfloat16)
        outputs = lax.dynamic_update_slice_in_dim(outputs, matmul(probs, value_h), head * HEAD, 1)
        log_sums = lax.dynamic_update_index_in_dim(
            log_sums, top_score[:, 0] + jnp.log(total[:, 0]), head, 0
        )
        return (outputs, log_sums)

    start_state = (
        jnp.zeros((queries.shape[0], heads * HEAD), jnp.float32),
        jnp.zeros((heads, queries.shape[0]), jnp.float32),
    )
    return lax.fori_loop(0, heads, head_step, start_state)


def attend_back(queries, keys, values, allowed, log_sums, grad_attended, heads):
    scale = HEAD ** (-0.5)

    def head_step(head, carry):
        grad_q, grad_k, grad_v = carry
        query_h = lax.dynamic_slice_in_dim(queries, head * HEAD, HEAD, 1)
        key_h = lax.dynamic_slice_in_dim(keys, head * HEAD, HEAD, 1)
        value_h = lax.dynamic_slice_in_dim(values, head * HEAD, HEAD, 1)
        grad_o = lax.dynamic_slice_in_dim(grad_attended, head * HEAD, HEAD, 1)
        scores = jnp.where(allowed, matmul_nt(query_h, key_h) * scale, -1e30)
        probs = jnp.exp(
            scores - lax.dynamic_index_in_dim(log_sums, head, 0, keepdims=False)[:, None]
        )
        grad_p = matmul_nt(grad_o, value_h)
        grad_s = (probs * (grad_p - jnp.sum(probs * grad_p, 1, keepdims=True))).astype(jnp.bfloat16)
        grad_q = lax.dynamic_update_slice_in_dim(
            grad_q, matmul(grad_s, key_h) * scale, head * HEAD, 1
        )
        grad_k = lax.dynamic_update_slice_in_dim(
            grad_k, matmul_tn(grad_s, query_h) * scale, head * HEAD, 1
        )
        grad_v = lax.dynamic_update_slice_in_dim(
            grad_v, matmul_tn(probs.astype(jnp.bfloat16), grad_o), head * HEAD, 1
        )
        return (grad_q, grad_k, grad_v)

    start_state = (
        jnp.zeros(queries.shape, jnp.float32),
        jnp.zeros(keys.shape, jnp.float32),
        jnp.zeros(values.shape, jnp.float32),
    )
    return lax.fori_loop(0, heads, head_step, start_state)


def add_block(buffer, block, start):
    length = block.shape[0]
    current = lax.dynamic_slice_in_dim(buffer, start, length, 0)
    return lax.dynamic_update_slice_in_dim(buffer, current + block, start, 0)


def body_general(
    tokens,
    cont_prompt,
    routes,
    norm1_gain,
    w_query,
    w_key,
    w_value,
    w_attn_out,
    norm2_gain,
    w_ffn_in,
    w_ffn_out,
    centroids,
    expert_in_a,
    expert_out_a,
    expert_in_b,
    expert_out_b,
    grad_out,
):
    experts = lax.axis_size("dp")
    pair_size = lax.axis_size("tensor")
    dp_index = lax.axis_index("dp")
    tensor_index = lax.axis_index("tensor")
    rows_dev = tokens.shape[0]
    rows_dp = rows_dev * pair_size
    prm_dev = rows_dp - CONT
    pkeys = experts * prm_dev
    heads = w_query.shape[1] // HEAD
    width = tokens.shape[1]
    span = PLEN // prm_dev
    owner_start = dp_index // span * PLEN
    mapped_start = cont_prompt[dp_index] * PLEN
    gain_one, query_full, key_full, value_full, attn_full, gain_two, ffn_in_full, ffn_out_full = (
        lax.all_gather(norm1_gain, "dp", axis=0, tiled=True),
        lax.all_gather(w_query, "dp", axis=0, tiled=True),
        lax.all_gather(w_key, "dp", axis=0, tiled=True),
        lax.all_gather(w_value, "dp", axis=0, tiled=True),
        lax.all_gather(w_attn_out, "dp", axis=1, tiled=True),
        lax.all_gather(norm2_gain, "dp", axis=0, tiled=True),
        lax.all_gather(w_ffn_in, "dp", axis=0, tiled=True),
        lax.all_gather(w_ffn_out, "dp", axis=1, tiled=True),
    )
    inputs = tokens.astype(jnp.float32)
    normed_one, hat_one, inv_one = norm_forward(inputs, gain_one.astype(jnp.float32))
    rows_one = rows_gather(normed_one.astype(jnp.bfloat16))
    queries = matmul(rows_one, query_full).astype(jnp.bfloat16)
    keys_own = matmul(rows_one, key_full).astype(jnp.bfloat16)
    values_own = matmul(rows_one, value_full).astype(jnp.bfloat16)
    prompt_keys, prompt_values = (
        lax.all_gather(keys_own[:prm_dev], "dp", axis=0, tiled=True),
        lax.all_gather(values_own[:prm_dev], "dp", axis=0, tiled=True),
    )
    keys_first = lax.dynamic_slice_in_dim(prompt_keys, owner_start, PLEN, 0)
    values_first = lax.dynamic_slice_in_dim(prompt_values, owner_start, PLEN, 0)
    first_row = lax.broadcasted_iota(jnp.int32, (prm_dev, 1), 0)
    first_column = lax.broadcasted_iota(jnp.int32, (1, PLEN), 1)
    allowed_first = first_column <= dp_index % span * prm_dev + first_row
    keys_second = jnp.concatenate(
        [lax.dynamic_slice_in_dim(prompt_keys, mapped_start, PLEN, 0), keys_own[prm_dev:]], 0
    )
    values_second = jnp.concatenate(
        [lax.dynamic_slice_in_dim(prompt_values, mapped_start, PLEN, 0), values_own[prm_dev:]], 0
    )
    second_row = lax.broadcasted_iota(jnp.int32, (CONT, 1), 0)
    second_column = lax.broadcasted_iota(jnp.int32, (1, PLEN + CONT), 1)
    allowed_second = (second_column < PLEN) | (second_column - PLEN <= second_row)
    attn_first, sums_first = attend(
        queries[:prm_dev], keys_first, values_first, allowed_first, heads
    )
    attn_second, sums_second = attend(
        queries[prm_dev:], keys_second, values_second, allowed_second, heads
    )
    attn_low = jnp.concatenate([attn_first, attn_second], 0).astype(jnp.bfloat16)
    hidden_one = inputs + rows_scatter(matmul(attn_low, attn_full))
    normed_two, hat_two, inv_two = norm_forward(hidden_one, gain_two.astype(jnp.float32))
    rows_two = rows_gather(normed_two.astype(jnp.bfloat16))
    ffn_pre = matmul(rows_two, ffn_in_full)
    ffn_act = jax.nn.gelu(ffn_pre).astype(jnp.bfloat16)
    hidden_two = hidden_one + rows_scatter(matmul(ffn_act, ffn_out_full))
    route = routes[:, 0]
    slots_per = max(2, (3 * rows_dev + 2 * experts - 1) // (2 * experts))
    capacity = 5 * rows_dp // 4
    expert_ids = lax.broadcasted_iota(jnp.int32, (1, experts), 1)
    onehot = (route[:, None] == expert_ids).astype(jnp.int32)
    offsets = carried_in(
        jnp.sum(onehot, 0), ("dp", "tensor"), add_counts, jnp.zeros((experts,), jnp.int32)
    )
    local_rank = jnp.sum((jnp.cumsum(onehot, 0) - 1) * onehot, 1)
    global_slot = local_rank + jnp.sum(onehot * offsets[None, :], 1)
    kept = global_slot < capacity
    target = route * slots_per + local_rank
    columns = lax.broadcasted_iota(jnp.int32, (1, experts * slots_per), 1)
    placer = ((columns == target[:, None]) & kept[:, None]).astype(jnp.bfloat16)
    sent_rows = (
        matmul_tn(placer, hidden_two.astype(jnp.bfloat16))
        .astype(jnp.bfloat16)
        .reshape(experts, slots_per, width)
    )
    expert_rows = rows_gather(to_experts(sent_rows)).reshape(-1, width)
    centre = centroids[0]
    gate_value = jax.nn.sigmoid(matmul(expert_rows, centre))
    pre_a = matmul(expert_rows, expert_in_a[0])
    act_a = jax.nn.gelu(pre_a).astype(jnp.bfloat16)
    branch_a = pair_total(matmul(act_a, expert_out_a[0]))
    middle = (expert_rows.astype(jnp.float32) + branch_a).astype(jnp.bfloat16)
    pre_b = matmul(middle, expert_in_b[0])
    act_b = jax.nn.gelu(pre_b).astype(jnp.bfloat16)
    branch_b = rows_scatter(matmul(act_b, expert_out_b[0]))
    half_rows = expert_rows.shape[0] // pair_size
    start_row = tensor_index * half_rows
    branch_half = lax.dynamic_slice_in_dim(branch_a, start_row, half_rows, 0) + branch_b
    gate_half = lax.dynamic_slice_in_dim(gate_value, start_row, half_rows, 0)
    returned = (
        (gate_half[:, None] * branch_half).astype(jnp.bfloat16).reshape(experts, slots_per, width)
    )
    came_back = to_experts(returned).reshape(experts * slots_per, width)
    output = hidden_two + matmul(placer, came_back)
    cotangent = grad_out.astype(jnp.float32)
    sent_grad = matmul_tn(placer, grad_out).astype(jnp.bfloat16).reshape(experts, slots_per, width)
    grad_half = to_experts(sent_grad).reshape(half_rows, width)
    grad_returned = rows_gather(grad_half).astype(jnp.float32)
    grad_gate_half = jnp.sum(grad_half.astype(jnp.float32) * branch_half, 1)
    grad_logit_half = grad_gate_half * gate_half * (1.0 - gate_half)
    rows_half = lax.dynamic_slice_in_dim(expert_rows, start_row, half_rows, 0)
    centre_part = matmul(grad_logit_half, rows_half.astype(jnp.float32))
    grad_branch = gate_value[:, None] * grad_returned
    grad_b = grad_branch.astype(jnp.bfloat16)
    grad_pre_b = gelu_grad(pre_b, matmul_nt(grad_b, expert_out_b[0])).astype(jnp.bfloat16)
    grad_out_b = matmul_tn(act_b, grad_b)
    grad_in_b = matmul_tn(middle, grad_pre_b)
    grad_middle = pair_total(matmul_nt(grad_pre_b, expert_in_b[0]))
    grad_a = (grad_branch + grad_middle).astype(jnp.bfloat16)
    grad_pre_a = gelu_grad(pre_a, matmul_nt(grad_a, expert_out_a[0])).astype(jnp.bfloat16)
    grad_out_a = matmul_tn(act_a, grad_a)
    grad_in_a = matmul_tn(expert_rows, grad_pre_a)
    grad_rows = (
        rows_scatter(matmul_nt(grad_pre_a, expert_in_a[0]))
        + lax.dynamic_slice_in_dim(grad_middle, start_row, half_rows, 0)
        + grad_logit_half[:, None] * centre.astype(jnp.float32)[None, :]
    )
    grad_back = to_experts(
        grad_rows.astype(jnp.bfloat16).reshape(experts, slots_per, width)
    ).reshape(experts * slots_per, width)
    grad_two = cotangent + matmul(placer, grad_back)
    gain_one, query_full, key_full, value_full, attn_full, gain_two, ffn_in_full, ffn_out_full = (
        lax.all_gather(norm1_gain, "dp", axis=0, tiled=True),
        lax.all_gather(w_query, "dp", axis=0, tiled=True),
        lax.all_gather(w_key, "dp", axis=0, tiled=True),
        lax.all_gather(w_value, "dp", axis=0, tiled=True),
        lax.all_gather(w_attn_out, "dp", axis=1, tiled=True),
        lax.all_gather(norm2_gain, "dp", axis=0, tiled=True),
        lax.all_gather(w_ffn_in, "dp", axis=0, tiled=True),
        lax.all_gather(w_ffn_out, "dp", axis=1, tiled=True),
    )
    rows_down = rows_gather(grad_two.astype(jnp.bfloat16))
    grad_ffn_pre = gelu_grad(ffn_pre, matmul_nt(rows_down, ffn_out_full)).astype(jnp.bfloat16)
    grad_ffn_out = matmul_tn(ffn_act, rows_down)
    grad_ffn_in = matmul_tn(rows_two, grad_ffn_pre)
    grad_norm_two = rows_scatter(matmul_nt(grad_ffn_pre, ffn_in_full))
    back_two, grad_gain_two = norm_backward(
        grad_norm_two, hat_two, inv_two, gain_two.astype(jnp.float32)
    )
    grad_one = grad_two + back_two
    rows_attn = rows_gather(grad_one.astype(jnp.bfloat16))
    grad_attn_out = matmul_tn(attn_low, rows_attn)
    grad_attended = matmul_nt(rows_attn, attn_full).astype(jnp.bfloat16)
    grad_q_first, grad_k_first, grad_v_first = attend_back(
        queries[:prm_dev],
        keys_first,
        values_first,
        allowed_first,
        sums_first,
        grad_attended[:prm_dev],
        heads,
    )
    grad_q_second, grad_k_second, grad_v_second = attend_back(
        queries[prm_dev:],
        keys_second,
        values_second,
        allowed_second,
        sums_second,
        grad_attended[prm_dev:],
        heads,
    )
    local_width = keys_own.shape[1]
    buffer_k = jnp.zeros((pkeys, local_width), jnp.float32)
    buffer_v = jnp.zeros((pkeys, local_width), jnp.float32)
    buffer_k = add_block(
        add_block(buffer_k, grad_k_first, owner_start), grad_k_second[:PLEN], mapped_start
    )
    buffer_v = add_block(
        add_block(buffer_v, grad_v_first, owner_start), grad_v_second[:PLEN], mapped_start
    )
    prompt_grad_k, prompt_grad_v = (
        lax.psum_scatter(buffer_k, "dp", scatter_dimension=0, tiled=True),
        lax.psum_scatter(buffer_v, "dp", scatter_dimension=0, tiled=True),
    )
    grad_keys = jnp.concatenate([prompt_grad_k, grad_k_second[PLEN:]], 0).astype(jnp.bfloat16)
    grad_values = jnp.concatenate([prompt_grad_v, grad_v_second[PLEN:]], 0).astype(jnp.bfloat16)
    grad_queries = jnp.concatenate([grad_q_first, grad_q_second], 0).astype(jnp.bfloat16)
    grad_query = matmul_tn(rows_one, grad_queries)
    grad_key = matmul_tn(rows_one, grad_keys)
    grad_value = matmul_tn(rows_one, grad_values)
    grad_norm_one = rows_scatter(
        matmul_nt(grad_queries, query_full)
        + matmul_nt(grad_keys, key_full)
        + matmul_nt(grad_values, value_full)
    )
    back_one, grad_gain_one = norm_backward(
        grad_norm_one, hat_one, inv_one, gain_one.astype(jnp.float32)
    )
    grad_input = grad_one + back_one
    (
        gain_one_part,
        query_shard,
        key_shard,
        value_shard,
        attn_shard,
        gain_two_part,
        ffn_in_shard,
        ffn_out_shard,
    ) = (
        lax.psum_scatter(grad_gain_one, "dp", scatter_dimension=0, tiled=True),
        lax.psum_scatter(grad_query, "dp", scatter_dimension=0, tiled=True),
        lax.psum_scatter(grad_key, "dp", scatter_dimension=0, tiled=True),
        lax.psum_scatter(grad_value, "dp", scatter_dimension=0, tiled=True),
        lax.psum_scatter(grad_attn_out, "dp", scatter_dimension=1, tiled=True),
        lax.psum_scatter(grad_gain_two, "dp", scatter_dimension=0, tiled=True),
        lax.psum_scatter(grad_ffn_in, "dp", scatter_dimension=0, tiled=True),
        lax.psum_scatter(grad_ffn_out, "dp", scatter_dimension=1, tiled=True),
    )
    gain_one_shard, gain_two_shard, centre_grad = pair_total(
        (gain_one_part, gain_two_part, centre_part)
    )
    return (
        output.astype(jnp.bfloat16),
        grad_input.astype(jnp.bfloat16),
        gain_one_shard,
        query_shard,
        key_shard,
        value_shard,
        attn_shard,
        gain_two_shard,
        ffn_in_shard,
        ffn_out_shard,
        centre_grad[None, :],
        grad_in_a[None],
        grad_out_a[None],
        grad_in_b[None],
        grad_out_b[None],
    )


LOG2E = 1.4426950408889634
GELU_A = 0.7978845608028654
GELU_B = 0.044715
BF16 = jnp.bfloat16
F32 = jnp.float32


def dot_tt(left, right):
    return lax.dot_general(left, right, (((0,), (0,)), ((), ())), preferred_element_type=F32)


def beside(blocks, at, count, start, stop):
    return jnp.concatenate([blocks[at + j, start:stop, :] for j in range(count)], 1)


def in_groups(sizes, first, count, take, carry):
    for size in sizes:
        groups = count // size
        step = take(size)
        carry = lax.fori_loop(
            0, groups, lambda k, value, at=first, n=size, f=step: f(at + k * n, value), carry
        )
        first, count = first + groups * size, count - groups * size
    return carry


def attn_fwd_kernel(plan, own, prompts, out, log_sums, values, *, head, factor):
    step_id = pl.program_id(0)
    block, full, first = plan[0, step_id], plan[1, step_id], plan[2, step_id]

    def with_ones(value):
        return jnp.concatenate([value.T, jnp.ones((value.shape[1], head), BF16)], 1)

    @pl.when(step_id == 0)
    def _():
        def turn(k, carry):
            values[k] = with_ones(prompts[k, head : 2 * head, :])
            return carry

        lax.fori_loop(0, prompts.shape[0], turn, 0)

    @pl.when(plan[3, step_id] > 0)
    def _():
        query = own[block, 0:head, :].T
        scores = matmul(query, own[block, head : 2 * head, :])
        query_at = lax.broadcasted_iota(jnp.int32, scores.shape, 0)
        key_at = lax.broadcasted_iota(jnp.int32, scores.shape, 1)
        scores = jnp.where(key_at <= query_at, scores, -1e30)
        top = jnp.max(scores, 1, keepdims=True) * factor
        expo = jnp.exp2(scores * factor - top)
        result = matmul(expo.astype(BF16), with_ones(own[block, 2 * head : 3 * head, :]))

        def take(count):
            def step(at, carry):
                before, result = carry
                scores = matmul(query, beside(prompts, at, count, 0, head))
                top = jnp.maximum(before, jnp.max(scores, 1, keepdims=True) * factor)
                expo = jnp.exp2(scores * factor - top).astype(BF16)
                rows = jnp.concatenate([values[at + j] for j in range(count)], 0)
                return top, result * jnp.exp2(before - top) + matmul(expo, rows)

            return step

        top, result = in_groups((4, 2, 1), first, full, take, (top, result))
        result = result.T
        total = result[head : head + 1]
        out[block] = (result[:head] / total).astype(BF16)
        top = jnp.broadcast_to(top, (top.shape[0], 128)).T[0:1]
        log_sums[block] = top + jnp.log2(total)


def attn_bwd_kernel(
    plan, own, prompts, grad, out, log_sums, grad_own, grad_prompts, sum_k, sum_v, *, head, factor, scale
):
    step_id = pl.program_id(0)
    block, full, first = plan[0, step_id], plan[1, step_id], plan[2, step_id]

    @pl.when(step_id == 0)
    def _():
        sum_k[...] = jnp.zeros_like(sum_k)
        sum_v[...] = jnp.zeros_like(sum_v)

    @pl.when(plan[3, step_id] > 0)
    def _():
        query_t, grad_t, log_sum = own[block, 0:head, :], grad[block], log_sums[block]
        inner = jnp.sum(grad_t.astype(F32) * out[block].astype(F32), 0, keepdims=True)
        query, grad_o = query_t.T, grad_t.T

        def tile(key, value, diagonal):
            probs = jnp.exp2(dot_tt(key, query_t) * factor - log_sum)
            if diagonal:
                key_at = lax.broadcasted_iota(jnp.int32, probs.shape, 0)
                query_at = lax.broadcasted_iota(jnp.int32, probs.shape, 1)
                probs = jnp.where(key_at <= query_at, probs, 0.0)
            grad_s = (probs * (dot_tt(value, grad_t) - inner)).astype(BF16)
            return matmul(grad_s, query), matmul(probs.astype(BF16), grad_o), matmul(key, grad_s)

        grad_k, grad_v, grad_q = tile(
            own[block, head : 2 * head, :], own[block, 2 * head : 3 * head, :], True
        )
        grad_own[block, head : 2 * head, :] = (grad_k * scale).T.astype(BF16)
        grad_own[block, 2 * head : 3 * head, :] = grad_v.T.astype(BF16)

        def take(count):
            def step(at, grad_q):
                more_k, more_v, more_q = tile(
                    beside(prompts, at, count, 0, head),
                    beside(prompts, at, count, head, 2 * head),
                    False,
                )
                length = more_k.shape[0] // count
                for j in range(count):
                    sum_k[at + j] += more_k[j * length : (j + 1) * length]
                    sum_v[at + j] += more_v[j * length : (j + 1) * length]
                return grad_q + more_q

            return step

        grad_q = in_groups((4, 2, 1), first, full, take, grad_q)
        grad_own[block, 0:head, :] = (grad_q * scale).astype(BF16)

    @pl.when(step_id == pl.num_programs(0) - 1)
    def _():
        def finish(k, carry):
            grad_prompts[k, 0:head, :] = (sum_k[k] * scale).T.astype(BF16)
            grad_prompts[k, head : 2 * head, :] = sum_v[k].T.astype(BF16)
            return carry

        lax.fori_loop(0, sum_k.shape[0], finish, 0)


def attn_forward(plan, own, prompts):
    blocks, triple, length = own.shape
    head = triple // 3
    whole = pl.BlockSpec(memory_space=pltpu.VMEM)
    return pl.pallas_call(
        functools.partial(attn_fwd_kernel, head=head, factor=head**-0.5 * LOG2E),
        grid_spec=pltpu.PrefetchScalarGridSpec(
            num_scalar_prefetch=1,
            grid=(plan.shape[1],),
            in_specs=[whole, whole],
            out_specs=[whole, whole],
            scratch_shapes=[pltpu.VMEM((prompts.shape[0], length, 2 * head), BF16)],
        ),
        out_shape=[
            jax.ShapeDtypeStruct((blocks, head, length), BF16),
            jax.ShapeDtypeStruct((blocks, 1, length), F32),
        ],
        compiler_params=pltpu.CompilerParams(vmem_limit_bytes=40 * 2**20),
        cost_estimate=pl.CostEstimate(
            flops=100 * length * length * 256 * 4,
            bytes_accessed=8 * 2**20,
            transcendentals=100 * length * length,
        ),
        name="attn_fwd",
    )(plan, own, prompts)


def attn_backward(plan, own, prompts, grad, out, log_sums):
    blocks, triple, length = own.shape
    head = triple // 3
    whole = pl.BlockSpec(memory_space=pltpu.VMEM)
    return pl.pallas_call(
        functools.partial(
            attn_bwd_kernel, head=head, factor=head**-0.5 * LOG2E, scale=head**-0.5
        ),
        grid_spec=pltpu.PrefetchScalarGridSpec(
            num_scalar_prefetch=1,
            grid=(plan.shape[1],),
            in_specs=[whole] * 5,
            out_specs=[whole, whole],
            scratch_shapes=[pltpu.VMEM((prompts.shape[0], length, head), F32)] * 2,
        ),
        out_shape=[
            jax.ShapeDtypeStruct(own.shape, BF16),
            jax.ShapeDtypeStruct(prompts.shape, BF16),
        ],
        compiler_params=pltpu.CompilerParams(vmem_limit_bytes=48 * 2**20),
        cost_estimate=pl.CostEstimate(
            flops=100 * length * length * 256 * 10,
            bytes_accessed=16 * 2**20,
            transcendentals=100 * length * length,
        ),
        name="attn_bwd",
    )(plan, own, prompts, grad, out, log_sums)


def swap(value):
    return lax.ppermute(value, "tensor", [(0, 1), (1, 0)])


def to_core_one(value):
    return lax.ppermute(value, "tensor", [(0, 1)])


def to_core_zero(value):
    return lax.ppermute(value, "tensor", [(1, 0)])


def with_other(value):
    return jnp.concatenate([value, swap(value)], 0)


def keep_rows(value):
    half = value.shape[0] // 2
    return value[:half].astype(F32) + swap(value[half:].astype(BF16)).astype(F32)


def gelu_pair(preact):
    square = preact * preact
    gate = 0.5 + 0.5 * jnp.tanh(preact * (GELU_A + GELU_A * GELU_B * square))
    act = preact * gate
    slope = gate + act * (1.0 - gate) * (2.0 * GELU_A + 6.0 * GELU_A * GELU_B * square)
    return act.astype(BF16), slope.astype(BF16)


def by_halves(run):
    early = pl.program_id(0) < pl.num_programs(0) // 2
    pl.when(early)(functools.partial(run, 0))
    pl.when(jnp.logical_not(early))(functools.partial(run, 1))


def take_terms(refs, kinds, half):
    values, at = [], 0
    for paired in kinds:
        values.append(refs[at + half * paired][...])
        at += 1 + paired
    return values, refs[at:]


def mlp_kernel(*refs, kinds, transposed, gated):
    def run(half):
        terms, rest = take_terms(refs, kinds, half)
        rows = terms[0]
        if len(terms) > 1:
            total = rows.astype(F32)
            for term in terms[1:]:
                total = total + term.astype(F32)
            rows = total.astype(BF16)
        if gated:
            centre, rest = rest[0], rest[1:]
            logit = jnp.sum(rows.astype(F32) * centre[...].astype(F32), 1, keepdims=True)
            rest[-1][...] = 1.0 / (1.0 + jnp.exp(-logit))
        w_in, w_out, kept_rows, kept_act, kept_slope, *results = rest[:7]
        kept_rows[...] = rows
        act, slope = gelu_pair(matmul(rows, w_in[...]))
        kept_act[...] = act
        kept_slope[...] = slope
        product = matmul_nt if transposed else matmul
        results[half][...] = product(act, w_out[...]).astype(BF16)

    by_halves(run)


def mlp_back_kernel(*refs, kinds, transposed, scaled):
    def run(half):
        factor, rest = (refs[0], refs[1:]) if scaled else (None, refs)
        terms, rest = take_terms(rest, kinds, half)
        grad = terms[0]
        if scaled:
            total = factor[...] * grad.astype(F32)
            for term in terms[1:]:
                total = total + term.astype(F32)
            grad = total.astype(BF16)
        w_out, w_in, slope, kept_grad, kept_pre, *results = rest
        kept_grad[...] = grad
        grad = (matmul_nt if transposed else matmul)(grad, w_out[...])
        grad_pre = (grad * slope[...].astype(F32)).astype(BF16)
        kept_pre[...] = grad_pre
        results[half][...] = matmul_nt(grad_pre, w_in[...]).astype(BF16)

    by_halves(run)


def mlp_blocks(terms, length):
    paired = [isinstance(term, tuple) for term in terms]
    arrays = [part for term in terms for part in (term if isinstance(term, tuple) else (term,))]
    half = max(part.shape[0] // length // (1 + (not pair)) for term, pair in zip(terms, paired) for part in (term if pair else (term,)))
    width = arrays[0].shape[1]
    block = pl.BlockSpec((length, width), lambda m: (m, 0))
    halves = [
        pl.BlockSpec((length, width), lambda m: (jnp.minimum(m, half - 1), 0)),
        pl.BlockSpec((length, width), lambda m: (jnp.maximum(m - half, 0), 0)),
    ]
    specs = [spec for pair in paired for spec in (halves if pair else [block])]
    return tuple(paired), arrays, specs, block, halves, 2 * half


def mlp_forward(terms, w_in, w_out, hidden, length, transposed=False, columns=(0, 0), centre=None):
    kinds, arrays, specs, block, halves, steps = mlp_blocks(terms, length)
    rows, width = steps * length, arrays[0].shape[1]
    hidden_block = pl.BlockSpec((length, hidden), lambda m: (m, 0))
    once = dict(pipeline_mode=pl.Buffered(1))
    in_block = pl.BlockSpec((width, hidden), lambda m: (0, columns[0]), **once)
    out_block = (
        pl.BlockSpec((width, hidden), lambda m: (0, columns[1]), **once)
        if transposed
        else pl.BlockSpec((hidden, width), lambda m: (0, 0), **once)
    )
    gated = centre is not None
    return pl.pallas_call(
        functools.partial(mlp_kernel, kinds=kinds, transposed=transposed, gated=gated),
        grid=(steps,),
        in_specs=specs + [pl.BlockSpec((1, width), lambda m: (0, 0))] * gated + [in_block, out_block],
        out_specs=[block, hidden_block, hidden_block]
        + halves
        + [pl.BlockSpec((length, 1), lambda m: (m, 0))] * gated,
        out_shape=[jax.ShapeDtypeStruct((rows, width), BF16)]
        + [jax.ShapeDtypeStruct((rows, hidden), BF16)] * 2
        + [jax.ShapeDtypeStruct((rows // 2, width), BF16)] * 2
        + [jax.ShapeDtypeStruct((rows, 1), F32)] * gated,
        compiler_params=pltpu.CompilerParams(vmem_limit_bytes=54 * 2**20),
        cost_estimate=pl.CostEstimate(
            flops=rows * width * hidden,
            bytes_accessed=width * hidden + rows * hidden + rows * width,
            transcendentals=0,
        ),
        name="mlp_fwd",
    )(*arrays, *([centre] * gated), w_in, w_out)


def mlp_backward(terms, w_out, w_in, slope, length, transposed=True, columns=(0, 0), factor=None):
    kinds, arrays, specs, block, halves, steps = mlp_blocks(terms, length)
    rows, width = steps * length, arrays[0].shape[1]
    hidden = slope.shape[1]
    hidden_block = pl.BlockSpec((length, hidden), lambda m: (m, 0))
    once = dict(pipeline_mode=pl.Buffered(1))
    out_block = (
        pl.BlockSpec((hidden, width), lambda m: (0, 0), **once)
        if transposed
        else pl.BlockSpec((width, hidden), lambda m: (0, columns[1]), **once)
    )
    in_block = pl.BlockSpec((width, hidden), lambda m: (0, columns[0]), **once)
    scaled = factor is not None
    return pl.pallas_call(
        functools.partial(mlp_back_kernel, kinds=kinds, transposed=transposed, scaled=scaled),
        grid=(steps,),
        in_specs=[pl.BlockSpec((length, 1), lambda m: (m, 0))] * scaled
        + specs
        + [out_block, in_block, hidden_block],
        out_specs=[block, hidden_block] + halves,
        out_shape=[
            jax.ShapeDtypeStruct((rows, width), BF16),
            jax.ShapeDtypeStruct((rows, hidden), BF16),
        ]
        + [jax.ShapeDtypeStruct((rows // 2, width), BF16)] * 2,
        compiler_params=pltpu.CompilerParams(vmem_limit_bytes=54 * 2**20),
        cost_estimate=pl.CostEstimate(
            flops=4 * rows * width * hidden,
            bytes_accessed=4 * width * hidden + 4 * rows * hidden + 4 * rows * width,
            transcendentals=0,
        ),
        name="mlp_bwd",
    )(*([factor] * scaled), *arrays, w_out, w_in, slope)


def from_bit(value, bit):
    return lax.ppermute(value, "dp", [(i, i ^ bit) for i in range(lax.axis_size("dp"))])


def chip_place():
    place = lax.axis_index("dp")
    return place // 4, place // 2 % 2, place % 2


def ordered(bit, own, other, axis):
    return jnp.where(
        bit == 0, jnp.stack([own, other], axis), jnp.stack([other, own], axis)
    )


def gather_line(value):
    planes = lax.axis_size("dp") // 4
    z = chip_place()[0]
    blocks = jnp.stack([value] + [from_bit(value, 4 * k) for k in range(1, planes)])
    return jnp.stack(
        [lax.dynamic_index_in_dim(blocks, z ^ k, 0, keepdims=False) for k in range(planes)]
    )


def gather_second(line):
    half = line.shape[-1] // 2
    y, x = chip_place()[1:]
    first, second = line[..., :half], line[..., half:]
    first = ordered(y, first, from_bit(first, 2), 1)
    second = ordered(x, second, from_bit(second, 1), 1)
    return first, second


def gather_third(first, second, cuts):
    y, x = chip_place()[1:]
    first_other, second_other = from_bit(first, 1), from_bit(second, 2)
    return (
        [ordered(x, first[at], first_other[at], 2) for at in cuts],
        [ordered(y, second[at], second_other[at], 1) for at in cuts],
    )


def halve(value, bit, axis, partner):
    lower = lax.index_in_dim(value, 0, axis, keepdims=False)
    upper = lax.index_in_dim(value, 1, axis, keepdims=False)
    keep, send = jnp.where(bit == 0, lower, upper), jnp.where(bit == 0, upper, lower)
    return keep.astype(F32) + from_bit(send, partner).astype(F32)


def scatter_chips(first, second):
    planes = first.shape[0]
    z, y, x = chip_place()
    first = halve(first, x, 2, 1).astype(BF16)
    second = halve(second, y, 1, 2).astype(BF16)
    line = jnp.concatenate([halve(first, y, 1, 2), halve(second, x, 1, 1)], -1).astype(BF16)
    total = lax.dynamic_index_in_dim(line, z, 0, keepdims=False).astype(F32)
    for k in range(1, planes):
        part = lax.dynamic_index_in_dim(line, z ^ k, 0, keepdims=False)
        total = total + from_bit(part, 4 * k).astype(F32)
    return total


def fits_paired(mesh):
    return mesh.shape["tensor"] == 2 and mesh.shape["dp"] == 16


def body_paired(
    tokens,
    cont_prompt,
    routes,
    norm1_gain,
    w_query,
    w_key,
    w_value,
    w_attn_out,
    norm2_gain,
    w_ffn_in,
    w_ffn_out,
    centroids,
    expert_in_a,
    expert_out_a,
    expert_in_b,
    expert_out_b,
    grad_out,
):
    experts = lax.axis_size("dp")
    dp_index = lax.axis_index("dp")
    core_zero = lax.axis_index("tensor") == 0
    rows, width = tokens.shape
    rows_dp = 2 * rows
    shard = w_query.shape[0]
    half_heads = w_query.shape[1] // HEAD
    hidden = w_ffn_in.shape[1]
    assert expert_in_a.shape[2] == hidden
    triple = 3 * HEAD
    heads = 2 * half_heads
    both = lambda lower, upper: (jnp.where(core_zero, lower, upper), jnp.where(core_zero, upper, lower))

    route = routes[:, 0]
    slots_per = max(2, (3 * rows + 2 * experts - 1) // (2 * experts))
    capacity = 5 * rows_dp // 4
    onehot = route[:, None] == lax.broadcasted_iota(jnp.int32, (1, experts), 1)
    onehot_low = onehot.astype(BF16)
    below = lax.broadcasted_iota(jnp.int32, (rows, rows), 0) > lax.broadcasted_iota(
        jnp.int32, (rows, rows), 1
    )
    earlier = matmul(below.astype(BF16), onehot_low)
    local_rank = jnp.sum(jnp.where(onehot, earlier, 0.0), 1).astype(jnp.int32)
    target = route * slots_per + local_rank
    half_rows = experts * slots_per
    columns = lax.broadcasted_iota(jnp.int32, (1, half_rows), 1)
    placer = (columns == target[:, None]).astype(BF16)
    counts = jnp.sum(onehot_low.astype(F32), 0).astype(BF16)
    counts_pair = jnp.concatenate(both(counts, swap(counts)), 0)

    qkv_shard = jnp.stack(
        [part.reshape(shard, half_heads, HEAD) for part in (w_query, w_key, w_value)], 2
    ).reshape(shard, half_heads * triple)
    extra = jnp.concatenate([norm1_gain, norm2_gain, counts_pair], 0)
    extra = jnp.pad(extra[None, :], ((0, 7), (0, half_heads * triple - extra.shape[0])))
    planes = experts // 4
    first_shard, second_shard = lax.optimization_barrier(
        (
            jnp.concatenate([qkv_shard, extra], 0),
            jnp.concatenate([w_ffn_in, w_ffn_out.T, w_attn_out.T], 1),
        )
    )
    second_line = lax.all_gather(
        second_shard,
        "dp",
        axis_index_groups=[[4 * z + k for z in range(planes)] for k in range(4)],
    )
    line_one = gather_line(first_shard)
    weight_rows, extra_row = np.s_[..., :shard, :], np.s_[..., shard, :]
    (first_all, extra_all), (last_all, unused) = gather_third(
        *gather_second(line_one), (weight_rows, extra_row)
    )
    qkv_full = jnp.concatenate([first_all, last_all], -1).reshape(width, half_heads * triple)
    extra_all = extra_all.reshape(experts, -1)
    gain_one = extra_all[:, :shard].reshape(width).astype(F32)
    gain_two = extra_all[:, shard : 2 * shard].reshape(width).astype(F32)
    counts_all = extra_all[:, 2 * shard : 2 * shard + 2 * experts].reshape(experts, 2, experts)

    pair_tokens = with_other(tokens).astype(F32)
    normed_one, hat_pair, inv_pair = norm_forward(pair_tokens, gain_one)
    inputs, hat_one, inv_one = pair_tokens[:rows], hat_pair[:rows], inv_pair[:rows]
    rows_one = normed_one.astype(BF16)
    other_t = lax.dot_general(
        qkv_full, rows_one[rows:], (((0,), (1,)), ((), ())), preferred_element_type=F32
    ).astype(BF16)
    own_t = lax.dot_general(
        qkv_full, rows_one[:rows], (((0,), (1,)), ((), ())), preferred_element_type=F32
    ).astype(BF16)
    qkv_t = jnp.concatenate(both(own_t, swap(other_t)), 0).reshape(heads, triple, rows)
    qkv_t, second_line, late_grad = lax.optimization_barrier((qkv_t, second_line, grad_out))
    sent_grad = matmul_tn(placer, late_grad).astype(BF16).reshape(experts, slots_per, width)
    by_head = lax.all_to_all(qkv_t, "dp", split_axis=0, concat_axis=0, tiled=True)

    by_head, sent_grad = lax.optimization_barrier((by_head, sent_grad))
    second_all = lax.all_gather(
        second_line, "dp", axis_index_groups=[[4 * z + k for k in range(4)] for z in range(planes)]
    )
    second_all = second_all.transpose(1, 0, 2, 3).reshape(width, -1)
    attn_half = second_all[:, 2 * hidden :]

    lent = experts // 4
    span = PLEN // rows
    own_blocks = jnp.concatenate([by_head, to_core_zero(by_head[:lent])], 0)
    prompt_kv = jnp.where(core_zero, by_head[:, HEAD:], to_core_one(by_head[:, HEAD:]))
    places = jnp.arange(experts + lent, dtype=jnp.int32)
    follows = cont_prompt * span
    plan_zero = jnp.stack(
        [
            places,
            jnp.where(places < experts, places % span, span),
            jnp.concatenate([places[:experts] // span * span, follows[:lent]], 0),
            jnp.ones_like(places),
        ]
    )
    plan_one = jnp.stack(
        [
            jnp.minimum(places + lent, experts - 1),
            jnp.full_like(places, span),
            jnp.concatenate([follows[lent:], jnp.zeros((2 * lent,), jnp.int32)], 0),
            (places < experts - lent).astype(jnp.int32),
        ]
    )
    plan = jnp.where(core_zero, plan_zero, plan_one)
    attn_blocks, log_sums = attn_forward(plan, own_blocks, prompt_kv)
    lent_back = to_core_one(attn_blocks[experts:])
    attn_own = jnp.concatenate(
        [jnp.where(core_zero, attn_blocks[:lent], lent_back), attn_blocks[lent:experts]], 0
    )
    attn_t = lax.all_to_all(attn_own, "dp", split_axis=0, concat_axis=0, tiled=True).reshape(
        width, rows
    )

    half_width = width // 2
    own_heads, other_heads = both(attn_t[:half_width], attn_t[half_width:])
    attn_other = swap(attn_half)
    hidden_one = (
        inputs
        + lax.dot_general(
            own_heads, attn_half, (((0,), (1,)), ((), ())), preferred_element_type=F32
        )
        + lax.dot_general(
            other_heads, attn_other, (((0,), (1,)), ((), ())), preferred_element_type=F32
        )
    )
    normed_two, hat_two, inv_two = norm_forward(hidden_one, gain_two)
    normed_two = normed_two.astype(BF16)
    rows_two, ffn_act, ffn_slope, ffn_own, ffn_other = mlp_forward(
        [(normed_two, swap(normed_two))],
        second_all,
        second_all,
        hidden,
        rows,
        transposed=True,
        columns=(0, 1),
    )
    hidden_two = hidden_one + ffn_own.astype(F32) + swap(ffn_other).astype(F32)

    sent_rows = (
        matmul_tn(placer, hidden_two.astype(BF16)).astype(BF16).reshape(experts, slots_per, width)
    )
    sent_rows, counts_all = lax.optimization_barrier((sent_rows, counts_all))
    mine = jnp.sum(
        jnp.where(lax.broadcasted_iota(jnp.int32, (1, 1, experts), 2) == dp_index, counts_all.astype(F32), 0.0),
        2,
    )
    per_chip = jnp.sum(mine, 1)
    chip_before = jnp.sum(
        jnp.where(
            lax.broadcasted_iota(jnp.int32, (experts, experts), 1)
            < lax.broadcasted_iota(jnp.int32, (experts, experts), 0),
            per_chip[None, :],
            0.0,
        ),
        1,
    )
    starts = both(chip_before, chip_before + mine[:, 0])
    slot_at = lax.broadcasted_iota(jnp.int32, (1, slots_per), 1).astype(F32)
    kept = jnp.concatenate(
        [(start[:, None] + slot_at < capacity).reshape(-1, 1) for start in starts], 0
    )
    own_rows, sent_grad, kept = lax.optimization_barrier((to_experts(sent_rows), sent_grad, kept))
    own_rows = own_rows.reshape(half_rows, width)
    grad_own = to_experts(sent_grad).reshape(half_rows, width)
    centre = centroids[0]
    length = half_rows // 2
    expert_rows, act_a, slope_a, own_a, other_a, gate_column = mlp_forward(
        [(own_rows, swap(own_rows))],
        expert_in_a[0],
        expert_out_a[0],
        hidden,
        length,
        centre=centroids,
    )
    from_a = (swap(other_a), swap(own_a))
    middle, act_b, slope_b, own_b, other_b = mlp_forward(
        [expert_rows, (own_a, other_a), from_a], expert_in_b[0], expert_out_b[0], hidden, length
    )
    own_b, grad_own = lax.optimization_barrier((own_b, grad_own))
    branch_half = (
        own_a.astype(F32) + from_a[0].astype(F32) + own_b.astype(F32) + swap(other_b).astype(F32)
    )
    gate_value = gate_column[:, 0]
    gate_half = gate_value[:half_rows]
    returned = (
        jnp.where(kept[:half_rows], gate_half[:, None] * branch_half, 0.0)
        .astype(BF16)
        .reshape(experts, slots_per, width)
    )
    came_back = to_experts(returned).reshape(half_rows, width)

    kept_half = kept[:half_rows, 0]
    grad_logit_half = jnp.where(
        kept_half,
        jnp.sum(grad_own.astype(F32) * branch_half, 1) * gate_half * (1.0 - gate_half),
        0.0,
    )
    centre_part = matmul(grad_logit_half, own_rows.astype(F32))
    kept_gate = jnp.where(kept, gate_column, 0.0)
    grad_pair = (grad_own, swap(grad_own))
    grad_b, grad_pre_b, own_m, other_m = mlp_backward(
        [grad_pair], expert_out_b[0], expert_in_b[0], slope_b, length, factor=kept_gate
    )
    from_m = (swap(other_m), swap(own_m))
    grad_a, grad_pre_a, own_x, other_x = mlp_backward(
        [grad_pair, (own_m, other_m), from_m],
        expert_out_a[0],
        expert_in_a[0],
        slope_a,
        length,
        factor=kept_gate,
    )
    grad_rows = (
        own_x.astype(F32)
        + swap(other_x).astype(F32)
        + own_m.astype(F32)
        + from_m[0].astype(F32)
        + grad_logit_half[:, None] * centre.astype(F32)[None, :]
    )
    grad_rows, came_back, act_a, grad_a, expert_rows, grad_pre_a = lax.optimization_barrier(
        (grad_rows.astype(BF16), came_back, act_a, grad_a, expert_rows, grad_pre_a)
    )
    grad_out_a = matmul_tn(act_a, grad_a)
    grad_in_a = matmul_tn(expert_rows, grad_pre_a)
    output = hidden_two + matmul(placer, came_back)
    grad_back = to_experts(grad_rows.reshape(experts, slots_per, width))
    grad_back, grad_out_a, grad_in_a = lax.optimization_barrier((grad_back, grad_out_a, grad_in_a))
    grad_back = grad_back.reshape(half_rows, width)
    grad_two = grad_out.astype(F32) + matmul(placer, grad_back)

    grad_down = grad_two.astype(BF16)
    rows_down, grad_ffn_pre, down_own, down_other = mlp_backward(
        [(grad_down, swap(grad_down))],
        second_all,
        second_all,
        ffn_slope,
        rows,
        transposed=False,
        columns=(0, 1),
    )
    grad_norm_two = down_own.astype(F32) + swap(down_other).astype(F32)
    back_two = norm_backward(grad_norm_two, hat_two, inv_two, gain_two)[0]
    grad_one = grad_two + back_two

    grad_branch_one = grad_one.astype(BF16)
    grad_halves = both(
        *(
            lax.dot_general(
                part, grad_branch_one, (((0,), (1,)), ((), ())), preferred_element_type=F32
            ).astype(BF16)
            for part in (attn_half, attn_other)
        )
    )
    grad_attn, rows_down, ffn_act, rows_two, grad_ffn_pre = lax.optimization_barrier(
        (
            jnp.concatenate(grad_halves, 0).reshape(heads, HEAD, rows),
            rows_down,
            ffn_act,
            rows_two,
            grad_ffn_pre,
        )
    )
    grad_by_head = lax.all_to_all(grad_attn, "dp", split_axis=0, concat_axis=0, tiled=True)
    grad_ffn_out_t = matmul_tn(rows_down, ffn_act)
    grad_ffn_in = matmul_tn(rows_two, grad_ffn_pre)
    part_own, part_other = (
        lax.dot_general(
            grad_branch_one, part, (((0,), (1,)), ((), ())), preferred_element_type=F32
        )
        for part in (own_heads, other_heads)
    )
    grad_attn_half = part_own + swap(part_other.astype(BF16)).astype(F32)
    second_part = jnp.concatenate(
        [grad_ffn_in.astype(BF16), grad_ffn_out_t.astype(BF16), grad_attn_half.astype(BF16)], 1
    )
    second_part = second_part.reshape(planes, 4, shard, -1).transpose(1, 0, 2, 3).reshape(width, -1)
    grad_by_head, second_part = lax.optimization_barrier((grad_by_head, second_part))
    second_plane = lax.psum_scatter(
        second_part,
        "dp",
        scatter_dimension=0,
        axis_index_groups=[[4 * z + k for k in range(4)] for z in range(planes)],
        tiled=True,
    )
    second_sum = lax.psum_scatter(
        second_plane,
        "dp",
        scatter_dimension=0,
        axis_index_groups=[[4 * z + k for z in range(planes)] for k in range(4)],
        tiled=True,
    ).astype(F32)
    grad_blocks = jnp.concatenate([grad_by_head, to_core_zero(grad_by_head[:lent])], 0)
    grad_own_blocks, grad_prompts = attn_backward(
        plan, own_blocks, prompt_kv, grad_blocks, attn_blocks, log_sums
    )
    lent_grad = to_core_one(grad_own_blocks[experts:])
    prompt_sum = grad_prompts.astype(F32) + to_core_zero(grad_prompts).astype(F32)
    prompt_part = jnp.concatenate(
        [
            grad_own_blocks[:experts, :HEAD],
            (grad_own_blocks[:experts, HEAD:].astype(F32) + prompt_sum).astype(BF16),
        ],
        1,
    )
    cont_part = jnp.concatenate([lent_grad, grad_own_blocks[lent:experts]], 0)
    grad_head, act_b, grad_b, middle, grad_pre_b = lax.optimization_barrier(
        (jnp.where(core_zero, prompt_part, cont_part), act_b, grad_b, middle, grad_pre_b)
    )
    grad_qkv = lax.all_to_all(grad_head, "dp", split_axis=0, concat_axis=0, tiled=True)
    grad_out_b = matmul_tn(act_b, grad_b)
    grad_in_b = matmul_tn(middle, grad_pre_b)
    grad_qkv, grad_out_b, grad_in_b = lax.optimization_barrier((grad_qkv, grad_out_b, grad_in_b))
    grad_qkv = grad_qkv.reshape(2, half_heads * triple, rows)
    keep_half, send_half = both(grad_qkv[0], grad_qkv[1])
    grad_qkv_t = jnp.concatenate([keep_half, swap(send_half)], 1)
    grad_qkv_w = lax.dot_general(
        rows_one, grad_qkv_t, (((0,), (1,)), ((), ())), preferred_element_type=F32
    ).astype(BF16)
    by_chip = grad_qkv_w.reshape(experts // 4, 2, 2, shard, half_heads * triple)
    half_columns = half_heads * triple // 2
    qkv_sum = scatter_chips(by_chip[..., :half_columns], by_chip[..., half_columns:])
    grad_norm_one = keep_rows(
        lax.dot_general(
            grad_qkv_t, qkv_full, (((0,), (1,)), ((), ())), preferred_element_type=F32
        )
    )
    back_one = norm_backward(grad_norm_one, hat_one, inv_one, gain_one)[0]
    grad_input = grad_one + back_one
    qkv_sum = qkv_sum.reshape(shard, half_heads, 3, HEAD)
    query_shard, key_shard, value_shard = (
        qkv_sum[:, :, part].reshape(shard, half_heads * HEAD) for part in range(3)
    )

    ffn_in_sum = second_sum[:, :hidden]
    gains = jnp.stack(
        [
            jnp.sum(query_shard * w_query + key_shard * w_key + value_shard * w_value, 1)
            / norm1_gain.astype(F32),
            jnp.sum(ffn_in_sum * w_ffn_in, 1) / norm2_gain.astype(F32),
        ]
    )
    gains = gains + swap(gains)
    centre_grad = centre_part + swap(centre_part)
    return (
        output.astype(BF16),
        grad_input.astype(BF16),
        gains[0],
        query_shard,
        key_shard,
        value_shard,
        second_sum[:, 2 * hidden :].T,
        gains[1],
        ffn_in_sum,
        second_sum[:, hidden : 2 * hidden].T,
        centre_grad[None, :],
        grad_in_a[None],
        grad_out_a[None],
        grad_in_b[None],
        grad_out_b[None],
    )


def solution(mesh):
    body = body_paired if fits_paired(mesh) else body_general
    return jax.shard_map(
        body,
        mesh=mesh,
        in_specs=(
            P(("dp", "tensor"), None),
            P(),
            P(("dp", "tensor"), None),
            P("dp"),
            P("dp", "tensor"),
            P("dp", "tensor"),
            P("dp", "tensor"),
            P("tensor", "dp"),
            P("dp"),
            P("dp", "tensor"),
            P("tensor", "dp"),
            P("dp", None),
            P("dp", None, "tensor"),
            P("dp", "tensor", None),
            P("dp", None, "tensor"),
            P("dp", "tensor", None),
            P(("dp", "tensor"), None),
        ),
        out_specs=(
            P(("dp", "tensor"), None),
            P(("dp", "tensor"), None),
            P("dp"),
            P("dp", "tensor"),
            P("dp", "tensor"),
            P("dp", "tensor"),
            P("tensor", "dp"),
            P("dp"),
            P("dp", "tensor"),
            P("tensor", "dp"),
            P("dp", None),
            P("dp", None, "tensor"),
            P("dp", "tensor", None),
            P("dp", None, "tensor"),
            P("dp", "tensor", None),
        ),
        check_vma=False,
    )
```

```python
import functools

import jax
import jax.numpy as jnp
import numpy as np
from jax import lax
from jax.experimental import pallas as pl
from jax.experimental.pallas import tpu as pltpu
from jax.sharding import PartitionSpec as P

HEAD = 64
PLEN = 4096
CONT = 512


def shortened(value):

    def short(part):
        return part.astype(jnp.bfloat16) if part.dtype == jnp.float32 else part

    return jax.tree.map(short, value)


def carried_in(value, axis, combine, identity):
    peers, place = (lax.axis_size(axis), lax.axis_index(axis))
    everything = lax.all_gather(value, axis)
    start = jnp.broadcast_to(jnp.asarray(identity, value.dtype), value.shape)

    def turn(k, before):
        reached = k < place
        new = combine(before, everything[k])
        return jnp.where(reached, new, before)

    return lax.fori_loop(0, peers, turn, start)


def rows_gather(value):
    return lax.all_gather(value, "tensor", axis=0, tiled=True)


def rows_scatter(value):
    return lax.psum_scatter(
        value.astype(jnp.bfloat16), "tensor", scatter_dimension=0, tiled=True
    ).astype(jnp.float32)


def pair_total(value):
    return jax.tree.map(lambda part: part.astype(jnp.float32), lax.psum(shortened(value), "tensor"))


def to_experts(value):
    return lax.all_to_all(value, "dp", split_axis=0, concat_axis=0, tiled=True)


def matmul(left, right):
    return jnp.dot(left, right, preferred_element_type=jnp.float32)


def matmul_tn(left, right):
    return lax.dot_general(
        left, right, (((0,), (0,)), ((), ())), preferred_element_type=jnp.float32
    )


def matmul_nt(left, right):
    return lax.dot_general(
        left, right, (((1,), (1,)), ((), ())), preferred_element_type=jnp.float32
    )


def norm_forward(hidden, gain):
    mean_row = jnp.mean(hidden, -1, keepdims=True)
    centred = hidden - mean_row
    scale_inv = lax.rsqrt(jnp.mean(centred * centred, -1, keepdims=True) + 1e-05)
    normed = centred * scale_inv
    return (normed * gain, normed, scale_inv)


def norm_backward(grad_m, normed, scale_inv, gain):
    grad_hat = grad_m * gain
    inner = (
        grad_hat
        - jnp.mean(grad_hat, -1, keepdims=True)
        - normed * jnp.mean(grad_hat * normed, -1, keepdims=True)
    )
    return (inner * scale_inv, jnp.sum(grad_m * normed, 0))


def gelu_grad(preact, grad):
    unused, pull = jax.vjp(jax.nn.gelu, preact)
    return pull(grad)[0]


def add_counts(first, second):
    return first + second


def attend(queries, keys, values, allowed, heads):
    scale = HEAD ** (-0.5)

    def head_step(head, carry):
        outputs, log_sums = carry
        query_h = lax.dynamic_slice_in_dim(queries, head * HEAD, HEAD, 1)
        key_h = lax.dynamic_slice_in_dim(keys, head * HEAD, HEAD, 1)
        value_h = lax.dynamic_slice_in_dim(values, head * HEAD, HEAD, 1)
        scores = jnp.where(allowed, matmul_nt(query_h, key_h) * scale, -1e30)
        top_score = jnp.max(scores, 1, keepdims=True)
        expo = jnp.exp(scores - top_score)
        total = jnp.sum(expo, 1, keepdims=True)
        probs = (expo / total).astype(jnp.bfloat16)
        outputs = lax.dynamic_update_slice_in_dim(outputs, matmul(probs, value_h), head * HEAD, 1)
        log_sums = lax.dynamic_update_index_in_dim(
            log_sums, top_score[:, 0] + jnp.log(total[:, 0]), head, 0
        )
        return (outputs, log_sums)

    start_state = (
        jnp.zeros((queries.shape[0], heads * HEAD), jnp.float32),
        jnp.zeros((heads, queries.shape[0]), jnp.float32),
    )
    return lax.fori_loop(0, heads, head_step, start_state)


def attend_back(queries, keys, values, allowed, log_sums, grad_attended, heads):
    scale = HEAD ** (-0.5)

    def head_step(head, carry):
        grad_q, grad_k, grad_v = carry
        query_h = lax.dynamic_slice_in_dim(queries, head * HEAD, HEAD, 1)
        key_h = lax.dynamic_slice_in_dim(keys, head * HEAD, HEAD, 1)
        value_h = lax.dynamic_slice_in_dim(values, head * HEAD, HEAD, 1)
        grad_o = lax.dynamic_slice_in_dim(grad_attended, head * HEAD, HEAD, 1)
        scores = jnp.where(allowed, matmul_nt(query_h, key_h) * scale, -1e30)
        probs = jnp.exp(
            scores - lax.dynamic_index_in_dim(log_sums, head, 0, keepdims=False)[:, None]
        )
        grad_p = matmul_nt(grad_o, value_h)
        grad_s = (probs * (grad_p - jnp.sum(probs * grad_p, 1, keepdims=True))).astype(jnp.bfloat16)
        grad_q = lax.dynamic_update_slice_in_dim(
            grad_q, matmul(grad_s, key_h) * scale, head * HEAD, 1
        )
        grad_k = lax.dynamic_update_slice_in_dim(
            grad_k, matmul_tn(grad_s, query_h) * scale, head * HEAD, 1
        )
        grad_v = lax.dynamic_update_slice_in_dim(
            grad_v, matmul_tn(probs.astype(jnp.bfloat16), grad_o), head * HEAD, 1
        )
        return (grad_q, grad_k, grad_v)

    start_state = (
        jnp.zeros(queries.shape, jnp.float32),
        jnp.zeros(keys.shape, jnp.float32),
        jnp.zeros(values.shape, jnp.float32),
    )
    return lax.fori_loop(0, heads, head_step, start_state)


def add_block(buffer, block, start):
    length = block.shape[0]
    current = lax.dynamic_slice_in_dim(buffer, start, length, 0)
    return lax.dynamic_update_slice_in_dim(buffer, current + block, start, 0)


def body_general(
    tokens,
    cont_prompt,
    routes,
    norm1_gain,
    w_query,
    w_key,
    w_value,
    w_attn_out,
    norm2_gain,
    w_ffn_in,
    w_ffn_out,
    centroids,
    expert_in_a,
    expert_out_a,
    expert_in_b,
    expert_out_b,
    grad_out,
):
    experts = lax.axis_size("dp")
    pair_size = lax.axis_size("tensor")
    dp_index = lax.axis_index("dp")
    tensor_index = lax.axis_index("tensor")
    rows_dev = tokens.shape[0]
    rows_dp = rows_dev * pair_size
    prm_dev = rows_dp - CONT
    pkeys = experts * prm_dev
    heads = w_query.shape[1] // HEAD
    width = tokens.shape[1]
    span = PLEN // prm_dev
    owner_start = dp_index // span * PLEN
    mapped_start = cont_prompt[dp_index] * PLEN
    gain_one, query_full, key_full, value_full, attn_full, gain_two, ffn_in_full, ffn_out_full = (
        lax.all_gather(norm1_gain, "dp", axis=0, tiled=True),
        lax.all_gather(w_query, "dp", axis=0, tiled=True),
        lax.all_gather(w_key, "dp", axis=0, tiled=True),
        lax.all_gather(w_value, "dp", axis=0, tiled=True),
        lax.all_gather(w_attn_out, "dp", axis=1, tiled=True),
        lax.all_gather(norm2_gain, "dp", axis=0, tiled=True),
        lax.all_gather(w_ffn_in, "dp", axis=0, tiled=True),
        lax.all_gather(w_ffn_out, "dp", axis=1, tiled=True),
    )
    inputs = tokens.astype(jnp.float32)
    normed_one, hat_one, inv_one = norm_forward(inputs, gain_one.astype(jnp.float32))
    rows_one = rows_gather(normed_one.astype(jnp.bfloat16))
    queries = matmul(rows_one, query_full).astype(jnp.bfloat16)
    keys_own = matmul(rows_one, key_full).astype(jnp.bfloat16)
    values_own = matmul(rows_one, value_full).astype(jnp.bfloat16)
    prompt_keys, prompt_values = (
        lax.all_gather(keys_own[:prm_dev], "dp", axis=0, tiled=True),
        lax.all_gather(values_own[:prm_dev], "dp", axis=0, tiled=True),
    )
    keys_first = lax.dynamic_slice_in_dim(prompt_keys, owner_start, PLEN, 0)
    values_first = lax.dynamic_slice_in_dim(prompt_values, owner_start, PLEN, 0)
    first_row = lax.broadcasted_iota(jnp.int32, (prm_dev, 1), 0)
    first_column = lax.broadcasted_iota(jnp.int32, (1, PLEN), 1)
    allowed_first = first_column <= dp_index % span * prm_dev + first_row
    keys_second = jnp.concatenate(
        [lax.dynamic_slice_in_dim(prompt_keys, mapped_start, PLEN, 0), keys_own[prm_dev:]], 0
    )
    values_second = jnp.concatenate(
        [lax.dynamic_slice_in_dim(prompt_values, mapped_start, PLEN, 0), values_own[prm_dev:]], 0
    )
    second_row = lax.broadcasted_iota(jnp.int32, (CONT, 1), 0)
    second_column = lax.broadcasted_iota(jnp.int32, (1, PLEN + CONT), 1)
    allowed_second = (second_column < PLEN) | (second_column - PLEN <= second_row)
    attn_first, sums_first = attend(
        queries[:prm_dev], keys_first, values_first, allowed_first, heads
    )
    attn_second, sums_second = attend(
        queries[prm_dev:], keys_second, values_second, allowed_second, heads
    )
    attn_low = jnp.concatenate([attn_first, attn_second], 0).astype(jnp.bfloat16)
    hidden_one = inputs + rows_scatter(matmul(attn_low, attn_full))
    normed_two, hat_two, inv_two = norm_forward(hidden_one, gain_two.astype(jnp.float32))
    rows_two = rows_gather(normed_two.astype(jnp.bfloat16))
    ffn_pre = matmul(rows_two, ffn_in_full)
    ffn_act = jax.nn.gelu(ffn_pre).astype(jnp.bfloat16)
    hidden_two = hidden_one + rows_scatter(matmul(ffn_act, ffn_out_full))
    route = routes[:, 0]
    slots_per = max(2, (3 * rows_dev + 2 * experts - 1) // (2 * experts))
    capacity = 5 * rows_dp // 4
    expert_ids = lax.broadcasted_iota(jnp.int32, (1, experts), 1)
    onehot = (route[:, None] == expert_ids).astype(jnp.int32)
    offsets = carried_in(
        jnp.sum(onehot, 0), ("dp", "tensor"), add_counts, jnp.zeros((experts,), jnp.int32)
    )
    local_rank = jnp.sum((jnp.cumsum(onehot, 0) - 1) * onehot, 1)
    global_slot = local_rank + jnp.sum(onehot * offsets[None, :], 1)
    kept = global_slot < capacity
    target = route * slots_per + local_rank
    columns = lax.broadcasted_iota(jnp.int32, (1, experts * slots_per), 1)
    placer = ((columns == target[:, None]) & kept[:, None]).astype(jnp.bfloat16)
    sent_rows = (
        matmul_tn(placer, hidden_two.astype(jnp.bfloat16))
        .astype(jnp.bfloat16)
        .reshape(experts, slots_per, width)
    )
    expert_rows = rows_gather(to_experts(sent_rows)).reshape(-1, width)
    centre = centroids[0]
    gate_value = jax.nn.sigmoid(matmul(expert_rows, centre))
    pre_a = matmul(expert_rows, expert_in_a[0])
    act_a = jax.nn.gelu(pre_a).astype(jnp.bfloat16)
    branch_a = pair_total(matmul(act_a, expert_out_a[0]))
    middle = (expert_rows.astype(jnp.float32) + branch_a).astype(jnp.bfloat16)
    pre_b = matmul(middle, expert_in_b[0])
    act_b = jax.nn.gelu(pre_b).astype(jnp.bfloat16)
    branch_b = rows_scatter(matmul(act_b, expert_out_b[0]))
    half_rows = expert_rows.shape[0] // pair_size
    start_row = tensor_index * half_rows
    branch_half = lax.dynamic_slice_in_dim(branch_a, start_row, half_rows, 0) + branch_b
    gate_half = lax.dynamic_slice_in_dim(gate_value, start_row, half_rows, 0)
    returned = (
        (gate_half[:, None] * branch_half).astype(jnp.bfloat16).reshape(experts, slots_per, width)
    )
    came_back = to_experts(returned).reshape(experts * slots_per, width)
    output = hidden_two + matmul(placer, came_back)
    cotangent = grad_out.astype(jnp.float32)
    sent_grad = matmul_tn(placer, grad_out).astype(jnp.bfloat16).reshape(experts, slots_per, width)
    grad_half = to_experts(sent_grad).reshape(half_rows, width)
    grad_returned = rows_gather(grad_half).astype(jnp.float32)
    grad_gate_half = jnp.sum(grad_half.astype(jnp.float32) * branch_half, 1)
    grad_logit_half = grad_gate_half * gate_half * (1.0 - gate_half)
    rows_half = lax.dynamic_slice_in_dim(expert_rows, start_row, half_rows, 0)
    centre_part = matmul(grad_logit_half, rows_half.astype(jnp.float32))
    grad_branch = gate_value[:, None] * grad_returned
    grad_b = grad_branch.astype(jnp.bfloat16)
    grad_pre_b = gelu_grad(pre_b, matmul_nt(grad_b, expert_out_b[0])).astype(jnp.bfloat16)
    grad_out_b = matmul_tn(act_b, grad_b)
    grad_in_b = matmul_tn(middle, grad_pre_b)
    grad_middle = pair_total(matmul_nt(grad_pre_b, expert_in_b[0]))
    grad_a = (grad_branch + grad_middle).astype(jnp.bfloat16)
    grad_pre_a = gelu_grad(pre_a, matmul_nt(grad_a, expert_out_a[0])).astype(jnp.bfloat16)
    grad_out_a = matmul_tn(act_a, grad_a)
    grad_in_a = matmul_tn(expert_rows, grad_pre_a)
    grad_rows = (
        rows_scatter(matmul_nt(grad_pre_a, expert_in_a[0]))
        + lax.dynamic_slice_in_dim(grad_middle, start_row, half_rows, 0)
        + grad_logit_half[:, None] * centre.astype(jnp.float32)[None, :]
    )
    grad_back = to_experts(
        grad_rows.astype(jnp.bfloat16).reshape(experts, slots_per, width)
    ).reshape(experts * slots_per, width)
    grad_two = cotangent + matmul(placer, grad_back)
    gain_one, query_full, key_full, value_full, attn_full, gain_two, ffn_in_full, ffn_out_full = (
        lax.all_gather(norm1_gain, "dp", axis=0, tiled=True),
        lax.all_gather(w_query, "dp", axis=0, tiled=True),
        lax.all_gather(w_key, "dp", axis=0, tiled=True),
        lax.all_gather(w_value, "dp", axis=0, tiled=True),
        lax.all_gather(w_attn_out, "dp", axis=1, tiled=True),
        lax.all_gather(norm2_gain, "dp", axis=0, tiled=True),
        lax.all_gather(w_ffn_in, "dp", axis=0, tiled=True),
        lax.all_gather(w_ffn_out, "dp", axis=1, tiled=True),
    )
    rows_down = rows_gather(grad_two.astype(jnp.bfloat16))
    grad_ffn_pre = gelu_grad(ffn_pre, matmul_nt(rows_down, ffn_out_full)).astype(jnp.bfloat16)
    grad_ffn_out = matmul_tn(ffn_act, rows_down)
    grad_ffn_in = matmul_tn(rows_two, grad_ffn_pre)
    grad_norm_two = rows_scatter(matmul_nt(grad_ffn_pre, ffn_in_full))
    back_two, grad_gain_two = norm_backward(
        grad_norm_two, hat_two, inv_two, gain_two.astype(jnp.float32)
    )
    grad_one = grad_two + back_two
    rows_attn = rows_gather(grad_one.astype(jnp.bfloat16))
    grad_attn_out = matmul_tn(attn_low, rows_attn)
    grad_attended = matmul_nt(rows_attn, attn_full).astype(jnp.bfloat16)
    grad_q_first, grad_k_first, grad_v_first = attend_back(
        queries[:prm_dev],
        keys_first,
        values_first,
        allowed_first,
        sums_first,
        grad_attended[:prm_dev],
        heads,
    )
    grad_q_second, grad_k_second, grad_v_second = attend_back(
        queries[prm_dev:],
        keys_second,
        values_second,
        allowed_second,
        sums_second,
        grad_attended[prm_dev:],
        heads,
    )
    local_width = keys_own.shape[1]
    buffer_k = jnp.zeros((pkeys, local_width), jnp.float32)
    buffer_v = jnp.zeros((pkeys, local_width), jnp.float32)
    buffer_k = add_block(
        add_block(buffer_k, grad_k_first, owner_start), grad_k_second[:PLEN], mapped_start
    )
    buffer_v = add_block(
        add_block(buffer_v, grad_v_first, owner_start), grad_v_second[:PLEN], mapped_start
    )
    prompt_grad_k, prompt_grad_v = (
        lax.psum_scatter(buffer_k, "dp", scatter_dimension=0, tiled=True),
        lax.psum_scatter(buffer_v, "dp", scatter_dimension=0, tiled=True),
    )
    grad_keys = jnp.concatenate([prompt_grad_k, grad_k_second[PLEN:]], 0).astype(jnp.bfloat16)
    grad_values = jnp.concatenate([prompt_grad_v, grad_v_second[PLEN:]], 0).astype(jnp.bfloat16)
    grad_queries = jnp.concatenate([grad_q_first, grad_q_second], 0).astype(jnp.bfloat16)
    grad_query = matmul_tn(rows_one, grad_queries)
    grad_key = matmul_tn(rows_one, grad_keys)
    grad_value = matmul_tn(rows_one, grad_values)
    grad_norm_one = rows_scatter(
        matmul_nt(grad_queries, query_full)
        + matmul_nt(grad_keys, key_full)
        + matmul_nt(grad_values, value_full)
    )
    back_one, grad_gain_one = norm_backward(
        grad_norm_one, hat_one, inv_one, gain_one.astype(jnp.float32)
    )
    grad_input = grad_one + back_one
    (
        gain_one_part,
        query_shard,
        key_shard,
        value_shard,
        attn_shard,
        gain_two_part,
        ffn_in_shard,
        ffn_out_shard,
    ) = (
        lax.psum_scatter(grad_gain_one, "dp", scatter_dimension=0, tiled=True),
        lax.psum_scatter(grad_query, "dp", scatter_dimension=0, tiled=True),
        lax.psum_scatter(grad_key, "dp", scatter_dimension=0, tiled=True),
        lax.psum_scatter(grad_value, "dp", scatter_dimension=0, tiled=True),
        lax.psum_scatter(grad_attn_out, "dp", scatter_dimension=1, tiled=True),
        lax.psum_scatter(grad_gain_two, "dp", scatter_dimension=0, tiled=True),
        lax.psum_scatter(grad_ffn_in, "dp", scatter_dimension=0, tiled=True),
        lax.psum_scatter(grad_ffn_out, "dp", scatter_dimension=1, tiled=True),
    )
    gain_one_shard, gain_two_shard, centre_grad = pair_total(
        (gain_one_part, gain_two_part, centre_part)
    )
    return (
        output.astype(jnp.bfloat16),
        grad_input.astype(jnp.bfloat16),
        gain_one_shard,
        query_shard,
        key_shard,
        value_shard,
        attn_shard,
        gain_two_shard,
        ffn_in_shard,
        ffn_out_shard,
        centre_grad[None, :],
        grad_in_a[None],
        grad_out_a[None],
        grad_in_b[None],
        grad_out_b[None],
    )


LOG2E = 1.4426950408889634
GELU_A = 0.7978845608028654
GELU_B = 0.044715
BF16 = jnp.bfloat16
F32 = jnp.float32


def dot_tt(left, right):
    return lax.dot_general(left, right, (((0,), (0,)), ((), ())), preferred_element_type=F32)


def beside(blocks, at, count, start, stop):
    return jnp.concatenate([blocks[at + j, start:stop, :] for j in range(count)], 1)


def in_groups(sizes, first, count, take, carry):
    for size in sizes:
        groups = count // size
        step = take(size)
        carry = lax.fori_loop(
            0, groups, lambda k, value, at=first, n=size, f=step: f(at + k * n, value), carry
        )
        first, count = first + groups * size, count - groups * size
    return carry


def attn_fwd_kernel(plan, own, prompts, out, log_sums, values, *, head, factor):
    step_id = pl.program_id(0)
    block, full, first = plan[0, step_id], plan[1, step_id], plan[2, step_id]

    def with_ones(value):
        return jnp.concatenate([value.T, jnp.ones((value.shape[1], head), BF16)], 1)

    @pl.when(step_id == 0)
    def _():
        def turn(k, carry):
            values[k] = with_ones(prompts[k, head : 2 * head, :])
            return carry

        lax.fori_loop(0, prompts.shape[0], turn, 0)

    @pl.when(plan[3, step_id] > 0)
    def _():
        query = own[block, 0:head, :].T
        scores = matmul(query, own[block, head : 2 * head, :])
        query_at = lax.broadcasted_iota(jnp.int32, scores.shape, 0)
        key_at = lax.broadcasted_iota(jnp.int32, scores.shape, 1)
        scores = jnp.where(key_at <= query_at, scores, -1e30)
        top = jnp.max(scores, 1, keepdims=True) * factor
        expo = jnp.exp2(scores * factor - top)
        result = matmul(expo.astype(BF16), with_ones(own[block, 2 * head : 3 * head, :]))

        def take(count):
            def step(at, carry):
                before, result = carry
                scores = matmul(query, beside(prompts, at, count, 0, head))
                top = jnp.maximum(before, jnp.max(scores, 1, keepdims=True) * factor)
                expo = jnp.exp2(scores * factor - top).astype(BF16)
                rows = jnp.concatenate([values[at + j] for j in range(count)], 0)
                return top, result * jnp.exp2(before - top) + matmul(expo, rows)

            return step

        top, result = in_groups((4, 2, 1), first, full, take, (top, result))
        result = result.T
        total = result[head : head + 1]
        out[block] = (result[:head] / total).astype(BF16)
        top = jnp.broadcast_to(top, (top.shape[0], 128)).T[0:1]
        log_sums[block] = top + jnp.log2(total)


def attn_bwd_kernel(
    plan, own, prompts, grad, out, log_sums, grad_own, grad_prompts, sum_k, sum_v, *, head, factor, scale
):
    step_id = pl.program_id(0)
    block, full, first = plan[0, step_id], plan[1, step_id], plan[2, step_id]

    @pl.when(step_id == 0)
    def _():
        sum_k[...] = jnp.zeros_like(sum_k)
        sum_v[...] = jnp.zeros_like(sum_v)

    @pl.when(plan[3, step_id] > 0)
    def _():
        query_t, grad_t, log_sum = own[block, 0:head, :], grad[block], log_sums[block]
        inner = jnp.sum(grad_t.astype(F32) * out[block].astype(F32), 0, keepdims=True)
        query, grad_o = query_t.T, grad_t.T

        def tile(key, value, diagonal):
            probs = jnp.exp2(dot_tt(key, query_t) * factor - log_sum)
            if diagonal:
                key_at = lax.broadcasted_iota(jnp.int32, probs.shape, 0)
                query_at = lax.broadcasted_iota(jnp.int32, probs.shape, 1)
                probs = jnp.where(key_at <= query_at, probs, 0.0)
            grad_s = (probs * (dot_tt(value, grad_t) - inner)).astype(BF16)
            return matmul(grad_s, query), matmul(probs.astype(BF16), grad_o), matmul(key, grad_s)

        grad_k, grad_v, grad_q = tile(
            own[block, head : 2 * head, :], own[block, 2 * head : 3 * head, :], True
        )
        grad_own[block, head : 2 * head, :] = (grad_k * scale).T.astype(BF16)
        grad_own[block, 2 * head : 3 * head, :] = grad_v.T.astype(BF16)

        def take(count):
            def step(at, grad_q):
                more_k, more_v, more_q = tile(
                    beside(prompts, at, count, 0, head),
                    beside(prompts, at, count, head, 2 * head),
                    False,
                )
                length = more_k.shape[0] // count
                for j in range(count):
                    sum_k[at + j] += more_k[j * length : (j + 1) * length]
                    sum_v[at + j] += more_v[j * length : (j + 1) * length]
                return grad_q + more_q

            return step

        grad_q = in_groups((4, 2, 1), first, full, take, grad_q)
        grad_own[block, 0:head, :] = (grad_q * scale).astype(BF16)

    @pl.when(step_id == pl.num_programs(0) - 1)
    def _():
        def finish(k, carry):
            grad_prompts[k, 0:head, :] = (sum_k[k] * scale).T.astype(BF16)
            grad_prompts[k, head : 2 * head, :] = sum_v[k].T.astype(BF16)
            return carry

        lax.fori_loop(0, sum_k.shape[0], finish, 0)


def attn_forward(plan, own, prompts):
    blocks, triple, length = own.shape
    head = triple // 3
    whole = pl.BlockSpec(memory_space=pltpu.VMEM)
    return pl.pallas_call(
        functools.partial(attn_fwd_kernel, head=head, factor=head**-0.5 * LOG2E),
        grid_spec=pltpu.PrefetchScalarGridSpec(
            num_scalar_prefetch=1,
            grid=(plan.shape[1],),
            in_specs=[whole, whole],
            out_specs=[whole, whole],
            scratch_shapes=[pltpu.VMEM((prompts.shape[0], length, 2 * head), BF16)],
        ),
        out_shape=[
            jax.ShapeDtypeStruct((blocks, head, length), BF16),
            jax.ShapeDtypeStruct((blocks, 1, length), F32),
        ],
        compiler_params=pltpu.CompilerParams(vmem_limit_bytes=40 * 2**20),
        cost_estimate=pl.CostEstimate(
            flops=100 * length * length * 256 * 4,
            bytes_accessed=8 * 2**20,
            transcendentals=100 * length * length,
        ),
        name="attn_fwd",
    )(plan, own, prompts)


def attn_backward(plan, own, prompts, grad, out, log_sums):
    blocks, triple, length = own.shape
    head = triple // 3
    whole = pl.BlockSpec(memory_space=pltpu.VMEM)
    return pl.pallas_call(
        functools.partial(
            attn_bwd_kernel, head=head, factor=head**-0.5 * LOG2E, scale=head**-0.5
        ),
        grid_spec=pltpu.PrefetchScalarGridSpec(
            num_scalar_prefetch=1,
            grid=(plan.shape[1],),
            in_specs=[whole] * 5,
            out_specs=[whole, whole],
            scratch_shapes=[pltpu.VMEM((prompts.shape[0], length, head), F32)] * 2,
        ),
        out_shape=[
            jax.ShapeDtypeStruct(own.shape, BF16),
            jax.ShapeDtypeStruct(prompts.shape, BF16),
        ],
        compiler_params=pltpu.CompilerParams(vmem_limit_bytes=48 * 2**20),
        cost_estimate=pl.CostEstimate(
            flops=100 * length * length * 256 * 10,
            bytes_accessed=16 * 2**20,
            transcendentals=100 * length * length,
        ),
        name="attn_bwd",
    )(plan, own, prompts, grad, out, log_sums)


def swap(value):
    return lax.ppermute(value, "tensor", [(0, 1), (1, 0)])


def to_core_one(value):
    return lax.ppermute(value, "tensor", [(0, 1)])


def to_core_zero(value):
    return lax.ppermute(value, "tensor", [(1, 0)])


def with_other(value):
    return jnp.concatenate([value, swap(value)], 0)


def keep_rows(value):
    half = value.shape[0] // 2
    return value[:half].astype(F32) + swap(value[half:].astype(BF16)).astype(F32)


def gelu_pair(preact):
    square = preact * preact
    gate = 0.5 + 0.5 * jnp.tanh(preact * (GELU_A + GELU_A * GELU_B * square))
    act = preact * gate
    slope = gate + act * (1.0 - gate) * (2.0 * GELU_A + 6.0 * GELU_A * GELU_B * square)
    return act.astype(BF16), slope.astype(BF16)


def by_halves(run):
    early = pl.program_id(0) < pl.num_programs(0) // 2
    pl.when(early)(functools.partial(run, 0))
    pl.when(jnp.logical_not(early))(functools.partial(run, 1))


def take_terms(refs, kinds, half):
    values, at = [], 0
    for paired in kinds:
        values.append(refs[at + half * paired][...])
        at += 1 + paired
    return values, refs[at:]


def mlp_kernel(*refs, kinds, transposed, gated):
    def run(half):
        terms, rest = take_terms(refs, kinds, half)
        rows = terms[0]
        if len(terms) > 1:
            total = rows.astype(F32)
            for term in terms[1:]:
                total = total + term.astype(F32)
            rows = total.astype(BF16)
        if gated:
            centre, rest = rest[0], rest[1:]
            logit = jnp.sum(rows.astype(F32) * centre[...].astype(F32), 1, keepdims=True)
            rest[-1][...] = 1.0 / (1.0 + jnp.exp(-logit))
        w_in, w_out, kept_rows, kept_act, kept_slope, *results = rest[:7]
        kept_rows[...] = rows
        act, slope = gelu_pair(matmul(rows, w_in[...]))
        kept_act[...] = act
        kept_slope[...] = slope
        product = matmul_nt if transposed else matmul
        results[half][...] = product(act, w_out[...]).astype(BF16)

    by_halves(run)


def mlp_back_kernel(*refs, kinds, transposed, scaled):
    def run(half):
        factor, rest = (refs[0], refs[1:]) if scaled else (None, refs)
        terms, rest = take_terms(rest, kinds, half)
        grad = terms[0]
        if scaled:
            total = factor[...] * grad.astype(F32)
            for term in terms[1:]:
                total = total + term.astype(F32)
            grad = total.astype(BF16)
        w_out, w_in, slope, kept_grad, kept_pre, *results = rest
        kept_grad[...] = grad
        grad = (matmul_nt if transposed else matmul)(grad, w_out[...])
        grad_pre = (grad * slope[...].astype(F32)).astype(BF16)
        kept_pre[...] = grad_pre
        results[half][...] = matmul_nt(grad_pre, w_in[...]).astype(BF16)

    by_halves(run)


def mlp_blocks(terms, length):
    paired = [isinstance(term, tuple) for term in terms]
    arrays = [part for term in terms for part in (term if isinstance(term, tuple) else (term,))]
    half = max(part.shape[0] // length // (1 + (not pair)) for term, pair in zip(terms, paired) for part in (term if pair else (term,)))
    width = arrays[0].shape[1]
    block = pl.BlockSpec((length, width), lambda m: (m, 0))
    halves = [
        pl.BlockSpec((length, width), lambda m: (jnp.minimum(m, half - 1), 0)),
        pl.BlockSpec((length, width), lambda m: (jnp.maximum(m - half, 0), 0)),
    ]
    specs = [spec for pair in paired for spec in (halves if pair else [block])]
    return tuple(paired), arrays, specs, block, halves, 2 * half


def mlp_forward(terms, w_in, w_out, hidden, length, transposed=False, columns=(0, 0), centre=None):
    kinds, arrays, specs, block, halves, steps = mlp_blocks(terms, length)
    rows, width = steps * length, arrays[0].shape[1]
    hidden_block = pl.BlockSpec((length, hidden), lambda m: (m, 0))
    once = dict(pipeline_mode=pl.Buffered(1))
    in_block = pl.BlockSpec((width, hidden), lambda m: (0, columns[0]), **once)
    out_block = (
        pl.BlockSpec((width, hidden), lambda m: (0, columns[1]), **once)
        if transposed
        else pl.BlockSpec((hidden, width), lambda m: (0, 0), **once)
    )
    gated = centre is not None
    return pl.pallas_call(
        functools.partial(mlp_kernel, kinds=kinds, transposed=transposed, gated=gated),
        grid=(steps,),
        in_specs=specs + [pl.BlockSpec((1, width), lambda m: (0, 0))] * gated + [in_block, out_block],
        out_specs=[block, hidden_block, hidden_block]
        + halves
        + [pl.BlockSpec((length, 1), lambda m: (m, 0))] * gated,
        out_shape=[jax.ShapeDtypeStruct((rows, width), BF16)]
        + [jax.ShapeDtypeStruct((rows, hidden), BF16)] * 2
        + [jax.ShapeDtypeStruct((rows // 2, width), BF16)] * 2
        + [jax.ShapeDtypeStruct((rows, 1), F32)] * gated,
        compiler_params=pltpu.CompilerParams(vmem_limit_bytes=54 * 2**20),
        cost_estimate=pl.CostEstimate(
            flops=rows * width * hidden,
            bytes_accessed=width * hidden + rows * hidden + rows * width,
            transcendentals=0,
        ),
        name="mlp_fwd",
    )(*arrays, *([centre] * gated), w_in, w_out)


def mlp_backward(terms, w_out, w_in, slope, length, transposed=True, columns=(0, 0), factor=None):
    kinds, arrays, specs, block, halves, steps = mlp_blocks(terms, length)
    rows, width = steps * length, arrays[0].shape[1]
    hidden = slope.shape[1]
    hidden_block = pl.BlockSpec((length, hidden), lambda m: (m, 0))
    once = dict(pipeline_mode=pl.Buffered(1))
    out_block = (
        pl.BlockSpec((hidden, width), lambda m: (0, 0), **once)
        if transposed
        else pl.BlockSpec((width, hidden), lambda m: (0, columns[1]), **once)
    )
    in_block = pl.BlockSpec((width, hidden), lambda m: (0, columns[0]), **once)
    scaled = factor is not None
    return pl.pallas_call(
        functools.partial(mlp_back_kernel, kinds=kinds, transposed=transposed, scaled=scaled),
        grid=(steps,),
        in_specs=[pl.BlockSpec((length, 1), lambda m: (m, 0))] * scaled
        + specs
        + [out_block, in_block, hidden_block],
        out_specs=[block, hidden_block] + halves,
        out_shape=[
            jax.ShapeDtypeStruct((rows, width), BF16),
            jax.ShapeDtypeStruct((rows, hidden), BF16),
        ]
        + [jax.ShapeDtypeStruct((rows // 2, width), BF16)] * 2,
        compiler_params=pltpu.CompilerParams(vmem_limit_bytes=54 * 2**20),
        cost_estimate=pl.CostEstimate(
            flops=4 * rows * width * hidden,
            bytes_accessed=4 * width * hidden + 4 * rows * hidden + 4 * rows * width,
            transcendentals=0,
        ),
        name="mlp_bwd",
    )(*([factor] * scaled), *arrays, w_out, w_in, slope)


def from_bit(value, bit):
    return lax.ppermute(value, "dp", [(i, i ^ bit) for i in range(lax.axis_size("dp"))])


def chip_place():
    place = lax.axis_index("dp")
    return place // 4, place // 2 % 2, place % 2


def ordered(bit, own, other, axis):
    return jnp.where(
        bit == 0, jnp.stack([own, other], axis), jnp.stack([other, own], axis)
    )


def gather_line(value):
    planes = lax.axis_size("dp") // 4
    z = chip_place()[0]
    blocks = jnp.stack([value] + [from_bit(value, 4 * k) for k in range(1, planes)])
    return jnp.stack(
        [lax.dynamic_index_in_dim(blocks, z ^ k, 0, keepdims=False) for k in range(planes)]
    )


def gather_second(line):
    half = line.shape[-1] // 2
    y, x = chip_place()[1:]
    first, second = line[..., :half], line[..., half:]
    first = ordered(y, first, from_bit(first, 2), 1)
    second = ordered(x, second, from_bit(second, 1), 1)
    return first, second


def gather_third(first, second, cuts):
    y, x = chip_place()[1:]
    first_other, second_other = from_bit(first, 1), from_bit(second, 2)
    return (
        [ordered(x, first[at], first_other[at], 2) for at in cuts],
        [ordered(y, second[at], second_other[at], 1) for at in cuts],
    )


def halve(value, bit, axis, partner):
    lower = lax.index_in_dim(value, 0, axis, keepdims=False)
    upper = lax.index_in_dim(value, 1, axis, keepdims=False)
    keep, send = jnp.where(bit == 0, lower, upper), jnp.where(bit == 0, upper, lower)
    return keep.astype(F32) + from_bit(send, partner).astype(F32)


def line_parts(line):
    z = chip_place()[0]
    return [
        from_bit(lax.dynamic_index_in_dim(line, z ^ k, 0, keepdims=False), 4 * k)
        for k in range(1, line.shape[0])
    ]


def line_sum(line, parts):
    total = lax.dynamic_index_in_dim(line, chip_place()[0], 0, keepdims=False).astype(F32)
    for part in parts:
        total = total + part.astype(F32)
    return total


def scatter_chips(first, second, before):
    z, y, x = chip_place()
    first = halve(first, x, 2, 1).astype(BF16)
    second = halve(second, y, 1, 2).astype(BF16)
    line = jnp.concatenate([halve(first, y, 1, 2), halve(second, x, 1, 1)], -1).astype(BF16)
    line, before = lax.optimization_barrier((line, before))
    return line_sum(line, line_parts(line)), before


def fits_paired(mesh):
    return mesh.shape["tensor"] == 2 and mesh.shape["dp"] == 16


def body_paired(
    tokens,
    cont_prompt,
    routes,
    norm1_gain,
    w_query,
    w_key,
    w_value,
    w_attn_out,
    norm2_gain,
    w_ffn_in,
    w_ffn_out,
    centroids,
    expert_in_a,
    expert_out_a,
    expert_in_b,
    expert_out_b,
    grad_out,
):
    experts = lax.axis_size("dp")
    dp_index = lax.axis_index("dp")
    core_zero = lax.axis_index("tensor") == 0
    rows, width = tokens.shape
    rows_dp = 2 * rows
    shard = w_query.shape[0]
    half_heads = w_query.shape[1] // HEAD
    hidden = w_ffn_in.shape[1]
    assert expert_in_a.shape[2] == hidden
    triple = 3 * HEAD
    heads = 2 * half_heads
    both = lambda lower, upper: (jnp.where(core_zero, lower, upper), jnp.where(core_zero, upper, lower))

    route = routes[:, 0]
    slots_per = max(2, (3 * rows + 2 * experts - 1) // (2 * experts))
    capacity = 5 * rows_dp // 4
    onehot = route[:, None] == lax.broadcasted_iota(jnp.int32, (1, experts), 1)
    onehot_low = onehot.astype(BF16)
    below = lax.broadcasted_iota(jnp.int32, (rows, rows), 0) > lax.broadcasted_iota(
        jnp.int32, (rows, rows), 1
    )
    earlier = matmul(below.astype(BF16), onehot_low)
    local_rank = jnp.sum(jnp.where(onehot, earlier, 0.0), 1).astype(jnp.int32)
    target = route * slots_per + local_rank
    half_rows = experts * slots_per
    columns = lax.broadcasted_iota(jnp.int32, (1, half_rows), 1)
    placer = (columns == target[:, None]).astype(BF16)
    counts = jnp.sum(onehot_low.astype(F32), 0).astype(BF16)
    counts_pair = jnp.concatenate(both(counts, swap(counts)), 0)

    qkv_shard = jnp.stack(
        [part.reshape(shard, half_heads, HEAD) for part in (w_query, w_key, w_value)], 2
    ).reshape(shard, half_heads * triple)
    extra = jnp.concatenate([norm1_gain, norm2_gain, counts_pair], 0)
    extra = jnp.pad(extra[None, :], ((0, 7), (0, half_heads * triple - extra.shape[0])))
    planes = experts // 4
    first_shard, second_shard = lax.optimization_barrier(
        (
            jnp.concatenate([qkv_shard, extra], 0),
            jnp.concatenate([w_ffn_in, w_ffn_out.T, w_attn_out.T], 1),
        )
    )
    second_line = lax.all_gather(
        second_shard,
        "dp",
        axis_index_groups=[[4 * z + k for z in range(planes)] for k in range(4)],
    )
    line_one = gather_line(first_shard)
    weight_rows, extra_row = np.s_[..., :shard, :], np.s_[..., shard, :]
    (first_all, extra_all), (last_all, unused) = gather_third(
        *gather_second(line_one), (weight_rows, extra_row)
    )
    qkv_full = jnp.concatenate([first_all, last_all], -1).reshape(width, half_heads * triple)
    extra_all = extra_all.reshape(experts, -1)
    gain_one = extra_all[:, :shard].reshape(width).astype(F32)
    gain_two = extra_all[:, shard : 2 * shard].reshape(width).astype(F32)
    counts_all = extra_all[:, 2 * shard : 2 * shard + 2 * experts].reshape(experts, 2, experts)

    pair_tokens = with_other(tokens).astype(F32)
    normed_one, hat_pair, inv_pair = norm_forward(pair_tokens, gain_one)
    inputs, hat_one, inv_one = pair_tokens[:rows], hat_pair[:rows], inv_pair[:rows]
    rows_one = normed_one.astype(BF16)
    other_t = lax.dot_general(
        qkv_full, rows_one[rows:], (((0,), (1,)), ((), ())), preferred_element_type=F32
    ).astype(BF16)
    own_t = lax.dot_general(
        qkv_full, rows_one[:rows], (((0,), (1,)), ((), ())), preferred_element_type=F32
    ).astype(BF16)
    qkv_t = jnp.concatenate(both(own_t, swap(other_t)), 0).reshape(heads, triple, rows)
    qkv_t, second_line, late_grad = lax.optimization_barrier((qkv_t, second_line, grad_out))
    sent_grad = matmul_tn(placer, late_grad).astype(BF16).reshape(experts, slots_per, width)
    by_head = lax.all_to_all(qkv_t, "dp", split_axis=0, concat_axis=0, tiled=True)

    by_head, sent_grad = lax.optimization_barrier((by_head, sent_grad))
    second_all = lax.all_gather(
        second_line, "dp", axis_index_groups=[[4 * z + k for k in range(4)] for z in range(planes)]
    )
    second_all = second_all.transpose(1, 0, 2, 3).reshape(width, -1)
    attn_half = second_all[:, 2 * hidden :]

    lent = experts // 4
    span = PLEN // rows
    own_blocks = jnp.concatenate([by_head, to_core_zero(by_head[:lent])], 0)
    prompt_kv = jnp.where(core_zero, by_head[:, HEAD:], to_core_one(by_head[:, HEAD:]))
    places = jnp.arange(experts + lent, dtype=jnp.int32)
    follows = cont_prompt * span
    plan_zero = jnp.stack(
        [
            places,
            jnp.where(places < experts, places % span, span),
            jnp.concatenate([places[:experts] // span * span, follows[:lent]], 0),
            jnp.ones_like(places),
        ]
    )
    plan_one = jnp.stack(
        [
            jnp.minimum(places + lent, experts - 1),
            jnp.full_like(places, span),
            jnp.concatenate([follows[lent:], jnp.zeros((2 * lent,), jnp.int32)], 0),
            (places < experts - lent).astype(jnp.int32),
        ]
    )
    plan = jnp.where(core_zero, plan_zero, plan_one)
    attn_blocks, log_sums = attn_forward(plan, own_blocks, prompt_kv)
    lent_back = to_core_one(attn_blocks[experts:])
    attn_own = jnp.concatenate(
        [jnp.where(core_zero, attn_blocks[:lent], lent_back), attn_blocks[lent:experts]], 0
    )
    attn_t = lax.all_to_all(attn_own, "dp", split_axis=0, concat_axis=0, tiled=True).reshape(
        width, rows
    )

    half_width = width // 2
    own_heads, other_heads = both(attn_t[:half_width], attn_t[half_width:])
    attn_other = swap(attn_half)
    hidden_one = (
        inputs
        + lax.dot_general(
            own_heads, attn_half, (((0,), (1,)), ((), ())), preferred_element_type=F32
        )
        + lax.dot_general(
            other_heads, attn_other, (((0,), (1,)), ((), ())), preferred_element_type=F32
        )
    )
    normed_two, hat_two, inv_two = norm_forward(hidden_one, gain_two)
    normed_two = normed_two.astype(BF16)
    rows_two, ffn_act, ffn_slope, ffn_own, ffn_other = mlp_forward(
        [(normed_two, swap(normed_two))],
        second_all,
        second_all,
        hidden,
        rows,
        transposed=True,
        columns=(0, 1),
    )
    hidden_two = hidden_one + ffn_own.astype(F32) + swap(ffn_other).astype(F32)

    sent_rows = (
        matmul_tn(placer, hidden_two.astype(BF16)).astype(BF16).reshape(experts, slots_per, width)
    )
    sent_rows, counts_all = lax.optimization_barrier((sent_rows, counts_all))
    mine = jnp.sum(
        jnp.where(lax.broadcasted_iota(jnp.int32, (1, 1, experts), 2) == dp_index, counts_all.astype(F32), 0.0),
        2,
    )
    per_chip = jnp.sum(mine, 1)
    chip_before = jnp.sum(
        jnp.where(
            lax.broadcasted_iota(jnp.int32, (experts, experts), 1)
            < lax.broadcasted_iota(jnp.int32, (experts, experts), 0),
            per_chip[None, :],
            0.0,
        ),
        1,
    )
    starts = both(chip_before, chip_before + mine[:, 0])
    slot_at = lax.broadcasted_iota(jnp.int32, (1, slots_per), 1).astype(F32)
    kept = jnp.concatenate(
        [(start[:, None] + slot_at < capacity).reshape(-1, 1) for start in starts], 0
    )
    own_rows, sent_grad, kept = lax.optimization_barrier((to_experts(sent_rows), sent_grad, kept))
    own_rows = own_rows.reshape(half_rows, width)
    grad_own = to_experts(sent_grad).reshape(half_rows, width)
    centre = centroids[0]
    length = half_rows // 2
    expert_rows, act_a, slope_a, own_a, other_a, gate_column = mlp_forward(
        [(own_rows, swap(own_rows))],
        expert_in_a[0],
        expert_out_a[0],
        hidden,
        length,
        centre=centroids,
    )
    from_a = (swap(other_a), swap(own_a))
    middle, act_b, slope_b, own_b, other_b = mlp_forward(
        [expert_rows, (own_a, other_a), from_a], expert_in_b[0], expert_out_b[0], hidden, length
    )
    own_b, grad_own = lax.optimization_barrier((own_b, grad_own))
    branch_half = (
        own_a.astype(F32) + from_a[0].astype(F32) + own_b.astype(F32) + swap(other_b).astype(F32)
    )
    gate_value = gate_column[:, 0]
    gate_half = gate_value[:half_rows]
    returned = (
        jnp.where(kept[:half_rows], gate_half[:, None] * branch_half, 0.0)
        .astype(BF16)
        .reshape(experts, slots_per, width)
    )
    came_back = to_experts(returned).reshape(half_rows, width)

    kept_half = kept[:half_rows, 0]
    grad_logit_half = jnp.where(
        kept_half,
        jnp.sum(grad_own.astype(F32) * branch_half, 1) * gate_half * (1.0 - gate_half),
        0.0,
    )
    centre_part = matmul(grad_logit_half, own_rows.astype(F32))
    kept_gate = jnp.where(kept, gate_column, 0.0)
    grad_pair = (grad_own, swap(grad_own))
    grad_b, grad_pre_b, own_m, other_m = mlp_backward(
        [grad_pair], expert_out_b[0], expert_in_b[0], slope_b, length, factor=kept_gate
    )
    from_m = (swap(other_m), swap(own_m))
    grad_a, grad_pre_a, own_x, other_x = mlp_backward(
        [grad_pair, (own_m, other_m), from_m],
        expert_out_a[0],
        expert_in_a[0],
        slope_a,
        length,
        factor=kept_gate,
    )
    grad_rows = (
        own_x.astype(F32)
        + swap(other_x).astype(F32)
        + own_m.astype(F32)
        + from_m[0].astype(F32)
        + grad_logit_half[:, None] * centre.astype(F32)[None, :]
    )
    grad_rows, came_back, act_a, grad_a, expert_rows, grad_pre_a = lax.optimization_barrier(
        (grad_rows.astype(BF16), came_back, act_a, grad_a, expert_rows, grad_pre_a)
    )
    grad_out_a = matmul_tn(act_a, grad_a)
    grad_in_a = matmul_tn(expert_rows, grad_pre_a)
    output = hidden_two + matmul(placer, came_back)
    grad_back = to_experts(grad_rows.reshape(experts, slots_per, width))
    grad_back, grad_out_a, grad_in_a = lax.optimization_barrier((grad_back, grad_out_a, grad_in_a))
    grad_back = grad_back.reshape(half_rows, width)
    grad_two = grad_out.astype(F32) + matmul(placer, grad_back)

    grad_down = grad_two.astype(BF16)
    rows_down, grad_ffn_pre, down_own, down_other = mlp_backward(
        [(grad_down, swap(grad_down))],
        second_all,
        second_all,
        ffn_slope,
        rows,
        transposed=False,
        columns=(0, 1),
    )
    grad_norm_two = down_own.astype(F32) + swap(down_other).astype(F32)
    back_two = norm_backward(grad_norm_two, hat_two, inv_two, gain_two)[0]
    grad_one = grad_two + back_two

    grad_branch_one = grad_one.astype(BF16)
    grad_halves = both(
        *(
            lax.dot_general(
                part, grad_branch_one, (((0,), (1,)), ((), ())), preferred_element_type=F32
            ).astype(BF16)
            for part in (attn_half, attn_other)
        )
    )
    grad_attn, rows_down, ffn_act, rows_two, grad_ffn_pre = lax.optimization_barrier(
        (
            jnp.concatenate(grad_halves, 0).reshape(heads, HEAD, rows),
            rows_down,
            ffn_act,
            rows_two,
            grad_ffn_pre,
        )
    )
    grad_by_head = lax.all_to_all(grad_attn, "dp", split_axis=0, concat_axis=0, tiled=True)
    grad_ffn_out_t = matmul_tn(rows_down, ffn_act)
    grad_ffn_in = matmul_tn(rows_two, grad_ffn_pre)
    part_own, part_other = (
        lax.dot_general(
            grad_branch_one, part, (((0,), (1,)), ((), ())), preferred_element_type=F32
        )
        for part in (own_heads, other_heads)
    )
    grad_attn_half = part_own + swap(part_other.astype(BF16)).astype(F32)
    second_part = jnp.concatenate(
        [grad_ffn_in.astype(BF16), grad_ffn_out_t.astype(BF16), grad_attn_half.astype(BF16)], 1
    )
    second_part = second_part.reshape(planes, 4, shard, -1).transpose(1, 0, 2, 3).reshape(width, -1)
    grad_by_head, second_part = lax.optimization_barrier((grad_by_head, second_part))
    second_plane = lax.psum_scatter(
        second_part,
        "dp",
        scatter_dimension=0,
        axis_index_groups=[[4 * z + k for k in range(4)] for z in range(planes)],
        tiled=True,
    )
    grad_blocks = jnp.concatenate([grad_by_head, to_core_zero(grad_by_head[:lent])], 0)
    grad_own_blocks, grad_prompts = attn_backward(
        plan, own_blocks, prompt_kv, grad_blocks, attn_blocks, log_sums
    )
    lent_grad = to_core_one(grad_own_blocks[experts:])
    prompt_sum = grad_prompts.astype(F32) + to_core_zero(grad_prompts).astype(F32)
    prompt_part = jnp.concatenate(
        [
            grad_own_blocks[:experts, :HEAD],
            (grad_own_blocks[:experts, HEAD:].astype(F32) + prompt_sum).astype(BF16),
        ],
        1,
    )
    cont_part = jnp.concatenate([lent_grad, grad_own_blocks[lent:experts]], 0)
    grad_head, act_b, grad_b, middle, grad_pre_b = lax.optimization_barrier(
        (jnp.where(core_zero, prompt_part, cont_part), act_b, grad_b, middle, grad_pre_b)
    )
    grad_qkv = lax.all_to_all(grad_head, "dp", split_axis=0, concat_axis=0, tiled=True)
    grad_out_b = matmul_tn(act_b, grad_b)
    grad_in_b = matmul_tn(middle, grad_pre_b)
    grad_qkv, grad_out_b, grad_in_b, second_plane = lax.optimization_barrier(
        (grad_qkv, grad_out_b, grad_in_b, second_plane.reshape(planes, shard, -1))
    )
    second_parts = line_parts(second_plane)
    grad_qkv = grad_qkv.reshape(2, half_heads * triple, rows)
    keep_half, send_half = both(grad_qkv[0], grad_qkv[1])
    grad_qkv_t = jnp.concatenate([keep_half, swap(send_half)], 1)
    grad_qkv_w = lax.dot_general(
        rows_one, grad_qkv_t, (((0,), (1,)), ((), ())), preferred_element_type=F32
    ).astype(BF16)
    by_chip = grad_qkv_w.reshape(experts // 4, 2, 2, shard, half_heads * triple)
    half_columns = half_heads * triple // 2
    qkv_sum, second_parts = scatter_chips(
        by_chip[..., :half_columns], by_chip[..., half_columns:], second_parts
    )
    second_sum = line_sum(second_plane, second_parts)
    grad_norm_one = keep_rows(
        lax.dot_general(
            grad_qkv_t, qkv_full, (((0,), (1,)), ((), ())), preferred_element_type=F32
        )
    )
    back_one = norm_backward(grad_norm_one, hat_one, inv_one, gain_one)[0]
    grad_input = grad_one + back_one
    qkv_sum = qkv_sum.reshape(shard, half_heads, 3, HEAD)
    query_shard, key_shard, value_shard = (
        qkv_sum[:, :, part].reshape(shard, half_heads * HEAD) for part in range(3)
    )

    ffn_in_sum = second_sum[:, :hidden]
    gains = jnp.stack(
        [
            jnp.sum(query_shard * w_query + key_shard * w_key + value_shard * w_value, 1)
            / norm1_gain.astype(F32),
            jnp.sum(ffn_in_sum * w_ffn_in, 1) / norm2_gain.astype(F32),
        ]
    )
    gains = gains + swap(gains)
    centre_grad = centre_part + swap(centre_part)
    return (
        output.astype(BF16),
        grad_input.astype(BF16),
        gains[0],
        query_shard,
        key_shard,
        value_shard,
        second_sum[:, 2 * hidden :].T,
        gains[1],
        ffn_in_sum,
        second_sum[:, hidden : 2 * hidden].T,
        centre_grad[None, :],
        grad_in_a[None],
        grad_out_a[None],
        grad_in_b[None],
        grad_out_b[None],
    )


def solution(mesh):
    body = body_paired if fits_paired(mesh) else body_general
    return jax.shard_map(
        body,
        mesh=mesh,
        in_specs=(
            P(("dp", "tensor"), None),
            P(),
            P(("dp", "tensor"), None),
            P("dp"),
            P("dp", "tensor"),
            P("dp", "tensor"),
            P("dp", "tensor"),
            P("tensor", "dp"),
            P("dp"),
            P("dp", "tensor"),
            P("tensor", "dp"),
            P("dp", None),
            P("dp", None, "tensor"),
            P("dp", "tensor", None),
            P("dp", None, "tensor"),
            P("dp", "tensor", None),
            P(("dp", "tensor"), None),
        ),
        out_specs=(
            P(("dp", "tensor"), None),
            P(("dp", "tensor"), None),
            P("dp"),
            P("dp", "tensor"),
            P("dp", "tensor"),
            P("dp", "tensor"),
            P("tensor", "dp"),
            P("dp"),
            P("dp", "tensor"),
            P("tensor", "dp"),
            P("dp", None),
            P("dp", None, "tensor"),
            P("dp", "tensor", None),
            P("dp", None, "tensor"),
            P("dp", "tensor", None),
        ),
        check_vma=False,
    )
```

```python
import functools

import jax
import jax.numpy as jnp
import numpy as np
from jax import lax
from jax.experimental import pallas as pl
from jax.experimental.pallas import tpu as pltpu
from jax.sharding import PartitionSpec as P

HEAD = 64
PLEN = 4096
CONT = 512


def shortened(value):

    def short(part):
        return part.astype(jnp.bfloat16) if part.dtype == jnp.float32 else part

    return jax.tree.map(short, value)


def carried_in(value, axis, combine, identity):
    peers, place = (lax.axis_size(axis), lax.axis_index(axis))
    everything = lax.all_gather(value, axis)
    start = jnp.broadcast_to(jnp.asarray(identity, value.dtype), value.shape)

    def turn(k, before):
        reached = k < place
        new = combine(before, everything[k])
        return jnp.where(reached, new, before)

    return lax.fori_loop(0, peers, turn, start)


def rows_gather(value):
    return lax.all_gather(value, "tensor", axis=0, tiled=True)


def rows_scatter(value):
    return lax.psum_scatter(
        value.astype(jnp.bfloat16), "tensor", scatter_dimension=0, tiled=True
    ).astype(jnp.float32)


def pair_total(value):
    return jax.tree.map(lambda part: part.astype(jnp.float32), lax.psum(shortened(value), "tensor"))


def to_experts(value):
    return lax.all_to_all(value, "dp", split_axis=0, concat_axis=0, tiled=True)


def matmul(left, right):
    return jnp.dot(left, right, preferred_element_type=jnp.float32)


def matmul_tn(left, right):
    return lax.dot_general(
        left, right, (((0,), (0,)), ((), ())), preferred_element_type=jnp.float32
    )


def matmul_nt(left, right):
    return lax.dot_general(
        left, right, (((1,), (1,)), ((), ())), preferred_element_type=jnp.float32
    )


def norm_forward(hidden, gain):
    mean_row = jnp.mean(hidden, -1, keepdims=True)
    centred = hidden - mean_row
    scale_inv = lax.rsqrt(jnp.mean(centred * centred, -1, keepdims=True) + 1e-05)
    normed = centred * scale_inv
    return (normed * gain, normed, scale_inv)


def norm_backward(grad_m, normed, scale_inv, gain):
    grad_hat = grad_m * gain
    inner = (
        grad_hat
        - jnp.mean(grad_hat, -1, keepdims=True)
        - normed * jnp.mean(grad_hat * normed, -1, keepdims=True)
    )
    return (inner * scale_inv, jnp.sum(grad_m * normed, 0))


def gelu_grad(preact, grad):
    unused, pull = jax.vjp(jax.nn.gelu, preact)
    return pull(grad)[0]


def add_counts(first, second):
    return first + second


def attend(queries, keys, values, allowed, heads):
    scale = HEAD ** (-0.5)

    def head_step(head, carry):
        outputs, log_sums = carry
        query_h = lax.dynamic_slice_in_dim(queries, head * HEAD, HEAD, 1)
        key_h = lax.dynamic_slice_in_dim(keys, head * HEAD, HEAD, 1)
        value_h = lax.dynamic_slice_in_dim(values, head * HEAD, HEAD, 1)
        scores = jnp.where(allowed, matmul_nt(query_h, key_h) * scale, -1e30)
        top_score = jnp.max(scores, 1, keepdims=True)
        expo = jnp.exp(scores - top_score)
        total = jnp.sum(expo, 1, keepdims=True)
        probs = (expo / total).astype(jnp.bfloat16)
        outputs = lax.dynamic_update_slice_in_dim(outputs, matmul(probs, value_h), head * HEAD, 1)
        log_sums = lax.dynamic_update_index_in_dim(
            log_sums, top_score[:, 0] + jnp.log(total[:, 0]), head, 0
        )
        return (outputs, log_sums)

    start_state = (
        jnp.zeros((queries.shape[0], heads * HEAD), jnp.float32),
        jnp.zeros((heads, queries.shape[0]), jnp.float32),
    )
    return lax.fori_loop(0, heads, head_step, start_state)


def attend_back(queries, keys, values, allowed, log_sums, grad_attended, heads):
    scale = HEAD ** (-0.5)

    def head_step(head, carry):
        grad_q, grad_k, grad_v = carry
        query_h = lax.dynamic_slice_in_dim(queries, head * HEAD, HEAD, 1)
        key_h = lax.dynamic_slice_in_dim(keys, head * HEAD, HEAD, 1)
        value_h = lax.dynamic_slice_in_dim(values, head * HEAD, HEAD, 1)
        grad_o = lax.dynamic_slice_in_dim(grad_attended, head * HEAD, HEAD, 1)
        scores = jnp.where(allowed, matmul_nt(query_h, key_h) * scale, -1e30)
        probs = jnp.exp(
            scores - lax.dynamic_index_in_dim(log_sums, head, 0, keepdims=False)[:, None]
        )
        grad_p = matmul_nt(grad_o, value_h)
        grad_s = (probs * (grad_p - jnp.sum(probs * grad_p, 1, keepdims=True))).astype(jnp.bfloat16)
        grad_q = lax.dynamic_update_slice_in_dim(
            grad_q, matmul(grad_s, key_h) * scale, head * HEAD, 1
        )
        grad_k = lax.dynamic_update_slice_in_dim(
            grad_k, matmul_tn(grad_s, query_h) * scale, head * HEAD, 1
        )
        grad_v = lax.dynamic_update_slice_in_dim(
            grad_v, matmul_tn(probs.astype(jnp.bfloat16), grad_o), head * HEAD, 1
        )
        return (grad_q, grad_k, grad_v)

    start_state = (
        jnp.zeros(queries.shape, jnp.float32),
        jnp.zeros(keys.shape, jnp.float32),
        jnp.zeros(values.shape, jnp.float32),
    )
    return lax.fori_loop(0, heads, head_step, start_state)


def add_block(buffer, block, start):
    length = block.shape[0]
    current = lax.dynamic_slice_in_dim(buffer, start, length, 0)
    return lax.dynamic_update_slice_in_dim(buffer, current + block, start, 0)


def body_general(
    tokens,
    cont_prompt,
    routes,
    norm1_gain,
    w_query,
    w_key,
    w_value,
    w_attn_out,
    norm2_gain,
    w_ffn_in,
    w_ffn_out,
    centroids,
    expert_in_a,
    expert_out_a,
    expert_in_b,
    expert_out_b,
    grad_out,
):
    experts = lax.axis_size("dp")
    pair_size = lax.axis_size("tensor")
    dp_index = lax.axis_index("dp")
    tensor_index = lax.axis_index("tensor")
    rows_dev = tokens.shape[0]
    rows_dp = rows_dev * pair_size
    prm_dev = rows_dp - CONT
    pkeys = experts * prm_dev
    heads = w_query.shape[1] // HEAD
    width = tokens.shape[1]
    span = PLEN // prm_dev
    owner_start = dp_index // span * PLEN
    mapped_start = cont_prompt[dp_index] * PLEN
    gain_one, query_full, key_full, value_full, attn_full, gain_two, ffn_in_full, ffn_out_full = (
        lax.all_gather(norm1_gain, "dp", axis=0, tiled=True),
        lax.all_gather(w_query, "dp", axis=0, tiled=True),
        lax.all_gather(w_key, "dp", axis=0, tiled=True),
        lax.all_gather(w_value, "dp", axis=0, tiled=True),
        lax.all_gather(w_attn_out, "dp", axis=1, tiled=True),
        lax.all_gather(norm2_gain, "dp", axis=0, tiled=True),
        lax.all_gather(w_ffn_in, "dp", axis=0, tiled=True),
        lax.all_gather(w_ffn_out, "dp", axis=1, tiled=True),
    )
    inputs = tokens.astype(jnp.float32)
    normed_one, hat_one, inv_one = norm_forward(inputs, gain_one.astype(jnp.float32))
    rows_one = rows_gather(normed_one.astype(jnp.bfloat16))
    queries = matmul(rows_one, query_full).astype(jnp.bfloat16)
    keys_own = matmul(rows_one, key_full).astype(jnp.bfloat16)
    values_own = matmul(rows_one, value_full).astype(jnp.bfloat16)
    prompt_keys, prompt_values = (
        lax.all_gather(keys_own[:prm_dev], "dp", axis=0, tiled=True),
        lax.all_gather(values_own[:prm_dev], "dp", axis=0, tiled=True),
    )
    keys_first = lax.dynamic_slice_in_dim(prompt_keys, owner_start, PLEN, 0)
    values_first = lax.dynamic_slice_in_dim(prompt_values, owner_start, PLEN, 0)
    first_row = lax.broadcasted_iota(jnp.int32, (prm_dev, 1), 0)
    first_column = lax.broadcasted_iota(jnp.int32, (1, PLEN), 1)
    allowed_first = first_column <= dp_index % span * prm_dev + first_row
    keys_second = jnp.concatenate(
        [lax.dynamic_slice_in_dim(prompt_keys, mapped_start, PLEN, 0), keys_own[prm_dev:]], 0
    )
    values_second = jnp.concatenate(
        [lax.dynamic_slice_in_dim(prompt_values, mapped_start, PLEN, 0), values_own[prm_dev:]], 0
    )
    second_row = lax.broadcasted_iota(jnp.int32, (CONT, 1), 0)
    second_column = lax.broadcasted_iota(jnp.int32, (1, PLEN + CONT), 1)
    allowed_second = (second_column < PLEN) | (second_column - PLEN <= second_row)
    attn_first, sums_first = attend(
        queries[:prm_dev], keys_first, values_first, allowed_first, heads
    )
    attn_second, sums_second = attend(
        queries[prm_dev:], keys_second, values_second, allowed_second, heads
    )
    attn_low = jnp.concatenate([attn_first, attn_second], 0).astype(jnp.bfloat16)
    hidden_one = inputs + rows_scatter(matmul(attn_low, attn_full))
    normed_two, hat_two, inv_two = norm_forward(hidden_one, gain_two.astype(jnp.float32))
    rows_two = rows_gather(normed_two.astype(jnp.bfloat16))
    ffn_pre = matmul(rows_two, ffn_in_full)
    ffn_act = jax.nn.gelu(ffn_pre).astype(jnp.bfloat16)
    hidden_two = hidden_one + rows_scatter(matmul(ffn_act, ffn_out_full))
    route = routes[:, 0]
    slots_per = max(2, (3 * rows_dev + 2 * experts - 1) // (2 * experts))
    capacity = 5 * rows_dp // 4
    expert_ids = lax.broadcasted_iota(jnp.int32, (1, experts), 1)
    onehot = (route[:, None] == expert_ids).astype(jnp.int32)
    offsets = carried_in(
        jnp.sum(onehot, 0), ("dp", "tensor"), add_counts, jnp.zeros((experts,), jnp.int32)
    )
    local_rank = jnp.sum((jnp.cumsum(onehot, 0) - 1) * onehot, 1)
    global_slot = local_rank + jnp.sum(onehot * offsets[None, :], 1)
    kept = global_slot < capacity
    target = route * slots_per + local_rank
    columns = lax.broadcasted_iota(jnp.int32, (1, experts * slots_per), 1)
    placer = ((columns == target[:, None]) & kept[:, None]).astype(jnp.bfloat16)
    sent_rows = (
        matmul_tn(placer, hidden_two.astype(jnp.bfloat16))
        .astype(jnp.bfloat16)
        .reshape(experts, slots_per, width)
    )
    expert_rows = rows_gather(to_experts(sent_rows)).reshape(-1, width)
    centre = centroids[0]
    gate_value = jax.nn.sigmoid(matmul(expert_rows, centre))
    pre_a = matmul(expert_rows, expert_in_a[0])
    act_a = jax.nn.gelu(pre_a).astype(jnp.bfloat16)
    branch_a = pair_total(matmul(act_a, expert_out_a[0]))
    middle = (expert_rows.astype(jnp.float32) + branch_a).astype(jnp.bfloat16)
    pre_b = matmul(middle, expert_in_b[0])
    act_b = jax.nn.gelu(pre_b).astype(jnp.bfloat16)
    branch_b = rows_scatter(matmul(act_b, expert_out_b[0]))
    half_rows = expert_rows.shape[0] // pair_size
    start_row = tensor_index * half_rows
    branch_half = lax.dynamic_slice_in_dim(branch_a, start_row, half_rows, 0) + branch_b
    gate_half = lax.dynamic_slice_in_dim(gate_value, start_row, half_rows, 0)
    returned = (
        (gate_half[:, None] * branch_half).astype(jnp.bfloat16).reshape(experts, slots_per, width)
    )
    came_back = to_experts(returned).reshape(experts * slots_per, width)
    output = hidden_two + matmul(placer, came_back)
    cotangent = grad_out.astype(jnp.float32)
    sent_grad = matmul_tn(placer, grad_out).astype(jnp.bfloat16).reshape(experts, slots_per, width)
    grad_half = to_experts(sent_grad).reshape(half_rows, width)
    grad_returned = rows_gather(grad_half).astype(jnp.float32)
    grad_gate_half = jnp.sum(grad_half.astype(jnp.float32) * branch_half, 1)
    grad_logit_half = grad_gate_half * gate_half * (1.0 - gate_half)
    rows_half = lax.dynamic_slice_in_dim(expert_rows, start_row, half_rows, 0)
    centre_part = matmul(grad_logit_half, rows_half.astype(jnp.float32))
    grad_branch = gate_value[:, None] * grad_returned
    grad_b = grad_branch.astype(jnp.bfloat16)
    grad_pre_b = gelu_grad(pre_b, matmul_nt(grad_b, expert_out_b[0])).astype(jnp.bfloat16)
    grad_out_b = matmul_tn(act_b, grad_b)
    grad_in_b = matmul_tn(middle, grad_pre_b)
    grad_middle = pair_total(matmul_nt(grad_pre_b, expert_in_b[0]))
    grad_a = (grad_branch + grad_middle).astype(jnp.bfloat16)
    grad_pre_a = gelu_grad(pre_a, matmul_nt(grad_a, expert_out_a[0])).astype(jnp.bfloat16)
    grad_out_a = matmul_tn(act_a, grad_a)
    grad_in_a = matmul_tn(expert_rows, grad_pre_a)
    grad_rows = (
        rows_scatter(matmul_nt(grad_pre_a, expert_in_a[0]))
        + lax.dynamic_slice_in_dim(grad_middle, start_row, half_rows, 0)
        + grad_logit_half[:, None] * centre.astype(jnp.float32)[None, :]
    )
    grad_back = to_experts(
        grad_rows.astype(jnp.bfloat16).reshape(experts, slots_per, width)
    ).reshape(experts * slots_per, width)
    grad_two = cotangent + matmul(placer, grad_back)
    gain_one, query_full, key_full, value_full, attn_full, gain_two, ffn_in_full, ffn_out_full = (
        lax.all_gather(norm1_gain, "dp", axis=0, tiled=True),
        lax.all_gather(w_query, "dp", axis=0, tiled=True),
        lax.all_gather(w_key, "dp", axis=0, tiled=True),
        lax.all_gather(w_value, "dp", axis=0, tiled=True),
        lax.all_gather(w_attn_out, "dp", axis=1, tiled=True),
        lax.all_gather(norm2_gain, "dp", axis=0, tiled=True),
        lax.all_gather(w_ffn_in, "dp", axis=0, tiled=True),
        lax.all_gather(w_ffn_out, "dp", axis=1, tiled=True),
    )
    rows_down = rows_gather(grad_two.astype(jnp.bfloat16))
    grad_ffn_pre = gelu_grad(ffn_pre, matmul_nt(rows_down, ffn_out_full)).astype(jnp.bfloat16)
    grad_ffn_out = matmul_tn(ffn_act, rows_down)
    grad_ffn_in = matmul_tn(rows_two, grad_ffn_pre)
    grad_norm_two = rows_scatter(matmul_nt(grad_ffn_pre, ffn_in_full))
    back_two, grad_gain_two = norm_backward(
        grad_norm_two, hat_two, inv_two, gain_two.astype(jnp.float32)
    )
    grad_one = grad_two + back_two
    rows_attn = rows_gather(grad_one.astype(jnp.bfloat16))
    grad_attn_out = matmul_tn(attn_low, rows_attn)
    grad_attended = matmul_nt(rows_attn, attn_full).astype(jnp.bfloat16)
    grad_q_first, grad_k_first, grad_v_first = attend_back(
        queries[:prm_dev],
        keys_first,
        values_first,
        allowed_first,
        sums_first,
        grad_attended[:prm_dev],
        heads,
    )
    grad_q_second, grad_k_second, grad_v_second = attend_back(
        queries[prm_dev:],
        keys_second,
        values_second,
        allowed_second,
        sums_second,
        grad_attended[prm_dev:],
        heads,
    )
    local_width = keys_own.shape[1]
    buffer_k = jnp.zeros((pkeys, local_width), jnp.float32)
    buffer_v = jnp.zeros((pkeys, local_width), jnp.float32)
    buffer_k = add_block(
        add_block(buffer_k, grad_k_first, owner_start), grad_k_second[:PLEN], mapped_start
    )
    buffer_v = add_block(
        add_block(buffer_v, grad_v_first, owner_start), grad_v_second[:PLEN], mapped_start
    )
    prompt_grad_k, prompt_grad_v = (
        lax.psum_scatter(buffer_k, "dp", scatter_dimension=0, tiled=True),
        lax.psum_scatter(buffer_v, "dp", scatter_dimension=0, tiled=True),
    )
    grad_keys = jnp.concatenate([prompt_grad_k, grad_k_second[PLEN:]], 0).astype(jnp.bfloat16)
    grad_values = jnp.concatenate([prompt_grad_v, grad_v_second[PLEN:]], 0).astype(jnp.bfloat16)
    grad_queries = jnp.concatenate([grad_q_first, grad_q_second], 0).astype(jnp.bfloat16)
    grad_query = matmul_tn(rows_one, grad_queries)
    grad_key = matmul_tn(rows_one, grad_keys)
    grad_value = matmul_tn(rows_one, grad_values)
    grad_norm_one = rows_scatter(
        matmul_nt(grad_queries, query_full)
        + matmul_nt(grad_keys, key_full)
        + matmul_nt(grad_values, value_full)
    )
    back_one, grad_gain_one = norm_backward(
        grad_norm_one, hat_one, inv_one, gain_one.astype(jnp.float32)
    )
    grad_input = grad_one + back_one
    (
        gain_one_part,
        query_shard,
        key_shard,
        value_shard,
        attn_shard,
        gain_two_part,
        ffn_in_shard,
        ffn_out_shard,
    ) = (
        lax.psum_scatter(grad_gain_one, "dp", scatter_dimension=0, tiled=True),
        lax.psum_scatter(grad_query, "dp", scatter_dimension=0, tiled=True),
        lax.psum_scatter(grad_key, "dp", scatter_dimension=0, tiled=True),
        lax.psum_scatter(grad_value, "dp", scatter_dimension=0, tiled=True),
        lax.psum_scatter(grad_attn_out, "dp", scatter_dimension=1, tiled=True),
        lax.psum_scatter(grad_gain_two, "dp", scatter_dimension=0, tiled=True),
        lax.psum_scatter(grad_ffn_in, "dp", scatter_dimension=0, tiled=True),
        lax.psum_scatter(grad_ffn_out, "dp", scatter_dimension=1, tiled=True),
    )
    gain_one_shard, gain_two_shard, centre_grad = pair_total(
        (gain_one_part, gain_two_part, centre_part)
    )
    return (
        output.astype(jnp.bfloat16),
        grad_input.astype(jnp.bfloat16),
        gain_one_shard,
        query_shard,
        key_shard,
        value_shard,
        attn_shard,
        gain_two_shard,
        ffn_in_shard,
        ffn_out_shard,
        centre_grad[None, :],
        grad_in_a[None],
        grad_out_a[None],
        grad_in_b[None],
        grad_out_b[None],
    )


LOG2E = 1.4426950408889634
GELU_A = 0.7978845608028654
GELU_B = 0.044715
BF16 = jnp.bfloat16
F32 = jnp.float32


def dot_tt(left, right):
    return lax.dot_general(left, right, (((0,), (0,)), ((), ())), preferred_element_type=F32)


def beside(blocks, at, count, start, stop):
    return jnp.concatenate([blocks[at + j, start:stop, :] for j in range(count)], 1)


def in_groups(sizes, first, count, take, carry):
    for size in sizes:
        groups = count // size
        step = take(size)
        carry = lax.fori_loop(
            0, groups, lambda k, value, at=first, n=size, f=step: f(at + k * n, value), carry
        )
        first, count = first + groups * size, count - groups * size
    return carry


def attn_fwd_kernel(plan, own, prompts, out, log_sums, values, *, head, factor):
    step_id = pl.program_id(0)
    block, full, first = plan[0, step_id], plan[1, step_id], plan[2, step_id]

    def with_ones(value):
        return jnp.concatenate([value.T, jnp.ones((value.shape[1], head), BF16)], 1)

    @pl.when(step_id == 0)
    def _():
        def turn(k, carry):
            values[k] = with_ones(prompts[k, head : 2 * head, :])
            return carry

        lax.fori_loop(0, prompts.shape[0], turn, 0)

    @pl.when(plan[3, step_id] > 0)
    def _():
        query = own[block, 0:head, :].T
        scores = matmul(query, own[block, head : 2 * head, :])
        query_at = lax.broadcasted_iota(jnp.int32, scores.shape, 0)
        key_at = lax.broadcasted_iota(jnp.int32, scores.shape, 1)
        scores = jnp.where(key_at <= query_at, scores, -1e30)
        top = jnp.max(scores, 1, keepdims=True) * factor
        expo = jnp.exp2(scores * factor - top)
        result = matmul(expo.astype(BF16), with_ones(own[block, 2 * head : 3 * head, :]))

        def take(count):
            def step(at, carry):
                before, result = carry
                scores = matmul(query, beside(prompts, at, count, 0, head))
                top = jnp.maximum(before, jnp.max(scores, 1, keepdims=True) * factor)
                expo = jnp.exp2(scores * factor - top).astype(BF16)
                rows = jnp.concatenate([values[at + j] for j in range(count)], 0)
                return top, result * jnp.exp2(before - top) + matmul(expo, rows)

            return step

        top, result = in_groups((4, 2, 1), first, full, take, (top, result))
        result = result.T
        total = result[head : head + 1]
        out[block] = (result[:head] / total).astype(BF16)
        top = jnp.broadcast_to(top, (top.shape[0], 128)).T[0:1]
        log_sums[block] = top + jnp.log2(total)


def attn_bwd_kernel(
    plan, own, prompts, grad, out, log_sums, grad_own, grad_prompts, sum_k, sum_v, *, head, factor, scale
):
    step_id = pl.program_id(0)
    block, full, first = plan[0, step_id], plan[1, step_id], plan[2, step_id]

    @pl.when(step_id == 0)
    def _():
        sum_k[...] = jnp.zeros_like(sum_k)
        sum_v[...] = jnp.zeros_like(sum_v)

    @pl.when(plan[3, step_id] > 0)
    def _():
        query_t, grad_t, log_sum = own[block, 0:head, :], grad[block], log_sums[block]
        inner = jnp.sum(grad_t.astype(F32) * out[block].astype(F32), 0, keepdims=True)
        query, grad_o = query_t.T, grad_t.T

        def tile(key, value, diagonal):
            probs = jnp.exp2(dot_tt(key, query_t) * factor - log_sum)
            if diagonal:
                key_at = lax.broadcasted_iota(jnp.int32, probs.shape, 0)
                query_at = lax.broadcasted_iota(jnp.int32, probs.shape, 1)
                probs = jnp.where(key_at <= query_at, probs, 0.0)
            grad_s = (probs * (dot_tt(value, grad_t) - inner)).astype(BF16)
            return matmul(grad_s, query), matmul(probs.astype(BF16), grad_o), matmul(key, grad_s)

        grad_k, grad_v, grad_q = tile(
            own[block, head : 2 * head, :], own[block, 2 * head : 3 * head, :], True
        )
        grad_own[block, head : 2 * head, :] = (grad_k * scale).T.astype(BF16)
        grad_own[block, 2 * head : 3 * head, :] = grad_v.T.astype(BF16)

        def take(count):
            def step(at, grad_q):
                more_k, more_v, more_q = tile(
                    beside(prompts, at, count, 0, head),
                    beside(prompts, at, count, head, 2 * head),
                    False,
                )
                length = more_k.shape[0] // count
                for j in range(count):
                    sum_k[at + j] += more_k[j * length : (j + 1) * length]
                    sum_v[at + j] += more_v[j * length : (j + 1) * length]
                return grad_q + more_q

            return step

        grad_q = in_groups((4, 2, 1), first, full, take, grad_q)
        grad_own[block, 0:head, :] = (grad_q * scale).astype(BF16)

    @pl.when(step_id == pl.num_programs(0) - 1)
    def _():
        def finish(k, carry):
            grad_prompts[k, 0:head, :] = (sum_k[k] * scale).T.astype(BF16)
            grad_prompts[k, head : 2 * head, :] = sum_v[k].T.astype(BF16)
            return carry

        lax.fori_loop(0, sum_k.shape[0], finish, 0)


def attn_forward(plan, own, prompts):
    blocks, triple, length = own.shape
    head = triple // 3
    whole = pl.BlockSpec(memory_space=pltpu.VMEM)
    return pl.pallas_call(
        functools.partial(attn_fwd_kernel, head=head, factor=head**-0.5 * LOG2E),
        grid_spec=pltpu.PrefetchScalarGridSpec(
            num_scalar_prefetch=1,
            grid=(plan.shape[1],),
            in_specs=[whole, whole],
            out_specs=[whole, whole],
            scratch_shapes=[pltpu.VMEM((prompts.shape[0], length, 2 * head), BF16)],
        ),
        out_shape=[
            jax.ShapeDtypeStruct((blocks, head, length), BF16),
            jax.ShapeDtypeStruct((blocks, 1, length), F32),
        ],
        compiler_params=pltpu.CompilerParams(vmem_limit_bytes=40 * 2**20),
        cost_estimate=pl.CostEstimate(
            flops=100 * length * length * 256 * 4,
            bytes_accessed=8 * 2**20,
            transcendentals=100 * length * length,
        ),
        name="attn_fwd",
    )(plan, own, prompts)


def attn_backward(plan, own, prompts, grad, out, log_sums):
    blocks, triple, length = own.shape
    head = triple // 3
    whole = pl.BlockSpec(memory_space=pltpu.VMEM)
    return pl.pallas_call(
        functools.partial(
            attn_bwd_kernel, head=head, factor=head**-0.5 * LOG2E, scale=head**-0.5
        ),
        grid_spec=pltpu.PrefetchScalarGridSpec(
            num_scalar_prefetch=1,
            grid=(plan.shape[1],),
            in_specs=[whole] * 5,
            out_specs=[whole, whole],
            scratch_shapes=[pltpu.VMEM((prompts.shape[0], length, head), F32)] * 2,
        ),
        out_shape=[
            jax.ShapeDtypeStruct(own.shape, BF16),
            jax.ShapeDtypeStruct(prompts.shape, BF16),
        ],
        compiler_params=pltpu.CompilerParams(vmem_limit_bytes=48 * 2**20),
        cost_estimate=pl.CostEstimate(
            flops=100 * length * length * 256 * 10,
            bytes_accessed=16 * 2**20,
            transcendentals=100 * length * length,
        ),
        name="attn_bwd",
    )(plan, own, prompts, grad, out, log_sums)


def swap(value):
    return lax.ppermute(value, "tensor", [(0, 1), (1, 0)])


def to_core_one(value):
    return lax.ppermute(value, "tensor", [(0, 1)])


def to_core_zero(value):
    return lax.ppermute(value, "tensor", [(1, 0)])


def with_other(value):
    return jnp.concatenate([value, swap(value)], 0)


def keep_rows(value):
    half = value.shape[0] // 2
    return value[:half].astype(F32) + swap(value[half:].astype(BF16)).astype(F32)


def gelu_pair(preact):
    square = preact * preact
    gate = 0.5 + 0.5 * jnp.tanh(preact * (GELU_A + GELU_A * GELU_B * square))
    act = preact * gate
    slope = gate + act * (1.0 - gate) * (2.0 * GELU_A + 6.0 * GELU_A * GELU_B * square)
    return act.astype(BF16), slope.astype(BF16)


def by_halves(run):
    early = pl.program_id(0) < pl.num_programs(0) // 2
    pl.when(early)(functools.partial(run, 0))
    pl.when(jnp.logical_not(early))(functools.partial(run, 1))


def take_terms(refs, kinds, half):
    values, at = [], 0
    for paired in kinds:
        values.append(refs[at + half * paired][...])
        at += 1 + paired
    return values, refs[at:]


def mlp_kernel(*refs, kinds, transposed, gated):
    def run(half):
        terms, rest = take_terms(refs, kinds, half)
        rows = terms[0]
        if len(terms) > 1:
            total = rows.astype(F32)
            for term in terms[1:]:
                total = total + term.astype(F32)
            rows = total.astype(BF16)
        if gated:
            centre, rest = rest[0], rest[1:]
            logit = jnp.sum(rows.astype(F32) * centre[...].astype(F32), 1, keepdims=True)
            rest[-1][...] = 1.0 / (1.0 + jnp.exp(-logit))
        w_in, w_out, kept_rows, kept_act, kept_slope, *results = rest[:7]
        kept_rows[...] = rows
        act, slope = gelu_pair(matmul(rows, w_in[...]))
        kept_act[...] = act
        kept_slope[...] = slope
        product = matmul_nt if transposed else matmul
        results[half][...] = product(act, w_out[...]).astype(BF16)

    by_halves(run)


def mlp_back_kernel(*refs, kinds, transposed, scaled):
    def run(half):
        factor, rest = (refs[0], refs[1:]) if scaled else (None, refs)
        terms, rest = take_terms(rest, kinds, half)
        grad = terms[0]
        if scaled:
            total = factor[...] * grad.astype(F32)
            for term in terms[1:]:
                total = total + term.astype(F32)
            grad = total.astype(BF16)
        w_out, w_in, slope, kept_grad, kept_pre, *results = rest
        kept_grad[...] = grad
        grad = (matmul_nt if transposed else matmul)(grad, w_out[...])
        grad_pre = (grad * slope[...].astype(F32)).astype(BF16)
        kept_pre[...] = grad_pre
        results[half][...] = matmul_nt(grad_pre, w_in[...]).astype(BF16)

    by_halves(run)


def mlp_blocks(terms, length):
    paired = [isinstance(term, tuple) for term in terms]
    arrays = [part for term in terms for part in (term if isinstance(term, tuple) else (term,))]
    half = max(part.shape[0] // length // (1 + (not pair)) for term, pair in zip(terms, paired) for part in (term if pair else (term,)))
    width = arrays[0].shape[1]
    block = pl.BlockSpec((length, width), lambda m: (m, 0))
    halves = [
        pl.BlockSpec((length, width), lambda m: (jnp.minimum(m, half - 1), 0)),
        pl.BlockSpec((length, width), lambda m: (jnp.maximum(m - half, 0), 0)),
    ]
    specs = [spec for pair in paired for spec in (halves if pair else [block])]
    return tuple(paired), arrays, specs, block, halves, 2 * half


def mlp_forward(terms, w_in, w_out, hidden, length, transposed=False, columns=(0, 0), centre=None):
    kinds, arrays, specs, block, halves, steps = mlp_blocks(terms, length)
    rows, width = steps * length, arrays[0].shape[1]
    hidden_block = pl.BlockSpec((length, hidden), lambda m: (m, 0))
    once = dict(pipeline_mode=pl.Buffered(1))
    in_block = pl.BlockSpec((width, hidden), lambda m: (0, columns[0]), **once)
    out_block = (
        pl.BlockSpec((width, hidden), lambda m: (0, columns[1]), **once)
        if transposed
        else pl.BlockSpec((hidden, width), lambda m: (0, 0), **once)
    )
    gated = centre is not None
    return pl.pallas_call(
        functools.partial(mlp_kernel, kinds=kinds, transposed=transposed, gated=gated),
        grid=(steps,),
        in_specs=specs + [pl.BlockSpec((1, width), lambda m: (0, 0))] * gated + [in_block, out_block],
        out_specs=[block, hidden_block, hidden_block]
        + halves
        + [pl.BlockSpec((length, 1), lambda m: (m, 0))] * gated,
        out_shape=[jax.ShapeDtypeStruct((rows, width), BF16)]
        + [jax.ShapeDtypeStruct((rows, hidden), BF16)] * 2
        + [jax.ShapeDtypeStruct((rows // 2, width), BF16)] * 2
        + [jax.ShapeDtypeStruct((rows, 1), F32)] * gated,
        compiler_params=pltpu.CompilerParams(vmem_limit_bytes=54 * 2**20),
        cost_estimate=pl.CostEstimate(
            flops=rows * width * hidden,
            bytes_accessed=width * hidden + rows * hidden + rows * width,
            transcendentals=0,
        ),
        name="mlp_fwd",
    )(*arrays, *([centre] * gated), w_in, w_out)


def mlp_backward(terms, w_out, w_in, slope, length, transposed=True, columns=(0, 0), factor=None):
    kinds, arrays, specs, block, halves, steps = mlp_blocks(terms, length)
    rows, width = steps * length, arrays[0].shape[1]
    hidden = slope.shape[1]
    hidden_block = pl.BlockSpec((length, hidden), lambda m: (m, 0))
    once = dict(pipeline_mode=pl.Buffered(1))
    out_block = (
        pl.BlockSpec((hidden, width), lambda m: (0, 0), **once)
        if transposed
        else pl.BlockSpec((width, hidden), lambda m: (0, columns[1]), **once)
    )
    in_block = pl.BlockSpec((width, hidden), lambda m: (0, columns[0]), **once)
    scaled = factor is not None
    return pl.pallas_call(
        functools.partial(mlp_back_kernel, kinds=kinds, transposed=transposed, scaled=scaled),
        grid=(steps,),
        in_specs=[pl.BlockSpec((length, 1), lambda m: (m, 0))] * scaled
        + specs
        + [out_block, in_block, hidden_block],
        out_specs=[block, hidden_block] + halves,
        out_shape=[
            jax.ShapeDtypeStruct((rows, width), BF16),
            jax.ShapeDtypeStruct((rows, hidden), BF16),
        ]
        + [jax.ShapeDtypeStruct((rows // 2, width), BF16)] * 2,
        compiler_params=pltpu.CompilerParams(vmem_limit_bytes=54 * 2**20),
        cost_estimate=pl.CostEstimate(
            flops=4 * rows * width * hidden,
            bytes_accessed=4 * width * hidden + 4 * rows * hidden + 4 * rows * width,
            transcendentals=0,
        ),
        name="mlp_bwd",
    )(*([factor] * scaled), *arrays, w_out, w_in, slope)


def from_bit(value, bit):
    return lax.ppermute(value, "dp", [(i, i ^ bit) for i in range(lax.axis_size("dp"))])


def chip_place():
    place = lax.axis_index("dp")
    return place // 4, place // 2 % 2, place % 2


def ordered(bit, own, other, axis):
    return jnp.where(
        bit == 0, jnp.stack([own, other], axis), jnp.stack([other, own], axis)
    )


def gather_line(value):
    planes = lax.axis_size("dp") // 4
    z = chip_place()[0]
    blocks = jnp.stack([value] + [from_bit(value, 4 * k) for k in range(1, planes)])
    return jnp.stack(
        [lax.dynamic_index_in_dim(blocks, z ^ k, 0, keepdims=False) for k in range(planes)]
    )


def gather_second(line):
    half = line.shape[-1] // 2
    y, x = chip_place()[1:]
    first, second = line[..., :half], line[..., half:]
    first = ordered(y, first, from_bit(first, 2), 1)
    second = ordered(x, second, from_bit(second, 1), 1)
    return first, second


def gather_third(first, second, cuts):
    y, x = chip_place()[1:]
    first_other, second_other = from_bit(first, 1), from_bit(second, 2)
    return (
        [ordered(x, first[at], first_other[at], 2) for at in cuts],
        [ordered(y, second[at], second_other[at], 1) for at in cuts],
    )


def halve(value, bit, axis, partner):
    lower = lax.index_in_dim(value, 0, axis, keepdims=False)
    upper = lax.index_in_dim(value, 1, axis, keepdims=False)
    keep, send = jnp.where(bit == 0, lower, upper), jnp.where(bit == 0, upper, lower)
    return keep.astype(F32) + from_bit(send, partner).astype(F32)


def scatter_chips(first, second):
    planes = first.shape[0]
    z, y, x = chip_place()
    first = halve(first, x, 2, 1).astype(BF16)
    second = halve(second, y, 1, 2).astype(BF16)
    line = jnp.concatenate([halve(first, y, 1, 2), halve(second, x, 1, 1)], -1).astype(BF16)
    total = lax.dynamic_index_in_dim(line, z, 0, keepdims=False).astype(F32)
    for k in range(1, planes):
        part = lax.dynamic_index_in_dim(line, z ^ k, 0, keepdims=False)
        total = total + from_bit(part, 4 * k).astype(F32)
    return total


def fits_paired(mesh):
    return mesh.shape["tensor"] == 2 and mesh.shape["dp"] == 16


def body_paired(
    tokens,
    cont_prompt,
    routes,
    norm1_gain,
    w_query,
    w_key,
    w_value,
    w_attn_out,
    norm2_gain,
    w_ffn_in,
    w_ffn_out,
    centroids,
    expert_in_a,
    expert_out_a,
    expert_in_b,
    expert_out_b,
    grad_out,
):
    experts = lax.axis_size("dp")
    dp_index = lax.axis_index("dp")
    core_zero = lax.axis_index("tensor") == 0
    rows, width = tokens.shape
    rows_dp = 2 * rows
    shard = w_query.shape[0]
    half_heads = w_query.shape[1] // HEAD
    hidden = w_ffn_in.shape[1]
    assert expert_in_a.shape[2] == hidden
    triple = 3 * HEAD
    heads = 2 * half_heads
    both = lambda lower, upper: (jnp.where(core_zero, lower, upper), jnp.where(core_zero, upper, lower))

    route = routes[:, 0]
    slots_per = max(2, (3 * rows + 2 * experts - 1) // (2 * experts))
    capacity = 5 * rows_dp // 4
    onehot = route[:, None] == lax.broadcasted_iota(jnp.int32, (1, experts), 1)
    onehot_low = onehot.astype(BF16)
    below = lax.broadcasted_iota(jnp.int32, (rows, rows), 0) > lax.broadcasted_iota(
        jnp.int32, (rows, rows), 1
    )
    earlier = matmul(below.astype(BF16), onehot_low)
    local_rank = jnp.sum(jnp.where(onehot, earlier, 0.0), 1).astype(jnp.int32)
    target = route * slots_per + local_rank
    half_rows = experts * slots_per
    columns = lax.broadcasted_iota(jnp.int32, (1, half_rows), 1)
    placer = (columns == target[:, None]).astype(BF16)
    counts = jnp.sum(onehot_low.astype(F32), 0).astype(BF16)
    counts_pair = jnp.concatenate(both(counts, swap(counts)), 0)

    qkv_shard = jnp.stack(
        [part.reshape(shard, half_heads, HEAD) for part in (w_query, w_key, w_value)], 2
    ).reshape(shard, half_heads * triple)
    extra = jnp.concatenate([norm1_gain, norm2_gain, counts_pair], 0)
    extra = jnp.pad(extra[None, :], ((0, 7), (0, half_heads * triple - extra.shape[0])))
    planes = experts // 4
    first_shard, second_shard = lax.optimization_barrier(
        (
            jnp.concatenate([qkv_shard, extra], 0),
            jnp.concatenate([w_ffn_in, w_ffn_out.T, w_attn_out.T], 1),
        )
    )
    second_line = lax.all_gather(
        second_shard,
        "dp",
        axis_index_groups=[[4 * z + k for z in range(planes)] for k in range(4)],
    )
    line_one = gather_line(first_shard)
    weight_rows, extra_row = np.s_[..., :shard, :], np.s_[..., shard, :]
    (first_all, extra_all), (last_all, unused) = gather_third(
        *gather_second(line_one), (weight_rows, extra_row)
    )
    qkv_full = jnp.concatenate([first_all, last_all], -1).reshape(width, half_heads * triple)
    extra_all = extra_all.reshape(experts, -1)
    gain_one = extra_all[:, :shard].reshape(width).astype(F32)
    gain_two = extra_all[:, shard : 2 * shard].reshape(width).astype(F32)
    counts_all = extra_all[:, 2 * shard : 2 * shard + 2 * experts].reshape(experts, 2, experts)

    pair_tokens = with_other(tokens).astype(F32)
    normed_one, hat_pair, inv_pair = norm_forward(pair_tokens, gain_one)
    inputs, hat_one, inv_one = pair_tokens[:rows], hat_pair[:rows], inv_pair[:rows]
    rows_one = normed_one.astype(BF16)
    other_t = lax.dot_general(
        qkv_full, rows_one[rows:], (((0,), (1,)), ((), ())), preferred_element_type=F32
    ).astype(BF16)
    own_t = lax.dot_general(
        qkv_full, rows_one[:rows], (((0,), (1,)), ((), ())), preferred_element_type=F32
    ).astype(BF16)
    qkv_t = jnp.concatenate(both(own_t, swap(other_t)), 0).reshape(heads, triple, rows)
    qkv_t, second_line, late_grad = lax.optimization_barrier((qkv_t, second_line, grad_out))
    sent_grad = matmul_tn(placer, late_grad).astype(BF16).reshape(experts, slots_per, width)
    by_head = lax.all_to_all(qkv_t, "dp", split_axis=0, concat_axis=0, tiled=True)

    by_head, sent_grad = lax.optimization_barrier((by_head, sent_grad))
    second_all = lax.all_gather(
        second_line, "dp", axis_index_groups=[[4 * z + k for k in range(4)] for z in range(planes)]
    )
    second_all = second_all.transpose(1, 0, 2, 3).reshape(width, -1)
    attn_half = second_all[:, 2 * hidden :]

    lent = experts // 4
    span = PLEN // rows
    own_blocks = jnp.concatenate([by_head, to_core_zero(by_head[:lent])], 0)
    prompt_kv = jnp.where(core_zero, by_head[:, HEAD:], to_core_one(by_head[:, HEAD:]))
    places = jnp.arange(experts + lent, dtype=jnp.int32)
    follows = cont_prompt * span
    plan_zero = jnp.stack(
        [
            places,
            jnp.where(places < experts, places % span, span),
            jnp.concatenate([places[:experts] // span * span, follows[:lent]], 0),
            jnp.ones_like(places),
        ]
    )
    plan_one = jnp.stack(
        [
            jnp.minimum(places + lent, experts - 1),
            jnp.full_like(places, span),
            jnp.concatenate([follows[lent:], jnp.zeros((2 * lent,), jnp.int32)], 0),
            (places < experts - lent).astype(jnp.int32),
        ]
    )
    plan = jnp.where(core_zero, plan_zero, plan_one)
    attn_blocks, log_sums = attn_forward(plan, own_blocks, prompt_kv)
    lent_back = to_core_one(attn_blocks[experts:])
    attn_own = jnp.concatenate(
        [jnp.where(core_zero, attn_blocks[:lent], lent_back), attn_blocks[lent:experts]], 0
    )
    attn_t = lax.all_to_all(attn_own, "dp", split_axis=0, concat_axis=0, tiled=True).reshape(
        width, rows
    )

    half_width = width // 2
    own_heads, other_heads = both(attn_t[:half_width], attn_t[half_width:])
    attn_other = swap(attn_half)
    hidden_one = (
        inputs
        + lax.dot_general(
            own_heads, attn_half, (((0,), (1,)), ((), ())), preferred_element_type=F32
        )
        + lax.dot_general(
            other_heads, attn_other, (((0,), (1,)), ((), ())), preferred_element_type=F32
        )
    )
    normed_two, hat_two, inv_two = norm_forward(hidden_one, gain_two)
    normed_two = normed_two.astype(BF16)
    rows_two, ffn_act, ffn_slope, ffn_own, ffn_other = mlp_forward(
        [(normed_two, swap(normed_two))],
        second_all,
        second_all,
        hidden,
        rows // 2,
        transposed=True,
        columns=(0, 1),
    )
    hidden_two = hidden_one + ffn_own.astype(F32) + swap(ffn_other).astype(F32)

    sent_rows = (
        matmul_tn(placer, hidden_two.astype(BF16)).astype(BF16).reshape(experts, slots_per, width)
    )
    sent_rows, counts_all = lax.optimization_barrier((sent_rows, counts_all))
    mine = jnp.sum(
        jnp.where(lax.broadcasted_iota(jnp.int32, (1, 1, experts), 2) == dp_index, counts_all.astype(F32), 0.0),
        2,
    )
    per_chip = jnp.sum(mine, 1)
    chip_before = jnp.sum(
        jnp.where(
            lax.broadcasted_iota(jnp.int32, (experts, experts), 1)
            < lax.broadcasted_iota(jnp.int32, (experts, experts), 0),
            per_chip[None, :],
            0.0,
        ),
        1,
    )
    starts = both(chip_before, chip_before + mine[:, 0])
    slot_at = lax.broadcasted_iota(jnp.int32, (1, slots_per), 1).astype(F32)
    kept = jnp.concatenate(
        [(start[:, None] + slot_at < capacity).reshape(-1, 1) for start in starts], 0
    )
    own_rows, sent_grad, kept = lax.optimization_barrier((to_experts(sent_rows), sent_grad, kept))
    own_rows = own_rows.reshape(half_rows, width)
    grad_own = to_experts(sent_grad).reshape(half_rows, width)
    centre = centroids[0]
    length = half_rows // 2
    expert_rows, act_a, slope_a, own_a, other_a, gate_column = mlp_forward(
        [(own_rows, swap(own_rows))],
        expert_in_a[0],
        expert_out_a[0],
        hidden,
        length,
        centre=centroids,
    )
    from_a = (swap(other_a), swap(own_a))
    middle, act_b, slope_b, own_b, other_b = mlp_forward(
        [expert_rows, (own_a, other_a), from_a], expert_in_b[0], expert_out_b[0], hidden, length
    )
    own_b, grad_own = lax.optimization_barrier((own_b, grad_own))
    branch_half = (
        own_a.astype(F32) + from_a[0].astype(F32) + own_b.astype(F32) + swap(other_b).astype(F32)
    )
    gate_value = gate_column[:, 0]
    gate_half = gate_value[:half_rows]
    returned = (
        jnp.where(kept[:half_rows], gate_half[:, None] * branch_half, 0.0)
        .astype(BF16)
        .reshape(experts, slots_per, width)
    )
    came_back = to_experts(returned).reshape(half_rows, width)

    kept_half = kept[:half_rows, 0]
    grad_logit_half = jnp.where(
        kept_half,
        jnp.sum(grad_own.astype(F32) * branch_half, 1) * gate_half * (1.0 - gate_half),
        0.0,
    )
    centre_part = matmul(grad_logit_half, own_rows.astype(F32))
    kept_gate = jnp.where(kept, gate_column, 0.0)
    grad_pair = (grad_own, swap(grad_own))
    grad_b, grad_pre_b, own_m, other_m = mlp_backward(
        [grad_pair], expert_out_b[0], expert_in_b[0], slope_b, length, factor=kept_gate
    )
    from_m = (swap(other_m), swap(own_m))
    grad_a, grad_pre_a, own_x, other_x = mlp_backward(
        [grad_pair, (own_m, other_m), from_m],
        expert_out_a[0],
        expert_in_a[0],
        slope_a,
        length,
        factor=kept_gate,
    )
    grad_rows = (
        own_x.astype(F32)
        + swap(other_x).astype(F32)
        + own_m.astype(F32)
        + from_m[0].astype(F32)
        + grad_logit_half[:, None] * centre.astype(F32)[None, :]
    )
    grad_rows, came_back, act_a, grad_a, expert_rows, grad_pre_a = lax.optimization_barrier(
        (grad_rows.astype(BF16), came_back, act_a, grad_a, expert_rows, grad_pre_a)
    )
    grad_out_a = matmul_tn(act_a, grad_a)
    grad_in_a = matmul_tn(expert_rows, grad_pre_a)
    output = hidden_two + matmul(placer, came_back)
    grad_back = to_experts(grad_rows.reshape(experts, slots_per, width))
    grad_back, grad_out_a, grad_in_a = lax.optimization_barrier((grad_back, grad_out_a, grad_in_a))
    grad_back = grad_back.reshape(half_rows, width)
    grad_two = grad_out.astype(F32) + matmul(placer, grad_back)

    grad_down = grad_two.astype(BF16)
    rows_down, grad_ffn_pre, down_own, down_other = mlp_backward(
        [(grad_down, swap(grad_down))],
        second_all,
        second_all,
        ffn_slope,
        rows // 2,
        transposed=False,
        columns=(0, 1),
    )
    grad_norm_two = down_own.astype(F32) + swap(down_other).astype(F32)
    back_two = norm_backward(grad_norm_two, hat_two, inv_two, gain_two)[0]
    grad_one = grad_two + back_two

    grad_branch_one = grad_one.astype(BF16)
    grad_halves = both(
        *(
            lax.dot_general(
                part, grad_branch_one, (((0,), (1,)), ((), ())), preferred_element_type=F32
            ).astype(BF16)
            for part in (attn_half, attn_other)
        )
    )
    grad_attn, rows_down, ffn_act, rows_two, grad_ffn_pre = lax.optimization_barrier(
        (
            jnp.concatenate(grad_halves, 0).reshape(heads, HEAD, rows),
            rows_down,
            ffn_act,
            rows_two,
            grad_ffn_pre,
        )
    )
    grad_by_head = lax.all_to_all(grad_attn, "dp", split_axis=0, concat_axis=0, tiled=True)
    grad_ffn_out_t = matmul_tn(rows_down, ffn_act)
    grad_ffn_in = matmul_tn(rows_two, grad_ffn_pre)
    part_own, part_other = (
        lax.dot_general(
            grad_branch_one, part, (((0,), (1,)), ((), ())), preferred_element_type=F32
        )
        for part in (own_heads, other_heads)
    )
    grad_attn_half = part_own + swap(part_other.astype(BF16)).astype(F32)
    second_part = jnp.concatenate(
        [grad_ffn_in.astype(BF16), grad_ffn_out_t.astype(BF16), grad_attn_half.astype(BF16)], 1
    )
    second_part = second_part.reshape(planes, 4, shard, -1).transpose(1, 0, 2, 3).reshape(width, -1)
    grad_by_head, second_part = lax.optimization_barrier((grad_by_head, second_part))
    second_plane = lax.psum_scatter(
        second_part,
        "dp",
        scatter_dimension=0,
        axis_index_groups=[[4 * z + k for k in range(4)] for z in range(planes)],
        tiled=True,
    )
    second_sum = lax.psum_scatter(
        second_plane,
        "dp",
        scatter_dimension=0,
        axis_index_groups=[[4 * z + k for z in range(planes)] for k in range(4)],
        tiled=True,
    ).astype(F32)
    grad_blocks = jnp.concatenate([grad_by_head, to_core_zero(grad_by_head[:lent])], 0)
    grad_own_blocks, grad_prompts = attn_backward(
        plan, own_blocks, prompt_kv, grad_blocks, attn_blocks, log_sums
    )
    lent_grad = to_core_one(grad_own_blocks[experts:])
    prompt_sum = grad_prompts.astype(F32) + to_core_zero(grad_prompts).astype(F32)
    prompt_part = jnp.concatenate(
        [
            grad_own_blocks[:experts, :HEAD],
            (grad_own_blocks[:experts, HEAD:].astype(F32) + prompt_sum).astype(BF16),
        ],
        1,
    )
    cont_part = jnp.concatenate([lent_grad, grad_own_blocks[lent:experts]], 0)
    grad_head, act_b, grad_b, middle, grad_pre_b = lax.optimization_barrier(
        (jnp.where(core_zero, prompt_part, cont_part), act_b, grad_b, middle, grad_pre_b)
    )
    grad_qkv = lax.all_to_all(grad_head, "dp", split_axis=0, concat_axis=0, tiled=True)
    grad_out_b = matmul_tn(act_b, grad_b)
    grad_in_b = matmul_tn(middle, grad_pre_b)
    grad_qkv, grad_out_b, grad_in_b = lax.optimization_barrier((grad_qkv, grad_out_b, grad_in_b))
    grad_qkv = grad_qkv.reshape(2, half_heads * triple, rows)
    keep_half, send_half = both(grad_qkv[0], grad_qkv[1])
    grad_qkv_t = jnp.concatenate([keep_half, swap(send_half)], 1)
    grad_qkv_w = lax.dot_general(
        rows_one, grad_qkv_t, (((0,), (1,)), ((), ())), preferred_element_type=F32
    ).astype(BF16)
    by_chip = grad_qkv_w.reshape(experts // 4, 2, 2, shard, half_heads * triple)
    half_columns = half_heads * triple // 2
    qkv_sum = scatter_chips(by_chip[..., :half_columns], by_chip[..., half_columns:])
    grad_norm_one = keep_rows(
        lax.dot_general(
            grad_qkv_t, qkv_full, (((0,), (1,)), ((), ())), preferred_element_type=F32
        )
    )
    back_one = norm_backward(grad_norm_one, hat_one, inv_one, gain_one)[0]
    grad_input = grad_one + back_one
    qkv_sum = qkv_sum.reshape(shard, half_heads, 3, HEAD)
    query_shard, key_shard, value_shard = (
        qkv_sum[:, :, part].reshape(shard, half_heads * HEAD) for part in range(3)
    )

    ffn_in_sum = second_sum[:, :hidden]
    gains = jnp.stack(
        [
            jnp.sum(query_shard * w_query + key_shard * w_key + value_shard * w_value, 1)
            / norm1_gain.astype(F32),
            jnp.sum(ffn_in_sum * w_ffn_in, 1) / norm2_gain.astype(F32),
        ]
    )
    gains = gains + swap(gains)
    centre_grad = centre_part + swap(centre_part)
    return (
        output.astype(BF16),
        grad_input.astype(BF16),
        gains[0],
        query_shard,
        key_shard,
        value_shard,
        second_sum[:, 2 * hidden :].T,
        gains[1],
        ffn_in_sum,
        second_sum[:, hidden : 2 * hidden].T,
        centre_grad[None, :],
        grad_in_a[None],
        grad_out_a[None],
        grad_in_b[None],
        grad_out_b[None],
    )


def solution(mesh):
    body = body_paired if fits_paired(mesh) else body_general
    return jax.shard_map(
        body,
        mesh=mesh,
        in_specs=(
            P(("dp", "tensor"), None),
            P(),
            P(("dp", "tensor"), None),
            P("dp"),
            P("dp", "tensor"),
            P("dp", "tensor"),
            P("dp", "tensor"),
            P("tensor", "dp"),
            P("dp"),
            P("dp", "tensor"),
            P("tensor", "dp"),
            P("dp", None),
            P("dp", None, "tensor"),
            P("dp", "tensor", None),
            P("dp", None, "tensor"),
            P("dp", "tensor", None),
            P(("dp", "tensor"), None),
        ),
        out_specs=(
            P(("dp", "tensor"), None),
            P(("dp", "tensor"), None),
            P("dp"),
            P("dp", "tensor"),
            P("dp", "tensor"),
            P("dp", "tensor"),
            P("tensor", "dp"),
            P("dp"),
            P("dp", "tensor"),
            P("tensor", "dp"),
            P("dp", None),
            P("dp", None, "tensor"),
            P("dp", "tensor", None),
            P("dp", None, "tensor"),
            P("dp", "tensor", None),
        ),
        check_vma=False,
    )
```
